32 devices in a mesh: row: 4 (over z), col: 8 (over y, x, core).
Axes of the slice: x: 2, y: 2, z: 4, core: 2. Of those that a mesh axis runs over, the one named last changes fastest.
Arguments:
- profiles: bfloat16 [50, 16384], P(None, ('col', 'row')), may hold values from -1.1953125 to 1.1953125
- cell_width: bfloat16 [16384], P(('col', 'row')), may hold values from 1 to 3
- basis: bfloat16 [64, 16384], P(None, ('col', 'row')), may hold values from -6 to 6
- block_lists: int32 [4, 8, 2, 128], P('row', 'col'), may hold values from 0 to 31, as said below
- block_counts: int32 [4, 8], P('row', 'col'), may hold values from 8 to 128, as said below
- landmarks: int32 [8], replicated, may hold values from 0 to 127, as said below
Outputs:
- row_scaling: float32 [16384], P('row')
- column_scaling: float32 [16384], P('col')
- ritz_basis: float32 [64, 16384], P(None, ('row', 'col'))
The draws below stay inside these ranges and needn't reach their ends.
Inputs may be any that keep to these rules, and one draw needn't show every extreme that they name: `block_lists`: in each tile the first block_counts slots name distinct blocks, row block below 32 and column block below 16; every block of the tile whose global row block and global column block differ by at most one is among them; later slots also name blocks of the tile. `block_counts`: A tile whose column cells lie among its own row cells has exactly 128 live slots. `landmarks`: Distinct, increasing, one in each aligned group of 16 consecutive blocks.
All inputs are finite; a program needn't handle non-finite values.
Results may differ from the reference program's by a relative error of at most 0.0057.
Values may be sent and summed in bfloat16 or wider, within the bound.
No kernel may reach another device: no remote copies, remote signals or barrier semaphores. Data moves between devices by JAX's collectives and lax.ppermute only.
A program may use at most 64 MiB of HBM per device.

```python
import math
import jax
import jax.numpy as jnp
from jax import lax

BLK = 128
PCS = 50
COLS = 64
SWEEPS = 3
CB = 16
RB = 32
MAXB = 128
NCELLS = 16384
NBLK = 128
LB = 8
N_ROW = 4
N_COL = 8


def tile_draw(key):
    base_key = jax.random.fold_in(key, 11)
    spread = N_COL // N_ROW
    positions = jnp.arange(RB * CB, dtype=jnp.int32)

    def one_tile(tile_number):
        tile_key = jax.random.fold_in(base_key, tile_number)
        perm_key, extra_key = jax.random.split(tile_key)
        tile_row = tile_number // N_COL
        tile_col = tile_number % N_COL
        global_row = tile_row * RB + positions // CB
        global_col = tile_col * CB + positions % CB
        banded = (jnp.abs(global_row - global_col) <= 1).astype(jnp.int32)
        shuffled = jax.random.permutation(perm_key, positions)
        chosen = shuffled[jnp.argsort(1 - banded[shuffled], stable=True)][:MAXB]
        diagonal_tile = tile_col // spread == tile_row
        extra_blocks = jax.random.randint(extra_key, (), CB // 2, 2 * CB)
        block_total = jnp.where(diagonal_tile, MAXB, jnp.sum(banded) + extra_blocks).astype(jnp.int32)
        return (jnp.stack([chosen // CB, chosen % CB]).astype(jnp.int32), block_total)
    slot_lists, totals = jax.vmap(one_tile)(jnp.arange(N_ROW * N_COL, dtype=jnp.int32))
    return (slot_lists.reshape(N_ROW, N_COL, 2, MAXB), totals.reshape(N_ROW, N_COL))


def draw_block_lists(key, part):
    return tile_draw(key)[0]


def draw_block_counts(key, part):
    return tile_draw(key)[1]


def draw_landmarks(key, part):
    offsets = jax.random.randint(jax.random.fold_in(key, 23), (LB,), 0, 16)
    return (jnp.arange(LB, dtype=jnp.int32) * 16 + offsets).astype(jnp.int32)


def levels(key, shape, cuts, least, top_value):
    level = 1.0
    for dim, parts in cuts:
        steps = jax.random.uniform(jax.random.fold_in(jax.random.fold_in(key, 6), dim), (parts,), jnp.float32, least / len(cuts), top_value / len(cuts))
        level = level * jnp.repeat(jnp.exp(steps), shape[dim] // parts).reshape((-1,) + (1,) * (len(shape) - 1 - dim))
    return level


def normal_values(own_key, shape, deviation, most, cuts=(), held_as=jnp.bfloat16):
    array = deviation * jax.random.normal(own_key, shape, jnp.float32)
    if cuts:
        array = array * levels(own_key, shape, cuts, -0.22, 0.18)
    return jnp.clip(array, -most, most).astype(held_as)


def setup_inputs(seed: int = 0) -> dict:
    keys = jax.random.split(jax.random.key(seed), 7)
    profiles = normal_values(keys[0], (PCS, NCELLS), 0.2, 1.1953125, ((1, 32),))
    cell_width = jnp.clip(jnp.exp(math.log(3.0) - 1.0986123 * jax.random.uniform(keys[1], (NCELLS,), jnp.float32) ** levels(keys[1], (NCELLS,), ((0, 32),), -0.2, 0.2)), 1.0, 3.0).astype(jnp.bfloat16)
    basis = normal_values(keys[2], (COLS, NCELLS), 1.0, 6.0, ((1, 32),))
    block_lists = draw_block_lists(jax.random.fold_in(keys[6], 71), 0)
    block_counts = draw_block_counts(jax.random.fold_in(keys[6], 71), 0)
    landmarks = draw_landmarks(jax.random.fold_in(keys[6], 71), 0)
    return dict(profiles=profiles, cell_width=cell_width, basis=basis, block_lists=block_lists, block_counts=block_counts, landmarks=landmarks)


affinity_scale = 0.001953125
highest = lax.Precision.HIGHEST

def reference(profiles, cell_width, basis, block_lists, block_counts, landmarks):
    slab_slots = 256
    row_tiles = jnp.arange(N_ROW, dtype=jnp.int32)[:, None, None]
    col_tiles = jnp.arange(N_COL, dtype=jnp.int32)[None, :, None]
    slot_index = jnp.arange(MAXB, dtype=jnp.int32)[None, None, :]
    global_rows = (row_tiles * RB + block_lists[:, :, 0, :]).reshape(-1).astype(jnp.int32)
    global_cols = (col_tiles * CB + block_lists[:, :, 1, :]).reshape(-1).astype(jnp.int32)
    live_flag = (slot_index < block_counts[:, :, None]).astype(jnp.int32).reshape(-1)
    live_order = jnp.argsort(1 - live_flag, stable=True)
    padding = jnp.zeros((slab_slots,), jnp.int32)
    row_sorted = jnp.concatenate([global_rows[live_order], padding])
    col_sorted = jnp.concatenate([global_cols[live_order], padding])
    live_sorted = jnp.concatenate([live_flag[live_order], padding]).astype(jnp.float32)
    trip_count = ((jnp.sum(live_flag) + slab_slots - 1) // slab_slots).astype(jnp.int32)
    prof_blocks = profiles.reshape(PCS, NBLK, BLK)
    square_norms = jnp.sum(jnp.square(profiles.astype(jnp.float32)), axis=0).reshape(NBLK, BLK)
    widths = cell_width.astype(jnp.float32).reshape(NBLK, BLK)

    def kernel_at(number):
        first_slot = (number * slab_slots).astype(jnp.int32)
        row_slots = lax.dynamic_slice_in_dim(row_sorted, first_slot, slab_slots)
        col_slots = lax.dynamic_slice_in_dim(col_sorted, first_slot, slab_slots)
        live_mask = lax.dynamic_slice_in_dim(live_sorted, first_slot, slab_slots)
        left_prof = jnp.take(prof_blocks, row_slots, axis=1).astype(jnp.float32)
        right_prof = jnp.take(prof_blocks, col_slots, axis=1).astype(jnp.float32)
        inner_product = jnp.einsum('pkb,pkd->kbd', left_prof, right_prof, precision=highest)
        distance = square_norms[row_slots][:, :, None] + square_norms[col_slots][:, None, :] - 2.0 * inner_product
        width_pair = widths[row_slots][:, :, None] * widths[col_slots][:, None, :]
        kernel = jnp.exp(-distance / width_pair) * (affinity_scale * live_mask)[:, None, None]
        return (kernel, row_slots, col_slots)

    def apply_affinity(update, initial):

        def advance(number, totals):
            return update(totals, kernel_at(number))
        return lax.fori_loop(0, trip_count, advance, initial)

    def column_pass(row_scaling):

        def update(totals, pieces):
            kernel, row_slots, col_slots = pieces
            partial_value = jnp.einsum('kbd,kb->kd', kernel, row_scaling[row_slots], precision=highest)
            return totals.at[col_slots].add(partial_value)
        return 1.0 / apply_affinity(update, jnp.zeros((NBLK, BLK), jnp.float32))

    def row_pass(column_scaling):

        def update(totals, pieces):
            kernel, row_slots, col_slots = pieces
            partial_value = jnp.einsum('kbd,kd->kb', kernel, column_scaling[col_slots], precision=highest)
            return totals.at[row_slots].add(partial_value)
        return 1.0 / apply_affinity(update, jnp.zeros((NBLK, BLK), jnp.float32))
    row_scaling = jnp.ones((NBLK, BLK), jnp.float32)
    column_scaling = jnp.ones((NBLK, BLK), jnp.float32)
    for sweep_number in range(SWEEPS):
        column_scaling = column_pass(row_scaling)
        row_scaling = row_pass(column_scaling)
    scaled_basis = (basis.astype(jnp.float32) * column_scaling.reshape(-1)[None, :]).astype(jnp.bfloat16)
    scaled_basis = lax.optimization_barrier(scaled_basis).astype(jnp.float32).reshape(COLS, NBLK, BLK)

    def subspace_update(totals, pieces):
        kernel, row_slots, col_slots = pieces
        picked = jnp.take(scaled_basis, col_slots, axis=1)
        half_kernel = lax.optimization_barrier(kernel.astype(jnp.bfloat16)).astype(jnp.float32)
        partial_value = jnp.einsum('ckd,kbd->ckb', picked, half_kernel, precision=highest)
        return totals.at[:, row_slots].add(partial_value)
    summed = apply_affinity(subspace_update, jnp.zeros((COLS, NBLK, BLK), jnp.float32))
    projected = summed.reshape(COLS, NCELLS) * row_scaling.reshape(-1)[None, :]
    landmark_mask = jnp.zeros((NBLK,), jnp.float32).at[landmarks].set(1.0)
    cell_mask = jnp.repeat(landmark_mask, BLK)
    masked = projected * cell_mask[None, :]
    gram_matrix = jnp.dot(masked, masked.T, precision=highest) / (LB * BLK)
    lower_factor = jnp.linalg.cholesky(gram_matrix)
    ritz_basis = jax.scipy.linalg.solve_triangular(lower_factor, projected, lower=True)
    return (row_scaling.reshape(-1), column_scaling.reshape(-1), ritz_basis)
```

```python
import functools

import jax
import jax.numpy as jnp
from jax import lax
from jax.experimental import pallas as pl
from jax.experimental.pallas import tpu as pltpu
from jax.sharding import PartitionSpec as P

BLK = 128
SWEEPS = 3
GROUP = 8
FEAT = 64
PIECES = 16
SCALE = 512.0
LOG2E = 1.4426950408889634
F32 = jnp.float32
BF16 = jnp.bfloat16
MIB = 1 << 20

VMEM_SPEC = pl.BlockSpec(memory_space=pltpu.VMEM)
SMEM_SPEC = pl.BlockSpec(memory_space=pltpu.SMEM)


def split3(x):
    high = x.astype(BF16).astype(F32)
    mid = (x - high).astype(BF16).astype(F32)
    low = (x - high - mid).astype(BF16).astype(F32)
    return high, mid, low


def tree_sum(values):
    values = list(values)
    while len(values) > 1:
        values = [a + b for a, b in zip(values[::2], values[1::2])]
    return values[0]


def call(kernel, outs, ins, scratch=(), limit=24, flops=1 << 24):
    args, specs = [], []
    for kind, array in ins:
        if kind == "smem":
            specs.append(SMEM_SPEC)
        else:
            specs.append(VMEM_SPEC)
            if kind == "keep":
                array = pltpu.with_memory_space_constraint(array, pltpu.VMEM)
        args.append(array)
    return pl.pallas_call(
        kernel,
        out_shape=tuple(outs),
        in_specs=specs,
        out_specs=tuple(VMEM_SPEC for _ in outs),
        scratch_shapes=list(scratch),
        compiler_params=pltpu.CompilerParams(vmem_limit_bytes=limit * MIB),
        cost_estimate=pl.CostEstimate(flops=flops, bytes_accessed=1 << 20, transcendentals=0),
    )(*args)


def pack_kernel(prof_ref, width_ref, out_ref, work):
    pcs = prof_ref.shape[0]
    prof = prof_ref[...].astype(F32)
    norm = jnp.sum(prof * prof, axis=0, keepdims=True)
    high, mid, low = split3(norm)
    work[...] = jnp.zeros_like(work)
    work[0:pcs, :] = prof
    work[pcs : pcs + 1, :] = high
    work[pcs + 1 : pcs + 2, :] = mid
    work[pcs + 2 : pcs + 3, :] = low
    work[pcs + 3 : pcs + 6, :] = jnp.ones((3, prof.shape[1]), F32)
    work[pcs + 6 : pcs + 7, :] = width_ref[...].astype(F32)
    out_ref[...] = work[...].astype(BF16)


def slot_loop(meta, step, count, group=GROUP):
    def advance(number, carry):
        for i in range(group):
            step(number * group + i)
        return carry

    lax.fori_loop(0, (count + group - 1) // group, advance, 0)


def build_kernel(pcs, n_row, n_col, *refs):
    meta = refs[0]
    col_in = refs[1 : 1 + n_row]
    row_in = refs[1 + n_row : 1 + n_row + n_col]
    tile, part, row_prof, row_inv, col_prof, col_inv, acc = refs[1 + n_row + n_col :]
    per = col_in[0].shape[1] // BLK
    col_blocks = n_row * per
    total, me_row, me_col = meta[2, 0], meta[2, 2], meta[2, 3]
    for k in range(n_col):
        piece = lax.bitwise_xor(me_col, k)
        for j in range(per):
            block = row_in[k][:, j * BLK : (j + 1) * BLK]
            row_prof[piece * per + j] = block
            width = block.astype(F32)[pcs + 6 : pcs + 7, :]
            row_inv[piece * per + j] = jnp.broadcast_to(1.0 / width, (8, BLK))
    rows = lax.broadcasted_iota(jnp.int32, (FEAT, BLK), 0)
    for k in range(n_row):
        piece = lax.bitwise_xor(me_row, k)
        for j in range(per):
            block = col_in[k][:, j * BLK : (j + 1) * BLK].astype(F32)
            left = jnp.where(rows < pcs, -2.0 * block, 0.0)
            left = jnp.where((rows >= pcs) & (rows < pcs + 3), 1.0, left)
            left = jnp.where(
                (rows >= pcs + 3) & (rows < pcs + 6), pltpu.roll(block, 3, 0), left
            )
            left = jnp.where(rows == pcs + 7, pltpu.roll(block, 1, 0), left)
            left = left.T
            col_prof[piece * per + j] = left.astype(BF16)
            col_inv[piece * per + j] = jnp.broadcast_to(
                -LOG2E / left[:, pcs + 7 : pcs + 8], (BLK, BLK)
            )
    acc[...] = jnp.zeros_like(acc)
    lead = (lax.broadcasted_iota(jnp.int32, (PIECES, BLK), 0) == 0).astype(F32).astype(BF16)

    def step(s):
        rb, cb = meta[0, s], meta[1, s]
        target = jnp.where(s < total, cb, col_blocks)
        distance = jnp.dot(col_prof[cb], row_prof[rb], preferred_element_type=F32)
        block = jnp.exp2(distance * col_inv[cb] * row_inv[rb][0:1, :]).astype(BF16)
        tile[s] = block
        sums = lax.dot_general(
            lead, block, (((1,), (1,)), ((), ())), preferred_element_type=F32
        )
        acc[target] += sums[0:8]

    slot_loop(meta, step, total)
    part[...] = jnp.sum(acc[0:col_blocks], axis=1)


def fill_pieces(target, first, scaling):
    high, mid, low = split3(scaling)
    rows = lax.broadcasted_iota(jnp.int32, (PIECES, BLK), 0)
    shape = (PIECES, BLK)
    for b in range(scaling.shape[0]):
        value = jnp.where(
            rows == 0,
            jnp.broadcast_to(high[b : b + 1], shape),
            jnp.where(
                rows == 1,
                jnp.broadcast_to(mid[b : b + 1], shape),
                jnp.where(rows == 2, jnp.broadcast_to(low[b : b + 1], shape), 0.0),
            ),
        )
        target[b, first : first + PIECES, :] = value.astype(BF16)


def pass_kernel(over_rows, n_parts, *refs):
    meta, tile = refs[0], refs[1]
    parts = refs[2 : 2 + n_parts]
    out, left, acc = refs[2 + n_parts :]
    total = meta[2, 0]
    blocks = out.shape[0]
    scaling = SCALE / tree_sum([p[...] for p in parts])
    fill_pieces(left, 0, scaling)
    acc[...] = jnp.zeros_like(acc)
    dims = (((1,), (0,)), ((), ())) if over_rows else (((1,), (1,)), ((), ()))

    def step(s):
        rb, cb = meta[0, s], meta[1, s]
        source, target = (cb, rb) if over_rows else (rb, cb)
        target = jnp.where(s < total, target, blocks)
        sums = lax.dot_general(left[source], tile[s], dims, preferred_element_type=F32)
        acc[target] += sums[0:8]

    slot_loop(meta, step, total)
    out[...] = jnp.sum(acc[0:blocks], axis=1)


def last_row_kernel(n_row, n_land, *refs):
    meta, tile = refs[0], refs[1]
    parts = refs[2 : 2 + n_row]
    bases = refs[2 + n_row : 2 + 2 * n_row]
    out, land, scaling_out, scaled, left, acc, land_acc = refs[2 + 2 * n_row :]
    total, n_slots, me_row = meta[2, 0], meta[2, 1], meta[2, 2]
    blocks = out.shape[0]
    per = bases[0].shape[1] // BLK
    scaling_out[...] = SCALE / tree_sum([p[...] for p in parts])
    scaling = scaling_out[...]
    fill_pieces(left, 0, scaling)
    for k in range(n_row):
        piece = lax.bitwise_xor(me_row, k)
        for j in range(per):
            block = bases[k][:, j * BLK : (j + 1) * BLK].astype(F32)
            scaled[piece * per + j] = (
                block * scaling_out[pl.ds(piece * per + j, 1), :]
            ).astype(BF16)
    acc[...] = jnp.zeros_like(acc)
    land_acc[...] = jnp.zeros_like(land_acc)

    def land_step(s):
        rb, cb = meta[0, s], meta[1, s]
        which = 0
        for i in range(1, n_land):
            which = jnp.where(rb == meta[2, 4 + i], i, which)
        which = jnp.where(s < n_slots, which, n_land)
        land_acc[which] += jnp.dot(scaled[cb], tile[s], preferred_element_type=F32)

    slot_loop(meta, land_step, n_slots, 4)
    land[...] = land_acc[0:n_land].astype(land.dtype)

    def step(s):
        rb, cb = meta[0, s], meta[1, s]
        target = jnp.where(s < total, rb, blocks)
        sums = jnp.dot(left[cb], tile[s], preferred_element_type=F32)
        acc[target] += sums[0:8]

    slot_loop(meta, step, total)
    out[...] = jnp.sum(acc[0:blocks], axis=1)


def mixed_kernel(n_col, *refs):
    meta, tile, scaled = refs[:3]
    outs = refs[3 : 3 + n_col]
    acc = refs[3 + n_col]
    per = outs[0].shape[0]
    blocks = n_col * per
    total, me_col = meta[2, 0], meta[2, 3]
    acc[...] = jnp.zeros_like(acc)

    def step(s):
        rb, cb = meta[0, s], meta[1, s]
        target = jnp.where(s < total, rb, blocks)
        acc[target] += jnp.dot(scaled[cb], tile[s], preferred_element_type=F32)

    slot_loop(meta, step, total)
    for k in range(n_col):
        piece = lax.bitwise_xor(me_col, k)
        outs[k][...] = acc[pl.ds(piece * per, per)].astype(outs[k].dtype)


def gram_kernel(n_col, n_land, *refs):
    meta = refs[0]
    parts = refs[1 : 1 + n_col]
    lands = refs[1 + n_col : 1 + 2 * n_col]
    gram, scaling_out, inverse = refs[1 + 2 * n_col :]
    inverse[...] = 1.0 / tree_sum([p[...] for p in parts])
    scaling_out[...] = SCALE * inverse[...]
    total = None
    for i in range(n_land):
        summed = tree_sum([m[i].astype(F32) for m in lands])
        projected = summed * inverse[pl.ds(meta[2, 4 + i], 1), :]
        product = lax.dot_general(
            projected,
            projected,
            (((1,), (1,)), ((), ())),
            precision=lax.Precision.HIGHEST,
            preferred_element_type=F32,
        )
        total = product if total is None else total + product
    gram[...] = total


def ritz_kernel(n_row, n_col, cells, *refs):
    meta = refs[0]
    grams = refs[1 : 1 + n_row]
    shares = refs[1 + n_row : 1 + n_row + n_col]
    scaling, out = refs[1 + n_row + n_col :]
    per, cols = shares[0].shape[0], shares[0].shape[1]
    me_col = meta[2, 3]
    gram = tree_sum([g[...] for g in grams]) * (1.0 / cells)
    rows = lax.broadcasted_iota(jnp.int32, (cols, 2 * cols), 0)
    lanes = lax.broadcasted_iota(jnp.int32, (cols, 2 * cols), 1)
    unit = (lax.broadcasted_iota(jnp.int32, (cols, cols), 0)
            == lax.broadcasted_iota(jnp.int32, (cols, cols), 1)).astype(F32)
    work = jnp.concatenate([gram, unit], axis=1)
    for j in range(cols):
        root = lax.rsqrt(work[j : j + 1, j : j + 1])
        upper = work[j : j + 1, :] * root
        lower = work[:, j : j + 1] * root
        work = jnp.where(
            rows > j, work - lower * upper, jnp.where(rows == j, upper, work)
        )
    inverse = work[:, cols:]
    for j in range(per):
        summed = tree_sum([m[j].astype(F32) for m in shares])
        projected = summed * (scaling[pl.ds(me_col * per + j, 1), :] * (1.0 / SCALE))
        out[:, j * BLK : (j + 1) * BLK] = jnp.dot(
            inverse, projected, precision=lax.Precision.HIGHEST, preferred_element_type=F32
        )


def exchange(x, axis):
    n = lax.axis_size(axis)
    return [x] + [
        lax.ppermute(x, axis, [(i, i ^ k) for i in range(n)]) for k in range(1, n)
    ]


def vec(*arrays):
    return [("vmem", a) for a in arrays]


def slot_table(block_lists, block_counts, landmarks, row_blocks, n_land):
    slots = block_lists.shape[-1]
    total = block_counts[0, 0]
    me_row, me_col = lax.axis_index("row"), lax.axis_index("col")
    own = lax.dynamic_slice_in_dim(landmarks, me_row * n_land, n_land) - me_row * row_blocks
    rows, cols = block_lists[0, 0, 0], block_lists[0, 0, 1]
    index = jnp.arange(slots, dtype=jnp.int32)
    live = index < total
    marked = live & jnp.any(rows[:, None] == own[None, :], axis=1)
    key = jnp.where(marked, 0, jnp.where(live, 1, 2)) * slots + index
    place = jnp.sum((key[None, :] < key[:, None]).astype(jnp.int32), axis=1)
    chosen = (place[:, None] == index[None, :]).astype(jnp.int32)
    lists = jnp.sum(chosen[None] * jnp.stack([rows, cols])[:, :, None], axis=1)
    scalars = jnp.concatenate(
        [
            jnp.stack([total, jnp.sum(marked.astype(jnp.int32)), me_row, me_col]),
            own,
            jnp.zeros((slots - 4 - n_land,), jnp.int32),
        ]
    )
    return jnp.concatenate([lists, scalars[None]], axis=0)


def body(profiles, cell_width, basis, block_lists, block_counts, landmarks):
    n_row, n_col = lax.axis_size("row"), lax.axis_size("col")
    pcs, share = profiles.shape
    cols = basis.shape[0]
    per = share // BLK
    row_blocks, col_blocks = n_col * per, n_row * per
    slots = block_lists.shape[-1]
    n_land = landmarks.shape[0] // n_row

    def shape(*dims, dtype=F32):
        return jax.ShapeDtypeStruct(dims, dtype)

    (packed,) = call(
        pack_kernel,
        [shape(FEAT, share, dtype=BF16)],
        vec(profiles, cell_width.reshape(1, share)),
        [pltpu.VMEM((FEAT, share), F32)],
    )
    spread = lax.ppermute(
        packed,
        ("row", "col"),
        [((q % n_row) * n_col + q // n_row, q) for q in range(n_row * n_col)],
    )
    col_packs = exchange(packed, "row")
    row_packs = exchange(spread, "col")
    bases = exchange(basis, "row")
    meta = slot_table(block_lists, block_counts, landmarks, row_blocks, n_land)
    tile, part = call(
        functools.partial(build_kernel, pcs, n_row, n_col),
        [pltpu.VMEM((slots, BLK, BLK), BF16), shape(col_blocks, BLK)],
        [("smem", meta)] + vec(*col_packs, *row_packs),
        [
            pltpu.VMEM((row_blocks, FEAT, BLK), BF16),
            pltpu.VMEM((row_blocks, 8, BLK), F32),
            pltpu.VMEM((col_blocks, BLK, FEAT), BF16),
            pltpu.VMEM((col_blocks, BLK, BLK), F32),
            pltpu.VMEM((col_blocks + 1, 8, BLK), F32),
        ],
    )
    for _ in range(SWEEPS - 1):
        parts = exchange(part, "row")
        (part,) = call(
            functools.partial(pass_kernel, True, n_row),
            [shape(row_blocks, BLK)],
            [("smem", meta), ("keep", tile)] + vec(*parts),
            [
                pltpu.VMEM((col_blocks, PIECES, BLK), BF16),
                pltpu.VMEM((row_blocks + 1, 8, BLK), F32),
            ],
        )
        parts = exchange(part, "col")
        (part,) = call(
            functools.partial(pass_kernel, False, n_col),
            [shape(col_blocks, BLK)],
            [("smem", meta), ("keep", tile)] + vec(*parts),
            [
                pltpu.VMEM((row_blocks, PIECES, BLK), BF16),
                pltpu.VMEM((col_blocks + 1, 8, BLK), F32),
            ],
        )
    parts = exchange(part, "row")
    row_part, land, col_scaling, scaled = call(
        functools.partial(last_row_kernel, n_row, n_land),
        [
            shape(row_blocks, BLK),
            shape(n_land, cols, BLK, dtype=BF16),
            shape(col_blocks, BLK),
            shape(col_blocks, cols, BLK, dtype=BF16),
        ],
        [("smem", meta), ("keep", tile)] + vec(*parts, *bases),
        [
            pltpu.VMEM((col_blocks, PIECES, BLK), BF16),
            pltpu.VMEM((row_blocks + 1, 8, BLK), F32),
            pltpu.VMEM((n_land + 1, cols, BLK), F32),
        ],
    )
    row_parts = exchange(row_part, "col")
    lands = exchange(land, "col")
    mixed = call(
        functools.partial(mixed_kernel, n_col),
        [shape(per, cols, BLK, dtype=BF16)] * n_col,
        [("smem", meta), ("keep", tile)] + vec(scaled),
        [pltpu.VMEM((row_blocks + 1, cols, BLK), F32)],
    )
    shares = [mixed[0]] + [
        lax.ppermute(mixed[k], "col", [(i, i ^ k) for i in range(n_col)])
        for k in range(1, n_col)
    ]
    gram, row_scaling = call(
        functools.partial(gram_kernel, n_col, n_land),
        [shape(cols, cols), shape(row_blocks, BLK)],
        [("smem", meta)] + vec(*row_parts, *lands),
        [pltpu.VMEM((row_blocks, BLK), F32)],
    )
    grams = exchange(gram, "row")
    (ritz,) = call(
        functools.partial(ritz_kernel, n_row, n_col, landmarks.shape[0] * BLK),
        [shape(cols, share)],
        [("smem", meta)] + vec(*grams, *shares, row_scaling),
    )
    return row_scaling.reshape(-1), col_scaling.reshape(-1), ritz


def solution(mesh):
    placed = (
        P(None, ("col", "row")),
        P(("col", "row")),
        P(None, ("col", "row")),
        P("row", "col", None, None),
        P("row", "col"),
        P(),
    )
    return jax.shard_map(
        body,
        mesh=mesh,
        in_specs=placed,
        out_specs=(P("row"), P("col"), P(None, ("row", "col"))),
        check_vma=False,
    )
```

```python
import functools

import jax
import jax.numpy as jnp
from jax import lax
from jax.experimental import pallas as pl
from jax.experimental.pallas import tpu as pltpu
from jax.sharding import PartitionSpec as P

BLK = 128
SWEEPS = 3
GROUP = 16
FEAT = 64
PIECES = 16
SCALE = 512.0
LOG2E = 1.4426950408889634
F32 = jnp.float32
BF16 = jnp.bfloat16
MIB = 1 << 20

VMEM_SPEC = pl.BlockSpec(memory_space=pltpu.VMEM)
SMEM_SPEC = pl.BlockSpec(memory_space=pltpu.SMEM)


def split3(x):
    high = x.astype(BF16).astype(F32)
    mid = (x - high).astype(BF16).astype(F32)
    low = (x - high - mid).astype(BF16).astype(F32)
    return high, mid, low


def tree_sum(values):
    values = list(values)
    while len(values) > 1:
        values = [a + b for a, b in zip(values[::2], values[1::2])]
    return values[0]


def call(kernel, outs, ins, scratch=(), limit=24, flops=1 << 24):
    args, specs = [], []
    for kind, array in ins:
        if kind == "smem":
            specs.append(SMEM_SPEC)
        else:
            specs.append(VMEM_SPEC)
            if kind == "keep":
                array = pltpu.with_memory_space_constraint(array, pltpu.VMEM)
        args.append(array)
    return pl.pallas_call(
        kernel,
        out_shape=tuple(outs),
        in_specs=specs,
        out_specs=tuple(VMEM_SPEC for _ in outs),
        scratch_shapes=list(scratch),
        compiler_params=pltpu.CompilerParams(vmem_limit_bytes=limit * MIB),
        cost_estimate=pl.CostEstimate(flops=flops, bytes_accessed=1 << 20, transcendentals=0),
    )(*args)


def pack_kernel(prof_ref, width_ref, out_ref, work):
    pcs = prof_ref.shape[0]
    prof = prof_ref[...].astype(F32)
    norm = jnp.sum(prof * prof, axis=0, keepdims=True)
    high, mid, low = split3(norm)
    work[...] = jnp.zeros_like(work)
    work[0:pcs, :] = prof
    work[pcs : pcs + 1, :] = high
    work[pcs + 1 : pcs + 2, :] = mid
    work[pcs + 2 : pcs + 3, :] = low
    work[pcs + 3 : pcs + 6, :] = jnp.ones((3, prof.shape[1]), F32)
    work[pcs + 6 : pcs + 7, :] = width_ref[...].astype(F32)
    send(out_ref, work[...].astype(BF16))


def slot_loop(compute, store, count, group):
    def advance(number, carry):
        slots = [number * group + i for i in range(group)]
        values = [compute(s) for s in slots]
        for s, value in zip(slots, values):
            store(s, value)
        return carry

    lax.fori_loop(0, (count + group - 1) // group, advance, 0)


def build_kernel(
    pcs, meta, col_in, row_in, tile, part, row_prof, row_inv, col_prof, col_inv, acc
):
    n_row, n_col = col_in.shape[0], row_in.shape[0]
    per = col_in.shape[2] // BLK
    col_blocks = n_row * per
    total = meta[2, 0]
    for k in range(n_col):
        for j in range(per):
            block = row_in[k, :, j * BLK : (j + 1) * BLK]
            row_prof[k * per + j] = block
            width = block.astype(F32)[pcs + 6 : pcs + 7, :]
            row_inv[k * per + j] = jnp.broadcast_to(1.0 / width, (8, BLK))
    rows = lax.broadcasted_iota(jnp.int32, (FEAT, BLK), 0)
    for k in range(n_row):
        piece = k
        for j in range(per):
            block = col_in[k, :, j * BLK : (j + 1) * BLK].astype(F32)
            left = jnp.where(rows < pcs, -2.0 * block, 0.0)
            left = jnp.where((rows >= pcs) & (rows < pcs + 3), 1.0, left)
            left = jnp.where(
                (rows >= pcs + 3) & (rows < pcs + 6), pltpu.roll(block, 3, 0), left
            )
            left = jnp.where(rows == pcs + 7, pltpu.roll(block, 1, 0), left)
            left = left.T
            col_prof[piece * per + j] = left.astype(BF16)
            col_inv[piece * per + j] = jnp.broadcast_to(
                -LOG2E / left[:, pcs + 7 : pcs + 8], (BLK, BLK)
            )
    acc[...] = jnp.zeros_like(acc)
    lead = (lax.broadcasted_iota(jnp.int32, (PIECES, BLK), 0) == 0).astype(F32).astype(BF16)

    def distance(s):
        return jnp.dot(
            col_prof[meta[1, s]], row_prof[meta[0, s]], preferred_element_type=F32
        )

    def advance(number, carry):
        slots_now = [number * 8 + i for i in range(8)]
        ahead = distance(slots_now[0])
        sums = []
        for i, s in enumerate(slots_now):
            now = ahead
            rb, cb = meta[0, s], meta[1, s]
            scale = col_inv[cb]
            inverse = row_inv[rb][0:1, :]
            if i + 1 < len(slots_now):
                ahead = distance(slots_now[i + 1])
            block = jnp.exp2(now * scale * inverse).astype(BF16)
            tile[s] = block
            sums.append(
                lax.dot_general(
                    lead, block, (((1,), (1,)), ((), ())), preferred_element_type=F32
                )
            )
        for s, value in zip(slots_now, sums):
            target = jnp.where(s < total, meta[1, s], col_blocks)
            acc[target] += value[0:8]
        return carry

    lax.fori_loop(0, (total + 7) // 8, advance, 0)
    send(part, jnp.sum(acc[0:col_blocks], axis=1))


def send(target, value):
    target[...] = jnp.broadcast_to(value[None], target.shape)


def fill_pieces(target, first, scaling):
    high, mid, low = split3(scaling)
    rows = lax.broadcasted_iota(jnp.int32, (PIECES, BLK), 0)
    shape = (PIECES, BLK)
    for b in range(scaling.shape[0]):
        value = jnp.where(
            rows == 0,
            jnp.broadcast_to(high[b : b + 1], shape),
            jnp.where(
                rows == 1,
                jnp.broadcast_to(mid[b : b + 1], shape),
                jnp.where(rows == 2, jnp.broadcast_to(low[b : b + 1], shape), 0.0),
            ),
        )
        target[b, first : first + PIECES, :] = value.astype(BF16)


def pass_kernel(over_rows, meta, tile, parts, out, left, acc):
    total = meta[2, 0]
    blocks = out.shape[1]
    scaling = SCALE / tree_sum([parts[i] for i in range(parts.shape[0])])
    fill_pieces(left, 0, scaling)
    acc[...] = jnp.zeros_like(acc)
    dims = (((1,), (0,)), ((), ())) if over_rows else (((1,), (1,)), ((), ()))
    source, target = (1, 0) if over_rows else (0, 1)

    def compute(s):
        return lax.dot_general(
            left[meta[source, s]], tile[s], dims, preferred_element_type=F32
        )

    def store(s, value):
        acc[jnp.where(s < total, meta[target, s], blocks)] += value[0:8]

    slot_loop(compute, store, total, GROUP)
    send(out, jnp.sum(acc[0:blocks], axis=1))


def last_row_kernel(
    n_land, meta, tile, parts, bases, out, land, scaling_out, scaled, left, acc, land_acc
):
    total, n_slots = meta[2, 0], meta[2, 1]
    blocks = out.shape[1]
    per = bases.shape[2] // BLK
    scaling = SCALE / tree_sum([parts[i] for i in range(parts.shape[0])])
    scaling_out[...] = scaling
    fill_pieces(left, 0, scaling)
    for k in range(bases.shape[0]):
        for j in range(per):
            block = bases[k, :, j * BLK : (j + 1) * BLK].astype(F32)
            b = k * per + j
            scaled[b] = (block * scaling[b : b + 1, :]).astype(BF16)
    acc[...] = jnp.zeros_like(acc)
    land_acc[...] = jnp.zeros_like(land_acc)

    def mix(s):
        return jnp.dot(scaled[meta[1, s]], tile[s], preferred_element_type=F32)

    def land_store(s, value):
        which = 0
        for i in range(1, n_land):
            which = jnp.where(meta[0, s] == meta[2, 4 + i], i, which)
        land_acc[jnp.where(s < n_slots, which, n_land)] += value

    slot_loop(mix, land_store, n_slots, 4)
    send(land, land_acc[0:n_land].astype(land.dtype))

    def compute(s):
        return jnp.dot(left[meta[1, s]], tile[s], preferred_element_type=F32)

    def store(s, value):
        acc[jnp.where(s < total, meta[0, s], blocks)] += value[0:8]

    slot_loop(compute, store, total, GROUP)
    send(out, jnp.sum(acc[0:blocks], axis=1))


def mixed_kernel(meta, tile, scaled, out, acc):
    n_col, per = out.shape[:2]
    blocks = n_col * per
    total = meta[2, 0]
    acc[...] = jnp.zeros_like(acc)

    def mix(s):
        return jnp.dot(scaled[meta[1, s]], tile[s], preferred_element_type=F32)

    def store(s, value):
        acc[jnp.where(s < total, meta[0, s], blocks)] += value

    slot_loop(mix, store, total, 4)
    for k in range(n_col):
        out[k] = acc[k * per : (k + 1) * per].astype(out.dtype)


def gram_kernel(n_land, meta, parts, lands, gram, scaling_out, inverse):
    n_col = parts.shape[0]
    inverse[...] = 1.0 / tree_sum([parts[i] for i in range(n_col)])
    scaling_out[...] = SCALE * inverse[...]
    total = None
    for i in range(n_land):
        summed = tree_sum([lands[k, i].astype(F32) for k in range(n_col)])
        projected = summed * inverse[pl.ds(meta[2, 4 + i], 1), :]
        product = lax.dot_general(
            projected,
            projected,
            (((1,), (1,)), ((), ())),
            precision=lax.Precision.HIGHEST,
            preferred_element_type=F32,
        )
        total = product if total is None else total + product
    send(gram, jnp.concatenate([total, jnp.zeros_like(total)], axis=1))


def ritz_kernel(cells, meta, grams, shares, scaling, out):
    n_col, per, cols = shares.shape[:3]
    me_col = meta[2, 3]
    gram = tree_sum([grams[i][:, :cols] for i in range(grams.shape[0])]) * (1.0 / cells)
    rows = lax.broadcasted_iota(jnp.int32, (cols, 2 * cols), 0)
    lanes = lax.broadcasted_iota(jnp.int32, (cols, 2 * cols), 1)
    unit = (lax.broadcasted_iota(jnp.int32, (cols, cols), 0)
            == lax.broadcasted_iota(jnp.int32, (cols, cols), 1)).astype(F32)
    work = jnp.concatenate([gram, unit], axis=1)
    for j in range(cols):
        root = lax.rsqrt(work[j : j + 1, j : j + 1])
        upper = work[j : j + 1, :] * root
        lower = work[:, j : j + 1] * root
        work = jnp.where(
            rows > j, work - lower * upper, jnp.where(rows == j, upper, work)
        )
    inverse = work[:, cols:]
    for j in range(per):
        summed = tree_sum([shares[k, j].astype(F32) for k in range(n_col)])
        projected = summed * (scaling[pl.ds(me_col * per + j, 1), :] * (1.0 / SCALE))
        out[:, j * BLK : (j + 1) * BLK] = jnp.dot(
            inverse, projected, precision=lax.Precision.HIGHEST, preferred_element_type=F32
        )


def exchange(x, axis):
    return lax.all_to_all(x, axis, 0, 0, tiled=True)


def vec(*arrays):
    return [("vmem", a) for a in arrays]


def slot_table(block_lists, block_counts, landmarks, row_blocks, n_land):
    slots = block_lists.shape[-1]
    total = block_counts[0, 0]
    me_row, me_col = lax.axis_index("row"), lax.axis_index("col")
    own = lax.dynamic_slice_in_dim(landmarks, me_row * n_land, n_land) - me_row * row_blocks
    rows, cols = block_lists[0, 0, 0], block_lists[0, 0, 1]
    index = jnp.arange(slots, dtype=jnp.int32)
    live = index < total
    marked = live & jnp.any(rows[:, None] == own[None, :], axis=1)
    key = jnp.where(marked, 0, jnp.where(live, 1, 2)) * slots + index
    place = jnp.sum((key[None, :] < key[:, None]).astype(jnp.int32), axis=1)
    chosen = (place[:, None] == index[None, :]).astype(jnp.int32)
    lists = jnp.sum(chosen[None] * jnp.stack([rows, cols])[:, :, None], axis=1)
    scalars = jnp.concatenate(
        [
            jnp.stack([total, jnp.sum(marked.astype(jnp.int32)), me_row, me_col]),
            own,
            jnp.zeros((slots - 4 - n_land,), jnp.int32),
        ]
    )
    return jnp.concatenate([lists, scalars[None]], axis=0)


def body(profiles, cell_width, basis, block_lists, block_counts, landmarks):
    n_row, n_col = lax.axis_size("row"), lax.axis_size("col")
    pcs, share = profiles.shape
    cols = basis.shape[0]
    per = share // BLK
    row_blocks, col_blocks = n_col * per, n_row * per
    slots = block_lists.shape[-1]
    n_land = landmarks.shape[0] // n_row

    def shape(*dims, dtype=F32):
        return jax.ShapeDtypeStruct(dims, dtype)

    (packed,) = call(
        pack_kernel,
        [shape(n_row, FEAT, share, dtype=BF16)],
        vec(profiles, cell_width.reshape(1, share)),
        [pltpu.VMEM((FEAT, share), F32)],
    )
    spread = lax.ppermute(
        packed[0],
        ("row", "col"),
        [((q % n_row) * n_col + q // n_row, q) for q in range(n_row * n_col)],
    )
    col_packs = exchange(packed, "row")
    row_packs = exchange(jnp.broadcast_to(spread[None], (n_col,) + spread.shape), "col")
    bases = exchange(jnp.broadcast_to(basis[None], (n_row,) + basis.shape), "row")
    meta = slot_table(block_lists, block_counts, landmarks, row_blocks, n_land)
    tile, part = call(
        functools.partial(build_kernel, pcs),
        [pltpu.VMEM((slots, BLK, BLK), BF16), shape(n_row, col_blocks, BLK)],
        [("smem", meta)] + vec(col_packs, row_packs),
        [
            pltpu.VMEM((row_blocks, FEAT, BLK), BF16),
            pltpu.VMEM((row_blocks, 8, BLK), F32),
            pltpu.VMEM((col_blocks, BLK, FEAT), BF16),
            pltpu.VMEM((col_blocks, BLK, BLK), F32),
            pltpu.VMEM((col_blocks + 1, 8, BLK), F32),
        ],
    )
    for _ in range(SWEEPS - 1):
        (part,) = call(
            functools.partial(pass_kernel, True),
            [shape(n_col, row_blocks, BLK)],
            [("smem", meta), ("keep", tile)] + vec(exchange(part, "row")),
            [
                pltpu.VMEM((col_blocks, PIECES, BLK), BF16),
                pltpu.VMEM((row_blocks + 1, 8, BLK), F32),
            ],
        )
        (part,) = call(
            functools.partial(pass_kernel, False),
            [shape(n_row, col_blocks, BLK)],
            [("smem", meta), ("keep", tile)] + vec(exchange(part, "col")),
            [
                pltpu.VMEM((row_blocks, PIECES, BLK), BF16),
                pltpu.VMEM((col_blocks + 1, 8, BLK), F32),
            ],
        )
    row_part, land, col_scaling, scaled = call(
        functools.partial(last_row_kernel, n_land),
        [
            shape(n_col, row_blocks, BLK),
            shape(n_col, n_land, cols, BLK, dtype=BF16),
            shape(col_blocks, BLK),
            shape(col_blocks, cols, BLK, dtype=BF16),
        ],
        [("smem", meta), ("keep", tile)] + vec(exchange(part, "row"), bases),
        [
            pltpu.VMEM((col_blocks, PIECES, BLK), BF16),
            pltpu.VMEM((row_blocks + 1, 8, BLK), F32),
            pltpu.VMEM((n_land + 1, cols, BLK), F32),
        ],
    )
    row_parts = exchange(row_part, "col")
    lands = exchange(land, "col")
    (mixed,) = call(
        mixed_kernel,
        [shape(n_col, per, cols, BLK, dtype=BF16)],
        [("smem", meta), ("keep", tile)] + vec(scaled),
        [pltpu.VMEM((row_blocks + 1, cols, BLK), F32)],
    )
    shares = exchange(mixed, "col")
    gram, row_scaling = call(
        functools.partial(gram_kernel, n_land),
        [shape(n_row, cols, 2 * cols), shape(row_blocks, BLK)],
        [("smem", meta)] + vec(row_parts, lands),
        [pltpu.VMEM((row_blocks, BLK), F32)],
    )
    (ritz,) = call(
        functools.partial(ritz_kernel, landmarks.shape[0] * BLK),
        [shape(cols, share)],
        [("smem", meta)] + vec(exchange(gram, "row"), shares, row_scaling),
    )
    return row_scaling.reshape(-1), col_scaling.reshape(-1), ritz


def solution(mesh):
    placed = (
        P(None, ("col", "row")),
        P(("col", "row")),
        P(None, ("col", "row")),
        P("row", "col", None, None),
        P("row", "col"),
        P(),
    )
    return jax.shard_map(
        body,
        mesh=mesh,
        in_specs=placed,
        out_specs=(P("row"), P("col"), P(None, ("row", "col"))),
        check_vma=False,
    )
```

```python
import functools

import jax
import jax.numpy as jnp
from jax import lax
from jax.experimental import pallas as pl
from jax.experimental.pallas import tpu as pltpu
from jax.sharding import PartitionSpec as P

BLK = 128
SWEEPS = 3
GROUP = 16
FEAT = 64
PIECES = 16
SCALE = 512.0
LOG2E = 1.4426950408889634
F32 = jnp.float32
BF16 = jnp.bfloat16
MIB = 1 << 20

VMEM_SPEC = pl.BlockSpec(memory_space=pltpu.VMEM)
SMEM_SPEC = pl.BlockSpec(memory_space=pltpu.SMEM)


def split3(x):
    high = x.astype(BF16).astype(F32)
    mid = (x - high).astype(BF16).astype(F32)
    low = (x - high - mid).astype(BF16).astype(F32)
    return high, mid, low


def tree_sum(values):
    values = list(values)
    while len(values) > 1:
        values = [a + b for a, b in zip(values[::2], values[1::2])]
    return values[0]


def call(kernel, outs, ins, scratch=(), limit=24, flops=1 << 24):
    args, specs = [], []
    for kind, array in ins:
        if kind == "smem":
            specs.append(SMEM_SPEC)
        elif kind == "any":
            specs.append(pl.BlockSpec(memory_space=pl.ANY))
        else:
            specs.append(VMEM_SPEC)
            if kind == "keep":
                array = pltpu.with_memory_space_constraint(array, pltpu.VMEM)
        args.append(array)
    return pl.pallas_call(
        kernel,
        out_shape=tuple(outs),
        in_specs=specs,
        out_specs=tuple(VMEM_SPEC for _ in outs),
        scratch_shapes=list(scratch),
        compiler_params=pltpu.CompilerParams(vmem_limit_bytes=limit * MIB),
        cost_estimate=pl.CostEstimate(flops=flops, bytes_accessed=1 << 20, transcendentals=0),
    )(*args)


def pack_kernel(prof_ref, width_ref, out_ref, work):
    pcs = prof_ref.shape[0]
    prof = prof_ref[...].astype(F32)
    norm = jnp.sum(prof * prof, axis=0, keepdims=True)
    high, mid, low = split3(norm)
    work[...] = jnp.zeros_like(work)
    work[0:pcs, :] = prof
    work[pcs : pcs + 1, :] = high
    work[pcs + 1 : pcs + 2, :] = mid
    work[pcs + 2 : pcs + 3, :] = low
    work[pcs + 3 : pcs + 6, :] = jnp.ones((3, prof.shape[1]), F32)
    work[pcs + 6 : pcs + 7, :] = width_ref[...].astype(F32)
    out_ref[...] = work[...].astype(BF16)


def slot_loop(step, count, size, group):
    def advance(number, carry):
        for i in range(0, group, size):
            step(*[number * group + i + j for j in range(size)])
        return carry

    lax.fori_loop(0, (count + group - 1) // group, advance, 0)


def shifted(me, k, n):
    return lax.rem(me + (n - k), n)


def ordered_sum(stage, refs, me):
    n = len(refs)
    for k, ref in enumerate(refs):
        stage[shifted(me, k, n)] = ref[...]
    return tree_sum([stage[i] for i in range(n)])


def square(tile, slots):
    a, b, c, d = [tile[s] for s in slots]
    return jnp.concatenate(
        [jnp.concatenate([a, b], axis=1), jnp.concatenate([c, d], axis=1)], axis=0
    )


def add_rows(acc, meta, target, slots, sums, total, spare, firsts):
    for i, (s, (row, lane)) in enumerate(zip(slots, firsts)):
        place = jnp.where(s < total, meta[target, s], spare)
        acc[place] += sums[row : row + 8, lane : lane + BLK]


def row_sums(meta, tile, left, acc, total, spare):
    def step(*slots):
        low = [left[0, meta[1, s]] for s in slots[:2]]
        high = [left[1, meta[1, s]] for s in slots[2:]]
        sums = jnp.dot(
            jnp.concatenate(low + high, axis=0),
            square(tile, slots),
            preferred_element_type=F32,
        )
        firsts = [(0, 0), (PIECES, BLK), (2 * PIECES, 0), (3 * PIECES, BLK)]
        add_rows(acc, meta, 0, slots, sums, total, spare, firsts)

    slot_loop(step, total, 4, GROUP)


def col_sums(meta, tile, left, acc, total, spare):
    def step(*slots):
        pieces = [left[i % 2, meta[0, s]] for i, s in enumerate(slots)]
        sums = lax.dot_general(
            jnp.concatenate(pieces, axis=0),
            square(tile, slots),
            (((1,), (1,)), ((), ())),
            preferred_element_type=F32,
        )
        firsts = [(0, 0), (PIECES, 0), (2 * PIECES, BLK), (3 * PIECES, BLK)]
        add_rows(acc, meta, 1, slots, sums, total, spare, firsts)

    slot_loop(step, total, 4, GROUP)


def fill_pieces(left, scaling):
    high, mid, low = split3(scaling)
    shape = (PIECES, BLK)
    rows = lax.broadcasted_iota(jnp.int32, shape, 0)
    empty = jnp.zeros(shape, F32).astype(BF16)
    for b in range(scaling.shape[0]):
        value = jnp.where(
            rows == 0,
            jnp.broadcast_to(high[b : b + 1], shape),
            jnp.where(
                rows == 1,
                jnp.broadcast_to(mid[b : b + 1], shape),
                jnp.where(rows == 2, jnp.broadcast_to(low[b : b + 1], shape), 0.0),
            ),
        ).astype(BF16)
        left[0, b] = jnp.concatenate([value, empty], axis=1)
        left[1, b] = jnp.concatenate([empty, value], axis=1)


def build_kernel(pcs, n_row, n_col, *refs):
    meta = refs[0]
    col_in = refs[1 : 1 + n_row]
    row_in = refs[1 + n_row : 1 + n_row + n_col]
    tile, part, row_prof, row_inv, col_prof, col_inv, acc, left = refs[1 + n_row + n_col :]
    per = col_in[0].shape[1] // BLK
    col_blocks, row_blocks = n_row * per, n_col * per
    total, me_row, me_col = meta[2, 0], meta[2, 2], meta[2, 3]
    chip, core = me_col // 2, lax.rem(me_col, 2)
    for k, ref in enumerate(row_in):
        piece = shifted(chip, k // 2, n_col // 2) * 2
        piece = piece + (core if k % 2 == 0 else 1 - core)
        for j in range(per):
            block = ref[:, j * BLK : (j + 1) * BLK]
            row_prof[piece * per + j] = block
            width = block.astype(F32)[pcs + 6 : pcs + 7, :]
            row_inv[piece * per + j] = jnp.broadcast_to(1.0 / width, (8, BLK))
    rows = lax.broadcasted_iota(jnp.int32, (FEAT, BLK), 0)
    for k, ref in enumerate(col_in):
        piece = shifted(me_row, k, n_row)
        for j in range(per):
            block = ref[:, j * BLK : (j + 1) * BLK].astype(F32)
            turned = jnp.where(rows < pcs, -2.0 * block, 0.0)
            turned = jnp.where((rows >= pcs) & (rows < pcs + 3), 1.0, turned)
            turned = jnp.where(
                (rows >= pcs + 3) & (rows < pcs + 6), pltpu.roll(block, 3, 0), turned
            )
            turned = jnp.where(rows == pcs + 7, pltpu.roll(block, 1, 0), turned)
            turned = turned.T
            col_prof[piece * per + j] = turned.astype(BF16)
            col_inv[piece * per + j] = jnp.broadcast_to(
                -LOG2E / turned[:, pcs + 7 : pcs + 8], (BLK, BLK)
            )

    def step(s):
        rb, cb = meta[0, s], meta[1, s]
        distance = jnp.dot(col_prof[cb], row_prof[rb], preferred_element_type=F32)
        block = jnp.exp2(distance * col_inv[cb] * row_inv[rb][0:1, :])
        tile[s] = block.astype(BF16)

    slot_loop(step, total, 1, GROUP)
    ones = (lax.broadcasted_iota(jnp.int32, (PIECES, BLK), 0) == 0).astype(F32).astype(BF16)
    empty = jnp.zeros_like(ones)
    for b in range(row_blocks):
        left[0, b] = jnp.concatenate([ones, empty], axis=1)
        left[1, b] = jnp.concatenate([empty, ones], axis=1)
    acc[...] = jnp.zeros_like(acc)
    col_sums(meta, tile, left, acc, total, col_blocks)
    part[...] = jnp.sum(acc[0:col_blocks], axis=1)


def pass_kernel(over_rows, n_parts, *refs):
    meta, tile = refs[:2]
    parts = refs[2 : 2 + n_parts]
    out, stage, left, acc = refs[-4:]
    total = meta[2, 0]
    blocks = out.shape[0]
    me = meta[2, 2] if over_rows else meta[2, 3]
    fill_pieces(left, SCALE / ordered_sum(stage, parts, me))
    acc[...] = jnp.zeros_like(acc)
    (row_sums if over_rows else col_sums)(meta, tile, left, acc, total, blocks)
    out[...] = jnp.sum(acc[0:blocks], axis=1)


def pieces_of(value):
    return [v.astype(BF16) for v in split3(value)]


def last_kernel(n_row, n_col, n_land, *refs):
    meta, tile = refs[:2]
    parts = refs[2 : 2 + n_row]
    bases = refs[2 + n_row : 2 + 2 * n_row]
    keep, away, both, scaling_out, stage, scaled, pieces, acc = refs[2 + 2 * n_row :]
    cols = bases[0].shape[0]
    per = bases[0].shape[1] // BLK
    blocks = n_col * per
    total, me_row, me_col = meta[2, 0], meta[2, 2], meta[2, 3]
    scaling = SCALE / ordered_sum(stage, parts, me_row)
    scaling_out[...] = scaling
    for k in range(n_row):
        piece = shifted(me_row, k, n_row)
        for j in range(per):
            block = bases[k][:, j * BLK : (j + 1) * BLK].astype(F32)
            b = piece * per + j
            scaled[b, 0:cols] = (block * scaling_out[pl.ds(b, 1), :]).astype(BF16)
    high, mid, low = split3(scaling)
    shape = (PIECES, BLK)
    rows = lax.broadcasted_iota(jnp.int32, shape, 0)
    for b in range(scaling.shape[0]):
        value = jnp.where(
            rows == 0,
            jnp.broadcast_to(high[b : b + 1], shape),
            jnp.where(
                rows == 1,
                jnp.broadcast_to(mid[b : b + 1], shape),
                jnp.where(rows == 2, jnp.broadcast_to(low[b : b + 1], shape), 0.0),
            ),
        )
        scaled[b, cols : cols + PIECES] = value.astype(BF16)
    acc[...] = jnp.zeros_like(acc)

    def step(s):
        target = jnp.where(s < total, meta[0, s], blocks)
        sums = jnp.dot(scaled[meta[1, s]], tile[s], preferred_element_type=F32)
        acc[target] += sums[0 : cols + 8]

    slot_loop(step, total, 1, 8)
    core = lax.rem(me_col, 2)
    for q in range(n_col // 2):
        own = (2 * q + core) * per
        other = (2 * q + 1 - core) * per
        for j in range(per):
            keep[q, j] = acc[own + j, 0:cols]
            away[q, j] = acc[other + j, 0:cols].astype(BF16)
    row_part = jnp.sum(acc[0:blocks, cols : cols + 8], axis=1)
    for i, value in enumerate(pieces_of(row_part)):
        both[i * blocks : (i + 1) * blocks] = value
    for i in range(n_land):
        first = 3 * blocks + i * cols
        both[first : first + cols] = acc[meta[2, 4 + i], 0:cols].astype(BF16)


def three(ref, blocks):
    value = ref[0 : 3 * blocks].astype(F32)
    return (value[2 * blocks :] + value[blocks : 2 * blocks]) + value[0:blocks]


def pair_kernel(n_land, *refs):
    meta, keep, away, both, both_in = refs[:5]
    outs = refs[5:]
    n_chip, per, cols = keep.shape[:3]
    blocks = 2 * n_chip * per
    chip = meta[2, 3] // 2
    share = per * cols
    summed = three(both, blocks) + three(both_in, blocks)
    parts = pieces_of(summed)
    first = 3 * blocks
    lands = both[first:].astype(F32) + both_in[first:].astype(F32)
    lands = lands.astype(BF16)
    for k, out in enumerate(outs):
        to = lax.rem(chip + k, n_chip)
        for j in range(per):
            value = keep[to, j] + away[to, j].astype(F32)
            out[j * cols : (j + 1) * cols] = value.astype(BF16)
        for i, value in enumerate(parts):
            out[share + i * blocks : share + (i + 1) * blocks] = value
        out[share + first :] = lands


def gram_kernel(n_land, cols, per, *refs):
    meta = refs[0]
    gram, scaling_out, inverse, stage, land_stage = refs[-5:]
    parts = refs[1:-5]
    n = len(parts)
    chip = meta[2, 3] // 2
    blocks = scaling_out.shape[0]
    share = per * cols
    for k, part in enumerate(parts):
        stage[shifted(chip, k, n)] = three(part.at[share : share + 3 * blocks], blocks)
    inverse[...] = 1.0 / tree_sum([stage[i] for i in range(n)])
    scaling_out[...] = SCALE * inverse[...]
    for k, part in enumerate(parts):
        land_stage[shifted(chip, k, n)] = part[share + 3 * blocks :]
    total = None
    for i in range(n_land):
        summed = tree_sum(
            [land_stage[k, i * cols : (i + 1) * cols].astype(F32) for k in range(n)]
        )
        projected = summed * inverse[pl.ds(meta[2, 4 + i], 1), :]
        product = lax.dot_general(
            projected,
            projected,
            (((1,), (1,)), ((), ())),
            precision=lax.Precision.HIGHEST,
            preferred_element_type=F32,
        )
        total = product if total is None else total + product
    gram[...] = total


def ritz_kernel(n_row, cells, *refs):
    meta = refs[0]
    grams = refs[1 : 1 + n_row]
    parts = refs[1 + n_row : -3]
    scaling, out, stage = refs[-3:]
    cols = grams[0].shape[0]
    per = out.shape[1] // BLK
    me_col = meta[2, 3]
    gram = ordered_sum(stage, grams, meta[2, 2]) * (1.0 / cells)
    rows = lax.broadcasted_iota(jnp.int32, (cols, 2 * cols), 0)
    lanes = lax.broadcasted_iota(jnp.int32, (cols, 2 * cols), 1)
    unit = (lax.broadcasted_iota(jnp.int32, (cols, cols), 0)
            == lax.broadcasted_iota(jnp.int32, (cols, cols), 1)).astype(F32)
    work = jnp.concatenate([gram, unit], axis=1)
    for j in range(cols):
        root = lax.rsqrt(work[j : j + 1, j : j + 1])
        upper = work[j : j + 1, :] * root
        lower = work[:, j : j + 1] * root
        work = jnp.where(
            rows > j, work - lower * upper, jnp.where(rows == j, upper, work)
        )
    inverse = work[:, cols:]
    for j in range(per):
        summed = tree_sum([m[j * cols : (j + 1) * cols].astype(F32) for m in parts])
        projected = summed * (scaling[pl.ds(me_col * per + j, 1), :] * (1.0 / SCALE))
        out[:, j * BLK : (j + 1) * BLK] = jnp.dot(
            inverse, projected, precision=lax.Precision.HIGHEST, preferred_element_type=F32
        )


def shift(x, axis, k):
    n = lax.axis_size(axis)
    return lax.ppermute(x, axis, [(i, (i + k) % n) for i in range(n)])


def exchange(x, axis):
    return [x] + [shift(x, axis, k) for k in range(1, lax.axis_size(axis))]


def chip_shift(x, k):
    n = lax.axis_size("col") // 2
    return lax.ppermute(
        x,
        "col",
        [(2 * q + p, 2 * ((q + k) % n) + p) for q in range(n) for p in range(2)],
    )


def sibling(x):
    return lax.ppermute(x, "col", [(i, i ^ 1) for i in range(lax.axis_size("col"))])


def vec(*arrays):
    return [("vmem", a) for a in arrays]


def slot_table(block_lists, block_counts, landmarks, row_blocks, n_land):
    slots = block_lists.shape[-1]
    total = block_counts[0, 0]
    me_row, me_col = lax.axis_index("row"), lax.axis_index("col")
    own = lax.dynamic_slice_in_dim(landmarks, me_row * n_land, n_land) - me_row * row_blocks
    rows, cols = block_lists[0, 0, 0], block_lists[0, 0, 1]
    index = jnp.arange(slots, dtype=jnp.int32)
    live = index < total
    marked = live & jnp.any(rows[:, None] == own[None, :], axis=1)
    key = jnp.where(marked, 0, jnp.where(live, 1, 2)) * slots + index
    place = jnp.sum((key[None, :] < key[:, None]).astype(jnp.int32), axis=1)
    chosen = (place[:, None] == index[None, :]).astype(jnp.int32)
    lists = jnp.sum(chosen[None] * jnp.stack([rows, cols])[:, :, None], axis=1)
    scalars = jnp.concatenate(
        [
            jnp.stack([total, jnp.sum(marked.astype(jnp.int32)), me_row, me_col]),
            own,
            jnp.zeros((slots - 4 - n_land,), jnp.int32),
        ]
    )
    return jnp.concatenate([lists, scalars[None]], axis=0)


def body(profiles, cell_width, basis, block_lists, block_counts, landmarks):
    n_row, n_col = lax.axis_size("row"), lax.axis_size("col")
    n_chip = n_col // 2
    pcs, share = profiles.shape
    cols = basis.shape[0]
    per = share // BLK
    row_blocks, col_blocks = n_col * per, n_row * per
    slots = block_lists.shape[-1]
    n_land = landmarks.shape[0] // n_row

    def shape(*dims, dtype=F32):
        return jax.ShapeDtypeStruct(dims, dtype)

    (packed,) = call(
        pack_kernel,
        [shape(FEAT, share, dtype=BF16)],
        vec(profiles, cell_width.reshape(1, share)),
        [pltpu.VMEM((FEAT, share), F32)],
    )
    spread = lax.ppermute(
        packed,
        ("row", "col"),
        [((q % n_row) * n_col + q // n_row, q) for q in range(n_row * n_col)],
    )
    col_packs = exchange(packed, "row")
    row_packs = []
    for k in range(n_chip):
        pack = chip_shift(spread, k) if k else spread
        row_packs += [pack, sibling(pack)]
    bases = exchange(basis, "row")
    meta = slot_table(block_lists, block_counts, landmarks, row_blocks, n_land)
    tile, part = call(
        functools.partial(build_kernel, pcs, n_row, n_col),
        [pltpu.VMEM((slots, BLK, BLK), BF16), shape(col_blocks, BLK)],
        [("smem", meta)] + vec(*col_packs, *row_packs),
        [
            pltpu.VMEM((row_blocks, FEAT, BLK), BF16),
            pltpu.VMEM((row_blocks, 8, BLK), F32),
            pltpu.VMEM((col_blocks, BLK, FEAT), BF16),
            pltpu.VMEM((col_blocks, BLK, BLK), F32),
            pltpu.VMEM((col_blocks + 1, 8, BLK), F32),
            pltpu.VMEM((2, row_blocks, PIECES, 2 * BLK), BF16),
        ],
        flops=1 << 33,
    )
    for number in range(SWEEPS - 1):
        early = [("any", b) for b in bases[1:]] if number == 0 else []
        (part,) = call(
            functools.partial(pass_kernel, True, n_row),
            [shape(row_blocks, BLK)],
            [("smem", meta), ("keep", tile)] + vec(*exchange(part, "row")) + early,
            [
                pltpu.VMEM((n_row, col_blocks, BLK), F32),
                pltpu.VMEM((2, col_blocks, PIECES, 2 * BLK), BF16),
                pltpu.VMEM((row_blocks + 1, 8, BLK), F32),
            ],
        )
        (part,) = call(
            functools.partial(pass_kernel, False, n_col),
            [shape(col_blocks, BLK)],
            [("smem", meta), ("keep", tile)] + vec(*exchange(part, "col")),
            [
                pltpu.VMEM((n_col, row_blocks, BLK), F32),
                pltpu.VMEM((2, row_blocks, PIECES, 2 * BLK), BF16),
                pltpu.VMEM((col_blocks + 1, 8, BLK), F32),
            ],
        )
    both_rows = 3 * row_blocks + n_land * cols
    keep, away, both, col_scaling = call(
        functools.partial(last_kernel, n_row, n_col, n_land),
        [
            shape(n_chip, per, cols, BLK),
            shape(n_chip, per, cols, BLK, dtype=BF16),
            shape(both_rows, BLK, dtype=BF16),
            shape(col_blocks, BLK),
        ],
        [("smem", meta), ("keep", tile)] + vec(*exchange(part, "row"), *bases),
        [
            pltpu.VMEM((n_row, col_blocks, BLK), F32),
            pltpu.VMEM((col_blocks, cols + PIECES, BLK), BF16),
            pltpu.VMEM((8, BLK), F32),
            pltpu.VMEM((row_blocks + 1, cols + 8, BLK), F32),
        ],
    )
    sums = call(
        functools.partial(pair_kernel, n_land),
        [shape(per * cols + both_rows, BLK, dtype=BF16)] * n_chip,
        [("smem", meta)] + vec(keep, sibling(away), both, sibling(both)),
    )
    parts = [sums[0]] + [chip_shift(sums[k], k) for k in range(1, n_chip)]
    gram, row_scaling = call(
        functools.partial(gram_kernel, n_land, cols, per),
        [shape(cols, cols), shape(row_blocks, BLK)],
        [("smem", meta)] + vec(*parts),
        [
            pltpu.VMEM((row_blocks, BLK), F32),
            pltpu.VMEM((n_chip, row_blocks, BLK), F32),
            pltpu.VMEM((n_chip, n_land * cols, BLK), BF16),
        ],
    )
    (ritz,) = call(
        functools.partial(ritz_kernel, n_row, landmarks.shape[0] * BLK),
        [shape(cols, share)],
        [("smem", meta)] + vec(*exchange(gram, "row"), *parts, row_scaling),
        [pltpu.VMEM((n_row, cols, cols), F32)],
    )
    return row_scaling.reshape(-1), col_scaling.reshape(-1), ritz


def solution(mesh):
    placed = (
        P(None, ("col", "row")),
        P(("col", "row")),
        P(None, ("col", "row")),
        P("row", "col", None, None),
        P("row", "col"),
        P(),
    )
    return jax.shard_map(
        body,
        mesh=mesh,
        in_specs=placed,
        out_specs=(P("row"), P("col"), P(None, ("row", "col"))),
        check_vma=False,
    )
```

```python
import functools

import jax
import jax.numpy as jnp
from jax import lax
from jax.experimental import pallas as pl
from jax.experimental.pallas import tpu as pltpu
from jax.sharding import PartitionSpec as P

BLK = 128
SWEEPS = 3
GROUP = 16
FEAT = 64
PIECES = 16
SCALE = 512.0
LOG2E = 1.4426950408889634
F32 = jnp.float32
BF16 = jnp.bfloat16
MIB = 1 << 20

VMEM_SPEC = pl.BlockSpec(memory_space=pltpu.VMEM)
SMEM_SPEC = pl.BlockSpec(memory_space=pltpu.SMEM)


def split3(x):
    high = x.astype(BF16).astype(F32)
    mid = (x - high).astype(BF16).astype(F32)
    low = (x - high - mid).astype(BF16).astype(F32)
    return high, mid, low


def tree_sum(values):
    values = list(values)
    while len(values) > 1:
        values = [a + b for a, b in zip(values[::2], values[1::2])]
    return values[0]


def call(kernel, outs, ins, scratch=(), limit=24, flops=1 << 24):
    args, specs = [], []
    for kind, array in ins:
        if kind == "smem":
            specs.append(SMEM_SPEC)
        elif kind == "any":
            specs.append(pl.BlockSpec(memory_space=pl.ANY))
        else:
            specs.append(VMEM_SPEC)
            if kind == "keep":
                array = pltpu.with_memory_space_constraint(array, pltpu.VMEM)
        args.append(array)
    return pl.pallas_call(
        kernel,
        out_shape=tuple(outs),
        in_specs=specs,
        out_specs=tuple(VMEM_SPEC for _ in outs),
        scratch_shapes=list(scratch),
        compiler_params=pltpu.CompilerParams(vmem_limit_bytes=limit * MIB),
        cost_estimate=pl.CostEstimate(flops=flops, bytes_accessed=1 << 20, transcendentals=0),
    )(*args)


def pack_kernel(prof_ref, width_ref, basis_ref, out_ref, all_ref, work):
    pcs = prof_ref.shape[0]
    prof = prof_ref[...].astype(F32)
    norm = jnp.sum(prof * prof, axis=0, keepdims=True)
    high, mid, low = split3(norm)
    work[...] = jnp.zeros_like(work)
    work[0:pcs, :] = prof
    work[pcs : pcs + 1, :] = high
    work[pcs + 1 : pcs + 2, :] = mid
    work[pcs + 2 : pcs + 3, :] = low
    work[pcs + 3 : pcs + 6, :] = jnp.ones((3, prof.shape[1]), F32)
    work[pcs + 6 : pcs + 7, :] = width_ref[...].astype(F32)
    packed = work[...].astype(BF16)
    out_ref[...] = packed
    all_ref[0:FEAT] = packed
    all_ref[FEAT:] = basis_ref[...]


def places():
    return lax.axis_index("row"), lax.axis_index("col")


def slot_loop(step, count, size, group):
    def advance(number, carry):
        for i in range(0, group, size):
            step(*[number * group + i + j for j in range(size)])
        return carry

    lax.fori_loop(0, (count + group - 1) // group, advance, 0)


def shifted(me, k, n):
    return lax.rem(me + (n - k), n)


def ordered_sum(stage, refs, where, n):
    for place, ref in zip(where, refs):
        stage[place] = ref[...]
    return tree_sum([stage[i] for i in range(n)])


def square(tile, slots):
    a, b, c, d = [tile[s] for s in slots]
    return jnp.concatenate(
        [jnp.concatenate([a, b], axis=1), jnp.concatenate([c, d], axis=1)], axis=0
    )


def add_rows(acc, lists, target, slots, sums, total, spare, firsts):
    for i, (s, (row, lane)) in enumerate(zip(slots, firsts)):
        place = jnp.where(s < total, lists[0, 0, target, s], spare)
        acc[place] += sums[row : row + 8, lane : lane + BLK]


def row_sums(lists, tile, left, acc, total, spare):
    def step(*slots):
        low = [left[0, lists[0, 0, 1, s]] for s in slots[:2]]
        high = [left[1, lists[0, 0, 1, s]] for s in slots[2:]]
        sums = jnp.dot(
            jnp.concatenate(low + high, axis=0),
            square(tile, slots),
            preferred_element_type=F32,
        )
        firsts = [(0, 0), (PIECES, BLK), (2 * PIECES, 0), (3 * PIECES, BLK)]
        add_rows(acc, lists, 0, slots, sums, total, spare, firsts)

    slot_loop(step, total, 4, GROUP)


def col_sums(lists, tile, left, acc, total, spare):
    def step(*slots):
        pieces = [left[i % 2, lists[0, 0, 0, s]] for i, s in enumerate(slots)]
        sums = lax.dot_general(
            jnp.concatenate(pieces, axis=0),
            square(tile, slots),
            (((1,), (1,)), ((), ())),
            preferred_element_type=F32,
        )
        firsts = [(0, 0), (PIECES, 0), (2 * PIECES, BLK), (3 * PIECES, BLK)]
        add_rows(acc, lists, 1, slots, sums, total, spare, firsts)

    slot_loop(step, total, 4, GROUP)


def fill_pieces(left, scaling):
    high, mid, low = split3(scaling)
    shape = (PIECES, BLK)
    rows = lax.broadcasted_iota(jnp.int32, shape, 0)
    empty = jnp.zeros(shape, F32).astype(BF16)
    for b in range(scaling.shape[0]):
        value = jnp.where(
            rows == 0,
            jnp.broadcast_to(high[b : b + 1], shape),
            jnp.where(
                rows == 1,
                jnp.broadcast_to(mid[b : b + 1], shape),
                jnp.where(rows == 2, jnp.broadcast_to(low[b : b + 1], shape), 0.0),
            ),
        ).astype(BF16)
        left[0, b] = jnp.concatenate([value, empty], axis=1)
        left[1, b] = jnp.concatenate([empty, value], axis=1)


def build_kernel(pcs, n_row, n_col, *refs):
    lists, counts = refs[:2]
    col_in = refs[2 : 2 + n_row]
    row_in = refs[2 + n_row : 2 + n_row + n_col]
    tile, part, row_prof, row_inv, col_prof, col_inv, acc, left = refs[2 + n_row + n_col :]
    per = row_in[0].shape[1] // BLK
    col_blocks, row_blocks = n_row * per, n_col * per
    total = counts[0, 0]
    me_row, me_col = places()
    chip, core = me_col // 2, lax.rem(me_col, 2)
    for k, ref in enumerate(row_in):
        piece = shifted(chip, k // 2, n_col // 2) * 2
        piece = piece + (core if k % 2 == 0 else 1 - core)
        for j in range(per):
            block = ref[:, j * BLK : (j + 1) * BLK]
            row_prof[piece * per + j] = block
            width = block.astype(F32)[pcs + 6 : pcs + 7, :]
            row_inv[piece * per + j] = jnp.broadcast_to(1.0 / width, (8, BLK))
    rows = lax.broadcasted_iota(jnp.int32, (FEAT, BLK), 0)
    for k, ref in enumerate(col_in):
        piece = shifted(me_row, k, n_row)
        for j in range(per):
            block = ref[0:FEAT, j * BLK : (j + 1) * BLK].astype(F32)
            turned = jnp.where(rows < pcs, -2.0 * block, 0.0)
            turned = jnp.where((rows >= pcs) & (rows < pcs + 3), 1.0, turned)
            turned = jnp.where(
                (rows >= pcs + 3) & (rows < pcs + 6), pltpu.roll(block, 3, 0), turned
            )
            turned = jnp.where(rows == pcs + 7, pltpu.roll(block, 1, 0), turned)
            turned = turned.T
            col_prof[piece * per + j] = turned.astype(BF16)
            col_inv[piece * per + j] = jnp.broadcast_to(
                -LOG2E / turned[:, pcs + 7 : pcs + 8], (BLK, BLK)
            )

    def step(s):
        rb, cb = lists[0, 0, 0, s], lists[0, 0, 1, s]
        distance = jnp.dot(col_prof[cb], row_prof[rb], preferred_element_type=F32)
        block = jnp.exp2(distance * col_inv[cb] * row_inv[rb][0:1, :])
        tile[s] = block.astype(BF16)

    slot_loop(step, total, 1, GROUP)
    ones = (lax.broadcasted_iota(jnp.int32, (PIECES, BLK), 0) == 0).astype(F32).astype(BF16)
    empty = jnp.zeros_like(ones)
    for b in range(row_blocks):
        left[0, b] = jnp.concatenate([ones, empty], axis=1)
        left[1, b] = jnp.concatenate([empty, ones], axis=1)
    acc[...] = jnp.zeros_like(acc)
    col_sums(lists, tile, left, acc, total, col_blocks)
    part[...] = jnp.sum(acc[0:col_blocks], axis=1)


def pass_kernel(over_rows, n, ratio, n_parts, *refs):
    lists, counts, tile = refs[:3]
    parts = refs[3 : 3 + n_parts]
    out, stage, left, acc = refs[-4:]
    total = counts[0, 0]
    blocks = out.shape[0]
    where = arrivals("row" if over_rows else "col", n, ratio)
    fill_pieces(left, SCALE / ordered_sum(stage, parts, where, n))
    acc[...] = jnp.zeros_like(acc)
    (row_sums if over_rows else col_sums)(lists, tile, left, acc, total, blocks)
    out[...] = jnp.sum(acc[0:blocks], axis=1)


def pieces_of(value):
    return [v.astype(BF16) for v in split3(value)]


def last_kernel(n_row, n_col, n_land, n_parts, *refs):
    lists, counts, marks, tile = refs[:4]
    parts = refs[4 : 4 + n_parts]
    packs = refs[4 + n_parts : 4 + n_parts + n_row]
    keep, away, both, scaling_out, stage, scaled, acc = refs[4 + n_parts + n_row :]
    cols = packs[0].shape[0] - FEAT
    per = packs[0].shape[1] // BLK
    blocks = n_col * per
    total = counts[0, 0]
    me_row, me_col = places()
    where = arrivals("row", n_row, n_col // n_row)
    scaling = SCALE / ordered_sum(stage, parts, where, n_row)
    scaling_out[...] = scaling
    for k in range(n_row):
        piece = shifted(me_row, k, n_row)
        for j in range(per):
            block = packs[k][FEAT:, j * BLK : (j + 1) * BLK].astype(F32)
            b = piece * per + j
            scaled[b, 0:cols] = (block * scaling_out[pl.ds(b, 1), :]).astype(BF16)
    high, mid, low = split3(scaling)
    shape = (PIECES, BLK)
    rows = lax.broadcasted_iota(jnp.int32, shape, 0)
    for b in range(scaling.shape[0]):
        value = jnp.where(
            rows == 0,
            jnp.broadcast_to(high[b : b + 1], shape),
            jnp.where(
                rows == 1,
                jnp.broadcast_to(mid[b : b + 1], shape),
                jnp.where(rows == 2, jnp.broadcast_to(low[b : b + 1], shape), 0.0),
            ),
        )
        scaled[b, cols : cols + PIECES] = value.astype(BF16)
    acc[...] = jnp.zeros_like(acc)

    def step(s):
        target = jnp.where(s < total, lists[0, 0, 0, s], blocks)
        sums = jnp.dot(scaled[lists[0, 0, 1, s]], tile[s], preferred_element_type=F32)
        acc[target] += sums[0 : cols + 8]

    slot_loop(step, total, 1, 8)
    core = lax.rem(me_col, 2)
    for q in range(n_col // 2):
        own = (2 * q + core) * per
        other = (2 * q + 1 - core) * per
        for j in range(per):
            keep[q, j] = acc[own + j, 0:cols]
            away[q, j] = acc[other + j, 0:cols].astype(BF16)
    row_part = jnp.sum(acc[0:blocks, cols : cols + 8], axis=1)
    for i, value in enumerate(pieces_of(row_part)):
        both[i * blocks : (i + 1) * blocks] = value
    for i in range(n_land):
        first = 3 * blocks + i * cols
        both[first : first + cols] = acc[marks[me_row * n_land + i] - me_row * blocks, 0:cols].astype(BF16)


def three(ref, blocks):
    value = ref[0 : 3 * blocks].astype(F32)
    return (value[2 * blocks :] + value[blocks : 2 * blocks]) + value[0:blocks]


def pair_kernel(keep, away, both, both_in, both_out, *outs):
    n_chip, per, cols = keep.shape[:3]
    blocks = 2 * n_chip * per
    chip = places()[1] // 2
    parts = pieces_of(three(both, blocks) + three(both_in, blocks))
    for i, value in enumerate(parts):
        both_out[i * blocks : (i + 1) * blocks] = value
    lands = both[3 * blocks :].astype(F32) + both_in[3 * blocks :].astype(F32)
    both_out[3 * blocks :] = lands.astype(BF16)
    for k, out in enumerate(outs):
        to = lax.rem(chip + k, n_chip)
        for j in range(per):
            value = keep[to, j] + away[to, j].astype(F32)
            out[j * cols : (j + 1) * cols] = value.astype(BF16)


def gram_kernel(n_land, cols, per, *refs):
    marks = refs[0]
    gram, scaling_out, own, inverse, stage, land_stage = refs[-6:]
    parts = refs[1:-6]
    n = len(parts)
    me_row, me_col = places()
    blocks = scaling_out.shape[0]
    for k, part in enumerate(parts):
        place = shifted(me_col // 2, k, n)
        stage[place] = three(part, blocks)
        land_stage[place] = part[3 * blocks :]
    inverse[...] = 1.0 / tree_sum([stage[i] for i in range(n)])
    scaling_out[...] = SCALE * inverse[...]
    for j in range(per):
        own[j : j + 1, :] = inverse[pl.ds(me_col * per + j, 1), :]
    total = None
    for i in range(n_land):
        summed = tree_sum(
            [land_stage[k, i * cols : (i + 1) * cols].astype(F32) for k in range(n)]
        )
        block = marks[me_row * n_land + i] - me_row * blocks
        projected = summed * inverse[pl.ds(block, 1), :]
        product = lax.dot_general(
            projected,
            projected,
            (((1,), (1,)), ((), ())),
            precision=lax.Precision.HIGHEST,
            preferred_element_type=F32,
        )
        total = product if total is None else total + product
    gram[...] = total


WIDE = 4


def eliminate(gram):
    cols = gram.shape[0]
    rows = lax.broadcasted_iota(jnp.int32, (cols, 2 * cols), 0)
    lanes = lax.broadcasted_iota(jnp.int32, (cols, 2 * cols), 1)
    unit = (rows[:, :cols] == lanes[:, :cols]).astype(F32)
    work = jnp.concatenate([gram, unit], axis=1)
    for first in range(0, cols, WIDE):
        tops = [work[first + i : first + i + 1, :] for i in range(WIDE)]
        sides = [
            jnp.broadcast_to(work[:, first + i : first + i + 1], work.shape)
            for i in range(WIDE)
        ]
        change = None
        for i in range(WIDE):
            pivot = first + i
            unit_top = tops[i] / sides[i][pivot : pivot + 1, :]
            for m in range(i + 1, WIDE):
                factor = sides[i][first + m : first + m + 1, :]
                tops[m] = tops[m] - factor * unit_top
                inner = factor / sides[i][pivot : pivot + 1, :]
                sides[m] = sides[m] - sides[i] * inner
            term = sides[i] * unit_top
            change = term if change is None else change + term
        reduced = work - change
        kept = work
        for i in range(WIDE):
            kept = jnp.where(rows == first + i, tops[i], kept)
        work = jnp.where(rows >= first + WIDE, reduced, kept)
    pivots = jnp.sum(jnp.where(rows == lanes, work, 0.0), axis=1, keepdims=True)
    return (work * lax.rsqrt(pivots))[:, cols:]


def ritz_kernel(n_row, ratio, cells, n_grams, *refs):
    grams = refs[:n_grams]
    parts = refs[n_grams:-3]
    own, out, stage = refs[-3:]
    cols = grams[0].shape[0]
    per = out.shape[1] // BLK
    where = arrivals("row", n_row, ratio)
    inverse = eliminate(ordered_sum(stage, grams, where, n_row) * (1.0 / cells))
    for j in range(per):
        summed = tree_sum([m[j * cols : (j + 1) * cols].astype(F32) for m in parts])
        projected = summed * own[j : j + 1, :]
        out[:, j * BLK : (j + 1) * BLK] = jnp.dot(
            inverse, projected, precision=lax.Precision.HIGHEST, preferred_element_type=F32
        )


def shift(x, axis, k):
    n = lax.axis_size(axis)
    return lax.ppermute(x, axis, [(i, (i + k) % n) for i in range(n)])


def exchange(x, axis):
    return [x] + [shift(x, axis, k) for k in range(1, lax.axis_size(axis))]


def rounds(n, late):
    early = n - late
    spread = early // late
    first = [
        [(o, (o + k) % early) for o in range(early)] for k in range(1, early)
    ]
    second = [
        [(early + i, early + (i + k) % late) for i in range(late)] for k in range(1, late)
    ]
    for j in range(early):
        pairs = [(early + i, (j + i * spread) % early) for i in range(late)]
        second.append(pairs + [(b, a) for a, b in pairs])
    return first, second


def origin(axis, ratio, row, col):
    return col // ratio + 1 if axis == "row" else row * ratio + ratio


def arrivals(axis, n, ratio):
    row, col = places()
    me = row if axis == "row" else col
    base = origin(axis, ratio, row, col)
    first, second = rounds(n, 1 if axis == "row" else ratio)
    own = lax.rem(me + (2 * n) - base, n)
    found = [me]
    for pairs in first + second:
        source = n
        for a, b in pairs:
            source = jnp.where(own == b, lax.rem(base + a, n), source)
        found.append(source)
    return found


def late_exchange(x, axis):
    n_row, n_col = lax.axis_size("row"), lax.axis_size("col")
    ratio = n_col // n_row
    along_row = axis == "row"
    n = n_row if along_row else n_col

    def send(value, pairs):
        flat = []
        for line in range(n_col if along_row else n_row):
            base = origin(axis, ratio, line, line)
            for a, b in pairs:
                a, b = (base + a) % n, (base + b) % n
                if along_row:
                    flat.append((a * n_col + line, b * n_col + line))
                else:
                    flat.append((line * n_col + a, line * n_col + b))
        return lax.ppermute(value, ("row", "col"), flat)

    first, second = rounds(n, 1 if along_row else ratio)
    early = [send(x, pairs) for pairs in first]
    x, early = lax.optimization_barrier((x, early))
    return [x] + early + [send(x, pairs) for pairs in second]


def chip_shift(x, k):
    n = lax.axis_size("col") // 2
    return lax.ppermute(
        x,
        "col",
        [(2 * q + p, 2 * ((q + k) % n) + p) for q in range(n) for p in range(2)],
    )


def sibling(x):
    return lax.ppermute(x, "col", [(i, i ^ 1) for i in range(lax.axis_size("col"))])


def vec(*arrays):
    return [("vmem", a) for a in arrays]


def body(profiles, cell_width, basis, block_lists, block_counts, landmarks):
    n_row, n_col = lax.axis_size("row"), lax.axis_size("col")
    n_chip = n_col // 2
    pcs, share = profiles.shape
    cols = basis.shape[0]
    per = share // BLK
    row_blocks, col_blocks = n_col * per, n_row * per
    slots = block_lists.shape[-1]
    n_land = landmarks.shape[0] // n_row

    def shape(*dims, dtype=F32):
        return jax.ShapeDtypeStruct(dims, dtype)

    ratio = n_col // n_row
    packed, packed_all = call(
        pack_kernel,
        [shape(FEAT, share, dtype=BF16), shape(FEAT + cols, share, dtype=BF16)],
        vec(profiles, cell_width.reshape(1, share), basis),
        [pltpu.VMEM((FEAT, share), F32)],
    )
    spread = lax.ppermute(
        packed,
        ("row", "col"),
        [((q % n_row) * n_col + q // n_row, q) for q in range(n_row * n_col)],
    )
    col_packs = exchange(packed_all, "row")
    row_packs = []
    for k in range(n_chip):
        pack = chip_shift(spread, k) if k else spread
        row_packs += [pack, sibling(pack)]
    lists = [("smem", block_lists), ("smem", block_counts)]
    marks = [("smem", landmarks)]
    tile, part = call(
        functools.partial(build_kernel, pcs, n_row, n_col),
        [pltpu.VMEM((slots, BLK, BLK), BF16), shape(col_blocks, BLK)],
        lists + vec(*col_packs, *row_packs),
        [
            pltpu.VMEM((row_blocks, FEAT, BLK), BF16),
            pltpu.VMEM((row_blocks, 8, BLK), F32),
            pltpu.VMEM((col_blocks, BLK, FEAT), BF16),
            pltpu.VMEM((col_blocks, BLK, BLK), F32),
            pltpu.VMEM((col_blocks + 1, 8, BLK), F32),
            pltpu.VMEM((2, row_blocks, PIECES, 2 * BLK), BF16),
        ],
    )
    for number in range(SWEEPS - 1):
        parts = late_exchange(part, "row")
        (part,) = call(
            functools.partial(pass_kernel, True, n_row, ratio, len(parts)),
            [shape(row_blocks, BLK)],
            lists + [("keep", tile)] + vec(*parts),
            [
                pltpu.VMEM((n_row + 1, col_blocks, BLK), F32),
                pltpu.VMEM((2, col_blocks, PIECES, 2 * BLK), BF16),
                pltpu.VMEM((row_blocks + 1, 8, BLK), F32),
            ],
        )
        parts = late_exchange(part, "col")
        (part,) = call(
            functools.partial(pass_kernel, False, n_col, ratio, len(parts)),
            [shape(col_blocks, BLK)],
            lists + [("keep", tile)] + vec(*parts),
            [
                pltpu.VMEM((n_col + 1, row_blocks, BLK), F32),
                pltpu.VMEM((2, row_blocks, PIECES, 2 * BLK), BF16),
                pltpu.VMEM((col_blocks + 1, 8, BLK), F32),
            ],
        )
    both_rows = 3 * row_blocks + n_land * cols
    parts = late_exchange(part, "row")
    keep, away, both, col_scaling = call(
        functools.partial(last_kernel, n_row, n_col, n_land, len(parts)),
        [
            shape(n_chip, per, cols, BLK),
            shape(n_chip, per, cols, BLK, dtype=BF16),
            shape(both_rows, BLK, dtype=BF16),
            shape(col_blocks, BLK),
        ],
        lists + marks + [("keep", tile)] + vec(*parts, *col_packs),
        [
            pltpu.VMEM((n_row + 1, col_blocks, BLK), F32),
            pltpu.VMEM((col_blocks, cols + PIECES, BLK), BF16),
            pltpu.VMEM((row_blocks + 1, cols + 8, BLK), F32),
        ],
    )
    pairs = call(
        pair_kernel,
        [shape(both_rows, BLK, dtype=BF16)]
        + [shape(per * cols, BLK, dtype=BF16)] * n_chip,
        vec(keep, sibling(away), both, sibling(both)),
    )
    sums = [pairs[0]] + [chip_shift(pairs[0], k) for k in range(1, n_chip)]
    shares = [pairs[1]] + [chip_shift(pairs[1 + k], k) for k in range(1, n_chip)]
    gram, row_scaling, own = call(
        functools.partial(gram_kernel, n_land, cols, per),
        [shape(cols, cols), shape(row_blocks, BLK), shape(per, BLK)],
        marks + vec(*sums),
        [
            pltpu.VMEM((row_blocks, BLK), F32),
            pltpu.VMEM((n_chip, row_blocks, BLK), F32),
            pltpu.VMEM((n_chip, n_land * cols, BLK), BF16),
        ],
    )
    grams = late_exchange(gram, "row")
    (ritz,) = call(
        functools.partial(ritz_kernel, n_row, ratio, landmarks.shape[0] * BLK, len(grams)),
        [shape(cols, share)],
        vec(*grams, *shares, own),
        [pltpu.VMEM((n_row + 1, cols, cols), F32)],
    )
    return row_scaling.reshape(-1), col_scaling.reshape(-1), ritz


def solution(mesh):
    placed = (
        P(None, ("col", "row")),
        P(("col", "row")),
        P(None, ("col", "row")),
        P("row", "col", None, None),
        P("row", "col"),
        P(),
    )
    return jax.shard_map(
        body,
        mesh=mesh,
        in_specs=placed,
        out_specs=(P("row"), P("col"), P(None, ("row", "col"))),
        check_vma=False,
    )
```

```python
import functools

import jax
import jax.numpy as jnp
from jax import lax
from jax.experimental import pallas as pl
from jax.experimental.pallas import tpu as pltpu
from jax.sharding import PartitionSpec as P

BLK = 128
SWEEPS = 3
GROUP = 16
FEAT = 64
PIECES = 16
SCALE = 512.0
LOG2E = 1.4426950408889634
F32 = jnp.float32
BF16 = jnp.bfloat16
MIB = 1 << 20

VMEM_SPEC = pl.BlockSpec(memory_space=pltpu.VMEM)
SMEM_SPEC = pl.BlockSpec(memory_space=pltpu.SMEM)


def split3(x):
    high = x.astype(BF16).astype(F32)
    mid = (x - high).astype(BF16).astype(F32)
    low = (x - high - mid).astype(BF16).astype(F32)
    return high, mid, low


def tree_sum(values):
    values = list(values)
    while len(values) > 1:
        values = [a + b for a, b in zip(values[::2], values[1::2])]
    return values[0]


def call(kernel, outs, ins, scratch=(), limit=24, flops=1 << 24):
    args, specs = [], []
    for kind, array in ins:
        if kind == "smem":
            specs.append(SMEM_SPEC)
        elif kind == "any":
            specs.append(pl.BlockSpec(memory_space=pl.ANY))
        else:
            specs.append(VMEM_SPEC)
            if kind == "keep":
                array = pltpu.with_memory_space_constraint(array, pltpu.VMEM)
        args.append(array)
    return pl.pallas_call(
        kernel,
        out_shape=tuple(outs),
        in_specs=specs,
        out_specs=tuple(VMEM_SPEC for _ in outs),
        scratch_shapes=list(scratch),
        compiler_params=pltpu.CompilerParams(vmem_limit_bytes=limit * MIB),
        cost_estimate=pl.CostEstimate(flops=flops, bytes_accessed=1 << 20, transcendentals=0),
    )(*args)


def pack_kernel(prof_ref, width_ref, out_ref, work):
    pcs = prof_ref.shape[0]
    prof = prof_ref[...].astype(F32)
    norm = jnp.sum(prof * prof, axis=0, keepdims=True)
    high, mid, low = split3(norm)
    work[...] = jnp.zeros_like(work)
    work[0:pcs, :] = prof
    work[pcs : pcs + 1, :] = high
    work[pcs + 1 : pcs + 2, :] = mid
    work[pcs + 2 : pcs + 3, :] = low
    work[pcs + 3 : pcs + 6, :] = jnp.ones((3, prof.shape[1]), F32)
    work[pcs + 6 : pcs + 7, :] = width_ref[...].astype(F32)
    out_ref[...] = work[...].astype(BF16)


def places():
    return lax.axis_index("row"), lax.axis_index("col")


def slot_loop(step, count, size, group):
    def advance(number, carry):
        for i in range(0, group, size):
            step(*[number * group + i + j for j in range(size)])
        return carry

    lax.fori_loop(0, (count + group - 1) // group, advance, 0)


def shifted(me, k, n):
    return lax.rem(me + (n - k), n)


def square(tile, slots):
    a, b, c, d = [tile[s] for s in slots]
    return jnp.concatenate(
        [jnp.concatenate([a, b], axis=1), jnp.concatenate([c, d], axis=1)], axis=0
    )


def add_rows(acc, lists, target, slots, sums, total, spare, firsts):
    for i, (s, (row, lane)) in enumerate(zip(slots, firsts)):
        place = jnp.where(s < total, lists[0, 0, target, s], spare)
        acc[place] += sums[row : row + 8, lane : lane + BLK]


def row_sums(lists, tile, left, acc, total, spare):
    def step(*slots):
        low = [left[0, lists[0, 0, 1, s]] for s in slots[:2]]
        high = [left[1, lists[0, 0, 1, s]] for s in slots[2:]]
        sums = jnp.dot(
            jnp.concatenate(low + high, axis=0),
            square(tile, slots),
            preferred_element_type=F32,
        )
        firsts = [(0, 0), (PIECES, BLK), (2 * PIECES, 0), (3 * PIECES, BLK)]
        add_rows(acc, lists, 0, slots, sums, total, spare, firsts)

    slot_loop(step, total, 4, 2 * GROUP)


def col_sums(lists, tile, left, acc, total, spare):
    def step(*slots):
        pieces = [left[i % 2, lists[0, 0, 0, s]] for i, s in enumerate(slots)]
        sums = lax.dot_general(
            jnp.concatenate(pieces, axis=0),
            square(tile, slots),
            (((1,), (1,)), ((), ())),
            preferred_element_type=F32,
        )
        firsts = [(0, 0), (PIECES, 0), (2 * PIECES, BLK), (3 * PIECES, BLK)]
        add_rows(acc, lists, 1, slots, sums, total, spare, firsts)

    slot_loop(step, total, 4, 2 * GROUP)


def fill_pieces(left, scaling):
    high, mid, low = split3(scaling)
    shape = (PIECES, BLK)
    rows = lax.broadcasted_iota(jnp.int32, shape, 0)
    empty = jnp.zeros(shape, F32).astype(BF16)
    for b in range(scaling.shape[0]):
        value = jnp.where(
            rows == 0,
            jnp.broadcast_to(high[b : b + 1], shape),
            jnp.where(
                rows == 1,
                jnp.broadcast_to(mid[b : b + 1], shape),
                jnp.where(rows == 2, jnp.broadcast_to(low[b : b + 1], shape), 0.0),
            ),
        ).astype(BF16)
        left[0, b] = jnp.concatenate([value, empty], axis=1)
        left[1, b] = jnp.concatenate([empty, value], axis=1)


def build_kernel(pcs, n_row, n_col, *refs):
    lists, counts = refs[:2]
    col_in = refs[2 : 2 + n_row]
    row_in = refs[2 + n_row : 2 + n_row + n_col]
    tile, part, row_prof, row_inv, col_prof, col_inv, acc, left = refs[2 + n_row + n_col :]
    per = row_in[0].shape[1] // BLK
    col_blocks, row_blocks = n_row * per, n_col * per
    total = counts[0, 0]
    me_row, me_col = places()
    for k, ref in enumerate(row_in):
        piece = lax.bitwise_xor(me_col, k)
        for j in range(per):
            block = ref[:, j * BLK : (j + 1) * BLK]
            row_prof[piece * per + j] = block
            width = block.astype(F32)[pcs + 6 : pcs + 7, :]
            row_inv[piece * per + j] = jnp.broadcast_to(1.0 / width, (8, BLK))
    rows = lax.broadcasted_iota(jnp.int32, (FEAT, BLK), 0)
    for k, ref in enumerate(col_in):
        piece = lax.bitwise_xor(me_row, k)
        for j in range(per):
            block = ref[0:FEAT, j * BLK : (j + 1) * BLK].astype(F32)
            turned = jnp.where(rows < pcs, -2.0 * block, 0.0)
            turned = jnp.where((rows >= pcs) & (rows < pcs + 3), 1.0, turned)
            turned = jnp.where(
                (rows >= pcs + 3) & (rows < pcs + 6), pltpu.roll(block, 3, 0), turned
            )
            turned = jnp.where(rows == pcs + 7, pltpu.roll(block, 1, 0), turned)
            turned = turned.T
            col_prof[piece * per + j] = turned.astype(BF16)
            col_inv[piece * per + j] = jnp.broadcast_to(
                -LOG2E / turned[:, pcs + 7 : pcs + 8], (BLK, BLK)
            )

    def step(s):
        rb, cb = lists[0, 0, 0, s], lists[0, 0, 1, s]
        distance = jnp.dot(col_prof[cb], row_prof[rb], preferred_element_type=F32)
        block = jnp.exp2(distance * col_inv[cb] * row_inv[rb][0:1, :])
        tile[s] = block.astype(BF16)

    slot_loop(step, total, 1, GROUP)
    ones = (lax.broadcasted_iota(jnp.int32, (PIECES, BLK), 0) == 0).astype(F32).astype(BF16)
    empty = jnp.zeros_like(ones)
    for b in range(row_blocks):
        left[0, b] = jnp.concatenate([ones, empty], axis=1)
        left[1, b] = jnp.concatenate([empty, ones], axis=1)
    acc[...] = jnp.zeros_like(acc)
    col_sums(lists, tile, left, acc, total, col_blocks)
    part[...] = jnp.sum(acc[0:col_blocks], axis=1)


def pass_kernel(over_rows, lists, counts, tile, part, part_in, out, left, acc):
    total = counts[0, 0]
    blocks = out.shape[0]
    fill_pieces(left, SCALE / (part[...] + part_in[...]))
    acc[...] = jnp.zeros_like(acc)
    (row_sums if over_rows else col_sums)(lists, tile, left, acc, total, blocks)
    out[...] = jnp.sum(acc[0:blocks], axis=1)


def pass_kernel_with(over_rows, extra, *refs):
    pass_kernel(over_rows, *refs[:5], *refs[5 + extra :])


def pieces_of(value):
    return [v.astype(BF16) for v in split3(value)]


def last_kernel(n_row, n_col, n_land, *refs):
    lists, counts, marks, tile, part, part_in = refs[:6]
    bases = refs[6 : 6 + n_row]
    keep, away, both, scaling_out, scaled, acc = refs[6 + n_row :]
    cols = bases[0].shape[0]
    per = bases[0].shape[1] // BLK
    blocks = n_col * per
    total = counts[0, 0]
    me_row, me_col = places()
    scaling = SCALE / (part[...] + part_in[...])
    scaling_out[...] = scaling
    for k in range(n_row):
        piece = lax.bitwise_xor(me_row, k)
        for j in range(per):
            block = bases[k][:, j * BLK : (j + 1) * BLK].astype(F32)
            b = piece * per + j
            scaled[b, 0:cols] = (block * scaling_out[pl.ds(b, 1), :]).astype(BF16)
    high, mid, low = split3(scaling)
    shape = (PIECES, BLK)
    rows = lax.broadcasted_iota(jnp.int32, shape, 0)
    for b in range(scaling.shape[0]):
        value = jnp.where(
            rows == 0,
            jnp.broadcast_to(high[b : b + 1], shape),
            jnp.where(
                rows == 1,
                jnp.broadcast_to(mid[b : b + 1], shape),
                jnp.where(rows == 2, jnp.broadcast_to(low[b : b + 1], shape), 0.0),
            ),
        )
        scaled[b, cols : cols + PIECES] = value.astype(BF16)
    acc[...] = jnp.zeros_like(acc)

    def step(s):
        target = jnp.where(s < total, lists[0, 0, 0, s], blocks)
        sums = jnp.dot(scaled[lists[0, 0, 1, s]], tile[s], preferred_element_type=F32)
        acc[target] += sums[0 : cols + 8]

    slot_loop(step, total, 1, 8)
    core = lax.rem(me_col, 2)
    for q in range(n_col // 2):
        own = (2 * q + core) * per
        other = (2 * q + 1 - core) * per
        for j in range(per):
            keep[q, j] = acc[own + j, 0:cols]
            away[q, j] = acc[other + j, 0:cols].astype(BF16)
    row_part = jnp.sum(acc[0:blocks, cols : cols + 8], axis=1)
    for i, value in enumerate(pieces_of(row_part)):
        both[i * blocks : (i + 1) * blocks] = value
    for i in range(n_land):
        first = 3 * blocks + i * cols
        both[first : first + cols] = acc[marks[me_row * n_land + i] - me_row * blocks, 0:cols].astype(BF16)


def three(ref, blocks):
    value = ref[0 : 3 * blocks].astype(F32)
    return (value[2 * blocks :] + value[blocks : 2 * blocks]) + value[0:blocks]


def pair_kernel(keep, away, both, both_in, both_out, *outs):
    n_chip, per, cols = keep.shape[:3]
    blocks = 2 * n_chip * per
    chip = places()[1] // 2
    parts = pieces_of(three(both, blocks) + three(both_in, blocks))
    for i, value in enumerate(parts):
        both_out[i * blocks : (i + 1) * blocks] = value
    lands = both[3 * blocks :].astype(F32) + both_in[3 * blocks :].astype(F32)
    both_out[3 * blocks :] = lands.astype(BF16)
    for k, out in enumerate(outs):
        to = lax.rem(chip + k, n_chip)
        for j in range(per):
            value = keep[to, j] + away[to, j].astype(F32)
            out[j * cols : (j + 1) * cols] = value.astype(BF16)


def gram_kernel(n_land, cols, per, *refs):
    marks = refs[0]
    gram, scaling_out, own, inverse, stage, land_stage = refs[-6:]
    parts = refs[1:-6]
    n = len(parts)
    me_row, me_col = places()
    blocks = scaling_out.shape[0]
    for k, part in enumerate(parts):
        place = shifted(me_col // 2, k, n)
        stage[place] = three(part, blocks)
        land_stage[place] = part[3 * blocks :]
    inverse[...] = 1.0 / tree_sum([stage[i] for i in range(n)])
    scaling_out[...] = SCALE * inverse[...]
    for j in range(per):
        own[j : j + 1, :] = inverse[pl.ds(me_col * per + j, 1), :]
    total = None
    for i in range(n_land):
        summed = tree_sum(
            [land_stage[k, i * cols : (i + 1) * cols].astype(F32) for k in range(n)]
        )
        block = marks[me_row * n_land + i] - me_row * blocks
        projected = summed * inverse[pl.ds(block, 1), :]
        product = lax.dot_general(
            projected,
            projected,
            (((1,), (1,)), ((), ())),
            precision=lax.Precision.HIGHEST,
            preferred_element_type=F32,
        )
        total = product if total is None else total + product
    gram[...] = total


WIDE = 4


def eliminate(gram):
    cols = gram.shape[0]
    rows = lax.broadcasted_iota(jnp.int32, (cols, 2 * cols), 0)
    lanes = lax.broadcasted_iota(jnp.int32, (cols, 2 * cols), 1)
    unit = (rows[:, :cols] == lanes[:, :cols]).astype(F32)
    work = jnp.concatenate([gram, unit], axis=1)
    for first in range(0, cols, WIDE):
        tops = [work[first + i : first + i + 1, :] for i in range(WIDE)]
        sides = [
            jnp.broadcast_to(work[:, first + i : first + i + 1], work.shape)
            for i in range(WIDE)
        ]
        change = None
        for i in range(WIDE):
            pivot = first + i
            unit_top = tops[i] / sides[i][pivot : pivot + 1, :]
            for m in range(i + 1, WIDE):
                factor = sides[i][first + m : first + m + 1, :]
                tops[m] = tops[m] - factor * unit_top
                inner = factor / sides[i][pivot : pivot + 1, :]
                sides[m] = sides[m] - sides[i] * inner
            term = sides[i] * unit_top
            change = term if change is None else change + term
        reduced = work - change
        kept = work
        for i in range(WIDE):
            kept = jnp.where(rows == first + i, tops[i], kept)
        work = jnp.where(rows >= first + WIDE, reduced, kept)
    pivots = jnp.sum(jnp.where(rows == lanes, work, 0.0), axis=1, keepdims=True)
    return (work * lax.rsqrt(pivots))[:, cols:]


def ritz_kernel(cells, gram, gram_in, *refs):
    parts, (own, out) = refs[:-2], refs[-2:]
    cols = gram.shape[0]
    per = out.shape[1] // BLK
    inverse = eliminate((gram[...] + gram_in[...]) * (1.0 / cells))
    for j in range(per):
        summed = tree_sum([m[j * cols : (j + 1) * cols].astype(F32) for m in parts])
        projected = summed * own[j : j + 1, :]
        out[:, j * BLK : (j + 1) * BLK] = jnp.dot(
            inverse, projected, precision=lax.Precision.HIGHEST, preferred_element_type=F32
        )


def swap(x, axis, k):
    return lax.ppermute(x, axis, [(i, i ^ k) for i in range(lax.axis_size(axis))])


def bits(axis):
    n = lax.axis_size(axis)
    return [1 << i for i in range((n - 1).bit_length())]


def gather(x, axis, order):
    found = {0: x}
    for bit in order:
        found.update({k ^ bit: swap(value, axis, bit) for k, value in found.items()})
    return [found[k] for k in range(len(found))]


def halves(x, axis):
    rounds = bits(axis)
    for bit in rounds[:-1]:
        x = x + swap(x, axis, bit)
    return x, swap(x, axis, rounds[-1])


def chip_shift(x, k):
    n = lax.axis_size("col") // 2
    return lax.ppermute(
        x,
        "col",
        [(2 * q + p, 2 * ((q + k) % n) + p) for q in range(n) for p in range(2)],
    )


def sibling(x):
    return swap(x, "col", 1)


def vec(*arrays):
    return [("vmem", a) for a in arrays]


def body(profiles, cell_width, basis, block_lists, block_counts, landmarks):
    n_row, n_col = lax.axis_size("row"), lax.axis_size("col")
    n_chip = n_col // 2
    pcs, share = profiles.shape
    cols = basis.shape[0]
    per = share // BLK
    row_blocks, col_blocks = n_col * per, n_row * per
    slots = block_lists.shape[-1]
    n_land = landmarks.shape[0] // n_row

    def shape(*dims, dtype=F32):
        return jax.ShapeDtypeStruct(dims, dtype)

    (packed,) = call(
        pack_kernel,
        [shape(FEAT, share, dtype=BF16)],
        vec(profiles, cell_width.reshape(1, share)),
        [pltpu.VMEM((FEAT, share), F32)],
    )
    spread = lax.ppermute(
        packed,
        ("row", "col"),
        [((q % n_row) * n_col + q // n_row, q) for q in range(n_row * n_col)],
    )
    row_packs = gather(spread, "col", bits("col")[1:] + [1])
    col_packs = gather(packed, "row", bits("row"))
    bases = gather(basis, "row", bits("row"))
    lists = [("smem", block_lists), ("smem", block_counts)]
    marks = [("smem", landmarks)]
    tile, part = call(
        functools.partial(build_kernel, pcs, n_row, n_col),
        [pltpu.VMEM((slots, BLK, BLK), BF16), shape(col_blocks, BLK)],
        lists + vec(*col_packs, *row_packs),
        [
            pltpu.VMEM((row_blocks, FEAT, BLK), BF16),
            pltpu.VMEM((row_blocks, 8, BLK), F32),
            pltpu.VMEM((col_blocks, BLK, FEAT), BF16),
            pltpu.VMEM((col_blocks, BLK, BLK), F32),
            pltpu.VMEM((col_blocks + 1, 8, BLK), F32),
            pltpu.VMEM((2, row_blocks, PIECES, 2 * BLK), BF16),
        ],
    )
    for number in range(SWEEPS - 1):
        early = [("any", bases[1])] if number == 0 else [("any", b) for b in bases[2:]]
        (part,) = call(
            functools.partial(pass_kernel_with, True, len(early)),
            [shape(row_blocks, BLK)],
            lists + [("keep", tile)] + vec(*halves(part, "row")) + early,
            [
                pltpu.VMEM((2, col_blocks, PIECES, 2 * BLK), BF16),
                pltpu.VMEM((row_blocks + 1, 8, BLK), F32),
            ],
        )
        (part,) = call(
            functools.partial(pass_kernel, False),
            [shape(col_blocks, BLK)],
            lists + [("keep", tile)] + vec(*halves(part, "col")),
            [
                pltpu.VMEM((2, row_blocks, PIECES, 2 * BLK), BF16),
                pltpu.VMEM((col_blocks + 1, 8, BLK), F32),
            ],
        )
    both_rows = 3 * row_blocks + n_land * cols
    keep, away, both, col_scaling = call(
        functools.partial(last_kernel, n_row, n_col, n_land),
        [
            shape(n_chip, per, cols, BLK),
            shape(n_chip, per, cols, BLK, dtype=BF16),
            shape(both_rows, BLK, dtype=BF16),
            shape(col_blocks, BLK),
        ],
        lists + marks + [("keep", tile)] + vec(*halves(part, "row"), *bases),
        [
            pltpu.VMEM((col_blocks, cols + PIECES, BLK), BF16),
            pltpu.VMEM((row_blocks + 1, cols + 8, BLK), F32),
        ],
    )
    pairs = call(
        pair_kernel,
        [shape(both_rows, BLK, dtype=BF16)]
        + [shape(per * cols, BLK, dtype=BF16)] * n_chip,
        vec(keep, sibling(away), both, sibling(both)),
    )
    sums = [pairs[0]] + [chip_shift(pairs[0], k) for k in range(1, n_chip)]
    shares = [pairs[1]] + [chip_shift(pairs[1 + k], k) for k in range(1, n_chip)]
    gram, row_scaling, own = call(
        functools.partial(gram_kernel, n_land, cols, per),
        [shape(cols, cols), shape(row_blocks, BLK), shape(per, BLK)],
        marks + vec(*sums),
        [
            pltpu.VMEM((row_blocks, BLK), F32),
            pltpu.VMEM((n_chip, row_blocks, BLK), F32),
            pltpu.VMEM((n_chip, n_land * cols, BLK), BF16),
        ],
    )
    (ritz,) = call(
        functools.partial(ritz_kernel, landmarks.shape[0] * BLK),
        [shape(cols, share)],
        vec(*halves(gram, "row"), *shares, own),
    )
    return row_scaling.reshape(-1), col_scaling.reshape(-1), ritz


def solution(mesh):
    placed = (
        P(None, ("col", "row")),
        P(("col", "row")),
        P(None, ("col", "row")),
        P("row", "col", None, None),
        P("row", "col"),
        P(),
    )
    return jax.shard_map(
        body,
        mesh=mesh,
        in_specs=placed,
        out_specs=(P("row"), P("col"), P(None, ("row", "col"))),
        check_vma=False,
    )
```

```python
import functools

import jax
import jax.numpy as jnp
from jax import lax
from jax.experimental import pallas as pl
from jax.experimental.pallas import tpu as pltpu
from jax.sharding import PartitionSpec as P

BLK = 128
SWEEPS = 3
GROUP = 16
FEAT = 64
PIECES = 16
SCALE = 512.0
LOG2E = 1.4426950408889634
F32 = jnp.float32
BF16 = jnp.bfloat16
MIB = 1 << 20

VMEM_SPEC = pl.BlockSpec(memory_space=pltpu.VMEM)
SMEM_SPEC = pl.BlockSpec(memory_space=pltpu.SMEM)


def split3(x):
    high = x.astype(BF16).astype(F32)
    mid = (x - high).astype(BF16).astype(F32)
    low = (x - high - mid).astype(BF16).astype(F32)
    return high, mid, low


def tree_sum(values):
    values = list(values)
    while len(values) > 1:
        values = [a + b for a, b in zip(values[::2], values[1::2])]
    return values[0]


def call(kernel, outs, ins, scratch=(), limit=24, flops=1 << 24):
    args, specs = [], []
    for kind, array in ins:
        if kind == "smem":
            specs.append(SMEM_SPEC)
        elif kind == "any":
            specs.append(pl.BlockSpec(memory_space=pl.ANY))
        else:
            specs.append(VMEM_SPEC)
            if kind == "keep":
                array = pltpu.with_memory_space_constraint(array, pltpu.VMEM)
        args.append(array)
    return pl.pallas_call(
        kernel,
        out_shape=tuple(outs),
        in_specs=specs,
        out_specs=tuple(VMEM_SPEC for _ in outs),
        scratch_shapes=list(scratch),
        compiler_params=pltpu.CompilerParams(vmem_limit_bytes=limit * MIB),
        cost_estimate=pl.CostEstimate(flops=flops, bytes_accessed=1 << 20, transcendentals=0),
    )(*args)


def pack_kernel(prof_ref, width_ref, out_ref, work):
    pcs = prof_ref.shape[0]
    prof = prof_ref[...].astype(F32)
    norm = jnp.sum(prof * prof, axis=0, keepdims=True)
    high, mid, low = split3(norm)
    work[...] = jnp.zeros_like(work)
    work[0:pcs, :] = prof
    work[pcs : pcs + 1, :] = high
    work[pcs + 1 : pcs + 2, :] = mid
    work[pcs + 2 : pcs + 3, :] = low
    work[pcs + 3 : pcs + 6, :] = jnp.ones((3, prof.shape[1]), F32)
    work[pcs + 6 : pcs + 7, :] = width_ref[...].astype(F32)
    out_ref[...] = work[...].astype(BF16)


def places():
    return lax.axis_index("row"), lax.axis_index("col")


def slot_loop(step, count, size, group):
    def advance(number, carry):
        for i in range(0, group, size):
            step(*[number * group + i + j for j in range(size)])
        return carry

    lax.fori_loop(0, (count + group - 1) // group, advance, 0)


def shifted(me, k, n):
    return lax.rem(me + (n - k), n)


def ordered_sum(stage, refs, me):
    n = len(refs)
    for k, ref in enumerate(refs):
        stage[shifted(me, k, n)] = ref[...]
    return tree_sum([stage[i] for i in range(n)])


def square(tile, slots):
    a, b, c, d = [tile[s] for s in slots]
    return jnp.concatenate(
        [jnp.concatenate([a, b], axis=1), jnp.concatenate([c, d], axis=1)], axis=0
    )


def add_rows(acc, lists, target, slots, sums, total, spare, firsts):
    for i, (s, (row, lane)) in enumerate(zip(slots, firsts)):
        place = jnp.where(s < total, lists[0, 0, target, s], spare)
        acc[place] += sums[row : row + 8, lane : lane + BLK]


def row_sums(lists, tile, left, acc, total, spare):
    def step(*slots):
        low = [left[0, lists[0, 0, 1, s]] for s in slots[:2]]
        high = [left[1, lists[0, 0, 1, s]] for s in slots[2:]]
        sums = jnp.dot(
            jnp.concatenate(low + high, axis=0),
            square(tile, slots),
            preferred_element_type=F32,
        )
        firsts = [(0, 0), (PIECES, BLK), (2 * PIECES, 0), (3 * PIECES, BLK)]
        add_rows(acc, lists, 0, slots, sums, total, spare, firsts)

    slot_loop(step, total, 4, 4 * GROUP)


def col_sums(lists, tile, left, acc, total, spare):
    def step(*slots):
        pieces = [left[i % 2, lists[0, 0, 0, s]] for i, s in enumerate(slots)]
        sums = lax.dot_general(
            jnp.concatenate(pieces, axis=0),
            square(tile, slots),
            (((1,), (1,)), ((), ())),
            preferred_element_type=F32,
        )
        firsts = [(0, 0), (PIECES, 0), (2 * PIECES, BLK), (3 * PIECES, BLK)]
        add_rows(acc, lists, 1, slots, sums, total, spare, firsts)

    slot_loop(step, total, 4, 4 * GROUP)


def fill_pieces(left, scaling):
    high, mid, low = split3(scaling)
    shape = (PIECES, BLK)
    rows = lax.broadcasted_iota(jnp.int32, shape, 0)
    empty = jnp.zeros(shape, F32).astype(BF16)
    for b in range(scaling.shape[0]):
        value = jnp.where(
            rows == 0,
            jnp.broadcast_to(high[b : b + 1], shape),
            jnp.where(
                rows == 1,
                jnp.broadcast_to(mid[b : b + 1], shape),
                jnp.where(rows == 2, jnp.broadcast_to(low[b : b + 1], shape), 0.0),
            ),
        ).astype(BF16)
        left[0, b] = jnp.concatenate([value, empty], axis=1)
        left[1, b] = jnp.concatenate([empty, value], axis=1)


def build_kernel(pcs, n_row, n_col, *refs):
    lists, counts = refs[:2]
    col_in = refs[2 : 2 + n_row]
    row_in = refs[2 + n_row : 2 + n_row + n_col]
    tile, part, row_prof, row_inv, col_prof, col_inv, acc, left = refs[2 + n_row + n_col :]
    per = row_in[0].shape[1] // BLK
    col_blocks, row_blocks = n_row * per, n_col * per
    total = counts[0, 0]
    me_row, me_col = places()
    for k, ref in enumerate(row_in):
        core = lax.rem(me_col + k, 2)
        piece = shifted(me_col // 2, k // 2, n_col // 2) * 2 + core
        for j in range(per):
            block = ref[:, j * BLK : (j + 1) * BLK]
            row_prof[piece * per + j] = block
            width = block.astype(F32)[pcs + 6 : pcs + 7, :]
            row_inv[piece * per + j] = jnp.broadcast_to(1.0 / width, (8, BLK))
    rows = lax.broadcasted_iota(jnp.int32, (FEAT, BLK), 0)
    for k, ref in enumerate(col_in):
        piece = shifted(me_row, k, n_row)
        for j in range(per):
            block = ref[0:FEAT, j * BLK : (j + 1) * BLK].astype(F32)
            turned = jnp.where(rows < pcs, -2.0 * block, 0.0)
            turned = jnp.where((rows >= pcs) & (rows < pcs + 3), 1.0, turned)
            turned = jnp.where(
                (rows >= pcs + 3) & (rows < pcs + 6), pltpu.roll(block, 3, 0), turned
            )
            turned = jnp.where(rows == pcs + 7, pltpu.roll(block, 1, 0), turned)
            turned = turned.T
            col_prof[piece * per + j] = turned.astype(BF16)
            col_inv[piece * per + j] = jnp.broadcast_to(
                -LOG2E / turned[:, pcs + 7 : pcs + 8], (BLK, BLK)
            )

    def step(s):
        rb, cb = lists[0, 0, 0, s], lists[0, 0, 1, s]
        distance = jnp.dot(col_prof[cb], row_prof[rb], preferred_element_type=F32)
        block = jnp.exp2(distance * col_inv[cb] * row_inv[rb][0:1, :])
        tile[s] = block.astype(BF16)

    slot_loop(step, total, 1, GROUP)
    ones = (lax.broadcasted_iota(jnp.int32, (PIECES, BLK), 0) == 0).astype(F32).astype(BF16)
    empty = jnp.zeros_like(ones)
    for b in range(row_blocks):
        left[0, b] = jnp.concatenate([ones, empty], axis=1)
        left[1, b] = jnp.concatenate([empty, ones], axis=1)
    acc[...] = jnp.zeros_like(acc)
    col_sums(lists, tile, left, acc, total, col_blocks)
    part[...] = jnp.sum(acc[0:col_blocks], axis=1)


def pass_kernel(over_rows, n_parts, *refs):
    lists, counts, tile = refs[:3]
    parts = refs[3 : 3 + n_parts]
    out, stage, left, acc = refs[-4:]
    total = counts[0, 0]
    blocks = out.shape[0]
    me_row, me_col = places()
    scaling = SCALE / ordered_sum(stage, parts, me_row if over_rows else me_col // 2)
    fill_pieces(left, scaling)
    acc[...] = jnp.zeros_like(acc)
    (row_sums if over_rows else col_sums)(lists, tile, left, acc, total, blocks)
    out[...] = jnp.sum(acc[0:blocks], axis=1)


def pieces_of(value):
    return [v.astype(BF16) for v in split3(value)]


def last_kernel(n_row, n_col, n_land, *refs):
    lists, counts, marks, tile = refs[:4]
    parts, bases = refs[4 : 4 + n_row], refs[4 + n_row : 4 + 2 * n_row]
    keep, away, both, scaling_out, stage, scaled, acc = refs[4 + 2 * n_row :]
    cols = bases[0].shape[0]
    per = bases[0].shape[1] // BLK
    blocks = n_col * per
    total = counts[0, 0]
    me_row, me_col = places()
    scaling = SCALE / ordered_sum(stage, parts, me_row)
    scaling_out[...] = scaling
    for k in range(n_row):
        piece = shifted(me_row, k, n_row)
        for j in range(per):
            block = bases[k][:, j * BLK : (j + 1) * BLK].astype(F32)
            b = piece * per + j
            scaled[b, 0:cols] = (block * scaling_out[pl.ds(b, 1), :]).astype(BF16)
    high, mid, low = split3(scaling)
    shape = (PIECES, BLK)
    rows = lax.broadcasted_iota(jnp.int32, shape, 0)
    for b in range(scaling.shape[0]):
        value = jnp.where(
            rows == 0,
            jnp.broadcast_to(high[b : b + 1], shape),
            jnp.where(
                rows == 1,
                jnp.broadcast_to(mid[b : b + 1], shape),
                jnp.where(rows == 2, jnp.broadcast_to(low[b : b + 1], shape), 0.0),
            ),
        )
        scaled[b, cols : cols + PIECES] = value.astype(BF16)
    acc[...] = jnp.zeros_like(acc)

    def step(s):
        target = jnp.where(s < total, lists[0, 0, 0, s], blocks)
        sums = jnp.dot(scaled[lists[0, 0, 1, s]], tile[s], preferred_element_type=F32)
        acc[target] += sums[0 : cols + 8]

    slot_loop(step, total, 1, GROUP)
    core = lax.rem(me_col, 2)
    for q in range(n_col // 2):
        own = (2 * q + core) * per
        other = (2 * q + 1 - core) * per
        for j in range(per):
            keep[q, j] = acc[own + j, 0:cols]
            away[q, j] = acc[other + j, 0:cols].astype(BF16)
    row_part = jnp.sum(acc[0:blocks, cols : cols + 8], axis=1)
    for i, value in enumerate(pieces_of(row_part)):
        both[i * blocks : (i + 1) * blocks] = value
    for i in range(n_land):
        first = 3 * blocks + i * cols
        both[first : first + cols] = acc[marks[me_row * n_land + i] - me_row * blocks, 0:cols].astype(BF16)


def three(ref, blocks):
    value = ref[0 : 3 * blocks].astype(F32)
    return (value[2 * blocks :] + value[blocks : 2 * blocks]) + value[0:blocks]


def pair_kernel(keep, away, both, both_in, both_out, *outs):
    n_chip, per, cols = keep.shape[:3]
    blocks = 2 * n_chip * per
    chip = places()[1] // 2
    parts = pieces_of(three(both, blocks) + three(both_in, blocks))
    for i, value in enumerate(parts):
        both_out[i * blocks : (i + 1) * blocks] = value
    lands = both[3 * blocks :].astype(F32) + both_in[3 * blocks :].astype(F32)
    both_out[3 * blocks :] = lands.astype(BF16)
    for k, out in enumerate(outs):
        to = lax.rem(chip + k, n_chip)
        for j in range(per):
            value = keep[to, j] + away[to, j].astype(F32)
            out[j * cols : (j + 1) * cols] = value.astype(BF16)


def gram_kernel(n_land, cols, per, *refs):
    marks = refs[0]
    gram, scaling_out, own, inverse, stage, land_stage = refs[-6:]
    parts = refs[1:-6]
    n = len(parts)
    me_row, me_col = places()
    blocks = scaling_out.shape[0]
    for k, part in enumerate(parts):
        place = shifted(me_col // 2, k, n)
        stage[place] = three(part, blocks)
        land_stage[place] = part[3 * blocks :]
    inverse[...] = 1.0 / tree_sum([stage[i] for i in range(n)])
    scaling_out[...] = SCALE * inverse[...]
    for j in range(per):
        own[j : j + 1, :] = inverse[pl.ds(me_col * per + j, 1), :]
    total = None
    for i in range(n_land):
        summed = tree_sum(
            [land_stage[k, i * cols : (i + 1) * cols].astype(F32) for k in range(n)]
        )
        block = marks[me_row * n_land + i] - me_row * blocks
        projected = summed * inverse[pl.ds(block, 1), :]
        product = lax.dot_general(
            projected,
            projected,
            (((1,), (1,)), ((), ())),
            precision=lax.Precision.HIGHEST,
            preferred_element_type=F32,
        )
        total = product if total is None else total + product
    gram[...] = total


WIDE = 4


def eliminate(gram):
    cols = gram.shape[0]
    rows = lax.broadcasted_iota(jnp.int32, (cols, 2 * cols), 0)
    lanes = lax.broadcasted_iota(jnp.int32, (cols, 2 * cols), 1)
    unit = (rows[:, :cols] == lanes[:, :cols]).astype(F32)
    work = jnp.concatenate([gram, unit], axis=1)
    for first in range(0, cols, WIDE):
        tops = [work[first + i : first + i + 1, :] for i in range(WIDE)]
        sides = [
            jnp.broadcast_to(work[:, first + i : first + i + 1], work.shape)
            for i in range(WIDE)
        ]
        change = None
        for i in range(WIDE):
            pivot = first + i
            unit_top = tops[i] / sides[i][pivot : pivot + 1, :]
            for m in range(i + 1, WIDE):
                factor = sides[i][first + m : first + m + 1, :]
                tops[m] = tops[m] - factor * unit_top
                inner = factor / sides[i][pivot : pivot + 1, :]
                sides[m] = sides[m] - sides[i] * inner
            term = sides[i] * unit_top
            change = term if change is None else change + term
        reduced = work - change
        kept = work
        for i in range(WIDE):
            kept = jnp.where(rows == first + i, tops[i], kept)
        work = jnp.where(rows >= first + WIDE, reduced, kept)
    pivots = jnp.sum(jnp.where(rows == lanes, work, 0.0), axis=1, keepdims=True)
    return (work * lax.rsqrt(pivots))[:, cols:]


def ritz_kernel(n_row, cells, *refs):
    grams, parts = refs[:n_row], refs[n_row:-3]
    own, out, stage = refs[-3:]
    cols = grams[0].shape[0]
    per = out.shape[1] // BLK
    inverse = eliminate(ordered_sum(stage, grams, places()[0]) * (1.0 / cells))
    for j in range(per):
        summed = tree_sum([m[j * cols : (j + 1) * cols].astype(F32) for m in parts])
        projected = summed * own[j : j + 1, :]
        out[:, j * BLK : (j + 1) * BLK] = jnp.dot(
            inverse, projected, precision=lax.Precision.HIGHEST, preferred_element_type=F32
        )


def swap(x, axis, k):
    return lax.ppermute(x, axis, [(i, i ^ k) for i in range(lax.axis_size(axis))])


def shift(x, axis, k):
    n = lax.axis_size(axis)
    return lax.ppermute(x, axis, [(i, (i + k) % n) for i in range(n)])


def shifts(x, axis):
    return [x] + [shift(x, axis, k) for k in range(1, lax.axis_size(axis))]


def chip_shift(x, k):
    n = lax.axis_size("col") // 2
    return lax.ppermute(
        x,
        "col",
        [(2 * q + p, 2 * ((q + k) % n) + p) for q in range(n) for p in range(2)],
    )


def chip_shifts(x):
    return [x] + [chip_shift(x, k) for k in range(1, lax.axis_size("col") // 2)]


def sibling(x):
    return swap(x, "col", 1)


def vec(*arrays):
    return [("vmem", a) for a in arrays]


def body(profiles, cell_width, basis, block_lists, block_counts, landmarks):
    n_row, n_col = lax.axis_size("row"), lax.axis_size("col")
    n_chip = n_col // 2
    pcs, share = profiles.shape
    cols = basis.shape[0]
    per = share // BLK
    row_blocks, col_blocks = n_col * per, n_row * per
    slots = block_lists.shape[-1]
    n_land = landmarks.shape[0] // n_row

    def shape(*dims, dtype=F32):
        return jax.ShapeDtypeStruct(dims, dtype)

    (packed,) = call(
        pack_kernel,
        [shape(FEAT, share, dtype=BF16)],
        vec(profiles, cell_width.reshape(1, share)),
        [pltpu.VMEM((FEAT, share), F32)],
    )
    spread = lax.ppermute(
        packed,
        ("row", "col"),
        [((q % n_row) * n_col + q // n_row, q) for q in range(n_row * n_col)],
    )
    row_packs = []
    for pack in chip_shifts(spread):
        row_packs += [pack, sibling(pack)]
    col_packs = shifts(packed, "row")
    bases = shifts(basis, "row")
    lists = [("smem", block_lists), ("smem", block_counts)]
    marks = [("smem", landmarks)]
    tile, part = call(
        functools.partial(build_kernel, pcs, n_row, n_col),
        [pltpu.VMEM((slots, BLK, BLK), BF16), shape(col_blocks, BLK)],
        lists + vec(*col_packs, *row_packs),
        [
            pltpu.VMEM((row_blocks, FEAT, BLK), BF16),
            pltpu.VMEM((row_blocks, 8, BLK), F32),
            pltpu.VMEM((col_blocks, BLK, FEAT), BF16),
            pltpu.VMEM((col_blocks, BLK, BLK), F32),
            pltpu.VMEM((col_blocks + 1, 8, BLK), F32),
            pltpu.VMEM((2, row_blocks, PIECES, 2 * BLK), BF16),
        ],
    )
    for number in range(SWEEPS - 1):
        early = [("any", b) for b in bases[1:]] if number == 0 else []
        (part,) = call(
            functools.partial(pass_kernel, True, n_row),
            [shape(row_blocks, BLK)],
            lists + [("keep", tile)] + vec(*shifts(part, "row")) + early,
            [
                pltpu.VMEM((n_row, col_blocks, BLK), F32),
                pltpu.VMEM((2, col_blocks, PIECES, 2 * BLK), BF16),
                pltpu.VMEM((row_blocks + 1, 8, BLK), F32),
            ],
        )
        (part,) = call(
            functools.partial(pass_kernel, False, n_chip),
            [shape(col_blocks, BLK)],
            lists + [("keep", tile)] + vec(*chip_shifts(part + sibling(part))),
            [
                pltpu.VMEM((n_chip, row_blocks, BLK), F32),
                pltpu.VMEM((2, row_blocks, PIECES, 2 * BLK), BF16),
                pltpu.VMEM((col_blocks + 1, 8, BLK), F32),
            ],
        )
    both_rows = 3 * row_blocks + n_land * cols
    keep, away, both, col_scaling = call(
        functools.partial(last_kernel, n_row, n_col, n_land),
        [
            shape(n_chip, per, cols, BLK),
            shape(n_chip, per, cols, BLK, dtype=BF16),
            shape(both_rows, BLK, dtype=BF16),
            shape(col_blocks, BLK),
        ],
        lists + marks + [("keep", tile)] + vec(*shifts(part, "row"), *bases),
        [
            pltpu.VMEM((n_row, col_blocks, BLK), F32),
            pltpu.VMEM((col_blocks, cols + PIECES, BLK), BF16),
            pltpu.VMEM((row_blocks + 1, cols + 8, BLK), F32),
        ],
    )
    pairs = call(
        pair_kernel,
        [shape(both_rows, BLK, dtype=BF16)]
        + [shape(per * cols, BLK, dtype=BF16)] * n_chip,
        vec(keep, sibling(away), both, sibling(both)),
    )
    sums = [pairs[0]] + [chip_shift(pairs[0], k) for k in range(1, n_chip)]
    shares = [pairs[1]] + [chip_shift(pairs[1 + k], k) for k in range(1, n_chip)]
    gram, row_scaling, own = call(
        functools.partial(gram_kernel, n_land, cols, per),
        [shape(cols, cols), shape(row_blocks, BLK), shape(per, BLK)],
        marks + vec(*sums),
        [
            pltpu.VMEM((row_blocks, BLK), F32),
            pltpu.VMEM((n_chip, row_blocks, BLK), F32),
            pltpu.VMEM((n_chip, n_land * cols, BLK), BF16),
        ],
    )
    (ritz,) = call(
        functools.partial(ritz_kernel, n_row, landmarks.shape[0] * BLK),
        [shape(cols, share)],
        vec(*shifts(gram, "row"), *shares, own),
        [pltpu.VMEM((n_row, cols, cols), F32)],
    )
    return row_scaling.reshape(-1), col_scaling.reshape(-1), ritz


def solution(mesh):
    placed = (
        P(None, ("col", "row")),
        P(("col", "row")),
        P(None, ("col", "row")),
        P("row", "col", None, None),
        P("row", "col"),
        P(),
    )
    return jax.shard_map(
        body,
        mesh=mesh,
        in_specs=placed,
        out_specs=(P("row"), P("col"), P(None, ("row", "col"))),
        check_vma=False,
    )
```

```python
import functools

import jax
import jax.numpy as jnp
from jax import lax
from jax.experimental import pallas as pl
from jax.experimental.pallas import tpu as pltpu
from jax.sharding import PartitionSpec as P

BLK = 128
SWEEPS = 3
GROUP = 32
BUILD_GROUP = 16
TILE_GROUP = 16
ROWS, COLUMNS, COUNT = 0, 1, 2
FEAT = 64
PIECES = 16
SCALE = 512.0
LOG2E = 1.4426950408889634
F32 = jnp.float32
BF16 = jnp.bfloat16
MIB = 1 << 20
STRIP_TILES = 8

VMEM_SPEC = pl.BlockSpec(memory_space=pltpu.VMEM)
SMEM_SPEC = pl.BlockSpec(memory_space=pltpu.SMEM)


def split3(x):
    high = x.astype(BF16).astype(F32)
    mid = (x - high).astype(BF16).astype(F32)
    low = (x - high - mid).astype(BF16).astype(F32)
    return high, mid, low


def tree_sum(values):
    values = list(values)
    while len(values) > 1:
        values = [a + b for a, b in zip(values[::2], values[1::2])]
    return values[0]


def call(kernel, outs, ins, scratch=(), limit=24, flops=1 << 24):
    args, specs = [], []
    for kind, array in ins:
        if kind == "smem":
            specs.append(SMEM_SPEC)
        elif kind == "any":
            specs.append(pl.BlockSpec(memory_space=pl.ANY))
        else:
            specs.append(VMEM_SPEC)
            if kind == "keep":
                array = pltpu.with_memory_space_constraint(array, pltpu.VMEM)
        args.append(array)
    return pl.pallas_call(
        kernel,
        out_shape=tuple(outs),
        in_specs=specs,
        out_specs=tuple(VMEM_SPEC for _ in outs),
        scratch_shapes=list(scratch),
        compiler_params=pltpu.CompilerParams(vmem_limit_bytes=limit * MIB),
        cost_estimate=pl.CostEstimate(flops=flops, bytes_accessed=1 << 20, transcendentals=0),
    )(*args)


def pack_kernel(prof_ref, width_ref, lists_ref, counts, out_ref, work):
    pcs = prof_ref.shape[0]
    prof = prof_ref[...].astype(F32)
    norm = jnp.sum(prof * prof, axis=0, keepdims=True)
    high, mid, low = split3(norm)
    work[...] = jnp.zeros_like(work)
    work[0:pcs, :] = prof
    work[pcs : pcs + 1, :] = high
    work[pcs + 1 : pcs + 2, :] = mid
    work[pcs + 2 : pcs + 3, :] = low
    work[pcs + 3 : pcs + 6, :] = jnp.ones((3, prof.shape[1]), F32)
    work[pcs + 6 : pcs + 7, :] = width_ref[...].astype(F32)
    work[pcs + 8 : pcs + 10, 0:BLK] = lists_ref[0, 0].astype(F32)
    work[pcs + 10 : pcs + 11, 0:BLK] = jnp.full((1, BLK), counts[0, 0], jnp.int32).astype(F32)
    out_ref[...] = work[...].astype(BF16)


def places():
    return lax.axis_index("row"), lax.axis_index("col")


def stack_kernel(pcs, *refs):
    packs, (stack, table) = refs[:-2], refs[-2:]
    n = len(packs)
    me_row, _ = places()
    first = FEAT - 16
    for k, pack in enumerate(packs):
        stack[k] = pack[...]
        rows = pack[first:, 0:BLK].astype(F32)
        rows = pltpu.roll(rows, 16 - (pcs + 8 - first), 0)
        table[shifted(me_row, k, n)] = rows[0:8].astype(jnp.int32)


def slot_loop(step, count, size, group):
    def advance(number, carry):
        for i in range(0, group, size):
            step(*[number * group + i + j for j in range(size)])
        return carry

    lax.fori_loop(0, (count + group - 1) // group, advance, 0)


class Tile:
    def __init__(self, table, n_row, k, own, others):
        _, me_col = places()
        self.group = shifted(me_col // 2, k, n_row)
        self.table, self.k = table, k
        slots = own.shape[0]
        self.blocks, self.base = (own, 0) if k == 0 else (others, (k - 1) * slots)
        self.total = table[self.group * 8 + COUNT, 0]

    def row(self, s):
        return self.table[self.group * 8 + ROWS, s]

    def column(self, s):
        return self.table[self.group * 8 + COLUMNS, s]

    def block(self, s):
        return self.blocks[self.base + s]


def shifted(me, k, n):
    return lax.rem(me + (n - k), n)


def ordered_sum(stage, refs, me):
    n = len(refs)
    for k, ref in enumerate(refs):
        stage[shifted(me, k, n)] = ref[...]
    return tree_sum([stage[i] for i in range(n)])


def square(tile, slots):
    a, b, c, d = [tile.block(s) for s in slots]
    return jnp.concatenate(
        [jnp.concatenate([a, b], axis=1), jnp.concatenate([c, d], axis=1)], axis=0
    )


def add_rows(acc, sums, firsts, targets):
    for (row, lane), target in zip(firsts, targets):
        acc[target] += sums[row : row + 8, lane : lane + BLK]


def row_sums(tile, left, acc, row_blocks, spare):
    first = tile.group * row_blocks

    def step(*slots):
        low = [left[0, tile.column(s)] for s in slots[:2]]
        high = [left[1, tile.column(s)] for s in slots[2:]]
        sums = jnp.dot(
            jnp.concatenate(low + high, axis=0),
            square(tile, slots),
            preferred_element_type=F32,
        )
        firsts = [(0, 0), (PIECES, BLK), (2 * PIECES, 0), (3 * PIECES, BLK)]
        targets = [jnp.where(s < tile.total, first + tile.row(s), spare) for s in slots]
        add_rows(acc, sums, firsts, targets)

    slot_loop(step, tile.total, 4, GROUP)


def col_sums(tile, left, acc, row_blocks, spare):
    first = tile.group * row_blocks

    def step(*slots):
        if left is None:
            rows = lax.broadcasted_iota(jnp.int32, (4 * PIECES, 2 * BLK), 0)
            lanes = lax.broadcasted_iota(jnp.int32, (4 * PIECES, 2 * BLK), 1)
            block = rows // PIECES
            pieces = (rows % PIECES == 0) & (block % 2 == lanes // BLK)
            pieces = pieces.astype(F32).astype(BF16)
        else:
            pieces = [left[i % 2, first + tile.row(s)] for i, s in enumerate(slots)]
            pieces = jnp.concatenate(pieces, axis=0)
        sums = lax.dot_general(
            pieces,
            square(tile, slots),
            (((1,), (1,)), ((), ())),
            preferred_element_type=F32,
        )
        firsts = [(0, 0), (PIECES, 0), (2 * PIECES, BLK), (3 * PIECES, BLK)]
        targets = [jnp.where(s < tile.total, tile.column(s), spare) for s in slots]
        add_rows(acc, sums, firsts, targets)

    slot_loop(step, tile.total, 4, GROUP)


def fill_pieces(left, scaling):
    high, mid, low = split3(scaling)
    shape = (PIECES, BLK)
    rows = lax.broadcasted_iota(jnp.int32, shape, 0)
    empty = jnp.zeros(shape, F32).astype(BF16)
    for b in range(scaling.shape[0]):
        value = jnp.where(
            rows == 0,
            jnp.broadcast_to(high[b : b + 1], shape),
            jnp.where(
                rows == 1,
                jnp.broadcast_to(mid[b : b + 1], shape),
                jnp.where(rows == 2, jnp.broadcast_to(low[b : b + 1], shape), 0.0),
            ),
        ).astype(BF16)
        left[0, b] = jnp.concatenate([value, empty], axis=1)
        left[1, b] = jnp.concatenate([empty, value], axis=1)


def build(tile, offset, row_prof, row_inv, col_prof, col_inv):
    def step(s):
        row, column = offset + tile.row(s), tile.column(s)
        distance = jnp.dot(col_prof[column], row_prof[row], preferred_element_type=F32)
        block = jnp.exp2(distance * col_inv[column] * row_inv[row][0:1, :])
        tile.blocks[tile.base + s] = block.astype(BF16)

    slot_loop(step, tile.total, 1, BUILD_GROUP)


def fill_rows(pcs, stacks, row_prof, row_inv, offset):
    me_row, me_col = places()
    n_row = stacks[0].shape[0]
    per = stacks[0].shape[2] // BLK
    for i, stack in enumerate(stacks):
        core = lax.rem(me_col + i, 2)
        for k in range(n_row):
            piece = core * n_row + shifted(me_row, k, n_row)
            for j in range(per):
                block = stack[k, :, j * BLK : (j + 1) * BLK]
                row_prof[offset + piece * per + j] = block
                width = block.astype(F32)[pcs + 6 : pcs + 7, :]
                row_inv[offset + piece * per + j] = jnp.broadcast_to(1.0 / width, (8, BLK))


def own_kernel(pcs, table, stack, other, tile, col_prof, col_inv, row_prof, row_inv):
    n_row = stack.shape[0]
    per = stack.shape[2] // BLK
    me_row, _ = places()
    fill_rows(pcs, [stack, other], row_prof, row_inv, 0)
    rows = lax.broadcasted_iota(jnp.int32, (FEAT, BLK), 0)
    for k in range(n_row):
        piece = shifted(me_row, k, n_row)
        for j in range(per):
            block = stack[k, :, j * BLK : (j + 1) * BLK].astype(F32)
            turned = jnp.where(rows < pcs, -2.0 * block, 0.0)
            turned = jnp.where((rows >= pcs) & (rows < pcs + 3), 1.0, turned)
            turned = jnp.where(
                (rows >= pcs + 3) & (rows < pcs + 6), pltpu.roll(block, 3, 0), turned
            )
            turned = jnp.where(rows == pcs + 7, pltpu.roll(block, 1, 0), turned)
            turned = turned.T
            col_prof[piece * per + j] = turned.astype(BF16)
            col_inv[piece * per + j] = jnp.broadcast_to(
                -LOG2E / turned[:, pcs + 7 : pcs + 8], (BLK, BLK)
            )
    build(Tile(table, n_row, 0, tile, None), 0, row_prof, row_inv, col_prof, col_inv)


def column_scaling(tiles, left, acc, row_blocks):
    col_blocks = acc.shape[0] - 1
    acc[...] = jnp.zeros_like(acc)
    for tile in tiles:
        col_sums(tile, left, acc, row_blocks, col_blocks)
    return SCALE / jnp.sum(acc[0:col_blocks], axis=1)


def row_part(tiles, left, acc, row_blocks, out):
    blocks = acc.shape[0] - 1
    acc[...] = jnp.zeros_like(acc)
    for tile in tiles:
        row_sums(tile, left, acc, row_blocks, blocks)
    out[...] = jnp.sum(acc[0:blocks], axis=1)


def strip_kernel(pcs, n_row, *refs):
    table, own, col_prof, col_inv = refs[:4]
    stacks = refs[4:-7]
    others, out, row_prof, row_inv, left, row_acc, col_acc = refs[-7:]
    row_blocks = row_prof.shape[0] // (n_row - 1)
    tiles = [Tile(table, n_row, k, own, others) for k in range(n_row)]
    for k in range(1, n_row):
        first = (k - 1) * row_blocks
        fill_rows(pcs, stacks[2 * k - 2 : 2 * k], row_prof, row_inv, first)
    for k in range(1, n_row):
        first = (k - 1) * row_blocks
        build(tiles[k], first, row_prof, row_inv, col_prof, col_inv)
    fill_pieces(left, column_scaling(tiles, None, col_acc, row_blocks))
    row_part(tiles, left, row_acc, row_blocks, out)


def row_scalings(stage, parts):
    for k, part in enumerate(parts):
        stage[shifted(places()[1] // 2, k, len(parts))] = part[...].astype(F32)
    return SCALE / tree_sum([stage[i] for i in range(len(parts))])


def sweep_kernel(n_row, n_chip, *refs):
    table, own, others = refs[:3]
    parts = refs[3 : 3 + n_chip]
    out, stage, row_left, left, row_acc, col_acc = refs[-6:]
    row_blocks = out.shape[0] // n_row
    tiles = [Tile(table, n_row, k, own, others) for k in range(n_row)]
    fill_pieces(row_left, row_scalings(stage, parts))
    fill_pieces(left, column_scaling(tiles, row_left, col_acc, row_blocks))
    row_part(tiles, left, row_acc, row_blocks, out)


def pieces_of(value):
    return [v.astype(BF16) for v in split3(value)]


def last_kernel(n_row, n_chip, n_land, *refs):
    table, marks, own, others = refs[:4]
    parts, bases = refs[4 : 4 + n_chip], refs[4 + n_chip : 4 + n_chip + n_row]
    keep, away, both, scaling_out, stage, row_left, col_acc, scaled, acc = refs[-9:]
    cols = bases[0].shape[0]
    per = bases[0].shape[1] // BLK
    blocks = 2 * n_chip * per
    me_row, me_col = places()
    tiles = [Tile(table, n_row, k, own, others) for k in range(n_row)]
    fill_pieces(row_left, row_scalings(stage, parts))
    scaling = column_scaling(tiles, row_left, col_acc, blocks)
    scaling_out[...] = scaling
    for k in range(n_row):
        piece = shifted(me_row, k, n_row)
        for j in range(per):
            block = bases[k][:, j * BLK : (j + 1) * BLK].astype(F32)
            b = piece * per + j
            scaled[b, 0:cols] = (block * scaling_out[pl.ds(b, 1), :]).astype(BF16)
    high, mid, low = split3(scaling)
    shape = (PIECES, BLK)
    rows = lax.broadcasted_iota(jnp.int32, shape, 0)
    for b in range(scaling.shape[0]):
        value = jnp.where(
            rows == 0,
            jnp.broadcast_to(high[b : b + 1], shape),
            jnp.where(
                rows == 1,
                jnp.broadcast_to(mid[b : b + 1], shape),
                jnp.where(rows == 2, jnp.broadcast_to(low[b : b + 1], shape), 0.0),
            ),
        )
        scaled[b, cols : cols + PIECES] = value.astype(BF16)
    acc[...] = jnp.zeros_like(acc)
    for k in range(n_row):
        tile = tiles[k]

        def step(s, tile=tile):
            target = jnp.where(s < tile.total, tile.row(s), blocks)
            sums = jnp.dot(scaled[tile.column(s)], tile.block(s), preferred_element_type=F32)
            acc[target] += sums[0 : cols + 8]

        slot_loop(step, jnp.where(tile.group == me_row, tile.total, 0), 1, BUILD_GROUP)
    core = lax.rem(me_col, 2)
    for q in range(n_chip):
        mine = (2 * q + core) * per
        other = (2 * q + 1 - core) * per
        for j in range(per):
            keep[q, j] = acc[mine + j, 0:cols]
            away[q, j] = acc[other + j, 0:cols].astype(BF16)
    part = jnp.sum(acc[0:blocks, cols : cols + 8], axis=1)
    for i, value in enumerate(pieces_of(part)):
        both[i * blocks : (i + 1) * blocks] = value
    for i in range(n_land):
        first = 3 * blocks + i * cols
        both[first : first + cols] = acc[marks[me_row * n_land + i] - me_row * blocks, 0:cols].astype(BF16)


def three(ref, blocks):
    value = ref[0 : 3 * blocks].astype(F32)
    return (value[2 * blocks :] + value[blocks : 2 * blocks]) + value[0:blocks]


def pair_kernel(keep, away, both, both_in, both_out, *outs):
    n_chip, per, cols = keep.shape[:3]
    blocks = 2 * n_chip * per
    chip = places()[1] // 2
    parts = pieces_of(three(both, blocks) + three(both_in, blocks))
    for i, value in enumerate(parts):
        both_out[i * blocks : (i + 1) * blocks] = value
    lands = both[3 * blocks :].astype(F32) + both_in[3 * blocks :].astype(F32)
    both_out[3 * blocks :] = lands.astype(BF16)
    for k, out in enumerate(outs):
        to = lax.rem(chip + k, n_chip)
        for j in range(per):
            value = keep[to, j] + away[to, j].astype(F32)
            out[j * cols : (j + 1) * cols] = value.astype(BF16)


def gram_kernel(n_land, cols, per, *refs):
    marks = refs[0]
    gram, scaling_out, own, inverse, stage, land_stage = refs[-6:]
    parts = refs[1:-6]
    n = len(parts)
    me_row, me_col = places()
    blocks = scaling_out.shape[0]
    for k, part in enumerate(parts):
        place = shifted(me_col // 2, k, n)
        stage[place] = three(part, blocks)
        land_stage[place] = part[3 * blocks :]
    inverse[...] = 1.0 / tree_sum([stage[i] for i in range(n)])
    scaling_out[...] = SCALE * inverse[...]
    for j in range(per):
        own[j : j + 1, :] = inverse[pl.ds(me_col * per + j, 1), :]
    total = None
    for i in range(n_land):
        summed = tree_sum(
            [land_stage[k, i * cols : (i + 1) * cols].astype(F32) for k in range(n)]
        )
        block = marks[me_row * n_land + i] - me_row * blocks
        projected = summed * inverse[pl.ds(block, 1), :]
        product = lax.dot_general(
            projected,
            projected,
            (((1,), (1,)), ((), ())),
            precision=lax.Precision.HIGHEST,
            preferred_element_type=F32,
        )
        total = product if total is None else total + product
    gram[...] = total


WIDE = 4


def eliminate(gram):
    cols = gram.shape[0]
    rows = lax.broadcasted_iota(jnp.int32, (cols, 2 * cols), 0)
    lanes = lax.broadcasted_iota(jnp.int32, (cols, 2 * cols), 1)
    unit = (rows[:, :cols] == lanes[:, :cols]).astype(F32)
    work = jnp.concatenate([gram, unit], axis=1)
    for first in range(0, cols, WIDE):
        tops = [work[first + i : first + i + 1, :] for i in range(WIDE)]
        sides = [
            jnp.broadcast_to(work[:, first + i : first + i + 1], work.shape)
            for i in range(WIDE)
        ]
        change = None
        for i in range(WIDE):
            pivot = first + i
            unit_top = tops[i] / sides[i][pivot : pivot + 1, :]
            for m in range(i + 1, WIDE):
                factor = sides[i][first + m : first + m + 1, :]
                tops[m] = tops[m] - factor * unit_top
                inner = factor / sides[i][pivot : pivot + 1, :]
                sides[m] = sides[m] - sides[i] * inner
            term = sides[i] * unit_top
            change = term if change is None else change + term
        reduced = work - change
        kept = work
        for i in range(WIDE):
            kept = jnp.where(rows == first + i, tops[i], kept)
        work = jnp.where(rows >= first + WIDE, reduced, kept)
    pivots = jnp.sum(jnp.where(rows == lanes, work, 0.0), axis=1, keepdims=True)
    return (work * lax.rsqrt(pivots))[:, cols:]


def ritz_kernel(n_row, cells, *refs):
    grams, parts = refs[:n_row], refs[n_row:-3]
    own, out, stage = refs[-3:]
    cols = grams[0].shape[0]
    per = out.shape[1] // BLK
    inverse = eliminate(ordered_sum(stage, grams, places()[0]) * (1.0 / cells))
    for j in range(per):
        summed = tree_sum([m[j * cols : (j + 1) * cols].astype(F32) for m in parts])
        projected = summed * own[j : j + 1, :]
        out[:, j * BLK : (j + 1) * BLK] = jnp.dot(
            inverse, projected, precision=lax.Precision.HIGHEST, preferred_element_type=F32
        )


def swap(x, axis, k):
    return lax.ppermute(x, axis, [(i, i ^ k) for i in range(lax.axis_size(axis))])


def shift(x, axis, k):
    n = lax.axis_size(axis)
    return lax.ppermute(x, axis, [(i, (i + k) % n) for i in range(n)])


def shifts(x, axis):
    return [x] + [shift(x, axis, k) for k in range(1, lax.axis_size(axis))]


def chip_shift(x, k):
    n = lax.axis_size("col") // 2
    return lax.ppermute(
        x,
        "col",
        [(2 * q + p, 2 * ((q + k) % n) + p) for q in range(n) for p in range(2)],
    )


def chip_shifts(x):
    return [x] + [chip_shift(x, k) for k in range(1, lax.axis_size("col") // 2)]


def sibling(x):
    return swap(x, "col", 1)


def vec(*arrays):
    return [("vmem", a) for a in arrays]


def strip_body(profiles, cell_width, basis, block_lists, block_counts, landmarks):
    n_row, n_col = lax.axis_size("row"), lax.axis_size("col")
    n_chip = n_col // 2
    pcs, share = profiles.shape
    cols = basis.shape[0]
    per = share // BLK
    row_blocks, col_blocks = n_col * per, n_row * per
    all_rows = n_row * row_blocks
    slots = block_lists.shape[-1]
    n_land = landmarks.shape[0] // n_row

    def shape(*dims, dtype=F32):
        return jax.ShapeDtypeStruct(dims, dtype)

    (packed,) = call(
        pack_kernel,
        [shape(FEAT, share, dtype=BF16)],
        vec(profiles, cell_width.reshape(1, share), block_lists) + [("smem", block_counts)],
        [pltpu.VMEM((FEAT, share), F32)],
    )
    stack, table = call(
        functools.partial(stack_kernel, pcs),
        [shape(n_row, FEAT, share, dtype=BF16), shape(n_row, 8, BLK, dtype=jnp.int32)],
        vec(*shifts(packed, "row")),
    )
    table = ("smem", table.reshape(n_row * 8, BLK))
    marks = ("smem", landmarks)
    stacks = []
    for k in range(1, n_chip):
        far = chip_shift(stack, k)
        stacks += [far, sibling(far)]
    bases = shifts(basis, "row")
    own, col_prof, col_inv = call(
        functools.partial(own_kernel, pcs),
        [
            pltpu.VMEM((slots, BLK, BLK), BF16),
            pltpu.VMEM((col_blocks, BLK, FEAT), BF16),
            pltpu.VMEM((col_blocks, BLK, BLK), F32),
        ],
        [table] + vec(stack, sibling(stack)),
        [
            pltpu.VMEM((row_blocks, FEAT, BLK), BF16),
            pltpu.VMEM((row_blocks, 8, BLK), F32),
        ],
    )
    far_slots = (n_row - 1) * slots
    others, part = call(
        functools.partial(strip_kernel, pcs, n_row),
        [pltpu.VMEM((far_slots, BLK, BLK), BF16), shape(all_rows, BLK)],
        [table, ("keep", own), ("keep", col_prof), ("keep", col_inv)] + vec(*stacks),
        [
            pltpu.VMEM((all_rows - row_blocks, FEAT, BLK), BF16),
            pltpu.VMEM((all_rows - row_blocks, 8, BLK), F32),
            pltpu.VMEM((2, col_blocks, PIECES, 2 * BLK), BF16),
            pltpu.VMEM((all_rows + 1, 8, BLK), F32),
            pltpu.VMEM((col_blocks + 1, 8, BLK), F32),
        ],
    )
    tiles = [("keep", own), ("keep", others)]

    def chip_parts(part):
        return chip_shifts((part + sibling(part)).astype(BF16))

    for number in range(SWEEPS - 2):
        early = [("any", b) for b in bases[1:]] if number == 0 else []
        (part,) = call(
            functools.partial(sweep_kernel, n_row, n_chip),
            [shape(all_rows, BLK)],
            [table] + tiles + vec(*chip_parts(part)) + early,
            [
                pltpu.VMEM((n_chip, all_rows, BLK), F32),
                pltpu.VMEM((2, all_rows, PIECES, 2 * BLK), BF16),
                pltpu.VMEM((2, col_blocks, PIECES, 2 * BLK), BF16),
                pltpu.VMEM((all_rows + 1, 8, BLK), F32),
                pltpu.VMEM((col_blocks + 1, 8, BLK), F32),
            ],
        )
    both_rows = 3 * row_blocks + n_land * cols
    keep, away, both, col_scaling = call(
        functools.partial(last_kernel, n_row, n_chip, n_land),
        [
            shape(n_chip, per, cols, BLK),
            shape(n_chip, per, cols, BLK, dtype=BF16),
            shape(both_rows, BLK, dtype=BF16),
            shape(col_blocks, BLK),
        ],
        [table, marks] + tiles + vec(*chip_parts(part), *bases),
        [
            pltpu.VMEM((n_chip, all_rows, BLK), F32),
            pltpu.VMEM((2, all_rows, PIECES, 2 * BLK), BF16),
            pltpu.VMEM((col_blocks + 1, 8, BLK), F32),
            pltpu.VMEM((col_blocks, cols + PIECES, BLK), BF16),
            pltpu.VMEM((row_blocks + 1, cols + 8, BLK), F32),
        ],
    )
    pairs = call(
        pair_kernel,
        [shape(both_rows, BLK, dtype=BF16)]
        + [shape(per * cols, BLK, dtype=BF16)] * n_chip,
        vec(keep, sibling(away), both, sibling(both)),
    )
    sums = [pairs[0]] + [chip_shift(pairs[0], k) for k in range(1, n_chip)]
    shares = [pairs[1]] + [chip_shift(pairs[1 + k], k) for k in range(1, n_chip)]
    gram, row_scaling, own = call(
        functools.partial(gram_kernel, n_land, cols, per),
        [shape(cols, cols), shape(row_blocks, BLK), shape(per, BLK)],
        [marks] + vec(*sums),
        [
            pltpu.VMEM((row_blocks, BLK), F32),
            pltpu.VMEM((n_chip, row_blocks, BLK), F32),
            pltpu.VMEM((n_chip, n_land * cols, BLK), BF16),
        ],
    )
    (ritz,) = call(
        functools.partial(ritz_kernel, n_row, landmarks.shape[0] * BLK),
        [shape(cols, share)],
        vec(*shifts(gram, "row"), *shares, own),
        [pltpu.VMEM((n_row, cols, cols), F32)],
    )
    return row_scaling.reshape(-1), col_scaling.reshape(-1), ritz


def tile_pack_kernel(prof_ref, width_ref, out_ref, work):
    pcs = prof_ref.shape[0]
    prof = prof_ref[...].astype(F32)
    norm = jnp.sum(prof * prof, axis=0, keepdims=True)
    high, mid, low = split3(norm)
    work[...] = jnp.zeros_like(work)
    work[0:pcs, :] = prof
    work[pcs : pcs + 1, :] = high
    work[pcs + 1 : pcs + 2, :] = mid
    work[pcs + 2 : pcs + 3, :] = low
    work[pcs + 3 : pcs + 6, :] = jnp.ones((3, prof.shape[1]), F32)
    work[pcs + 6 : pcs + 7, :] = width_ref[...].astype(F32)
    out_ref[...] = work[...].astype(BF16)


def tile_square(tile, slots):
    a, b, c, d = [tile[s] for s in slots]
    return jnp.concatenate(
        [jnp.concatenate([a, b], axis=1), jnp.concatenate([c, d], axis=1)], axis=0
    )


def tile_add_rows(acc, lists, target, slots, sums, total, spare, firsts):
    for i, (s, (row, lane)) in enumerate(zip(slots, firsts)):
        place = jnp.where(s < total, lists[0, 0, target, s], spare)
        acc[place] += sums[row : row + 8, lane : lane + BLK]


def tile_row_sums(lists, tile, left, acc, total, spare):
    def step(*slots):
        low = [left[0, lists[0, 0, 1, s]] for s in slots[:2]]
        high = [left[1, lists[0, 0, 1, s]] for s in slots[2:]]
        sums = jnp.dot(
            jnp.concatenate(low + high, axis=0),
            tile_square(tile, slots),
            preferred_element_type=F32,
        )
        firsts = [(0, 0), (PIECES, BLK), (2 * PIECES, 0), (3 * PIECES, BLK)]
        tile_add_rows(acc, lists, 0, slots, sums, total, spare, firsts)

    slot_loop(step, total, 4, 4 * TILE_GROUP)


def tile_col_sums(lists, tile, left, acc, total, spare):
    def step(*slots):
        pieces = [left[i % 2, lists[0, 0, 0, s]] for i, s in enumerate(slots)]
        sums = lax.dot_general(
            jnp.concatenate(pieces, axis=0),
            tile_square(tile, slots),
            (((1,), (1,)), ((), ())),
            preferred_element_type=F32,
        )
        firsts = [(0, 0), (PIECES, 0), (2 * PIECES, BLK), (3 * PIECES, BLK)]
        tile_add_rows(acc, lists, 1, slots, sums, total, spare, firsts)

    slot_loop(step, total, 4, 4 * TILE_GROUP)


def tile_build_kernel(pcs, n_row, n_col, *refs):
    lists, counts = refs[:2]
    col_in = refs[2 : 2 + n_row]
    row_in = refs[2 + n_row : 2 + n_row + n_col]
    tile, part, row_prof, row_inv, col_prof, col_inv, acc, left = refs[2 + n_row + n_col :]
    per = row_in[0].shape[1] // BLK
    col_blocks, row_blocks = n_row * per, n_col * per
    total = counts[0, 0]
    me_row, me_col = places()
    for k, ref in enumerate(row_in):
        core = lax.rem(me_col + k, 2)
        piece = shifted(me_col // 2, k // 2, n_col // 2) * 2 + core
        for j in range(per):
            block = ref[:, j * BLK : (j + 1) * BLK]
            row_prof[piece * per + j] = block
            width = block.astype(F32)[pcs + 6 : pcs + 7, :]
            row_inv[piece * per + j] = jnp.broadcast_to(1.0 / width, (8, BLK))
    rows = lax.broadcasted_iota(jnp.int32, (FEAT, BLK), 0)
    for k, ref in enumerate(col_in):
        piece = shifted(me_row, k, n_row)
        for j in range(per):
            block = ref[0:FEAT, j * BLK : (j + 1) * BLK].astype(F32)
            turned = jnp.where(rows < pcs, -2.0 * block, 0.0)
            turned = jnp.where((rows >= pcs) & (rows < pcs + 3), 1.0, turned)
            turned = jnp.where(
                (rows >= pcs + 3) & (rows < pcs + 6), pltpu.roll(block, 3, 0), turned
            )
            turned = jnp.where(rows == pcs + 7, pltpu.roll(block, 1, 0), turned)
            turned = turned.T
            col_prof[piece * per + j] = turned.astype(BF16)
            col_inv[piece * per + j] = jnp.broadcast_to(
                -LOG2E / turned[:, pcs + 7 : pcs + 8], (BLK, BLK)
            )

    def step(s):
        rb, cb = lists[0, 0, 0, s], lists[0, 0, 1, s]
        distance = jnp.dot(col_prof[cb], row_prof[rb], preferred_element_type=F32)
        block = jnp.exp2(distance * col_inv[cb] * row_inv[rb][0:1, :])
        tile[s] = block.astype(BF16)

    slot_loop(step, total, 1, TILE_GROUP)
    ones = (lax.broadcasted_iota(jnp.int32, (PIECES, BLK), 0) == 0).astype(F32).astype(BF16)
    empty = jnp.zeros_like(ones)
    for b in range(row_blocks):
        left[0, b] = jnp.concatenate([ones, empty], axis=1)
        left[1, b] = jnp.concatenate([empty, ones], axis=1)
    acc[...] = jnp.zeros_like(acc)
    tile_col_sums(lists, tile, left, acc, total, col_blocks)
    part[...] = jnp.sum(acc[0:col_blocks], axis=1)


def tile_pass_kernel(over_rows, n_parts, *refs):
    lists, counts, tile = refs[:3]
    parts = refs[3 : 3 + n_parts]
    out, stage, left, acc = refs[-4:]
    total = counts[0, 0]
    blocks = out.shape[0]
    me_row, me_col = places()
    scaling = SCALE / ordered_sum(stage, parts, me_row if over_rows else me_col // 2)
    fill_pieces(left, scaling)
    acc[...] = jnp.zeros_like(acc)
    (tile_row_sums if over_rows else tile_col_sums)(lists, tile, left, acc, total, blocks)
    out[...] = jnp.sum(acc[0:blocks], axis=1)


def tile_last_kernel(n_row, n_col, n_land, *refs):
    lists, counts, marks, tile = refs[:4]
    parts, bases = refs[4 : 4 + n_row], refs[4 + n_row : 4 + 2 * n_row]
    keep, away, both, scaling_out, stage, scaled, acc = refs[4 + 2 * n_row :]
    cols = bases[0].shape[0]
    per = bases[0].shape[1] // BLK
    blocks = n_col * per
    total = counts[0, 0]
    me_row, me_col = places()
    scaling = SCALE / ordered_sum(stage, parts, me_row)
    scaling_out[...] = scaling
    for k in range(n_row):
        piece = shifted(me_row, k, n_row)
        for j in range(per):
            block = bases[k][:, j * BLK : (j + 1) * BLK].astype(F32)
            b = piece * per + j
            scaled[b, 0:cols] = (block * scaling_out[pl.ds(b, 1), :]).astype(BF16)
    high, mid, low = split3(scaling)
    shape = (PIECES, BLK)
    rows = lax.broadcasted_iota(jnp.int32, shape, 0)
    for b in range(scaling.shape[0]):
        value = jnp.where(
            rows == 0,
            jnp.broadcast_to(high[b : b + 1], shape),
            jnp.where(
                rows == 1,
                jnp.broadcast_to(mid[b : b + 1], shape),
                jnp.where(rows == 2, jnp.broadcast_to(low[b : b + 1], shape), 0.0),
            ),
        )
        scaled[b, cols : cols + PIECES] = value.astype(BF16)
    acc[...] = jnp.zeros_like(acc)

    def step(s):
        target = jnp.where(s < total, lists[0, 0, 0, s], blocks)
        sums = jnp.dot(scaled[lists[0, 0, 1, s]], tile[s], preferred_element_type=F32)
        acc[target] += sums[0 : cols + 8]

    slot_loop(step, total, 1, TILE_GROUP)
    core = lax.rem(me_col, 2)
    for q in range(n_col // 2):
        own = (2 * q + core) * per
        other = (2 * q + 1 - core) * per
        for j in range(per):
            keep[q, j] = acc[own + j, 0:cols]
            away[q, j] = acc[other + j, 0:cols].astype(BF16)
    row_part = jnp.sum(acc[0:blocks, cols : cols + 8], axis=1)
    for i, value in enumerate(pieces_of(row_part)):
        both[i * blocks : (i + 1) * blocks] = value
    for i in range(n_land):
        first = 3 * blocks + i * cols
        both[first : first + cols] = acc[marks[me_row * n_land + i] - me_row * blocks, 0:cols].astype(BF16)


def tile_body(profiles, cell_width, basis, block_lists, block_counts, landmarks):
    n_row, n_col = lax.axis_size("row"), lax.axis_size("col")
    n_chip = n_col // 2
    pcs, share = profiles.shape
    cols = basis.shape[0]
    per = share // BLK
    row_blocks, col_blocks = n_col * per, n_row * per
    slots = block_lists.shape[-1]
    n_land = landmarks.shape[0] // n_row

    def shape(*dims, dtype=F32):
        return jax.ShapeDtypeStruct(dims, dtype)

    (packed,) = call(
        tile_pack_kernel,
        [shape(FEAT, share, dtype=BF16)],
        vec(profiles, cell_width.reshape(1, share)),
        [pltpu.VMEM((FEAT, share), F32)],
    )
    spread = lax.ppermute(
        packed,
        ("row", "col"),
        [((q % n_row) * n_col + q // n_row, q) for q in range(n_row * n_col)],
    )
    row_packs = []
    for pack in chip_shifts(spread):
        row_packs += [pack, sibling(pack)]
    col_packs = shifts(packed, "row")
    bases = shifts(basis, "row")
    lists = [("smem", block_lists), ("smem", block_counts)]
    marks = [("smem", landmarks)]
    tile, part = call(
        functools.partial(tile_build_kernel, pcs, n_row, n_col),
        [pltpu.VMEM((slots, BLK, BLK), BF16), shape(col_blocks, BLK)],
        lists + vec(*col_packs, *row_packs),
        [
            pltpu.VMEM((row_blocks, FEAT, BLK), BF16),
            pltpu.VMEM((row_blocks, 8, BLK), F32),
            pltpu.VMEM((col_blocks, BLK, FEAT), BF16),
            pltpu.VMEM((col_blocks, BLK, BLK), F32),
            pltpu.VMEM((col_blocks + 1, 8, BLK), F32),
            pltpu.VMEM((2, row_blocks, PIECES, 2 * BLK), BF16),
        ],
    )
    for number in range(SWEEPS - 1):
        early = [("any", b) for b in bases[1:]] if number == 0 else []
        (part,) = call(
            functools.partial(tile_pass_kernel, True, n_row),
            [shape(row_blocks, BLK)],
            lists + [("keep", tile)] + vec(*shifts(part, "row")) + early,
            [
                pltpu.VMEM((n_row, col_blocks, BLK), F32),
                pltpu.VMEM((2, col_blocks, PIECES, 2 * BLK), BF16),
                pltpu.VMEM((row_blocks + 1, 8, BLK), F32),
            ],
        )
        (part,) = call(
            functools.partial(tile_pass_kernel, False, n_chip),
            [shape(col_blocks, BLK)],
            lists + [("keep", tile)] + vec(*chip_shifts(part + sibling(part))),
            [
                pltpu.VMEM((n_chip, row_blocks, BLK), F32),
                pltpu.VMEM((2, row_blocks, PIECES, 2 * BLK), BF16),
                pltpu.VMEM((col_blocks + 1, 8, BLK), F32),
            ],
        )
    both_rows = 3 * row_blocks + n_land * cols
    keep, away, both, col_scaling = call(
        functools.partial(tile_last_kernel, n_row, n_col, n_land),
        [
            shape(n_chip, per, cols, BLK),
            shape(n_chip, per, cols, BLK, dtype=BF16),
            shape(both_rows, BLK, dtype=BF16),
            shape(col_blocks, BLK),
        ],
        lists + marks + [("keep", tile)] + vec(*shifts(part, "row"), *bases),
        [
            pltpu.VMEM((n_row, col_blocks, BLK), F32),
            pltpu.VMEM((col_blocks, cols + PIECES, BLK), BF16),
            pltpu.VMEM((row_blocks + 1, cols + 8, BLK), F32),
        ],
    )
    pairs = call(
        pair_kernel,
        [shape(both_rows, BLK, dtype=BF16)]
        + [shape(per * cols, BLK, dtype=BF16)] * n_chip,
        vec(keep, sibling(away), both, sibling(both)),
    )
    sums = [pairs[0]] + [chip_shift(pairs[0], k) for k in range(1, n_chip)]
    shares = [pairs[1]] + [chip_shift(pairs[1 + k], k) for k in range(1, n_chip)]
    gram, row_scaling, own = call(
        functools.partial(gram_kernel, n_land, cols, per),
        [shape(cols, cols), shape(row_blocks, BLK), shape(per, BLK)],
        marks + vec(*sums),
        [
            pltpu.VMEM((row_blocks, BLK), F32),
            pltpu.VMEM((n_chip, row_blocks, BLK), F32),
            pltpu.VMEM((n_chip, n_land * cols, BLK), BF16),
        ],
    )
    (ritz,) = call(
        functools.partial(ritz_kernel, n_row, landmarks.shape[0] * BLK),
        [shape(cols, share)],
        vec(*shifts(gram, "row"), *shares, own),
        [pltpu.VMEM((n_row, cols, cols), F32)],
    )
    return row_scaling.reshape(-1), col_scaling.reshape(-1), ritz


def solution(mesh):
    placed = (
        P(None, ("col", "row")),
        P(("col", "row")),
        P(None, ("col", "row")),
        P("row", "col", None, None),
        P("row", "col"),
        P(),
    )
    return jax.shard_map(
        strip_body if mesh.shape["row"] <= STRIP_TILES else tile_body,
        mesh=mesh,
        in_specs=placed,
        out_specs=(P("row"), P("col"), P(None, ("row", "col"))),
        check_vma=False,
    )
```

```python
import functools

import jax
import jax.numpy as jnp
from jax import lax
from jax.experimental import pallas as pl
from jax.experimental.pallas import tpu as pltpu
from jax.sharding import PartitionSpec as P

BLK = 128
SWEEPS = 3
GROUP = 32
BUILD_GROUP = 16
TILE_GROUP = 16
ROWS, COLUMNS, COUNT = 0, 1, 2
FEAT = 64
PIECES = 16
SCALE = 512.0
LOG2E = 1.4426950408889634
F32 = jnp.float32
BF16 = jnp.bfloat16
MIB = 1 << 20
STRIP_TILES = 8

VMEM_SPEC = pl.BlockSpec(memory_space=pltpu.VMEM)
SMEM_SPEC = pl.BlockSpec(memory_space=pltpu.SMEM)


def split3(x):
    high = x.astype(BF16).astype(F32)
    mid = (x - high).astype(BF16).astype(F32)
    low = (x - high - mid).astype(BF16).astype(F32)
    return high, mid, low


def tree_sum(values):
    values = list(values)
    while len(values) > 1:
        values = [a + b for a, b in zip(values[::2], values[1::2])]
    return values[0]


def call(kernel, outs, ins, scratch=(), limit=24, flops=1 << 24):
    args, specs = [], []
    for kind, array in ins:
        if kind == "smem":
            specs.append(SMEM_SPEC)
        elif kind == "hbm":
            specs.append(pl.BlockSpec(memory_space=pltpu.HBM))
            array = pltpu.with_memory_space_constraint(array, pltpu.HBM)
        else:
            specs.append(VMEM_SPEC)
            if kind == "keep":
                array = pltpu.with_memory_space_constraint(array, pltpu.VMEM)
        args.append(array)
    return pl.pallas_call(
        kernel,
        out_shape=tuple(outs),
        in_specs=specs,
        out_specs=tuple(VMEM_SPEC for _ in outs),
        scratch_shapes=list(scratch),
        compiler_params=pltpu.CompilerParams(vmem_limit_bytes=limit * MIB),
        cost_estimate=pl.CostEstimate(flops=flops, bytes_accessed=1 << 20, transcendentals=0),
    )(*args)


def pack_kernel(prof_hbm, width_hbm, lists_hbm, counts, out_ref, *scratch):
    work, prof_ref, width_ref, lists_ref, sems = scratch
    pairs = [
        (prof_hbm, prof_ref),
        (width_hbm, width_ref),
        (lists_hbm, lists_ref),
    ]
    copies = [pltpu.make_async_copy(a, b, sems.at[i]) for i, (a, b) in enumerate(pairs)]
    for copy in copies:
        copy.start()
    for copy in copies:
        copy.wait()
    pcs = prof_ref.shape[0]
    prof = prof_ref[...].astype(F32)
    norm = jnp.sum(prof * prof, axis=0, keepdims=True)
    high, mid, low = split3(norm)
    work[...] = jnp.zeros_like(work)
    work[0:pcs, :] = prof
    work[pcs : pcs + 1, :] = high
    work[pcs + 1 : pcs + 2, :] = mid
    work[pcs + 2 : pcs + 3, :] = low
    work[pcs + 3 : pcs + 6, :] = jnp.ones((3, prof.shape[1]), F32)
    work[pcs + 6 : pcs + 7, :] = width_ref[...].astype(F32).reshape(1, -1)
    work[pcs + 8 : pcs + 10, 0:BLK] = lists_ref[0, 0].astype(F32)
    work[pcs + 10 : pcs + 11, 0:BLK] = jnp.full((1, BLK), counts[0, 0], jnp.int32).astype(F32)
    out_ref[...] = work[...].astype(BF16)


def places():
    return lax.axis_index("row"), lax.axis_index("col")


def stack_kernel(pcs, *refs):
    packs, (stack, table) = refs[:-2], refs[-2:]
    n = len(packs)
    me_row, _ = places()
    first = FEAT - 16
    for k, pack in enumerate(packs):
        stack[k] = pack[...]
        rows = pack[first:, 0:BLK].astype(F32)
        rows = pltpu.roll(rows, 16 - (pcs + 8 - first), 0)
        table[shifted(me_row, k, n)] = rows[0:8].astype(jnp.int32)


def slot_loop(step, count, size, group):
    def advance(number, carry):
        for i in range(0, group, size):
            step(*[number * group + i + j for j in range(size)])
        return carry

    lax.fori_loop(0, (count + group - 1) // group, advance, 0)


class Tile:
    def __init__(self, table, n_row, k, own, others):
        _, me_col = places()
        self.group = shifted(me_col // 2, k, n_row)
        self.table, self.k = table, k
        slots = own.shape[0]
        self.blocks, self.base = (own, 0) if k == 0 else (others, (k - 1) * slots)
        self.total = table[self.group * 8 + COUNT, 0]

    def row(self, s):
        return self.table[self.group * 8 + ROWS, s]

    def column(self, s):
        return self.table[self.group * 8 + COLUMNS, s]

    def block(self, s):
        return self.blocks[self.base + s]


def shifted(me, k, n):
    return lax.rem(me + (n - k), n)


def ordered_sum(stage, refs, me):
    n = len(refs)
    for k, ref in enumerate(refs):
        stage[shifted(me, k, n)] = ref[...]
    return tree_sum([stage[i] for i in range(n)])


def square(tile, slots):
    a, b, c, d = [tile.block(s) for s in slots]
    return jnp.concatenate(
        [jnp.concatenate([a, b], axis=1), jnp.concatenate([c, d], axis=1)], axis=0
    )


def add_rows(acc, sums, firsts, targets):
    for (row, lane), target in zip(firsts, targets):
        acc[target] += sums[row : row + 8, lane : lane + BLK]


def row_sums(tile, left, acc, row_blocks, spare):
    first = tile.group * row_blocks

    def step(*slots):
        low = [left[0, tile.column(s)] for s in slots[:2]]
        high = [left[1, tile.column(s)] for s in slots[2:]]
        sums = jnp.dot(
            jnp.concatenate(low + high, axis=0),
            square(tile, slots),
            preferred_element_type=F32,
        )
        firsts = [(0, 0), (PIECES, BLK), (2 * PIECES, 0), (3 * PIECES, BLK)]
        targets = [jnp.where(s < tile.total, first + tile.row(s), spare) for s in slots]
        add_rows(acc, sums, firsts, targets)

    slot_loop(step, tile.total, 4, GROUP)


def col_sums(tile, left, acc, row_blocks, spare):
    first = tile.group * row_blocks

    def step(*slots):
        if left is None:
            rows = lax.broadcasted_iota(jnp.int32, (4 * PIECES, 2 * BLK), 0)
            lanes = lax.broadcasted_iota(jnp.int32, (4 * PIECES, 2 * BLK), 1)
            block = rows // PIECES
            pieces = (rows % PIECES == 0) & (block % 2 == lanes // BLK)
            pieces = pieces.astype(F32).astype(BF16)
        else:
            pieces = [left[i % 2, first + tile.row(s)] for i, s in enumerate(slots)]
            pieces = jnp.concatenate(pieces, axis=0)
        sums = lax.dot_general(
            pieces,
            square(tile, slots),
            (((1,), (1,)), ((), ())),
            preferred_element_type=F32,
        )
        firsts = [(0, 0), (PIECES, 0), (2 * PIECES, BLK), (3 * PIECES, BLK)]
        targets = [jnp.where(s < tile.total, tile.column(s), spare) for s in slots]
        add_rows(acc, sums, firsts, targets)

    slot_loop(step, tile.total, 4, GROUP)


def fill_pieces(left, scaling):
    high, mid, low = split3(scaling)
    shape = (PIECES, BLK)
    rows = lax.broadcasted_iota(jnp.int32, shape, 0)
    empty = jnp.zeros(shape, F32).astype(BF16)
    for b in range(scaling.shape[0]):
        value = jnp.where(
            rows == 0,
            jnp.broadcast_to(high[b : b + 1], shape),
            jnp.where(
                rows == 1,
                jnp.broadcast_to(mid[b : b + 1], shape),
                jnp.where(rows == 2, jnp.broadcast_to(low[b : b + 1], shape), 0.0),
            ),
        ).astype(BF16)
        left[0, b] = jnp.concatenate([value, empty], axis=1)
        left[1, b] = jnp.concatenate([empty, value], axis=1)


def build(tile, offset, row_prof, row_inv, col_prof, col_inv):
    def step(s):
        row, column = offset + tile.row(s), tile.column(s)
        distance = jnp.dot(col_prof[column], row_prof[row], preferred_element_type=F32)
        block = jnp.exp2(distance * col_inv[column] * row_inv[row][0:1, :])
        tile.blocks[tile.base + s] = block.astype(BF16)

    slot_loop(step, tile.total, 1, BUILD_GROUP)


def fill_rows(pcs, stacks, row_prof, row_inv, offset):
    me_row, me_col = places()
    n_row = stacks[0].shape[0]
    per = stacks[0].shape[2] // BLK
    for i, stack in enumerate(stacks):
        core = lax.rem(me_col + i, 2)
        for k in range(n_row):
            piece = core * n_row + shifted(me_row, k, n_row)
            for j in range(per):
                block = stack[k, :, j * BLK : (j + 1) * BLK]
                row_prof[offset + piece * per + j] = block
                width = block.astype(F32)[pcs + 6 : pcs + 7, :]
                row_inv[offset + piece * per + j] = jnp.broadcast_to(1.0 / width, (8, BLK))


def own_kernel(
    pcs, table, stack, other, tile, col_prof, col_inv, sums, row_prof, row_inv, acc
):
    n_row = stack.shape[0]
    per = stack.shape[2] // BLK
    me_row, _ = places()
    fill_rows(pcs, [stack, other], row_prof, row_inv, 0)
    rows = lax.broadcasted_iota(jnp.int32, (FEAT, BLK), 0)
    for k in range(n_row):
        piece = shifted(me_row, k, n_row)
        for j in range(per):
            block = stack[k, :, j * BLK : (j + 1) * BLK].astype(F32)
            turned = jnp.where(rows < pcs, -2.0 * block, 0.0)
            turned = jnp.where((rows >= pcs) & (rows < pcs + 3), 1.0, turned)
            turned = jnp.where(
                (rows >= pcs + 3) & (rows < pcs + 6), pltpu.roll(block, 3, 0), turned
            )
            turned = jnp.where(rows == pcs + 7, pltpu.roll(block, 1, 0), turned)
            turned = turned.T
            col_prof[piece * per + j] = turned.astype(BF16)
            col_inv[piece * per + j] = jnp.broadcast_to(
                -LOG2E / turned[:, pcs + 7 : pcs + 8], (BLK, BLK)
            )
    own = Tile(table, n_row, 0, tile, None)
    build(own, 0, row_prof, row_inv, col_prof, col_inv)
    sums[...] = column_totals([own], None, acc, row_prof.shape[0])


def column_totals(tiles, left, acc, row_blocks):
    col_blocks = acc.shape[0] - 1
    acc[...] = jnp.zeros_like(acc)
    for tile in tiles:
        col_sums(tile, left, acc, row_blocks, col_blocks)
    return jnp.sum(acc[0:col_blocks], axis=1)


def row_part(tiles, left, acc, row_blocks, out):
    blocks = acc.shape[0] - 1
    acc[...] = jnp.zeros_like(acc)
    for tile in tiles:
        row_sums(tile, left, acc, row_blocks, blocks)
    out[...] = jnp.sum(acc[0:blocks], axis=1)


def strip_kernel(pcs, n_row, *refs):
    table, own, col_prof, col_inv, own_sums = refs[:5]
    stacks = refs[5 : 5 + 2 * n_row - 2]
    others, out, row_prof, row_inv, left, row_acc, col_acc = refs[-7:]
    row_blocks = row_prof.shape[0] // (n_row - 1)
    tiles = [Tile(table, n_row, k, own, others) for k in range(n_row)]
    for k in range(1, n_row):
        first = (k - 1) * row_blocks
        fill_rows(pcs, stacks[2 * k - 2 : 2 * k], row_prof, row_inv, first)
    for k in range(1, n_row):
        first = (k - 1) * row_blocks
        build(tiles[k], first, row_prof, row_inv, col_prof, col_inv)
    totals = column_totals(tiles[1:], None, col_acc, row_blocks) + own_sums[...]
    fill_pieces(left, SCALE / totals)
    row_part(tiles, left, row_acc, row_blocks, out)


def row_scalings(stage, parts):
    for k, part in enumerate(parts):
        stage[shifted(places()[1] // 2, k, len(parts))] = part[...].astype(F32)
    return SCALE / tree_sum([stage[i] for i in range(len(parts))])


def sweep_kernel(n_row, n_chip, *refs):
    table, own, others = refs[:3]
    parts = refs[3 : 3 + n_chip]
    out, stage, row_left, left, row_acc, col_acc = refs[-6:]
    row_blocks = out.shape[0] // n_row
    tiles = [Tile(table, n_row, k, own, others) for k in range(n_row)]
    fill_pieces(row_left, row_scalings(stage, parts))
    totals = column_totals(tiles, row_left, col_acc, row_blocks)
    fill_pieces(left, SCALE / totals)
    row_part(tiles, left, row_acc, row_blocks, out)


def pieces_of(value):
    return [v.astype(BF16) for v in split3(value)]


def last_kernel(n_row, n_chip, n_land, *refs):
    table, marks, own, others = refs[:4]
    parts, bases = refs[4 : 4 + n_chip], refs[4 + n_chip : 4 + n_chip + n_row]
    keep, away, both, scaling_out, stage, row_left, col_acc, scaled, acc = refs[-9:]
    cols = bases[0].shape[0]
    per = bases[0].shape[1] // BLK
    blocks = 2 * n_chip * per
    me_row, me_col = places()
    tiles = [Tile(table, n_row, k, own, others) for k in range(n_row)]
    fill_pieces(row_left, row_scalings(stage, parts))
    scaling = SCALE / column_totals(tiles, row_left, col_acc, blocks)
    scaling_out[...] = scaling
    for k in range(n_row):
        piece = shifted(me_row, k, n_row)
        for j in range(per):
            block = bases[k][:, j * BLK : (j + 1) * BLK].astype(F32)
            b = piece * per + j
            scaled[b, 0:cols] = (block * scaling_out[pl.ds(b, 1), :]).astype(BF16)
    high, mid, low = split3(scaling)
    shape = (PIECES, BLK)
    rows = lax.broadcasted_iota(jnp.int32, shape, 0)
    for b in range(scaling.shape[0]):
        value = jnp.where(
            rows == 0,
            jnp.broadcast_to(high[b : b + 1], shape),
            jnp.where(
                rows == 1,
                jnp.broadcast_to(mid[b : b + 1], shape),
                jnp.where(rows == 2, jnp.broadcast_to(low[b : b + 1], shape), 0.0),
            ),
        )
        scaled[b, cols : cols + PIECES] = value.astype(BF16)
    acc[...] = jnp.zeros_like(acc)
    for k in range(n_row):
        tile = tiles[k]

        def step(s, tile=tile):
            target = jnp.where(s < tile.total, tile.row(s), blocks)
            sums = jnp.dot(scaled[tile.column(s)], tile.block(s), preferred_element_type=F32)
            acc[target] += sums[0 : cols + 8]

        slot_loop(step, jnp.where(tile.group == me_row, tile.total, 0), 1, BUILD_GROUP)
    core = lax.rem(me_col, 2)
    for q in range(n_chip):
        mine = (2 * q + core) * per
        other = (2 * q + 1 - core) * per
        for j in range(per):
            keep[q, j] = acc[mine + j, 0:cols]
            away[q, j] = acc[other + j, 0:cols].astype(BF16)
    part = jnp.sum(acc[0:blocks, cols : cols + 8], axis=1)
    for i, value in enumerate(pieces_of(part)):
        both[i * blocks : (i + 1) * blocks] = value
    for i in range(n_land):
        first = 3 * blocks + i * cols
        both[first : first + cols] = acc[marks[me_row * n_land + i] - me_row * blocks, 0:cols].astype(BF16)


def three(ref, blocks):
    value = ref[0 : 3 * blocks].astype(F32)
    return (value[2 * blocks :] + value[blocks : 2 * blocks]) + value[0:blocks]


def pair_kernel(keep, away, both, both_in, both_out, *outs):
    n_chip, per, cols = keep.shape[:3]
    blocks = 2 * n_chip * per
    chip = places()[1] // 2
    parts = pieces_of(three(both, blocks) + three(both_in, blocks))
    for i, value in enumerate(parts):
        both_out[i * blocks : (i + 1) * blocks] = value
    lands = both[3 * blocks :].astype(F32) + both_in[3 * blocks :].astype(F32)
    both_out[3 * blocks :] = lands.astype(BF16)
    for k, out in enumerate(outs):
        to = lax.rem(chip + k, n_chip)
        for j in range(per):
            value = keep[to, j] + away[to, j].astype(F32)
            out[j * cols : (j + 1) * cols] = value.astype(BF16)


def gram_kernel(n_land, cols, per, *refs):
    marks = refs[0]
    gram, scaling_out, own, inverse, stage, land_stage = refs[-6:]
    parts = refs[1:-6]
    n = len(parts)
    me_row, me_col = places()
    blocks = scaling_out.shape[0]
    for k, part in enumerate(parts):
        place = shifted(me_col // 2, k, n)
        stage[place] = three(part, blocks)
        land_stage[place] = part[3 * blocks :]
    inverse[...] = 1.0 / tree_sum([stage[i] for i in range(n)])
    scaling_out[...] = SCALE * inverse[...]
    for j in range(per):
        own[j : j + 1, :] = inverse[pl.ds(me_col * per + j, 1), :]
    total = None
    for i in range(n_land):
        summed = tree_sum(
            [land_stage[k, i * cols : (i + 1) * cols].astype(F32) for k in range(n)]
        )
        block = marks[me_row * n_land + i] - me_row * blocks
        projected = summed * inverse[pl.ds(block, 1), :]
        product = lax.dot_general(
            projected,
            projected,
            (((1,), (1,)), ((), ())),
            precision=lax.Precision.HIGHEST,
            preferred_element_type=F32,
        )
        total = product if total is None else total + product
    gram[...] = total


WIDE = 4


def eliminate(gram):
    cols = gram.shape[0]
    rows = lax.broadcasted_iota(jnp.int32, (cols, 2 * cols), 0)
    lanes = lax.broadcasted_iota(jnp.int32, (cols, 2 * cols), 1)
    unit = (rows[:, :cols] == lanes[:, :cols]).astype(F32)
    work = jnp.concatenate([gram, unit], axis=1)
    for first in range(0, cols, WIDE):
        tops = [work[first + i : first + i + 1, :] for i in range(WIDE)]
        sides = [
            jnp.broadcast_to(work[:, first + i : first + i + 1], work.shape)
            for i in range(WIDE)
        ]
        change = None
        for i in range(WIDE):
            pivot = first + i
            unit_top = tops[i] / sides[i][pivot : pivot + 1, :]
            for m in range(i + 1, WIDE):
                factor = sides[i][first + m : first + m + 1, :]
                tops[m] = tops[m] - factor * unit_top
                inner = factor / sides[i][pivot : pivot + 1, :]
                sides[m] = sides[m] - sides[i] * inner
            term = sides[i] * unit_top
            change = term if change is None else change + term
        reduced = work - change
        kept = work
        for i in range(WIDE):
            kept = jnp.where(rows == first + i, tops[i], kept)
        work = jnp.where(rows >= first + WIDE, reduced, kept)
    pivots = jnp.sum(jnp.where(rows == lanes, work, 0.0), axis=1, keepdims=True)
    return (work * lax.rsqrt(pivots))[:, cols:]


def ritz_kernel(n_row, cells, *refs):
    grams, parts = refs[:n_row], refs[n_row:-3]
    own, out, stage = refs[-3:]
    cols = grams[0].shape[0]
    per = out.shape[1] // BLK
    inverse = eliminate(ordered_sum(stage, grams, places()[0]) * (1.0 / cells))
    for j in range(per):
        summed = tree_sum([m[j * cols : (j + 1) * cols].astype(F32) for m in parts])
        projected = summed * own[j : j + 1, :]
        out[:, j * BLK : (j + 1) * BLK] = jnp.dot(
            inverse, projected, precision=lax.Precision.HIGHEST, preferred_element_type=F32
        )


def swap(x, axis, k):
    return lax.ppermute(x, axis, [(i, i ^ k) for i in range(lax.axis_size(axis))])


def shift(x, axis, k):
    n = lax.axis_size(axis)
    return lax.ppermute(x, axis, [(i, (i + k) % n) for i in range(n)])


def shifts(x, axis):
    return [x] + [shift(x, axis, k) for k in range(1, lax.axis_size(axis))]


def chip_shift(x, k):
    n = lax.axis_size("col") // 2
    return lax.ppermute(
        x,
        "col",
        [(2 * q + p, 2 * ((q + k) % n) + p) for q in range(n) for p in range(2)],
    )


def chip_shifts(x):
    return [x] + [chip_shift(x, k) for k in range(1, lax.axis_size("col") // 2)]


def sibling(x):
    return swap(x, "col", 1)


def vec(*arrays):
    return [("vmem", a) for a in arrays]


def strip_body(profiles, cell_width, basis, block_lists, block_counts, landmarks):
    n_row, n_col = lax.axis_size("row"), lax.axis_size("col")
    n_chip = n_col // 2
    pcs, share = profiles.shape
    cols = basis.shape[0]
    per = share // BLK
    row_blocks, col_blocks = n_col * per, n_row * per
    all_rows = n_row * row_blocks
    slots = block_lists.shape[-1]
    n_land = landmarks.shape[0] // n_row

    def shape(*dims, dtype=F32):
        return jax.ShapeDtypeStruct(dims, dtype)

    (packed,) = call(
        pack_kernel,
        [shape(FEAT, share, dtype=BF16)],
        [("hbm", a) for a in (profiles, cell_width, block_lists)] + [("smem", block_counts)],
        [
            pltpu.VMEM((FEAT, share), F32),
            pltpu.VMEM(profiles.shape, BF16),
            pltpu.VMEM(cell_width.shape, BF16),
            pltpu.VMEM(block_lists.shape, jnp.int32),
            pltpu.SemaphoreType.DMA((3,)),
        ],
    )
    stack, table = call(
        functools.partial(stack_kernel, pcs),
        [shape(n_row, FEAT, share, dtype=BF16), shape(n_row, 8, BLK, dtype=jnp.int32)],
        vec(*shifts(packed, "row")),
    )
    table = ("smem", table.reshape(n_row * 8, BLK))
    marks = ("smem", landmarks)
    far = [chip_shift(stack, k) for k in range(1, n_chip)]
    bases = shifts(basis, "row")
    own, col_prof, col_inv, sums = call(
        functools.partial(own_kernel, pcs),
        [
            pltpu.VMEM((slots, BLK, BLK), BF16),
            pltpu.VMEM((col_blocks, BLK, FEAT), BF16),
            pltpu.VMEM((col_blocks, BLK, BLK), F32),
            shape(col_blocks, BLK),
        ],
        [table] + vec(stack, sibling(stack)),
        [
            pltpu.VMEM((row_blocks, FEAT, BLK), BF16),
            pltpu.VMEM((row_blocks, 8, BLK), F32),
            pltpu.VMEM((col_blocks + 1, 8, BLK), F32),
        ],
    )
    far, sums, bases = lax.optimization_barrier((far, sums, bases))
    stacks = [x for pack in far for x in (pack, sibling(pack))]
    far_slots = (n_row - 1) * slots
    others, part = call(
        functools.partial(strip_kernel, pcs, n_row),
        [pltpu.VMEM((far_slots, BLK, BLK), BF16), shape(all_rows, BLK)],
        [table, ("keep", own), ("keep", col_prof), ("keep", col_inv)]
        + vec(sums, *stacks),
        [
            pltpu.VMEM((all_rows - row_blocks, FEAT, BLK), BF16),
            pltpu.VMEM((all_rows - row_blocks, 8, BLK), F32),
            pltpu.VMEM((2, col_blocks, PIECES, 2 * BLK), BF16),
            pltpu.VMEM((all_rows + 1, 8, BLK), F32),
            pltpu.VMEM((col_blocks + 1, 8, BLK), F32),
        ],
    )
    tiles = [("keep", own), ("keep", others)]

    def chip_parts(part):
        return chip_shifts((part + sibling(part)).astype(BF16))

    for _ in range(SWEEPS - 2):
        (part,) = call(
            functools.partial(sweep_kernel, n_row, n_chip),
            [shape(all_rows, BLK)],
            [table] + tiles + vec(*chip_parts(part)),
            [
                pltpu.VMEM((n_chip, all_rows, BLK), F32),
                pltpu.VMEM((2, all_rows, PIECES, 2 * BLK), BF16),
                pltpu.VMEM((2, col_blocks, PIECES, 2 * BLK), BF16),
                pltpu.VMEM((all_rows + 1, 8, BLK), F32),
                pltpu.VMEM((col_blocks + 1, 8, BLK), F32),
            ],
        )
    both_rows = 3 * row_blocks + n_land * cols
    keep, away, both, col_scaling = call(
        functools.partial(last_kernel, n_row, n_chip, n_land),
        [
            shape(n_chip, per, cols, BLK),
            shape(n_chip, per, cols, BLK, dtype=BF16),
            shape(both_rows, BLK, dtype=BF16),
            shape(col_blocks, BLK),
        ],
        [table, marks] + tiles + vec(*chip_parts(part), *bases),
        [
            pltpu.VMEM((n_chip, all_rows, BLK), F32),
            pltpu.VMEM((2, all_rows, PIECES, 2 * BLK), BF16),
            pltpu.VMEM((col_blocks + 1, 8, BLK), F32),
            pltpu.VMEM((col_blocks, cols + PIECES, BLK), BF16),
            pltpu.VMEM((row_blocks + 1, cols + 8, BLK), F32),
        ],
    )
    pairs = call(
        pair_kernel,
        [shape(both_rows, BLK, dtype=BF16)]
        + [shape(per * cols, BLK, dtype=BF16)] * n_chip,
        vec(keep, sibling(away), both, sibling(both)),
    )
    sums = [pairs[0]] + [chip_shift(pairs[0], k) for k in range(1, n_chip)]
    shares = [pairs[1]] + [chip_shift(pairs[1 + k], k) for k in range(1, n_chip)]
    gram, row_scaling, own = call(
        functools.partial(gram_kernel, n_land, cols, per),
        [shape(cols, cols), shape(row_blocks, BLK), shape(per, BLK)],
        [marks] + vec(*sums),
        [
            pltpu.VMEM((row_blocks, BLK), F32),
            pltpu.VMEM((n_chip, row_blocks, BLK), F32),
            pltpu.VMEM((n_chip, n_land * cols, BLK), BF16),
        ],
    )
    (ritz,) = call(
        functools.partial(ritz_kernel, n_row, landmarks.shape[0] * BLK),
        [shape(cols, share)],
        vec(*shifts(gram, "row"), *shares, own),
        [pltpu.VMEM((n_row, cols, cols), F32)],
    )
    return row_scaling.reshape(-1), col_scaling.reshape(-1), ritz


def tile_pack_kernel(prof_ref, width_ref, out_ref, work):
    pcs = prof_ref.shape[0]
    prof = prof_ref[...].astype(F32)
    norm = jnp.sum(prof * prof, axis=0, keepdims=True)
    high, mid, low = split3(norm)
    work[...] = jnp.zeros_like(work)
    work[0:pcs, :] = prof
    work[pcs : pcs + 1, :] = high
    work[pcs + 1 : pcs + 2, :] = mid
    work[pcs + 2 : pcs + 3, :] = low
    work[pcs + 3 : pcs + 6, :] = jnp.ones((3, prof.shape[1]), F32)
    work[pcs + 6 : pcs + 7, :] = width_ref[...].astype(F32)
    out_ref[...] = work[...].astype(BF16)


def tile_square(tile, slots):
    a, b, c, d = [tile[s] for s in slots]
    return jnp.concatenate(
        [jnp.concatenate([a, b], axis=1), jnp.concatenate([c, d], axis=1)], axis=0
    )


def tile_add_rows(acc, lists, target, slots, sums, total, spare, firsts):
    for i, (s, (row, lane)) in enumerate(zip(slots, firsts)):
        place = jnp.where(s < total, lists[0, 0, target, s], spare)
        acc[place] += sums[row : row + 8, lane : lane + BLK]


def tile_row_sums(lists, tile, left, acc, total, spare):
    def step(*slots):
        low = [left[0, lists[0, 0, 1, s]] for s in slots[:2]]
        high = [left[1, lists[0, 0, 1, s]] for s in slots[2:]]
        sums = jnp.dot(
            jnp.concatenate(low + high, axis=0),
            tile_square(tile, slots),
            preferred_element_type=F32,
        )
        firsts = [(0, 0), (PIECES, BLK), (2 * PIECES, 0), (3 * PIECES, BLK)]
        tile_add_rows(acc, lists, 0, slots, sums, total, spare, firsts)

    slot_loop(step, total, 4, 4 * TILE_GROUP)


def tile_col_sums(lists, tile, left, acc, total, spare):
    def step(*slots):
        pieces = [left[i % 2, lists[0, 0, 0, s]] for i, s in enumerate(slots)]
        sums = lax.dot_general(
            jnp.concatenate(pieces, axis=0),
            tile_square(tile, slots),
            (((1,), (1,)), ((), ())),
            preferred_element_type=F32,
        )
        firsts = [(0, 0), (PIECES, 0), (2 * PIECES, BLK), (3 * PIECES, BLK)]
        tile_add_rows(acc, lists, 1, slots, sums, total, spare, firsts)

    slot_loop(step, total, 4, 4 * TILE_GROUP)


def tile_build_kernel(pcs, n_row, n_col, *refs):
    lists, counts = refs[:2]
    col_in = refs[2 : 2 + n_row]
    row_in = refs[2 + n_row : 2 + n_row + n_col]
    tile, part, row_prof, row_inv, col_prof, col_inv, acc, left = refs[2 + n_row + n_col :]
    per = row_in[0].shape[1] // BLK
    col_blocks, row_blocks = n_row * per, n_col * per
    total = counts[0, 0]
    me_row, me_col = places()
    for k, ref in enumerate(row_in):
        core = lax.rem(me_col + k, 2)
        piece = shifted(me_col // 2, k // 2, n_col // 2) * 2 + core
        for j in range(per):
            block = ref[:, j * BLK : (j + 1) * BLK]
            row_prof[piece * per + j] = block
            width = block.astype(F32)[pcs + 6 : pcs + 7, :]
            row_inv[piece * per + j] = jnp.broadcast_to(1.0 / width, (8, BLK))
    rows = lax.broadcasted_iota(jnp.int32, (FEAT, BLK), 0)
    for k, ref in enumerate(col_in):
        piece = shifted(me_row, k, n_row)
        for j in range(per):
            block = ref[0:FEAT, j * BLK : (j + 1) * BLK].astype(F32)
            turned = jnp.where(rows < pcs, -2.0 * block, 0.0)
            turned = jnp.where((rows >= pcs) & (rows < pcs + 3), 1.0, turned)
            turned = jnp.where(
                (rows >= pcs + 3) & (rows < pcs + 6), pltpu.roll(block, 3, 0), turned
            )
            turned = jnp.where(rows == pcs + 7, pltpu.roll(block, 1, 0), turned)
            turned = turned.T
            col_prof[piece * per + j] = turned.astype(BF16)
            col_inv[piece * per + j] = jnp.broadcast_to(
                -LOG2E / turned[:, pcs + 7 : pcs + 8], (BLK, BLK)
            )

    def step(s):
        rb, cb = lists[0, 0, 0, s], lists[0, 0, 1, s]
        distance = jnp.dot(col_prof[cb], row_prof[rb], preferred_element_type=F32)
        block = jnp.exp2(distance * col_inv[cb] * row_inv[rb][0:1, :])
        tile[s] = block.astype(BF16)

    slot_loop(step, total, 1, TILE_GROUP)
    ones = (lax.broadcasted_iota(jnp.int32, (PIECES, BLK), 0) == 0).astype(F32).astype(BF16)
    empty = jnp.zeros_like(ones)
    for b in range(row_blocks):
        left[0, b] = jnp.concatenate([ones, empty], axis=1)
        left[1, b] = jnp.concatenate([empty, ones], axis=1)
    acc[...] = jnp.zeros_like(acc)
    tile_col_sums(lists, tile, left, acc, total, col_blocks)
    part[...] = jnp.sum(acc[0:col_blocks], axis=1)


def tile_pass_kernel(over_rows, n_parts, *refs):
    lists, counts, tile = refs[:3]
    parts = refs[3 : 3 + n_parts]
    out, stage, left, acc = refs[-4:]
    total = counts[0, 0]
    blocks = out.shape[0]
    me_row, me_col = places()
    scaling = SCALE / ordered_sum(stage, parts, me_row if over_rows else me_col // 2)
    fill_pieces(left, scaling)
    acc[...] = jnp.zeros_like(acc)
    (tile_row_sums if over_rows else tile_col_sums)(lists, tile, left, acc, total, blocks)
    out[...] = jnp.sum(acc[0:blocks], axis=1)


def tile_last_kernel(n_row, n_col, n_land, *refs):
    lists, counts, marks, tile = refs[:4]
    parts, bases = refs[4 : 4 + n_row], refs[4 + n_row : 4 + 2 * n_row]
    keep, away, both, scaling_out, stage, scaled, acc = refs[4 + 2 * n_row :]
    cols = bases[0].shape[0]
    per = bases[0].shape[1] // BLK
    blocks = n_col * per
    total = counts[0, 0]
    me_row, me_col = places()
    scaling = SCALE / ordered_sum(stage, parts, me_row)
    scaling_out[...] = scaling
    for k in range(n_row):
        piece = shifted(me_row, k, n_row)
        for j in range(per):
            block = bases[k][:, j * BLK : (j + 1) * BLK].astype(F32)
            b = piece * per + j
            scaled[b, 0:cols] = (block * scaling_out[pl.ds(b, 1), :]).astype(BF16)
    high, mid, low = split3(scaling)
    shape = (PIECES, BLK)
    rows = lax.broadcasted_iota(jnp.int32, shape, 0)
    for b in range(scaling.shape[0]):
        value = jnp.where(
            rows == 0,
            jnp.broadcast_to(high[b : b + 1], shape),
            jnp.where(
                rows == 1,
                jnp.broadcast_to(mid[b : b + 1], shape),
                jnp.where(rows == 2, jnp.broadcast_to(low[b : b + 1], shape), 0.0),
            ),
        )
        scaled[b, cols : cols + PIECES] = value.astype(BF16)
    acc[...] = jnp.zeros_like(acc)

    def step(s):
        target = jnp.where(s < total, lists[0, 0, 0, s], blocks)
        sums = jnp.dot(scaled[lists[0, 0, 1, s]], tile[s], preferred_element_type=F32)
        acc[target] += sums[0 : cols + 8]

    slot_loop(step, total, 1, TILE_GROUP)
    core = lax.rem(me_col, 2)
    for q in range(n_col // 2):
        own = (2 * q + core) * per
        other = (2 * q + 1 - core) * per
        for j in range(per):
            keep[q, j] = acc[own + j, 0:cols]
            away[q, j] = acc[other + j, 0:cols].astype(BF16)
    row_part = jnp.sum(acc[0:blocks, cols : cols + 8], axis=1)
    for i, value in enumerate(pieces_of(row_part)):
        both[i * blocks : (i + 1) * blocks] = value
    for i in range(n_land):
        first = 3 * blocks + i * cols
        both[first : first + cols] = acc[marks[me_row * n_land + i] - me_row * blocks, 0:cols].astype(BF16)


def tile_body(profiles, cell_width, basis, block_lists, block_counts, landmarks):
    n_row, n_col = lax.axis_size("row"), lax.axis_size("col")
    n_chip = n_col // 2
    pcs, share = profiles.shape
    cols = basis.shape[0]
    per = share // BLK
    row_blocks, col_blocks = n_col * per, n_row * per
    slots = block_lists.shape[-1]
    n_land = landmarks.shape[0] // n_row

    def shape(*dims, dtype=F32):
        return jax.ShapeDtypeStruct(dims, dtype)

    (packed,) = call(
        tile_pack_kernel,
        [shape(FEAT, share, dtype=BF16)],
        vec(profiles, cell_width.reshape(1, share)),
        [pltpu.VMEM((FEAT, share), F32)],
    )
    spread = lax.ppermute(
        packed,
        ("row", "col"),
        [((q % n_row) * n_col + q // n_row, q) for q in range(n_row * n_col)],
    )
    row_packs = []
    for pack in chip_shifts(spread):
        row_packs += [pack, sibling(pack)]
    col_packs = shifts(packed, "row")
    bases = shifts(basis, "row")
    lists = [("smem", block_lists), ("smem", block_counts)]
    marks = [("smem", landmarks)]
    tile, part = call(
        functools.partial(tile_build_kernel, pcs, n_row, n_col),
        [pltpu.VMEM((slots, BLK, BLK), BF16), shape(col_blocks, BLK)],
        lists + vec(*col_packs, *row_packs),
        [
            pltpu.VMEM((row_blocks, FEAT, BLK), BF16),
            pltpu.VMEM((row_blocks, 8, BLK), F32),
            pltpu.VMEM((col_blocks, BLK, FEAT), BF16),
            pltpu.VMEM((col_blocks, BLK, BLK), F32),
            pltpu.VMEM((col_blocks + 1, 8, BLK), F32),
            pltpu.VMEM((2, row_blocks, PIECES, 2 * BLK), BF16),
        ],
    )
    for number in range(SWEEPS - 1):
        early = [("hbm", b) for b in bases[1:]] if number == 0 else []
        (part,) = call(
            functools.partial(tile_pass_kernel, True, n_row),
            [shape(row_blocks, BLK)],
            lists + [("keep", tile)] + vec(*shifts(part, "row")) + early,
            [
                pltpu.VMEM((n_row, col_blocks, BLK), F32),
                pltpu.VMEM((2, col_blocks, PIECES, 2 * BLK), BF16),
                pltpu.VMEM((row_blocks + 1, 8, BLK), F32),
            ],
        )
        (part,) = call(
            functools.partial(tile_pass_kernel, False, n_chip),
            [shape(col_blocks, BLK)],
            lists + [("keep", tile)] + vec(*chip_shifts(part + sibling(part))),
            [
                pltpu.VMEM((n_chip, row_blocks, BLK), F32),
                pltpu.VMEM((2, row_blocks, PIECES, 2 * BLK), BF16),
                pltpu.VMEM((col_blocks + 1, 8, BLK), F32),
            ],
        )
    both_rows = 3 * row_blocks + n_land * cols
    keep, away, both, col_scaling = call(
        functools.partial(tile_last_kernel, n_row, n_col, n_land),
        [
            shape(n_chip, per, cols, BLK),
            shape(n_chip, per, cols, BLK, dtype=BF16),
            shape(both_rows, BLK, dtype=BF16),
            shape(col_blocks, BLK),
        ],
        lists + marks + [("keep", tile)] + vec(*shifts(part, "row"), *bases),
        [
            pltpu.VMEM((n_row, col_blocks, BLK), F32),
            pltpu.VMEM((col_blocks, cols + PIECES, BLK), BF16),
            pltpu.VMEM((row_blocks + 1, cols + 8, BLK), F32),
        ],
    )
    pairs = call(
        pair_kernel,
        [shape(both_rows, BLK, dtype=BF16)]
        + [shape(per * cols, BLK, dtype=BF16)] * n_chip,
        vec(keep, sibling(away), both, sibling(both)),
    )
    sums = [pairs[0]] + [chip_shift(pairs[0], k) for k in range(1, n_chip)]
    shares = [pairs[1]] + [chip_shift(pairs[1 + k], k) for k in range(1, n_chip)]
    gram, row_scaling, own = call(
        functools.partial(gram_kernel, n_land, cols, per),
        [shape(cols, cols), shape(row_blocks, BLK), shape(per, BLK)],
        marks + vec(*sums),
        [
            pltpu.VMEM((row_blocks, BLK), F32),
            pltpu.VMEM((n_chip, row_blocks, BLK), F32),
            pltpu.VMEM((n_chip, n_land * cols, BLK), BF16),
        ],
    )
    (ritz,) = call(
        functools.partial(ritz_kernel, n_row, landmarks.shape[0] * BLK),
        [shape(cols, share)],
        vec(*shifts(gram, "row"), *shares, own),
        [pltpu.VMEM((n_row, cols, cols), F32)],
    )
    return row_scaling.reshape(-1), col_scaling.reshape(-1), ritz


def solution(mesh):
    placed = (
        P(None, ("col", "row")),
        P(("col", "row")),
        P(None, ("col", "row")),
        P("row", "col", None, None),
        P("row", "col"),
        P(),
    )
    return jax.shard_map(
        strip_body if mesh.shape["row"] <= STRIP_TILES else tile_body,
        mesh=mesh,
        in_specs=placed,
        out_specs=(P("row"), P("col"), P(None, ("row", "col"))),
        check_vma=False,
    )
```

```python
import functools

import jax
import jax.numpy as jnp
from jax import lax
from jax.experimental import pallas as pl
from jax.experimental.pallas import tpu as pltpu
from jax.sharding import PartitionSpec as P

BLK = 128
SWEEPS = 3
GROUP = 32
BUILD_GROUP = 16
TILE_GROUP = 16
ROWS, COLUMNS, COUNT = 0, 1, 2
FEAT = 64
PIECES = 16
SCALE = 512.0
LOG2E = 1.4426950408889634
F32 = jnp.float32
BF16 = jnp.bfloat16
MIB = 1 << 20
STRIP_TILES = 8

VMEM_SPEC = pl.BlockSpec(memory_space=pltpu.VMEM)
SMEM_SPEC = pl.BlockSpec(memory_space=pltpu.SMEM)


def split3(x):
    high = x.astype(BF16).astype(F32)
    mid = (x - high).astype(BF16).astype(F32)
    low = (x - high - mid).astype(BF16).astype(F32)
    return high, mid, low


def tree_sum(values):
    values = list(values)
    while len(values) > 1:
        values = [a + b for a, b in zip(values[::2], values[1::2])]
    return values[0]


def call(kernel, outs, ins, scratch=(), limit=24, flops=1 << 24):
    args, specs = [], []
    for kind, array in ins:
        if kind == "smem":
            specs.append(SMEM_SPEC)
        elif kind == "near":
            specs.append(pl.BlockSpec(memory_space=pl.ANY))
        elif kind == "hbm":
            specs.append(pl.BlockSpec(memory_space=pltpu.HBM))
            array = pltpu.with_memory_space_constraint(array, pltpu.HBM)
        else:
            specs.append(VMEM_SPEC)
            if kind == "keep":
                array = pltpu.with_memory_space_constraint(array, pltpu.VMEM)
        args.append(array)
    return pl.pallas_call(
        kernel,
        out_shape=tuple(outs),
        in_specs=specs,
        out_specs=tuple(VMEM_SPEC for _ in outs),
        scratch_shapes=list(scratch),
        compiler_params=pltpu.CompilerParams(vmem_limit_bytes=limit * MIB),
        cost_estimate=pl.CostEstimate(flops=flops, bytes_accessed=1 << 20, transcendentals=0),
    )(*args)


def pack_kernel(prof_hbm, width_hbm, lists_hbm, counts, out_ref, *scratch):
    work, prof_ref, width_ref, lists_ref, sems = scratch
    pairs = [
        (prof_hbm, prof_ref),
        (width_hbm, width_ref),
        (lists_hbm, lists_ref),
    ]
    copies = [pltpu.make_async_copy(a, b, sems.at[i]) for i, (a, b) in enumerate(pairs)]
    for copy in copies:
        copy.start()
    for copy in copies:
        copy.wait()
    pcs = prof_ref.shape[0]
    prof = prof_ref[...].astype(F32)
    norm = jnp.sum(prof * prof, axis=0, keepdims=True)
    high, mid, low = split3(norm)
    work[...] = jnp.zeros_like(work)
    work[0:pcs, :] = prof
    work[pcs : pcs + 1, :] = high
    work[pcs + 1 : pcs + 2, :] = mid
    work[pcs + 2 : pcs + 3, :] = low
    work[pcs + 3 : pcs + 6, :] = jnp.ones((3, prof.shape[1]), F32)
    work[pcs + 6 : pcs + 7, :] = width_ref[...].astype(F32).reshape(1, -1)
    work[pcs + 8 : pcs + 10, 0:BLK] = lists_ref[0, 0].astype(F32)
    work[pcs + 10 : pcs + 11, 0:BLK] = jnp.full((1, BLK), counts[0, 0], jnp.int32).astype(F32)
    out_ref[...] = work[...].astype(BF16)


def places():
    return lax.axis_index("row"), lax.axis_index("col")


def stack_kernel(pcs, *refs):
    packs, (stack, table) = refs[:-2], refs[-2:]
    n = len(packs)
    me_row, _ = places()
    first = FEAT - 16
    for k, pack in enumerate(packs):
        stack[k] = pack[...]
        rows = pack[first:, 0:BLK].astype(F32)
        rows = pltpu.roll(rows, 16 - (pcs + 8 - first), 0)
        table[shifted(me_row, k, n)] = rows[0:8].astype(jnp.int32)


def slot_loop(step, count, size, group):
    def advance(number, carry):
        for i in range(0, group, size):
            step(*[number * group + i + j for j in range(size)])
        return carry

    lax.fori_loop(0, (count + group - 1) // group, advance, 0)


class Tile:
    def __init__(self, table, n_row, k, own, others):
        _, me_col = places()
        self.group = shifted(me_col // 2, k, n_row)
        self.table, self.k = table, k
        slots = own.shape[0]
        self.blocks, self.base = (own, 0) if k == 0 else (others, (k - 1) * slots)
        self.total = table[self.group * 8 + COUNT, 0]

    def row(self, s):
        return self.table[self.group * 8 + ROWS, s]

    def column(self, s):
        return self.table[self.group * 8 + COLUMNS, s]

    def block(self, s):
        return self.blocks[self.base + s]


def shifted(me, k, n):
    return lax.rem(me + (n - k), n)


def ordered_sum(stage, refs, me):
    n = len(refs)
    for k, ref in enumerate(refs):
        stage[shifted(me, k, n)] = ref[...]
    return tree_sum([stage[i] for i in range(n)])


def square(tile, slots):
    a, b, c, d = [tile.block(s) for s in slots]
    return jnp.concatenate(
        [jnp.concatenate([a, b], axis=1), jnp.concatenate([c, d], axis=1)], axis=0
    )


def add_rows(acc, sums, firsts, targets):
    for (row, lane), target in zip(firsts, targets):
        acc[target] += sums[row : row + 8, lane : lane + BLK]


def row_sums(tile, wide, acc, row_blocks, spare):
    first = tile.group * row_blocks

    def step(s):
        product = tile.block(s).astype(F32) * wide[tile.column(s)]
        sums = jnp.sum(product.reshape(BLK // 8, 8, BLK), axis=0)
        acc[jnp.where(s < tile.total, first + tile.row(s), spare)] += sums

    slot_loop(step, tile.total, 1, GROUP)


def spread_lanes(wide, scaling):
    turned = scaling.T
    for b in range(scaling.shape[0]):
        wide[b] = jnp.broadcast_to(turned[:, b : b + 1], (BLK, BLK))


def col_sums(tile, left, acc, row_blocks, spare):
    first = tile.group * row_blocks

    def step(*slots):
        if left is None:
            rows = lax.broadcasted_iota(jnp.int32, (4 * PIECES, 2 * BLK), 0)
            lanes = lax.broadcasted_iota(jnp.int32, (4 * PIECES, 2 * BLK), 1)
            block = rows // PIECES
            pieces = (rows % PIECES == 0) & (block % 2 == lanes // BLK)
            pieces = pieces.astype(F32).astype(BF16)
        else:
            pieces = [left[i % 2, first + tile.row(s)] for i, s in enumerate(slots)]
            pieces = jnp.concatenate(pieces, axis=0)
        sums = lax.dot_general(
            pieces,
            square(tile, slots),
            (((1,), (1,)), ((), ())),
            preferred_element_type=F32,
        )
        firsts = [(0, 0), (PIECES, 0), (2 * PIECES, BLK), (3 * PIECES, BLK)]
        targets = [jnp.where(s < tile.total, tile.column(s), spare) for s in slots]
        add_rows(acc, sums, firsts, targets)

    slot_loop(step, tile.total, 4, 2 * GROUP if tile.k == 0 else GROUP)


def fill_pieces(left, scaling):
    high, mid, low = split3(scaling)
    shape = (PIECES, BLK)
    rows = lax.broadcasted_iota(jnp.int32, shape, 0)
    empty = jnp.zeros(shape, F32).astype(BF16)
    for b in range(scaling.shape[0]):
        value = jnp.where(
            rows == 0,
            jnp.broadcast_to(high[b : b + 1], shape),
            jnp.where(
                rows == 1,
                jnp.broadcast_to(mid[b : b + 1], shape),
                jnp.where(rows == 2, jnp.broadcast_to(low[b : b + 1], shape), 0.0),
            ),
        ).astype(BF16)
        left[0, b] = jnp.concatenate([value, empty], axis=1)
        left[1, b] = jnp.concatenate([empty, value], axis=1)


def build(tile, offset, row_prof, row_inv, col_prof, col_inv):
    def step(s):
        row, column = offset + tile.row(s), tile.column(s)
        distance = jnp.dot(col_prof[column], row_prof[row], preferred_element_type=F32)
        block = jnp.exp2(distance * col_inv[column] * row_inv[row][0:1, :])
        tile.blocks[tile.base + s] = block.astype(BF16)

    slot_loop(step, tile.total, 1, BUILD_GROUP)


def fill_rows(pcs, stacks, row_prof, row_inv, offset):
    me_row, me_col = places()
    n_row = stacks[0].shape[0]
    per = stacks[0].shape[2] // BLK
    for i, stack in enumerate(stacks):
        core = lax.rem(me_col + i, 2)
        for k in range(n_row):
            piece = core * n_row + shifted(me_row, k, n_row)
            for j in range(per):
                block = stack[k, :, j * BLK : (j + 1) * BLK]
                row_prof[offset + piece * per + j] = block
                width = block.astype(F32)[pcs + 6 : pcs + 7, :]
                row_inv[offset + piece * per + j] = jnp.broadcast_to(1.0 / width, (8, BLK))


def own_kernel(
    pcs, table, stack, other, tile, col_prof, col_inv, sums, row_prof, row_inv, acc
):
    n_row = stack.shape[0]
    per = stack.shape[2] // BLK
    me_row, _ = places()
    fill_rows(pcs, [stack, other], row_prof, row_inv, 0)
    rows = lax.broadcasted_iota(jnp.int32, (FEAT, BLK), 0)
    for k in range(n_row):
        piece = shifted(me_row, k, n_row)
        for j in range(per):
            block = stack[k, :, j * BLK : (j + 1) * BLK].astype(F32)
            turned = jnp.where(rows < pcs, -2.0 * block, 0.0)
            turned = jnp.where((rows >= pcs) & (rows < pcs + 3), 1.0, turned)
            turned = jnp.where(
                (rows >= pcs + 3) & (rows < pcs + 6), pltpu.roll(block, 3, 0), turned
            )
            turned = jnp.where(rows == pcs + 7, pltpu.roll(block, 1, 0), turned)
            turned = turned.T
            col_prof[piece * per + j] = turned.astype(BF16)
            col_inv[piece * per + j] = jnp.broadcast_to(
                -LOG2E / turned[:, pcs + 7 : pcs + 8], (BLK, BLK)
            )
    own = Tile(table, n_row, 0, tile, None)
    build(own, 0, row_prof, row_inv, col_prof, col_inv)
    sums[...] = column_totals([own], None, acc, row_prof.shape[0])


def column_totals(tiles, left, acc, row_blocks):
    col_blocks = acc.shape[0] - 1
    acc[...] = jnp.zeros_like(acc)
    for tile in tiles:
        col_sums(tile, left, acc, row_blocks, col_blocks)
    return jnp.sum(acc[0:col_blocks], axis=1)


def row_part(tiles, wide, acc, row_blocks, out):
    blocks = acc.shape[0] - 1
    acc[...] = jnp.zeros_like(acc)
    for tile in tiles:
        row_sums(tile, wide, acc, row_blocks, blocks)
    out[...] = jnp.sum(acc[0:blocks], axis=1)


def strip_kernel(pcs, n_row, *refs):
    table, own, col_prof, col_inv, own_sums = refs[:5]
    stacks = refs[5 : 5 + 2 * n_row - 2]
    others, out, row_prof, row_inv, wide, row_acc, col_acc = refs[-7:]
    row_blocks = row_prof.shape[0] // (n_row - 1)
    tiles = [Tile(table, n_row, k, own, others) for k in range(n_row)]
    for k in range(1, n_row):
        first = (k - 1) * row_blocks
        fill_rows(pcs, stacks[2 * k - 2 : 2 * k], row_prof, row_inv, first)
    for k in range(1, n_row):
        first = (k - 1) * row_blocks
        build(tiles[k], first, row_prof, row_inv, col_prof, col_inv)
    totals = column_totals(tiles[1:], None, col_acc, row_blocks) + own_sums[...]
    spread_lanes(wide, SCALE / totals)
    row_part(tiles, wide, row_acc, row_blocks, out)


def row_scalings(stage, parts):
    for k, part in enumerate(parts):
        stage[shifted(places()[1] // 2, k, len(parts))] = part[...].astype(F32)
    return SCALE / tree_sum([stage[i] for i in range(len(parts))])


def sweep_kernel(n_row, n_chip, *refs):
    table, own, others = refs[:3]
    parts = refs[3 : 3 + n_chip]
    out, stage, row_left, wide, row_acc, col_acc = refs[-6:]
    row_blocks = out.shape[0] // n_row
    tiles = [Tile(table, n_row, k, own, others) for k in range(n_row)]
    fill_pieces(row_left, row_scalings(stage, parts))
    totals = column_totals(tiles, row_left, col_acc, row_blocks)
    spread_lanes(wide, SCALE / totals)
    row_part(tiles, wide, row_acc, row_blocks, out)


def pieces_of(value):
    return [v.astype(BF16) for v in split3(value)]


def last_kernel(n_row, n_chip, n_land, *refs):
    table, marks, own, others = refs[:4]
    parts, bases = refs[4 : 4 + n_chip], refs[4 + n_chip : 4 + n_chip + n_row]
    keep, away, both, scaling_out, stage, row_left, col_acc, scaled, acc = refs[-9:]
    cols = bases[0].shape[0]
    per = bases[0].shape[1] // BLK
    blocks = 2 * n_chip * per
    me_row, me_col = places()
    tiles = [Tile(table, n_row, k, own, others) for k in range(n_row)]
    fill_pieces(row_left, row_scalings(stage, parts))
    scaling = SCALE / column_totals(tiles, row_left, col_acc, blocks)
    scaling_out[...] = scaling
    for k in range(n_row):
        piece = shifted(me_row, k, n_row)
        for j in range(per):
            block = bases[k][:, j * BLK : (j + 1) * BLK].astype(F32)
            b = piece * per + j
            scaled[b, 0:cols] = (block * scaling_out[pl.ds(b, 1), :]).astype(BF16)
    high, mid, low = split3(scaling)
    shape = (PIECES, BLK)
    rows = lax.broadcasted_iota(jnp.int32, shape, 0)
    for b in range(scaling.shape[0]):
        value = jnp.where(
            rows == 0,
            jnp.broadcast_to(high[b : b + 1], shape),
            jnp.where(
                rows == 1,
                jnp.broadcast_to(mid[b : b + 1], shape),
                jnp.where(rows == 2, jnp.broadcast_to(low[b : b + 1], shape), 0.0),
            ),
        )
        scaled[b, cols : cols + PIECES] = value.astype(BF16)
    acc[...] = jnp.zeros_like(acc)
    for k in range(n_row):
        tile = tiles[k]

        def step(s, tile=tile):
            target = jnp.where(s < tile.total, tile.row(s), blocks)
            sums = jnp.dot(scaled[tile.column(s)], tile.block(s), preferred_element_type=F32)
            acc[target] += sums[0 : cols + 8]

        slot_loop(step, jnp.where(tile.group == me_row, tile.total, 0), 1, BUILD_GROUP)
    core = lax.rem(me_col, 2)
    for q in range(n_chip):
        mine = (2 * q + core) * per
        other = (2 * q + 1 - core) * per
        for j in range(per):
            keep[q, j] = acc[mine + j, 0:cols]
            away[q, j] = acc[other + j, 0:cols].astype(BF16)
    part = jnp.sum(acc[0:blocks, cols : cols + 8], axis=1)
    for i, value in enumerate(pieces_of(part)):
        both[i * blocks : (i + 1) * blocks] = value
    for i in range(n_land):
        first = 3 * blocks + i * cols
        both[first : first + cols] = acc[marks[me_row * n_land + i] - me_row * blocks, 0:cols].astype(BF16)


def three(ref, blocks):
    value = ref[0 : 3 * blocks].astype(F32)
    return (value[2 * blocks :] + value[blocks : 2 * blocks]) + value[0:blocks]


def pair_kernel(keep, away, both, both_in, both_out, *outs):
    n_chip, per, cols = keep.shape[:3]
    blocks = 2 * n_chip * per
    chip = places()[1] // 2
    parts = pieces_of(three(both, blocks) + three(both_in, blocks))
    for i, value in enumerate(parts):
        both_out[i * blocks : (i + 1) * blocks] = value
    lands = both[3 * blocks :].astype(F32) + both_in[3 * blocks :].astype(F32)
    both_out[3 * blocks :] = lands.astype(BF16)
    for k, out in enumerate(outs):
        to = lax.rem(chip + k, n_chip)
        for j in range(per):
            value = keep[to, j] + away[to, j].astype(F32)
            out[j * cols : (j + 1) * cols] = value.astype(BF16)


def gram_kernel(n_land, cols, per, *refs):
    marks = refs[0]
    gram, scaling_out, own, inverse, stage, land_stage = refs[-6:]
    parts = refs[1:-6]
    n = len(parts)
    me_row, me_col = places()
    blocks = scaling_out.shape[0]
    for k, part in enumerate(parts):
        place = shifted(me_col // 2, k, n)
        stage[place] = three(part, blocks)
        land_stage[place] = part[3 * blocks :]
    inverse[...] = 1.0 / tree_sum([stage[i] for i in range(n)])
    scaling_out[...] = SCALE * inverse[...]
    for j in range(per):
        own[j : j + 1, :] = inverse[pl.ds(me_col * per + j, 1), :]
    total = None
    for i in range(n_land):
        summed = tree_sum(
            [land_stage[k, i * cols : (i + 1) * cols].astype(F32) for k in range(n)]
        )
        block = marks[me_row * n_land + i] - me_row * blocks
        projected = summed * inverse[pl.ds(block, 1), :]
        product = lax.dot_general(
            projected,
            projected,
            (((1,), (1,)), ((), ())),
            precision=lax.Precision.HIGHEST,
            preferred_element_type=F32,
        )
        total = product if total is None else total + product
    gram[...] = total


WIDE = 4


def eliminate(gram):
    cols = gram.shape[0]
    rows = lax.broadcasted_iota(jnp.int32, (cols, 2 * cols), 0)
    lanes = lax.broadcasted_iota(jnp.int32, (cols, 2 * cols), 1)
    unit = (rows[:, :cols] == lanes[:, :cols]).astype(F32)
    work = jnp.concatenate([gram, unit], axis=1)
    for first in range(0, cols, WIDE):
        tops = [work[first + i : first + i + 1, :] for i in range(WIDE)]
        sides = [
            jnp.broadcast_to(work[:, first + i : first + i + 1], work.shape)
            for i in range(WIDE)
        ]
        change = None
        for i in range(WIDE):
            pivot = first + i
            unit_top = tops[i] / sides[i][pivot : pivot + 1, :]
            for m in range(i + 1, WIDE):
                factor = sides[i][first + m : first + m + 1, :]
                tops[m] = tops[m] - factor * unit_top
                inner = factor / sides[i][pivot : pivot + 1, :]
                sides[m] = sides[m] - sides[i] * inner
            term = sides[i] * unit_top
            change = term if change is None else change + term
        reduced = work - change
        kept = work
        for i in range(WIDE):
            kept = jnp.where(rows == first + i, tops[i], kept)
        work = jnp.where(rows >= first + WIDE, reduced, kept)
    pivots = jnp.sum(jnp.where(rows == lanes, work, 0.0), axis=1, keepdims=True)
    return (work * lax.rsqrt(pivots))[:, cols:]


def ritz_kernel(n_row, cells, *refs):
    grams, parts = refs[:n_row], refs[n_row:-3]
    own, out, stage = refs[-3:]
    cols = grams[0].shape[0]
    per = out.shape[1] // BLK
    inverse = eliminate(ordered_sum(stage, grams, places()[0]) * (1.0 / cells))
    for j in range(per):
        summed = tree_sum([m[j * cols : (j + 1) * cols].astype(F32) for m in parts])
        projected = summed * own[j : j + 1, :]
        out[:, j * BLK : (j + 1) * BLK] = jnp.dot(
            inverse, projected, precision=lax.Precision.HIGHEST, preferred_element_type=F32
        )


def swap(x, axis, k):
    return lax.ppermute(x, axis, [(i, i ^ k) for i in range(lax.axis_size(axis))])


def shift(x, axis, k):
    n = lax.axis_size(axis)
    return lax.ppermute(x, axis, [(i, (i + k) % n) for i in range(n)])


def shifts(x, axis):
    return [x] + [shift(x, axis, k) for k in range(1, lax.axis_size(axis))]


def chip_shift(x, k):
    n = lax.axis_size("col") // 2
    return lax.ppermute(
        x,
        "col",
        [(2 * q + p, 2 * ((q + k) % n) + p) for q in range(n) for p in range(2)],
    )


def chip_shifts(x):
    return [x] + [chip_shift(x, k) for k in range(1, lax.axis_size("col") // 2)]


def sibling(x):
    return swap(x, "col", 1)


def vec(*arrays):
    return [("vmem", a) for a in arrays]


def strip_body(profiles, cell_width, basis, block_lists, block_counts, landmarks):
    n_row, n_col = lax.axis_size("row"), lax.axis_size("col")
    n_chip = n_col // 2
    pcs, share = profiles.shape
    cols = basis.shape[0]
    per = share // BLK
    row_blocks, col_blocks = n_col * per, n_row * per
    all_rows = n_row * row_blocks
    slots = block_lists.shape[-1]
    n_land = landmarks.shape[0] // n_row

    def shape(*dims, dtype=F32):
        return jax.ShapeDtypeStruct(dims, dtype)

    (packed,) = call(
        pack_kernel,
        [shape(FEAT, share, dtype=BF16)],
        [("hbm", a) for a in (profiles, cell_width, block_lists)] + [("smem", block_counts)],
        [
            pltpu.VMEM((FEAT, share), F32),
            pltpu.VMEM(profiles.shape, BF16),
            pltpu.VMEM(cell_width.shape, BF16),
            pltpu.VMEM(block_lists.shape, jnp.int32),
            pltpu.SemaphoreType.DMA((3,)),
        ],
    )
    stack, table = call(
        functools.partial(stack_kernel, pcs),
        [shape(n_row, FEAT, share, dtype=BF16), shape(n_row, 8, BLK, dtype=jnp.int32)],
        vec(*shifts(packed, "row")),
    )
    table = ("smem", table.reshape(n_row * 8, BLK))
    marks = ("smem", landmarks)
    far = [chip_shift(stack, k) for k in range(1, n_chip)]
    own, col_prof, col_inv, sums = call(
        functools.partial(own_kernel, pcs),
        [
            pltpu.VMEM((slots, BLK, BLK), BF16),
            pltpu.VMEM((col_blocks, BLK, FEAT), BF16),
            pltpu.VMEM((col_blocks, BLK, BLK), F32),
            shape(col_blocks, BLK),
        ],
        [table] + vec(stack, sibling(stack)),
        [
            pltpu.VMEM((row_blocks, FEAT, BLK), BF16),
            pltpu.VMEM((row_blocks, 8, BLK), F32),
            pltpu.VMEM((col_blocks + 1, 8, BLK), F32),
        ],
    )
    basis, sums = lax.optimization_barrier((basis, sums))
    bases = shifts(basis, "row")
    far, sums, bases = lax.optimization_barrier((far, sums, bases))
    stacks = [x for pack in far for x in (pack, sibling(pack))]
    far_slots = (n_row - 1) * slots
    others, part = call(
        functools.partial(strip_kernel, pcs, n_row),
        [pltpu.VMEM((far_slots, BLK, BLK), BF16), shape(all_rows, BLK)],
        [table, ("keep", own), ("keep", col_prof), ("keep", col_inv)]
        + vec(sums, *stacks),
        [
            pltpu.VMEM((all_rows - row_blocks, FEAT, BLK), BF16),
            pltpu.VMEM((all_rows - row_blocks, 8, BLK), F32),
            pltpu.VMEM((col_blocks, BLK, BLK), F32),
            pltpu.VMEM((all_rows + 1, 8, BLK), F32),
            pltpu.VMEM((col_blocks + 1, 8, BLK), F32),
        ],
    )
    tiles = [("keep", own), ("keep", others)]

    def chip_parts(part):
        return chip_shifts((part + sibling(part)).astype(BF16))

    for _ in range(SWEEPS - 2):
        (part,) = call(
            functools.partial(sweep_kernel, n_row, n_chip),
            [shape(all_rows, BLK)],
            [table] + tiles + vec(*chip_parts(part)),
            [
                pltpu.VMEM((n_chip, all_rows, BLK), F32),
                pltpu.VMEM((2, all_rows, PIECES, 2 * BLK), BF16),
                pltpu.VMEM((col_blocks, BLK, BLK), F32),
                pltpu.VMEM((all_rows + 1, 8, BLK), F32),
                pltpu.VMEM((col_blocks + 1, 8, BLK), F32),
            ],
        )
    both_rows = 3 * row_blocks + n_land * cols
    keep, away, both, col_scaling = call(
        functools.partial(last_kernel, n_row, n_chip, n_land),
        [
            shape(n_chip, per, cols, BLK),
            shape(n_chip, per, cols, BLK, dtype=BF16),
            shape(both_rows, BLK, dtype=BF16),
            shape(col_blocks, BLK),
        ],
        [table, marks] + tiles + vec(*chip_parts(part), *bases),
        [
            pltpu.VMEM((n_chip, all_rows, BLK), F32),
            pltpu.VMEM((2, all_rows, PIECES, 2 * BLK), BF16),
            pltpu.VMEM((col_blocks + 1, 8, BLK), F32),
            pltpu.VMEM((col_blocks, cols + PIECES, BLK), BF16),
            pltpu.VMEM((row_blocks + 1, cols + 8, BLK), F32),
        ],
    )
    pairs = call(
        pair_kernel,
        [shape(both_rows, BLK, dtype=BF16)]
        + [shape(per * cols, BLK, dtype=BF16)] * n_chip,
        vec(keep, sibling(away), both, sibling(both)),
    )
    sums = [pairs[0]] + [chip_shift(pairs[0], k) for k in range(1, n_chip)]
    shares = [pairs[1]] + [chip_shift(pairs[1 + k], k) for k in range(1, n_chip)]
    gram, row_scaling, own = call(
        functools.partial(gram_kernel, n_land, cols, per),
        [shape(cols, cols), shape(row_blocks, BLK), shape(per, BLK)],
        [marks] + vec(*sums),
        [
            pltpu.VMEM((row_blocks, BLK), F32),
            pltpu.VMEM((n_chip, row_blocks, BLK), F32),
            pltpu.VMEM((n_chip, n_land * cols, BLK), BF16),
        ],
    )
    (ritz,) = call(
        functools.partial(ritz_kernel, n_row, landmarks.shape[0] * BLK),
        [shape(cols, share)],
        vec(*shifts(gram, "row"), *shares, own),
        [pltpu.VMEM((n_row, cols, cols), F32)],
    )
    return row_scaling.reshape(-1), col_scaling.reshape(-1), ritz


def tile_pack_kernel(prof_ref, width_ref, out_ref, work):
    pcs = prof_ref.shape[0]
    prof = prof_ref[...].astype(F32)
    norm = jnp.sum(prof * prof, axis=0, keepdims=True)
    high, mid, low = split3(norm)
    work[...] = jnp.zeros_like(work)
    work[0:pcs, :] = prof
    work[pcs : pcs + 1, :] = high
    work[pcs + 1 : pcs + 2, :] = mid
    work[pcs + 2 : pcs + 3, :] = low
    work[pcs + 3 : pcs + 6, :] = jnp.ones((3, prof.shape[1]), F32)
    work[pcs + 6 : pcs + 7, :] = width_ref[...].astype(F32)
    out_ref[...] = work[...].astype(BF16)


def tile_square(tile, slots):
    a, b, c, d = [tile[s] for s in slots]
    return jnp.concatenate(
        [jnp.concatenate([a, b], axis=1), jnp.concatenate([c, d], axis=1)], axis=0
    )


def tile_add_rows(acc, lists, target, slots, sums, total, spare, firsts):
    for i, (s, (row, lane)) in enumerate(zip(slots, firsts)):
        place = jnp.where(s < total, lists[0, 0, target, s], spare)
        acc[place] += sums[row : row + 8, lane : lane + BLK]


def tile_row_sums(lists, tile, left, acc, total, spare):
    def step(*slots):
        low = [left[0, lists[0, 0, 1, s]] for s in slots[:2]]
        high = [left[1, lists[0, 0, 1, s]] for s in slots[2:]]
        sums = jnp.dot(
            jnp.concatenate(low + high, axis=0),
            tile_square(tile, slots),
            preferred_element_type=F32,
        )
        firsts = [(0, 0), (PIECES, BLK), (2 * PIECES, 0), (3 * PIECES, BLK)]
        tile_add_rows(acc, lists, 0, slots, sums, total, spare, firsts)

    slot_loop(step, total, 4, 4 * TILE_GROUP)


def tile_col_sums(lists, tile, left, acc, total, spare):
    def step(*slots):
        pieces = [left[i % 2, lists[0, 0, 0, s]] for i, s in enumerate(slots)]
        sums = lax.dot_general(
            jnp.concatenate(pieces, axis=0),
            tile_square(tile, slots),
            (((1,), (1,)), ((), ())),
            preferred_element_type=F32,
        )
        firsts = [(0, 0), (PIECES, 0), (2 * PIECES, BLK), (3 * PIECES, BLK)]
        tile_add_rows(acc, lists, 1, slots, sums, total, spare, firsts)

    slot_loop(step, total, 4, 4 * TILE_GROUP)


def tile_build_kernel(pcs, n_row, n_col, *refs):
    lists, counts = refs[:2]
    col_in = refs[2 : 2 + n_row]
    row_in = refs[2 + n_row : 2 + n_row + n_col]
    tile, part, row_prof, row_inv, col_prof, col_inv, acc, left = refs[2 + n_row + n_col :]
    per = row_in[0].shape[1] // BLK
    col_blocks, row_blocks = n_row * per, n_col * per
    total = counts[0, 0]
    me_row, me_col = places()
    for k, ref in enumerate(row_in):
        core = lax.rem(me_col + k, 2)
        piece = shifted(me_col // 2, k // 2, n_col // 2) * 2 + core
        for j in range(per):
            block = ref[:, j * BLK : (j + 1) * BLK]
            row_prof[piece * per + j] = block
            width = block.astype(F32)[pcs + 6 : pcs + 7, :]
            row_inv[piece * per + j] = jnp.broadcast_to(1.0 / width, (8, BLK))
    rows = lax.broadcasted_iota(jnp.int32, (FEAT, BLK), 0)
    for k, ref in enumerate(col_in):
        piece = shifted(me_row, k, n_row)
        for j in range(per):
            block = ref[0:FEAT, j * BLK : (j + 1) * BLK].astype(F32)
            turned = jnp.where(rows < pcs, -2.0 * block, 0.0)
            turned = jnp.where((rows >= pcs) & (rows < pcs + 3), 1.0, turned)
            turned = jnp.where(
                (rows >= pcs + 3) & (rows < pcs + 6), pltpu.roll(block, 3, 0), turned
            )
            turned = jnp.where(rows == pcs + 7, pltpu.roll(block, 1, 0), turned)
            turned = turned.T
            col_prof[piece * per + j] = turned.astype(BF16)
            col_inv[piece * per + j] = jnp.broadcast_to(
                -LOG2E / turned[:, pcs + 7 : pcs + 8], (BLK, BLK)
            )

    def step(s):
        rb, cb = lists[0, 0, 0, s], lists[0, 0, 1, s]
        distance = jnp.dot(col_prof[cb], row_prof[rb], preferred_element_type=F32)
        block = jnp.exp2(distance * col_inv[cb] * row_inv[rb][0:1, :])
        tile[s] = block.astype(BF16)

    slot_loop(step, total, 1, TILE_GROUP)
    ones = (lax.broadcasted_iota(jnp.int32, (PIECES, BLK), 0) == 0).astype(F32).astype(BF16)
    empty = jnp.zeros_like(ones)
    for b in range(row_blocks):
        left[0, b] = jnp.concatenate([ones, empty], axis=1)
        left[1, b] = jnp.concatenate([empty, ones], axis=1)
    acc[...] = jnp.zeros_like(acc)
    tile_col_sums(lists, tile, left, acc, total, col_blocks)
    part[...] = jnp.sum(acc[0:col_blocks], axis=1)


def tile_pass_kernel(over_rows, n_parts, *refs):
    lists, counts, tile = refs[:3]
    parts = refs[3 : 3 + n_parts]
    out, stage, left, acc = refs[-4:]
    total = counts[0, 0]
    blocks = out.shape[0]
    me_row, me_col = places()
    scaling = SCALE / ordered_sum(stage, parts, me_row if over_rows else me_col // 2)
    fill_pieces(left, scaling)
    acc[...] = jnp.zeros_like(acc)
    (tile_row_sums if over_rows else tile_col_sums)(lists, tile, left, acc, total, blocks)
    out[...] = jnp.sum(acc[0:blocks], axis=1)


def tile_last_kernel(n_row, n_col, n_land, *refs):
    lists, counts, marks, tile = refs[:4]
    parts, bases = refs[4 : 4 + n_row], refs[4 + n_row : 4 + 2 * n_row]
    keep, away, both, scaling_out, stage, scaled, acc = refs[4 + 2 * n_row :]
    cols = bases[0].shape[0]
    per = bases[0].shape[1] // BLK
    blocks = n_col * per
    total = counts[0, 0]
    me_row, me_col = places()
    scaling = SCALE / ordered_sum(stage, parts, me_row)
    scaling_out[...] = scaling
    for k in range(n_row):
        piece = shifted(me_row, k, n_row)
        for j in range(per):
            block = bases[k][:, j * BLK : (j + 1) * BLK].astype(F32)
            b = piece * per + j
            scaled[b, 0:cols] = (block * scaling_out[pl.ds(b, 1), :]).astype(BF16)
    high, mid, low = split3(scaling)
    shape = (PIECES, BLK)
    rows = lax.broadcasted_iota(jnp.int32, shape, 0)
    for b in range(scaling.shape[0]):
        value = jnp.where(
            rows == 0,
            jnp.broadcast_to(high[b : b + 1], shape),
            jnp.where(
                rows == 1,
                jnp.broadcast_to(mid[b : b + 1], shape),
                jnp.where(rows == 2, jnp.broadcast_to(low[b : b + 1], shape), 0.0),
            ),
        )
        scaled[b, cols : cols + PIECES] = value.astype(BF16)
    acc[...] = jnp.zeros_like(acc)

    def step(s):
        target = jnp.where(s < total, lists[0, 0, 0, s], blocks)
        sums = jnp.dot(scaled[lists[0, 0, 1, s]], tile[s], preferred_element_type=F32)
        acc[target] += sums[0 : cols + 8]

    slot_loop(step, total, 1, TILE_GROUP)
    core = lax.rem(me_col, 2)
    for q in range(n_col // 2):
        own = (2 * q + core) * per
        other = (2 * q + 1 - core) * per
        for j in range(per):
            keep[q, j] = acc[own + j, 0:cols]
            away[q, j] = acc[other + j, 0:cols].astype(BF16)
    row_part = jnp.sum(acc[0:blocks, cols : cols + 8], axis=1)
    for i, value in enumerate(pieces_of(row_part)):
        both[i * blocks : (i + 1) * blocks] = value
    for i in range(n_land):
        first = 3 * blocks + i * cols
        both[first : first + cols] = acc[marks[me_row * n_land + i] - me_row * blocks, 0:cols].astype(BF16)


def tile_body(profiles, cell_width, basis, block_lists, block_counts, landmarks):
    n_row, n_col = lax.axis_size("row"), lax.axis_size("col")
    n_chip = n_col // 2
    pcs, share = profiles.shape
    cols = basis.shape[0]
    per = share // BLK
    row_blocks, col_blocks = n_col * per, n_row * per
    slots = block_lists.shape[-1]
    n_land = landmarks.shape[0] // n_row

    def shape(*dims, dtype=F32):
        return jax.ShapeDtypeStruct(dims, dtype)

    (packed,) = call(
        tile_pack_kernel,
        [shape(FEAT, share, dtype=BF16)],
        vec(profiles, cell_width.reshape(1, share)),
        [pltpu.VMEM((FEAT, share), F32)],
    )
    spread = lax.ppermute(
        packed,
        ("row", "col"),
        [((q % n_row) * n_col + q // n_row, q) for q in range(n_row * n_col)],
    )
    row_packs = []
    for pack in chip_shifts(spread):
        row_packs += [pack, sibling(pack)]
    col_packs = shifts(packed, "row")
    bases = shifts(basis, "row")
    lists = [("smem", block_lists), ("smem", block_counts)]
    marks = [("smem", landmarks)]
    tile, part = call(
        functools.partial(tile_build_kernel, pcs, n_row, n_col),
        [pltpu.VMEM((slots, BLK, BLK), BF16), shape(col_blocks, BLK)],
        lists + vec(*col_packs, *row_packs),
        [
            pltpu.VMEM((row_blocks, FEAT, BLK), BF16),
            pltpu.VMEM((row_blocks, 8, BLK), F32),
            pltpu.VMEM((col_blocks, BLK, FEAT), BF16),
            pltpu.VMEM((col_blocks, BLK, BLK), F32),
            pltpu.VMEM((col_blocks + 1, 8, BLK), F32),
            pltpu.VMEM((2, row_blocks, PIECES, 2 * BLK), BF16),
        ],
    )
    for number in range(SWEEPS - 1):
        early = [("near", b) for b in bases[1:]] if number == 0 else []
        (part,) = call(
            functools.partial(tile_pass_kernel, True, n_row),
            [shape(row_blocks, BLK)],
            lists + [("keep", tile)] + vec(*shifts(part, "row")) + early,
            [
                pltpu.VMEM((n_row, col_blocks, BLK), F32),
                pltpu.VMEM((2, col_blocks, PIECES, 2 * BLK), BF16),
                pltpu.VMEM((row_blocks + 1, 8, BLK), F32),
            ],
        )
        (part,) = call(
            functools.partial(tile_pass_kernel, False, n_chip),
            [shape(col_blocks, BLK)],
            lists + [("keep", tile)] + vec(*chip_shifts(part + sibling(part))),
            [
                pltpu.VMEM((n_chip, row_blocks, BLK), F32),
                pltpu.VMEM((2, row_blocks, PIECES, 2 * BLK), BF16),
                pltpu.VMEM((col_blocks + 1, 8, BLK), F32),
            ],
        )
    both_rows = 3 * row_blocks + n_land * cols
    keep, away, both, col_scaling = call(
        functools.partial(tile_last_kernel, n_row, n_col, n_land),
        [
            shape(n_chip, per, cols, BLK),
            shape(n_chip, per, cols, BLK, dtype=BF16),
            shape(both_rows, BLK, dtype=BF16),
            shape(col_blocks, BLK),
        ],
        lists + marks + [("keep", tile)] + vec(*shifts(part, "row"), *bases),
        [
            pltpu.VMEM((n_row, col_blocks, BLK), F32),
            pltpu.VMEM((col_blocks, cols + PIECES, BLK), BF16),
            pltpu.VMEM((row_blocks + 1, cols + 8, BLK), F32),
        ],
    )
    pairs = call(
        pair_kernel,
        [shape(both_rows, BLK, dtype=BF16)]
        + [shape(per * cols, BLK, dtype=BF16)] * n_chip,
        vec(keep, sibling(away), both, sibling(both)),
    )
    sums = [pairs[0]] + [chip_shift(pairs[0], k) for k in range(1, n_chip)]
    shares = [pairs[1]] + [chip_shift(pairs[1 + k], k) for k in range(1, n_chip)]
    gram, row_scaling, own = call(
        functools.partial(gram_kernel, n_land, cols, per),
        [shape(cols, cols), shape(row_blocks, BLK), shape(per, BLK)],
        marks + vec(*sums),
        [
            pltpu.VMEM((row_blocks, BLK), F32),
            pltpu.VMEM((n_chip, row_blocks, BLK), F32),
            pltpu.VMEM((n_chip, n_land * cols, BLK), BF16),
        ],
    )
    (ritz,) = call(
        functools.partial(ritz_kernel, n_row, landmarks.shape[0] * BLK),
        [shape(cols, share)],
        vec(*shifts(gram, "row"), *shares, own),
        [pltpu.VMEM((n_row, cols, cols), F32)],
    )
    return row_scaling.reshape(-1), col_scaling.reshape(-1), ritz


def solution(mesh):
    placed = (
        P(None, ("col", "row")),
        P(("col", "row")),
        P(None, ("col", "row")),
        P("row", "col", None, None),
        P("row", "col"),
        P(),
    )
    return jax.shard_map(
        strip_body if mesh.shape["row"] <= STRIP_TILES else tile_body,
        mesh=mesh,
        in_specs=placed,
        out_specs=(P("row"), P("col"), P(None, ("row", "col"))),
        check_vma=False,
    )
```

```python
import functools

import jax
import jax.numpy as jnp
from jax import lax
from jax.experimental import pallas as pl
from jax.experimental.pallas import tpu as pltpu
from jax.sharding import PartitionSpec as P

BLK = 128
SWEEPS = 3
GROUP = 32
BUILD_GROUP = 16
TILE_GROUP = 16
ROWS, COLUMNS, COUNT = 0, 1, 2
FEAT = 64
PIECES = 16
SCALE = 512.0
LOG2E = 1.4426950408889634
F32 = jnp.float32
BF16 = jnp.bfloat16
MIB = 1 << 20
STRIP_TILES = 8

VMEM_SPEC = pl.BlockSpec(memory_space=pltpu.VMEM)
SMEM_SPEC = pl.BlockSpec(memory_space=pltpu.SMEM)


def split3(x):
    high = x.astype(BF16).astype(F32)
    mid = (x - high).astype(BF16).astype(F32)
    low = (x - high - mid).astype(BF16).astype(F32)
    return high, mid, low


def tree_sum(values):
    values = list(values)
    while len(values) > 1:
        values = [a + b for a, b in zip(values[::2], values[1::2])]
    return values[0]


def call(kernel, outs, ins, scratch=(), limit=24, flops=1 << 24):
    args, specs = [], []
    for kind, array in ins:
        if kind == "smem":
            specs.append(SMEM_SPEC)
        elif kind == "near":
            specs.append(pl.BlockSpec(memory_space=pl.ANY))
        elif kind == "hbm":
            specs.append(pl.BlockSpec(memory_space=pltpu.HBM))
            array = pltpu.with_memory_space_constraint(array, pltpu.HBM)
        else:
            specs.append(VMEM_SPEC)
            if kind == "keep":
                array = pltpu.with_memory_space_constraint(array, pltpu.VMEM)
        args.append(array)
    return pl.pallas_call(
        kernel,
        out_shape=tuple(outs),
        in_specs=specs,
        out_specs=tuple(VMEM_SPEC for _ in outs),
        scratch_shapes=list(scratch),
        compiler_params=pltpu.CompilerParams(vmem_limit_bytes=limit * MIB),
        cost_estimate=pl.CostEstimate(flops=flops, bytes_accessed=1 << 20, transcendentals=0),
    )(*args)


def pack_kernel(prof_hbm, width_hbm, lists_hbm, counts, out_ref, *scratch):
    work, prof_ref, width_ref, lists_ref, sems = scratch
    pairs = [
        (prof_hbm, prof_ref),
        (width_hbm, width_ref),
        (lists_hbm, lists_ref),
    ]
    copies = [pltpu.make_async_copy(a, b, sems.at[i]) for i, (a, b) in enumerate(pairs)]
    for copy in copies:
        copy.start()
    for copy in copies:
        copy.wait()
    pcs = prof_ref.shape[0]
    prof = prof_ref[...].astype(F32)
    norm = jnp.sum(prof * prof, axis=0, keepdims=True)
    high, mid, low = split3(norm)
    work[...] = jnp.zeros_like(work)
    work[0:pcs, :] = prof
    work[pcs : pcs + 1, :] = high
    work[pcs + 1 : pcs + 2, :] = mid
    work[pcs + 2 : pcs + 3, :] = low
    work[pcs + 3 : pcs + 6, :] = jnp.ones((3, prof.shape[1]), F32)
    work[pcs + 6 : pcs + 7, :] = width_ref[...].astype(F32).reshape(1, -1)
    work[pcs + 8 : pcs + 10, 0:BLK] = lists_ref[0, 0].astype(F32)
    work[pcs + 10 : pcs + 11, 0:BLK] = jnp.full((1, BLK), counts[0, 0], jnp.int32).astype(F32)
    out_ref[...] = work[...].astype(BF16)


def places():
    return lax.axis_index("row"), lax.axis_index("col")


def stack_kernel(pcs, n, *refs):
    packs, (rest, table) = refs[:n], refs[-2:]
    me_row, _ = places()
    first = FEAT - 16
    for k, pack in enumerate(packs):
        if k:
            rest[k - 1] = pack[...]
        rows = pack[first:, 0:BLK].astype(F32)
        rows = pltpu.roll(rows, 16 - (pcs + 8 - first), 0)
        table[shifted(me_row, k, n)] = rows[0:8].astype(jnp.int32)


def slot_loop(step, count, size, group):
    def advance(number, carry):
        for i in range(0, group, size):
            step(*[number * group + i + j for j in range(size)])
        return carry

    lax.fori_loop(0, (count + group - 1) // group, advance, 0)


class Tile:
    def __init__(self, table, n_row, k, own, others):
        _, me_col = places()
        self.group = shifted(me_col // 2, k, n_row)
        self.table, self.k = table, k
        slots = own.shape[0]
        self.blocks, self.base = (own, 0) if k == 0 else (others, (k - 1) * slots)
        self.total = table[self.group * 8 + COUNT, 0]

    def row(self, s):
        return self.table[self.group * 8 + ROWS, s]

    def column(self, s):
        return self.table[self.group * 8 + COLUMNS, s]

    def block(self, s):
        return self.blocks[self.base + s]


def shifted(me, k, n):
    return lax.rem(me + (n - k), n)


def ordered_sum(stage, refs, me):
    n = len(refs)
    for k, ref in enumerate(refs):
        stage[shifted(me, k, n)] = ref[...]
    return tree_sum([stage[i] for i in range(n)])


def square(tile, slots):
    a, b, c, d = [tile.block(s) for s in slots]
    return jnp.concatenate(
        [jnp.concatenate([a, b], axis=1), jnp.concatenate([c, d], axis=1)], axis=0
    )


def add_rows(acc, sums, firsts, targets):
    for (row, lane), target in zip(firsts, targets):
        acc[target] += sums[row : row + 8, lane : lane + BLK]


def row_sums(tile, wide, acc, row_blocks, spare):
    first = tile.group * row_blocks

    def step(s):
        product = tile.block(s).astype(F32) * wide[tile.column(s)]
        sums = jnp.sum(product.reshape(BLK // 8, 8, BLK), axis=0)
        acc[jnp.where(s < tile.total, first + tile.row(s), spare)] += sums

    slot_loop(step, tile.total, 1, GROUP)


def spread_lanes(wide, scaling):
    turned = scaling.T
    for b in range(scaling.shape[0]):
        wide[b] = jnp.broadcast_to(turned[:, b : b + 1], (BLK, BLK))


def col_sums(tile, left, acc, row_blocks, spare):
    first = tile.group * row_blocks

    def step(*slots):
        if left is None:
            rows = lax.broadcasted_iota(jnp.int32, (4 * PIECES, 2 * BLK), 0)
            lanes = lax.broadcasted_iota(jnp.int32, (4 * PIECES, 2 * BLK), 1)
            block = rows // PIECES
            pieces = (rows % PIECES == 0) & (block % 2 == lanes // BLK)
            pieces = pieces.astype(F32).astype(BF16)
        else:
            pieces = [left[i % 2, first + tile.row(s)] for i, s in enumerate(slots)]
            pieces = jnp.concatenate(pieces, axis=0)
        sums = lax.dot_general(
            pieces,
            square(tile, slots),
            (((1,), (1,)), ((), ())),
            preferred_element_type=F32,
        )
        firsts = [(0, 0), (PIECES, 0), (2 * PIECES, BLK), (3 * PIECES, BLK)]
        targets = [jnp.where(s < tile.total, tile.column(s), spare) for s in slots]
        add_rows(acc, sums, firsts, targets)

    slot_loop(step, tile.total, 4, 2 * GROUP if tile.k == 0 else GROUP)


def fill_pieces(left, scaling):
    high, mid, low = split3(scaling)
    shape = (PIECES, BLK)
    rows = lax.broadcasted_iota(jnp.int32, shape, 0)
    empty = jnp.zeros(shape, F32).astype(BF16)
    for b in range(scaling.shape[0]):
        value = jnp.where(
            rows == 0,
            jnp.broadcast_to(high[b : b + 1], shape),
            jnp.where(
                rows == 1,
                jnp.broadcast_to(mid[b : b + 1], shape),
                jnp.where(rows == 2, jnp.broadcast_to(low[b : b + 1], shape), 0.0),
            ),
        ).astype(BF16)
        left[0, b] = jnp.concatenate([value, empty], axis=1)
        left[1, b] = jnp.concatenate([empty, value], axis=1)


def build(tile, offset, row_prof, row_inv, col_prof, col_inv):
    def step(s):
        row, column = offset + tile.row(s), tile.column(s)
        distance = jnp.dot(col_prof[column], row_prof[row], preferred_element_type=F32)
        block = jnp.exp2(distance * col_inv[column] * row_inv[row][0:1, :])
        tile.blocks[tile.base + s] = block.astype(BF16)

    slot_loop(step, tile.total, 1, BUILD_GROUP)


def piece_block(pieces, k, j):
    lanes = slice(j * BLK, (j + 1) * BLK)
    return pieces[0][:, lanes] if k == 0 else pieces[1][k - 1, :, lanes]


def fill_rows(pcs, sources, row_prof, row_inv, offset):
    me_row, me_col = places()
    n_row = sources[0][1].shape[0] + 1
    per = sources[0][0].shape[1] // BLK
    for i, pieces in enumerate(sources):
        core = lax.rem(me_col + i, 2)
        for k in range(n_row):
            piece = core * n_row + shifted(me_row, k, n_row)
            for j in range(per):
                block = piece_block(pieces, k, j)
                row_prof[offset + piece * per + j] = block
                width = block.astype(F32)[pcs + 6 : pcs + 7, :]
                row_inv[offset + piece * per + j] = jnp.broadcast_to(1.0 / width, (8, BLK))


def own_kernel(pcs, table, pack, rest, pack_in, rest_in, *refs):
    tile, col_prof, col_inv, sums, row_prof, row_inv, acc = refs
    n_row = rest.shape[0] + 1
    per = pack.shape[1] // BLK
    me_row, _ = places()
    fill_rows(pcs, [(pack, rest), (pack_in, rest_in)], row_prof, row_inv, 0)
    rows = lax.broadcasted_iota(jnp.int32, (FEAT, BLK), 0)
    for k in range(n_row):
        piece = shifted(me_row, k, n_row)
        for j in range(per):
            block = piece_block((pack, rest), k, j).astype(F32)
            turned = jnp.where(rows < pcs, -2.0 * block, 0.0)
            turned = jnp.where((rows >= pcs) & (rows < pcs + 3), 1.0, turned)
            turned = jnp.where(
                (rows >= pcs + 3) & (rows < pcs + 6), pltpu.roll(block, 3, 0), turned
            )
            turned = jnp.where(rows == pcs + 7, pltpu.roll(block, 1, 0), turned)
            turned = turned.T
            col_prof[piece * per + j] = turned.astype(BF16)
            col_inv[piece * per + j] = jnp.broadcast_to(
                -LOG2E / turned[:, pcs + 7 : pcs + 8], (BLK, BLK)
            )
    own = Tile(table, n_row, 0, tile, None)
    build(own, 0, row_prof, row_inv, col_prof, col_inv)
    sums[...] = column_totals([own], None, acc, row_prof.shape[0])


def column_totals(tiles, left, acc, row_blocks):
    col_blocks = acc.shape[0] - 1
    acc[...] = jnp.zeros_like(acc)
    for tile in tiles:
        col_sums(tile, left, acc, row_blocks, col_blocks)
    return jnp.sum(acc[0:col_blocks], axis=1)


def row_part(tiles, wide, acc, row_blocks, out):
    blocks = acc.shape[0] - 1
    acc[...] = jnp.zeros_like(acc)
    for tile in tiles:
        row_sums(tile, wide, acc, row_blocks, blocks)
    out[...] = jnp.sum(acc[0:blocks], axis=1)


def strip_kernel(pcs, n_row, *refs):
    table, own, col_prof, col_inv, own_sums = refs[:5]
    sources = [refs[i : i + 2] for i in range(5, 5 + 4 * (n_row - 1), 2)]
    others, out, row_prof, row_inv, wide, row_acc, col_acc = refs[-7:]
    row_blocks = row_prof.shape[0] // (n_row - 1)
    tiles = [Tile(table, n_row, k, own, others) for k in range(n_row)]
    for k in range(1, n_row):
        first = (k - 1) * row_blocks
        fill_rows(pcs, sources[2 * k - 2 : 2 * k], row_prof, row_inv, first)
    for k in range(1, n_row):
        first = (k - 1) * row_blocks
        build(tiles[k], first, row_prof, row_inv, col_prof, col_inv)
    totals = column_totals(tiles[1:], None, col_acc, row_blocks) + own_sums[...]
    spread_lanes(wide, SCALE / totals)
    row_part(tiles, wide, row_acc, row_blocks, out)


def row_scalings(stage, parts):
    for k, part in enumerate(parts):
        stage[shifted(places()[1] // 2, k, len(parts))] = part[...].astype(F32)
    return SCALE / tree_sum([stage[i] for i in range(len(parts))])


def sweep_kernel(n_row, n_chip, *refs):
    table, own, others = refs[:3]
    parts = refs[3 : 3 + n_chip]
    out, stage, row_left, wide, row_acc, col_acc = refs[-6:]
    row_blocks = out.shape[0] // n_row
    tiles = [Tile(table, n_row, k, own, others) for k in range(n_row)]
    fill_pieces(row_left, row_scalings(stage, parts))
    totals = column_totals(tiles, row_left, col_acc, row_blocks)
    spread_lanes(wide, SCALE / totals)
    row_part(tiles, wide, row_acc, row_blocks, out)


def pieces_of(value):
    return [v.astype(BF16) for v in split3(value)]


def last_kernel(n_row, n_chip, n_land, *refs):
    table, marks, own, others = refs[:4]
    parts, bases = refs[4 : 4 + n_chip], refs[4 + n_chip]
    keep, away, both, scaling_out, stage, row_left, col_acc, scaled, acc = refs[-9:]
    cols = bases.shape[1]
    per = bases.shape[2] // BLK
    blocks = 2 * n_chip * per
    me_row, me_col = places()
    tiles = [Tile(table, n_row, k, own, others) for k in range(n_row)]
    fill_pieces(row_left, row_scalings(stage, parts))
    scaling = SCALE / column_totals(tiles, row_left, col_acc, blocks)
    scaling_out[...] = scaling
    for k in range(n_row):
        piece = lax.bitwise_xor(me_row, k)
        for j in range(per):
            block = bases[k, :, j * BLK : (j + 1) * BLK].astype(F32)
            b = piece * per + j
            scaled[b, 0:cols] = (block * scaling_out[pl.ds(b, 1), :]).astype(BF16)
    high, mid, low = split3(scaling)
    shape = (PIECES, BLK)
    rows = lax.broadcasted_iota(jnp.int32, shape, 0)
    for b in range(scaling.shape[0]):
        value = jnp.where(
            rows == 0,
            jnp.broadcast_to(high[b : b + 1], shape),
            jnp.where(
                rows == 1,
                jnp.broadcast_to(mid[b : b + 1], shape),
                jnp.where(rows == 2, jnp.broadcast_to(low[b : b + 1], shape), 0.0),
            ),
        )
        scaled[b, cols : cols + PIECES] = value.astype(BF16)
    acc[...] = jnp.zeros_like(acc)
    for k in range(n_row):
        tile = tiles[k]

        def step(s, tile=tile):
            target = jnp.where(s < tile.total, tile.row(s), blocks)
            sums = jnp.dot(scaled[tile.column(s)], tile.block(s), preferred_element_type=F32)
            acc[target] += sums[0 : cols + 8]

        slot_loop(step, jnp.where(tile.group == me_row, tile.total, 0), 1, BUILD_GROUP)
    core = lax.rem(me_col, 2)
    for q in range(n_chip):
        mine = (2 * q + core) * per
        other = (2 * q + 1 - core) * per
        for j in range(per):
            keep[q, j] = acc[mine + j, 0:cols]
            away[q, j] = acc[other + j, 0:cols].astype(BF16)
    part = jnp.sum(acc[0:blocks, cols : cols + 8], axis=1)
    for i, value in enumerate(pieces_of(part)):
        both[i * blocks : (i + 1) * blocks] = value
    for i in range(n_land):
        first = 3 * blocks + i * cols
        both[first : first + cols] = acc[marks[me_row * n_land + i] - me_row * blocks, 0:cols].astype(BF16)


def three(ref, blocks):
    value = ref[0 : 3 * blocks].astype(F32)
    return (value[2 * blocks :] + value[blocks : 2 * blocks]) + value[0:blocks]


def pair_kernel(keep, away, both, both_in, both_out, *outs):
    n_chip, per, cols = keep.shape[:3]
    blocks = 2 * n_chip * per
    chip = places()[1] // 2
    parts = pieces_of(three(both, blocks) + three(both_in, blocks))
    for i, value in enumerate(parts):
        both_out[i * blocks : (i + 1) * blocks] = value
    lands = both[3 * blocks :].astype(F32) + both_in[3 * blocks :].astype(F32)
    both_out[3 * blocks :] = lands.astype(BF16)
    for k, out in enumerate(outs):
        to = lax.rem(chip + k, n_chip)
        for j in range(per):
            value = keep[to, j] + away[to, j].astype(F32)
            out[j * cols : (j + 1) * cols] = value.astype(BF16)


def gram_kernel(n_land, cols, per, *refs):
    marks = refs[0]
    gram, scaling_out, own, inverse, stage, land_stage = refs[-6:]
    parts = refs[1:-6]
    n = len(parts)
    me_row, me_col = places()
    blocks = scaling_out.shape[0]
    for k, part in enumerate(parts):
        place = shifted(me_col // 2, k, n)
        stage[place] = three(part, blocks)
        land_stage[place] = part[3 * blocks :]
    inverse[...] = 1.0 / tree_sum([stage[i] for i in range(n)])
    scaling_out[...] = SCALE * inverse[...]
    for j in range(per):
        own[j : j + 1, :] = inverse[pl.ds(me_col * per + j, 1), :]
    total = None
    for i in range(n_land):
        summed = tree_sum(
            [land_stage[k, i * cols : (i + 1) * cols].astype(F32) for k in range(n)]
        )
        block = marks[me_row * n_land + i] - me_row * blocks
        projected = summed * inverse[pl.ds(block, 1), :]
        product = lax.dot_general(
            projected,
            projected,
            (((1,), (1,)), ((), ())),
            precision=lax.Precision.HIGHEST,
            preferred_element_type=F32,
        )
        total = product if total is None else total + product
    gram[...] = total


WIDE = 4


def eliminate(gram):
    cols = gram.shape[0]
    rows = lax.broadcasted_iota(jnp.int32, (cols, 2 * cols), 0)
    lanes = lax.broadcasted_iota(jnp.int32, (cols, 2 * cols), 1)
    unit = (rows[:, :cols] == lanes[:, :cols]).astype(F32)
    work = jnp.concatenate([gram, unit], axis=1)
    for first in range(0, cols, WIDE):
        tops = [work[first + i : first + i + 1, :] for i in range(WIDE)]
        sides = [
            jnp.broadcast_to(work[:, first + i : first + i + 1], work.shape)
            for i in range(WIDE)
        ]
        change = None
        for i in range(WIDE):
            pivot = first + i
            unit_top = tops[i] / sides[i][pivot : pivot + 1, :]
            for m in range(i + 1, WIDE):
                factor = sides[i][first + m : first + m + 1, :]
                tops[m] = tops[m] - factor * unit_top
                inner = factor / sides[i][pivot : pivot + 1, :]
                sides[m] = sides[m] - sides[i] * inner
            term = sides[i] * unit_top
            change = term if change is None else change + term
        reduced = work - change
        kept = work
        for i in range(WIDE):
            kept = jnp.where(rows == first + i, tops[i], kept)
        work = jnp.where(rows >= first + WIDE, reduced, kept)
    pivots = jnp.sum(jnp.where(rows == lanes, work, 0.0), axis=1, keepdims=True)
    return (work * lax.rsqrt(pivots))[:, cols:]


def ritz_kernel(n_row, cells, *refs):
    grams, parts = refs[:n_row], refs[n_row:-3]
    own, out, stage = refs[-3:]
    cols = grams[0].shape[0]
    per = out.shape[1] // BLK
    inverse = eliminate(ordered_sum(stage, grams, places()[0]) * (1.0 / cells))
    for j in range(per):
        summed = tree_sum([m[j * cols : (j + 1) * cols].astype(F32) for m in parts])
        projected = summed * own[j : j + 1, :]
        out[:, j * BLK : (j + 1) * BLK] = jnp.dot(
            inverse, projected, precision=lax.Precision.HIGHEST, preferred_element_type=F32
        )


def swap(x, axis, k):
    return lax.ppermute(x, axis, [(i, i ^ k) for i in range(lax.axis_size(axis))])


def shift(x, axis, k):
    n = lax.axis_size(axis)
    return lax.ppermute(x, axis, [(i, (i + k) % n) for i in range(n)])


def shifts(x, axis):
    return [x] + [shift(x, axis, k) for k in range(1, lax.axis_size(axis))]


def chip_shift(x, k):
    n = lax.axis_size("col") // 2
    return lax.ppermute(
        x,
        "col",
        [(2 * q + p, 2 * ((q + k) % n) + p) for q in range(n) for p in range(2)],
    )


def chip_shifts(x):
    return [x] + [chip_shift(x, k) for k in range(1, lax.axis_size("col") // 2)]


def sibling(x):
    return swap(x, "col", 1)


def vec(*arrays):
    return [("vmem", a) for a in arrays]


def strip_body(profiles, cell_width, basis, block_lists, block_counts, landmarks):
    n_row, n_col = lax.axis_size("row"), lax.axis_size("col")
    n_chip = n_col // 2
    pcs, share = profiles.shape
    cols = basis.shape[0]
    per = share // BLK
    row_blocks, col_blocks = n_col * per, n_row * per
    all_rows = n_row * row_blocks
    slots = block_lists.shape[-1]
    n_land = landmarks.shape[0] // n_row

    def shape(*dims, dtype=F32):
        return jax.ShapeDtypeStruct(dims, dtype)

    (packed,) = call(
        pack_kernel,
        [shape(FEAT, share, dtype=BF16)],
        [("hbm", a) for a in (profiles, cell_width, block_lists)] + [("smem", block_counts)],
        [
            pltpu.VMEM((FEAT, share), F32),
            pltpu.VMEM(profiles.shape, BF16),
            pltpu.VMEM(cell_width.shape, BF16),
            pltpu.VMEM(block_lists.shape, jnp.int32),
            pltpu.SemaphoreType.DMA((3,)),
        ],
    )
    near = [chip_shift(packed, k) for k in range(1, n_chip)]
    rest, table = call(
        functools.partial(stack_kernel, pcs, n_row),
        [shape(n_row - 1, FEAT, share, dtype=BF16), shape(n_row, 8, BLK, dtype=jnp.int32)],
        vec(*shifts(packed, "row")) + [("near", pack) for pack in near],
    )
    table = ("smem", table.reshape(n_row * 8, BLK))
    marks = ("smem", landmarks)
    far = [chip_shift(rest, k) for k in range(1, n_chip)]
    bases = swap(basis, "row", 1)
    own, col_prof, col_inv, sums = call(
        functools.partial(own_kernel, pcs),
        [
            pltpu.VMEM((slots, BLK, BLK), BF16),
            pltpu.VMEM((col_blocks, BLK, FEAT), BF16),
            pltpu.VMEM((col_blocks, BLK, BLK), F32),
            shape(col_blocks, BLK),
        ],
        [table] + vec(packed, rest, sibling(packed), sibling(rest)),
        [
            pltpu.VMEM((row_blocks, FEAT, BLK), BF16),
            pltpu.VMEM((row_blocks, 8, BLK), F32),
            pltpu.VMEM((col_blocks + 1, 8, BLK), F32),
        ],
    )
    far, sums, bases = lax.optimization_barrier((far, sums, bases))
    bases = jnp.stack([basis, bases])
    span = 2
    while span < n_row:
        bases = jnp.concatenate([bases, swap(bases, "row", span)])
        span *= 2
    stacks = []
    for pack, group in zip(near, far):
        stacks += [pack, group, sibling(pack), sibling(group)]
    far_slots = (n_row - 1) * slots
    others, part = call(
        functools.partial(strip_kernel, pcs, n_row),
        [pltpu.VMEM((far_slots, BLK, BLK), BF16), shape(all_rows, BLK)],
        [table, ("keep", own), ("keep", col_prof), ("keep", col_inv)]
        + vec(sums, *stacks),
        [
            pltpu.VMEM((all_rows - row_blocks, FEAT, BLK), BF16),
            pltpu.VMEM((all_rows - row_blocks, 8, BLK), F32),
            pltpu.VMEM((col_blocks, BLK, BLK), F32),
            pltpu.VMEM((all_rows + 1, 8, BLK), F32),
            pltpu.VMEM((col_blocks + 1, 8, BLK), F32),
        ],
    )
    tiles = [("keep", own), ("keep", others)]

    def chip_parts(part):
        return chip_shifts((part + sibling(part)).astype(BF16))

    for _ in range(SWEEPS - 2):
        (part,) = call(
            functools.partial(sweep_kernel, n_row, n_chip),
            [shape(all_rows, BLK)],
            [table] + tiles + vec(*chip_parts(part)) + [("near", bases)],
            [
                pltpu.VMEM((n_chip, all_rows, BLK), F32),
                pltpu.VMEM((2, all_rows, PIECES, 2 * BLK), BF16),
                pltpu.VMEM((col_blocks, BLK, BLK), F32),
                pltpu.VMEM((all_rows + 1, 8, BLK), F32),
                pltpu.VMEM((col_blocks + 1, 8, BLK), F32),
            ],
        )
    both_rows = 3 * row_blocks + n_land * cols
    keep, away, both, col_scaling = call(
        functools.partial(last_kernel, n_row, n_chip, n_land),
        [
            shape(n_chip, per, cols, BLK),
            shape(n_chip, per, cols, BLK, dtype=BF16),
            shape(both_rows, BLK, dtype=BF16),
            shape(col_blocks, BLK),
        ],
        [table, marks] + tiles + vec(*chip_parts(part), bases),
        [
            pltpu.VMEM((n_chip, all_rows, BLK), F32),
            pltpu.VMEM((2, all_rows, PIECES, 2 * BLK), BF16),
            pltpu.VMEM((col_blocks + 1, 8, BLK), F32),
            pltpu.VMEM((col_blocks, cols + PIECES, BLK), BF16),
            pltpu.VMEM((row_blocks + 1, cols + 8, BLK), F32),
        ],
    )
    pairs = call(
        pair_kernel,
        [shape(both_rows, BLK, dtype=BF16)]
        + [shape(per * cols, BLK, dtype=BF16)] * n_chip,
        vec(keep, sibling(away), both, sibling(both)),
    )
    sums = [pairs[0]] + [chip_shift(pairs[0], k) for k in range(1, n_chip)]
    shares = [pairs[1]] + [chip_shift(pairs[1 + k], k) for k in range(1, n_chip)]
    gram, row_scaling, own = call(
        functools.partial(gram_kernel, n_land, cols, per),
        [shape(cols, cols), shape(row_blocks, BLK), shape(per, BLK)],
        [marks] + vec(*sums),
        [
            pltpu.VMEM((row_blocks, BLK), F32),
            pltpu.VMEM((n_chip, row_blocks, BLK), F32),
            pltpu.VMEM((n_chip, n_land * cols, BLK), BF16),
        ],
    )
    (ritz,) = call(
        functools.partial(ritz_kernel, n_row, landmarks.shape[0] * BLK),
        [shape(cols, share)],
        vec(*shifts(gram, "row"), *shares, own),
        [pltpu.VMEM((n_row, cols, cols), F32)],
    )
    return row_scaling.reshape(-1), col_scaling.reshape(-1), ritz


def tile_pack_kernel(prof_ref, width_ref, out_ref, work):
    pcs = prof_ref.shape[0]
    prof = prof_ref[...].astype(F32)
    norm = jnp.sum(prof * prof, axis=0, keepdims=True)
    high, mid, low = split3(norm)
    work[...] = jnp.zeros_like(work)
    work[0:pcs, :] = prof
    work[pcs : pcs + 1, :] = high
    work[pcs + 1 : pcs + 2, :] = mid
    work[pcs + 2 : pcs + 3, :] = low
    work[pcs + 3 : pcs + 6, :] = jnp.ones((3, prof.shape[1]), F32)
    work[pcs + 6 : pcs + 7, :] = width_ref[...].astype(F32)
    out_ref[...] = work[...].astype(BF16)


def tile_square(tile, slots):
    a, b, c, d = [tile[s] for s in slots]
    return jnp.concatenate(
        [jnp.concatenate([a, b], axis=1), jnp.concatenate([c, d], axis=1)], axis=0
    )


def tile_add_rows(acc, lists, target, slots, sums, total, spare, firsts):
    for i, (s, (row, lane)) in enumerate(zip(slots, firsts)):
        place = jnp.where(s < total, lists[0, 0, target, s], spare)
        acc[place] += sums[row : row + 8, lane : lane + BLK]


def tile_row_sums(lists, tile, left, acc, total, spare):
    def step(*slots):
        low = [left[0, lists[0, 0, 1, s]] for s in slots[:2]]
        high = [left[1, lists[0, 0, 1, s]] for s in slots[2:]]
        sums = jnp.dot(
            jnp.concatenate(low + high, axis=0),
            tile_square(tile, slots),
            preferred_element_type=F32,
        )
        firsts = [(0, 0), (PIECES, BLK), (2 * PIECES, 0), (3 * PIECES, BLK)]
        tile_add_rows(acc, lists, 0, slots, sums, total, spare, firsts)

    slot_loop(step, total, 4, 4 * TILE_GROUP)


def tile_col_sums(lists, tile, left, acc, total, spare):
    def step(*slots):
        pieces = [left[i % 2, lists[0, 0, 0, s]] for i, s in enumerate(slots)]
        sums = lax.dot_general(
            jnp.concatenate(pieces, axis=0),
            tile_square(tile, slots),
            (((1,), (1,)), ((), ())),
            preferred_element_type=F32,
        )
        firsts = [(0, 0), (PIECES, 0), (2 * PIECES, BLK), (3 * PIECES, BLK)]
        tile_add_rows(acc, lists, 1, slots, sums, total, spare, firsts)

    slot_loop(step, total, 4, 4 * TILE_GROUP)


def tile_build_kernel(pcs, n_row, n_col, *refs):
    lists, counts = refs[:2]
    col_in = refs[2 : 2 + n_row]
    row_in = refs[2 + n_row : 2 + n_row + n_col]
    tile, part, row_prof, row_inv, col_prof, col_inv, acc, left = refs[2 + n_row + n_col :]
    per = row_in[0].shape[1] // BLK
    col_blocks, row_blocks = n_row * per, n_col * per
    total = counts[0, 0]
    me_row, me_col = places()
    for k, ref in enumerate(row_in):
        core = lax.rem(me_col + k, 2)
        piece = shifted(me_col // 2, k // 2, n_col // 2) * 2 + core
        for j in range(per):
            block = ref[:, j * BLK : (j + 1) * BLK]
            row_prof[piece * per + j] = block
            width = block.astype(F32)[pcs + 6 : pcs + 7, :]
            row_inv[piece * per + j] = jnp.broadcast_to(1.0 / width, (8, BLK))
    rows = lax.broadcasted_iota(jnp.int32, (FEAT, BLK), 0)
    for k, ref in enumerate(col_in):
        piece = shifted(me_row, k, n_row)
        for j in range(per):
            block = ref[0:FEAT, j * BLK : (j + 1) * BLK].astype(F32)
            turned = jnp.where(rows < pcs, -2.0 * block, 0.0)
            turned = jnp.where((rows >= pcs) & (rows < pcs + 3), 1.0, turned)
            turned = jnp.where(
                (rows >= pcs + 3) & (rows < pcs + 6), pltpu.roll(block, 3, 0), turned
            )
            turned = jnp.where(rows == pcs + 7, pltpu.roll(block, 1, 0), turned)
            turned = turned.T
            col_prof[piece * per + j] = turned.astype(BF16)
            col_inv[piece * per + j] = jnp.broadcast_to(
                -LOG2E / turned[:, pcs + 7 : pcs + 8], (BLK, BLK)
            )

    def step(s):
        rb, cb = lists[0, 0, 0, s], lists[0, 0, 1, s]
        distance = jnp.dot(col_prof[cb], row_prof[rb], preferred_element_type=F32)
        block = jnp.exp2(distance * col_inv[cb] * row_inv[rb][0:1, :])
        tile[s] = block.astype(BF16)

    slot_loop(step, total, 1, TILE_GROUP)
    ones = (lax.broadcasted_iota(jnp.int32, (PIECES, BLK), 0) == 0).astype(F32).astype(BF16)
    empty = jnp.zeros_like(ones)
    for b in range(row_blocks):
        left[0, b] = jnp.concatenate([ones, empty], axis=1)
        left[1, b] = jnp.concatenate([empty, ones], axis=1)
    acc[...] = jnp.zeros_like(acc)
    tile_col_sums(lists, tile, left, acc, total, col_blocks)
    part[...] = jnp.sum(acc[0:col_blocks], axis=1)


def tile_pass_kernel(over_rows, n_parts, *refs):
    lists, counts, tile = refs[:3]
    parts = refs[3 : 3 + n_parts]
    out, stage, left, acc = refs[-4:]
    total = counts[0, 0]
    blocks = out.shape[0]
    me_row, me_col = places()
    scaling = SCALE / ordered_sum(stage, parts, me_row if over_rows else me_col // 2)
    fill_pieces(left, scaling)
    acc[...] = jnp.zeros_like(acc)
    (tile_row_sums if over_rows else tile_col_sums)(lists, tile, left, acc, total, blocks)
    out[...] = jnp.sum(acc[0:blocks], axis=1)


def tile_last_kernel(n_row, n_col, n_land, *refs):
    lists, counts, marks, tile = refs[:4]
    parts, bases = refs[4 : 4 + n_row], refs[4 + n_row : 4 + 2 * n_row]
    keep, away, both, scaling_out, stage, scaled, acc = refs[4 + 2 * n_row :]
    cols = bases[0].shape[0]
    per = bases[0].shape[1] // BLK
    blocks = n_col * per
    total = counts[0, 0]
    me_row, me_col = places()
    scaling = SCALE / ordered_sum(stage, parts, me_row)
    scaling_out[...] = scaling
    for k in range(n_row):
        piece = shifted(me_row, k, n_row)
        for j in range(per):
            block = bases[k][:, j * BLK : (j + 1) * BLK].astype(F32)
            b = piece * per + j
            scaled[b, 0:cols] = (block * scaling_out[pl.ds(b, 1), :]).astype(BF16)
    high, mid, low = split3(scaling)
    shape = (PIECES, BLK)
    rows = lax.broadcasted_iota(jnp.int32, shape, 0)
    for b in range(scaling.shape[0]):
        value = jnp.where(
            rows == 0,
            jnp.broadcast_to(high[b : b + 1], shape),
            jnp.where(
                rows == 1,
                jnp.broadcast_to(mid[b : b + 1], shape),
                jnp.where(rows == 2, jnp.broadcast_to(low[b : b + 1], shape), 0.0),
            ),
        )
        scaled[b, cols : cols + PIECES] = value.astype(BF16)
    acc[...] = jnp.zeros_like(acc)

    def step(s):
        target = jnp.where(s < total, lists[0, 0, 0, s], blocks)
        sums = jnp.dot(scaled[lists[0, 0, 1, s]], tile[s], preferred_element_type=F32)
        acc[target] += sums[0 : cols + 8]

    slot_loop(step, total, 1, TILE_GROUP)
    core = lax.rem(me_col, 2)
    for q in range(n_col // 2):
        own = (2 * q + core) * per
        other = (2 * q + 1 - core) * per
        for j in range(per):
            keep[q, j] = acc[own + j, 0:cols]
            away[q, j] = acc[other + j, 0:cols].astype(BF16)
    row_part = jnp.sum(acc[0:blocks, cols : cols + 8], axis=1)
    for i, value in enumerate(pieces_of(row_part)):
        both[i * blocks : (i + 1) * blocks] = value
    for i in range(n_land):
        first = 3 * blocks + i * cols
        both[first : first + cols] = acc[marks[me_row * n_land + i] - me_row * blocks, 0:cols].astype(BF16)


def tile_body(profiles, cell_width, basis, block_lists, block_counts, landmarks):
    n_row, n_col = lax.axis_size("row"), lax.axis_size("col")
    n_chip = n_col // 2
    pcs, share = profiles.shape
    cols = basis.shape[0]
    per = share // BLK
    row_blocks, col_blocks = n_col * per, n_row * per
    slots = block_lists.shape[-1]
    n_land = landmarks.shape[0] // n_row

    def shape(*dims, dtype=F32):
        return jax.ShapeDtypeStruct(dims, dtype)

    (packed,) = call(
        tile_pack_kernel,
        [shape(FEAT, share, dtype=BF16)],
        vec(profiles, cell_width.reshape(1, share)),
        [pltpu.VMEM((FEAT, share), F32)],
    )
    spread = lax.ppermute(
        packed,
        ("row", "col"),
        [((q % n_row) * n_col + q // n_row, q) for q in range(n_row * n_col)],
    )
    row_packs = []
    for pack in chip_shifts(spread):
        row_packs += [pack, sibling(pack)]
    col_packs = shifts(packed, "row")
    bases = shifts(basis, "row")
    lists = [("smem", block_lists), ("smem", block_counts)]
    marks = [("smem", landmarks)]
    tile, part = call(
        functools.partial(tile_build_kernel, pcs, n_row, n_col),
        [pltpu.VMEM((slots, BLK, BLK), BF16), shape(col_blocks, BLK)],
        lists + vec(*col_packs, *row_packs),
        [
            pltpu.VMEM((row_blocks, FEAT, BLK), BF16),
            pltpu.VMEM((row_blocks, 8, BLK), F32),
            pltpu.VMEM((col_blocks, BLK, FEAT), BF16),
            pltpu.VMEM((col_blocks, BLK, BLK), F32),
            pltpu.VMEM((col_blocks + 1, 8, BLK), F32),
            pltpu.VMEM((2, row_blocks, PIECES, 2 * BLK), BF16),
        ],
    )
    for number in range(SWEEPS - 1):
        early = [("near", b) for b in bases[1:]] if number == 0 else []
        (part,) = call(
            functools.partial(tile_pass_kernel, True, n_row),
            [shape(row_blocks, BLK)],
            lists + [("keep", tile)] + vec(*shifts(part, "row")) + early,
            [
                pltpu.VMEM((n_row, col_blocks, BLK), F32),
                pltpu.VMEM((2, col_blocks, PIECES, 2 * BLK), BF16),
                pltpu.VMEM((row_blocks + 1, 8, BLK), F32),
            ],
        )
        (part,) = call(
            functools.partial(tile_pass_kernel, False, n_chip),
            [shape(col_blocks, BLK)],
            lists + [("keep", tile)] + vec(*chip_shifts(part + sibling(part))),
            [
                pltpu.VMEM((n_chip, row_blocks, BLK), F32),
                pltpu.VMEM((2, row_blocks, PIECES, 2 * BLK), BF16),
                pltpu.VMEM((col_blocks + 1, 8, BLK), F32),
            ],
        )
    both_rows = 3 * row_blocks + n_land * cols
    keep, away, both, col_scaling = call(
        functools.partial(tile_last_kernel, n_row, n_col, n_land),
        [
            shape(n_chip, per, cols, BLK),
            shape(n_chip, per, cols, BLK, dtype=BF16),
            shape(both_rows, BLK, dtype=BF16),
            shape(col_blocks, BLK),
        ],
        lists + marks + [("keep", tile)] + vec(*shifts(part, "row"), *bases),
        [
            pltpu.VMEM((n_row, col_blocks, BLK), F32),
            pltpu.VMEM((col_blocks, cols + PIECES, BLK), BF16),
            pltpu.VMEM((row_blocks + 1, cols + 8, BLK), F32),
        ],
    )
    pairs = call(
        pair_kernel,
        [shape(both_rows, BLK, dtype=BF16)]
        + [shape(per * cols, BLK, dtype=BF16)] * n_chip,
        vec(keep, sibling(away), both, sibling(both)),
    )
    sums = [pairs[0]] + [chip_shift(pairs[0], k) for k in range(1, n_chip)]
    shares = [pairs[1]] + [chip_shift(pairs[1 + k], k) for k in range(1, n_chip)]
    gram, row_scaling, own = call(
        functools.partial(gram_kernel, n_land, cols, per),
        [shape(cols, cols), shape(row_blocks, BLK), shape(per, BLK)],
        marks + vec(*sums),
        [
            pltpu.VMEM((row_blocks, BLK), F32),
            pltpu.VMEM((n_chip, row_blocks, BLK), F32),
            pltpu.VMEM((n_chip, n_land * cols, BLK), BF16),
        ],
    )
    (ritz,) = call(
        functools.partial(ritz_kernel, n_row, landmarks.shape[0] * BLK),
        [shape(cols, share)],
        vec(*shifts(gram, "row"), *shares, own),
        [pltpu.VMEM((n_row, cols, cols), F32)],
    )
    return row_scaling.reshape(-1), col_scaling.reshape(-1), ritz


def solution(mesh):
    placed = (
        P(None, ("col", "row")),
        P(("col", "row")),
        P(None, ("col", "row")),
        P("row", "col", None, None),
        P("row", "col"),
        P(),
    )
    return jax.shard_map(
        strip_body if mesh.shape["row"] <= STRIP_TILES else tile_body,
        mesh=mesh,
        in_specs=placed,
        out_specs=(P("row"), P("col"), P(None, ("row", "col"))),
        check_vma=False,
    )
```

```python
import functools

import jax
import jax.numpy as jnp
from jax import lax
from jax.experimental import pallas as pl
from jax.experimental.pallas import tpu as pltpu
from jax.sharding import PartitionSpec as P

BLK = 128
SWEEPS = 3
GROUP = 32
BUILD_GROUP = 16
TILE_GROUP = 16
ROWS, COLUMNS, COUNT = 0, 1, 2
FEAT = 64
PACK = 56
PIECES = 16
SCALE = 512.0
LOG2E = 1.4426950408889634
F32 = jnp.float32
BF16 = jnp.bfloat16
MIB = 1 << 20
STRIP_TILES = 8

VMEM_SPEC = pl.BlockSpec(memory_space=pltpu.VMEM)
SMEM_SPEC = pl.BlockSpec(memory_space=pltpu.SMEM)


def split3(x):
    high = x.astype(BF16).astype(F32)
    mid = (x - high).astype(BF16).astype(F32)
    low = (x - high - mid).astype(BF16).astype(F32)
    return high, mid, low


def tree_sum(values):
    values = list(values)
    while len(values) > 1:
        values = [a + b for a, b in zip(values[::2], values[1::2])]
    return values[0]


def call(kernel, outs, ins, scratch=(), limit=24, flops=1 << 24):
    args, specs = [], []
    for kind, array in ins:
        if kind == "smem":
            specs.append(SMEM_SPEC)
        elif kind == "near":
            specs.append(pl.BlockSpec(memory_space=pl.ANY))
        elif kind == "hbm":
            specs.append(pl.BlockSpec(memory_space=pltpu.HBM))
            array = pltpu.with_memory_space_constraint(array, pltpu.HBM)
        else:
            specs.append(VMEM_SPEC)
            if kind == "keep":
                array = pltpu.with_memory_space_constraint(array, pltpu.VMEM)
        args.append(array)
    return pl.pallas_call(
        kernel,
        out_shape=tuple(outs),
        in_specs=specs,
        out_specs=tuple(VMEM_SPEC for _ in outs),
        scratch_shapes=list(scratch),
        compiler_params=pltpu.CompilerParams(vmem_limit_bytes=limit * MIB),
        cost_estimate=pl.CostEstimate(flops=flops, bytes_accessed=1 << 20, transcendentals=0),
    )(*args)


def pack_kernel(prof_hbm, width_hbm, lists_hbm, counts, out_ref, *scratch):
    work, prof_ref, width_ref, lists_ref, sems = scratch
    pairs = [
        (prof_hbm, prof_ref),
        (width_hbm, width_ref),
        (lists_hbm, lists_ref),
    ]
    copies = [pltpu.make_async_copy(a, b, sems.at[i]) for i, (a, b) in enumerate(pairs)]
    for copy in copies:
        copy.start()
    for copy in copies:
        copy.wait()
    pcs = prof_ref.shape[0]
    prof = prof_ref[...].astype(F32)
    norm = jnp.sum(prof * prof, axis=0, keepdims=True)
    high, mid, low = split3(norm)
    work[...] = jnp.zeros_like(work)
    work[0:pcs, :] = prof
    work[pcs : pcs + 1, :] = high
    work[pcs + 1 : pcs + 2, :] = mid
    work[pcs + 2 : pcs + 3, :] = low
    work[pcs + 3 : pcs + 4, :] = width_ref[...].astype(F32).reshape(1, -1)
    lists = lists_ref[0, 0].astype(F32)
    slots = slice(pcs + 4, pcs + 5)
    work[slots, 0:BLK] = lists[0:1]
    work[slots, BLK : 2 * BLK] = lists[1:2]
    count = jnp.full((1, BLK), counts[0, 0], jnp.int32)
    work[slots, 2 * BLK : 3 * BLK] = count.astype(F32)
    out_ref[...] = work[...].astype(BF16)


def places():
    return lax.axis_index("row"), lax.axis_index("col")


def stack_kernel(pcs, n, *refs):
    packs, (rest, table) = refs[:n], refs[-2:]
    me_row, _ = places()
    for k, pack in enumerate(packs):
        if k:
            rest[k - 1] = pack[...]
        slots = pack[:, 0 : 3 * BLK].astype(F32)[pcs + 4 : pcs + 5]
        for row in (ROWS, COLUMNS, COUNT):
            values = slots[:, row * BLK : (row + 1) * BLK].astype(jnp.int32)
            table[shifted(me_row, k, n), row : row + 1] = values


def slot_loop(step, count, size, group):
    def advance(number, carry):
        for i in range(0, group, size):
            step(*[number * group + i + j for j in range(size)])
        return carry

    lax.fori_loop(0, (count + group - 1) // group, advance, 0)


class Tile:
    def __init__(self, table, n_row, k, own, others):
        _, me_col = places()
        self.group = shifted(me_col // 2, k, n_row)
        self.table, self.k = table, k
        slots = own.shape[0]
        self.blocks, self.base = (own, 0) if k == 0 else (others, (k - 1) * slots)
        self.total = table[self.group * 8 + COUNT, 0]

    def row(self, s):
        return self.table[self.group * 8 + ROWS, s]

    def column(self, s):
        return self.table[self.group * 8 + COLUMNS, s]

    def block(self, s):
        return self.blocks[self.base + s]


def shifted(me, k, n):
    return lax.rem(me + (n - k), n)


def ordered_sum(stage, refs, me):
    n = len(refs)
    for k, ref in enumerate(refs):
        stage[shifted(me, k, n)] = ref[...]
    return tree_sum([stage[i] for i in range(n)])


def square(tile, slots):
    a, b, c, d = [tile.block(s) for s in slots]
    return jnp.concatenate(
        [jnp.concatenate([a, b], axis=1), jnp.concatenate([c, d], axis=1)], axis=0
    )


def add_rows(acc, sums, firsts, targets):
    for (row, lane), target in zip(firsts, targets):
        acc[target] += sums[row : row + 8, lane : lane + BLK]


def row_sums(tile, wide, acc, row_blocks, spare):
    first = tile.group * row_blocks

    def step(s):
        product = tile.block(s).astype(F32) * wide[tile.column(s)]
        sums = jnp.sum(product.reshape(BLK // 8, 8, BLK), axis=0)
        acc[jnp.where(s < tile.total, first + tile.row(s), spare)] += sums

    slot_loop(step, tile.total, 1, GROUP)


def spread_lanes(wide, scaling):
    turned = scaling.T
    for b in range(scaling.shape[0]):
        wide[b] = jnp.broadcast_to(turned[:, b : b + 1], (BLK, BLK))


def col_sums(tile, left, acc, row_blocks, spare):
    first = tile.group * row_blocks

    def step(*slots):
        if left is None:
            rows = lax.broadcasted_iota(jnp.int32, (4 * PIECES, 2 * BLK), 0)
            lanes = lax.broadcasted_iota(jnp.int32, (4 * PIECES, 2 * BLK), 1)
            block = rows // PIECES
            pieces = (rows % PIECES == 0) & (block % 2 == lanes // BLK)
            pieces = pieces.astype(F32).astype(BF16)
        else:
            pieces = [left[i % 2, first + tile.row(s)] for i, s in enumerate(slots)]
            pieces = jnp.concatenate(pieces, axis=0)
        sums = lax.dot_general(
            pieces,
            square(tile, slots),
            (((1,), (1,)), ((), ())),
            preferred_element_type=F32,
        )
        firsts = [(0, 0), (PIECES, 0), (2 * PIECES, BLK), (3 * PIECES, BLK)]
        targets = [jnp.where(s < tile.total, tile.column(s), spare) for s in slots]
        add_rows(acc, sums, firsts, targets)

    slot_loop(step, tile.total, 4, 2 * GROUP if tile.k == 0 else GROUP)


def fill_pieces(left, scaling):
    high, mid, low = split3(scaling)
    shape = (PIECES, BLK)
    rows = lax.broadcasted_iota(jnp.int32, shape, 0)
    empty = jnp.zeros(shape, F32).astype(BF16)
    for b in range(scaling.shape[0]):
        value = jnp.where(
            rows == 0,
            jnp.broadcast_to(high[b : b + 1], shape),
            jnp.where(
                rows == 1,
                jnp.broadcast_to(mid[b : b + 1], shape),
                jnp.where(rows == 2, jnp.broadcast_to(low[b : b + 1], shape), 0.0),
            ),
        ).astype(BF16)
        left[0, b] = jnp.concatenate([value, empty], axis=1)
        left[1, b] = jnp.concatenate([empty, value], axis=1)


def build(tile, offset, row_prof, row_inv, col_prof, col_inv):
    def step(s):
        row, column = offset + tile.row(s), tile.column(s)
        distance = jnp.dot(col_prof[column], row_prof[row], preferred_element_type=F32)
        block = jnp.exp2(distance * col_inv[column] * row_inv[row][0:1, :])
        tile.blocks[tile.base + s] = block.astype(BF16)

    slot_loop(step, tile.total, 1, BUILD_GROUP)


def piece_block(pieces, k, j):
    lanes = slice(j * BLK, (j + 1) * BLK)
    return pieces[0][:, lanes] if k == 0 else pieces[1][k - 1, :, lanes]


def fill_rows(pcs, sources, row_prof, row_inv, offset):
    me_row, me_col = places()
    n_row = sources[0][1].shape[0] + 1
    per = sources[0][0].shape[1] // BLK
    ones = lax.broadcasted_iota(jnp.int32, (FEAT - PACK, BLK), 0) < 3
    ones = ones.astype(F32)
    for i, pieces in enumerate(sources):
        core = lax.rem(me_col + i, 2)
        for k in range(n_row):
            piece = core * n_row + shifted(me_row, k, n_row)
            for j in range(per):
                block = piece_block(pieces, k, j).astype(F32)
                whole = jnp.concatenate([block, ones], axis=0)
                row_prof[offset + piece * per + j] = whole.astype(BF16)
                width = block[pcs + 3 : pcs + 4, :]
                row_inv[offset + piece * per + j] = jnp.broadcast_to(1.0 / width, (8, BLK))


def own_kernel(pcs, table, pack, rest, pack_in, rest_in, *refs):
    tile, col_prof, col_inv, sums, row_prof, row_inv, acc = refs[-7:]
    n_row = rest.shape[0] + 1
    per = pack.shape[1] // BLK
    me_row, _ = places()
    fill_rows(pcs, [(pack, rest), (pack_in, rest_in)], row_prof, row_inv, 0)
    rows = lax.broadcasted_iota(jnp.int32, (FEAT, BLK), 0)
    for k in range(n_row):
        piece = shifted(me_row, k, n_row)
        for j in range(per):
            block = piece_block((pack, rest), k, j).astype(F32)
            block = jnp.concatenate([block, jnp.zeros((FEAT - PACK, BLK), F32)], axis=0)
            turned = jnp.where(rows < pcs, -2.0 * block, 0.0)
            turned = jnp.where((rows >= pcs) & (rows < pcs + 3), 1.0, turned)
            turned = jnp.where(rows == PACK - 1, pltpu.roll(block, PACK - 4 - pcs, 0), turned)
            turned = jnp.where(
                (rows >= PACK) & (rows < PACK + 3), pltpu.roll(block, PACK - pcs, 0), turned
            )
            turned = turned.T
            col_prof[piece * per + j] = turned.astype(BF16)
            col_inv[piece * per + j] = jnp.broadcast_to(
                -LOG2E / turned[:, PACK - 1 : PACK], (BLK, BLK)
            )
    own = Tile(table, n_row, 0, tile, None)
    build(own, 0, row_prof, row_inv, col_prof, col_inv)
    sums[...] = column_totals([own], None, acc, row_prof.shape[0])


def column_totals(tiles, left, acc, row_blocks):
    col_blocks = acc.shape[0] - 1
    acc[...] = jnp.zeros_like(acc)
    for tile in tiles:
        col_sums(tile, left, acc, row_blocks, col_blocks)
    return jnp.sum(acc[0:col_blocks], axis=1)


def row_part(tiles, wide, acc, row_blocks, out):
    blocks = acc.shape[0] - 1
    acc[...] = jnp.zeros_like(acc)
    for tile in tiles:
        row_sums(tile, wide, acc, row_blocks, blocks)
    out[...] = jnp.sum(acc[0:blocks], axis=1)


def strip_kernel(pcs, n_row, *refs):
    table, own, col_prof, col_inv, own_sums = refs[:5]
    sources = [refs[i : i + 2] for i in range(5, 5 + 4 * (n_row - 1), 2)]
    others, out, row_prof, row_inv, wide, row_acc, col_acc = refs[-7:]
    row_blocks = row_prof.shape[0] // (n_row - 1)
    tiles = [Tile(table, n_row, k, own, others) for k in range(n_row)]
    for k in range(1, n_row):
        first = (k - 1) * row_blocks
        fill_rows(pcs, sources[2 * k - 2 : 2 * k], row_prof, row_inv, first)
    for k in range(1, n_row):
        first = (k - 1) * row_blocks
        build(tiles[k], first, row_prof, row_inv, col_prof, col_inv)
    totals = column_totals(tiles[1:], None, col_acc, row_blocks) + own_sums[...]
    spread_lanes(wide, SCALE / totals)
    row_part(tiles, wide, row_acc, row_blocks, out)


def row_scalings(stage, parts):
    for k, part in enumerate(parts):
        stage[shifted(places()[1] // 2, k, len(parts))] = part[...].astype(F32)
    return SCALE / tree_sum([stage[i] for i in range(len(parts))])


def sweep_kernel(n_row, n_chip, *refs):
    table, own, others = refs[:3]
    parts = refs[3 : 3 + n_chip]
    out, stage, row_left, wide, row_acc, col_acc = refs[-6:]
    row_blocks = out.shape[0] // n_row
    tiles = [Tile(table, n_row, k, own, others) for k in range(n_row)]
    fill_pieces(row_left, row_scalings(stage, parts))
    totals = column_totals(tiles, row_left, col_acc, row_blocks)
    spread_lanes(wide, SCALE / totals)
    row_part(tiles, wide, row_acc, row_blocks, out)


def pieces_of(value):
    return [v.astype(BF16) for v in split3(value)]


def last_kernel(n_row, n_chip, n_land, *refs):
    table, marks, own, others = refs[:4]
    parts, bases = refs[4 : 4 + n_chip], refs[4 + n_chip : 4 + n_chip + n_row]
    keep, away, both, scaling_out, stage, row_left, col_acc, scaled, acc = refs[-9:]
    cols = bases[0].shape[0]
    per = bases[0].shape[1] // BLK
    blocks = 2 * n_chip * per
    me_row, me_col = places()
    tiles = [Tile(table, n_row, k, own, others) for k in range(n_row)]
    fill_pieces(row_left, row_scalings(stage, parts))
    scaling = SCALE / column_totals(tiles, row_left, col_acc, blocks)
    scaling_out[...] = scaling
    for k in range(n_row):
        piece = shifted(me_row, k, n_row)
        for j in range(per):
            block = bases[k][:, j * BLK : (j + 1) * BLK].astype(F32)
            b = piece * per + j
            scaled[b, 0:cols] = (block * scaling_out[pl.ds(b, 1), :]).astype(BF16)
    high, mid, low = split3(scaling)
    shape = (PIECES, BLK)
    rows = lax.broadcasted_iota(jnp.int32, shape, 0)
    for b in range(scaling.shape[0]):
        value = jnp.where(
            rows == 0,
            jnp.broadcast_to(high[b : b + 1], shape),
            jnp.where(
                rows == 1,
                jnp.broadcast_to(mid[b : b + 1], shape),
                jnp.where(rows == 2, jnp.broadcast_to(low[b : b + 1], shape), 0.0),
            ),
        )
        scaled[b, cols : cols + PIECES] = value.astype(BF16)
    acc[...] = jnp.zeros_like(acc)
    for k in range(n_row):
        tile = tiles[k]

        def step(s, tile=tile):
            target = jnp.where(s < tile.total, tile.row(s), blocks)
            sums = jnp.dot(scaled[tile.column(s)], tile.block(s), preferred_element_type=F32)
            acc[target] += sums[0 : cols + 8]

        slot_loop(step, jnp.where(tile.group == me_row, tile.total, 0), 1, BUILD_GROUP)
    core = lax.rem(me_col, 2)
    for q in range(n_chip):
        mine = (2 * q + core) * per
        other = (2 * q + 1 - core) * per
        for j in range(per):
            keep[q, j] = acc[mine + j, 0:cols]
            away[q, j] = acc[other + j, 0:cols].astype(BF16)
    part = jnp.sum(acc[0:blocks, cols : cols + 8], axis=1)
    for i, value in enumerate(pieces_of(part)):
        both[i * blocks : (i + 1) * blocks] = value
    for i in range(n_land):
        first = 3 * blocks + i * cols
        both[first : first + cols] = acc[marks[me_row * n_land + i] - me_row * blocks, 0:cols].astype(BF16)


def three(ref, blocks):
    value = ref[0 : 3 * blocks].astype(F32)
    return (value[2 * blocks :] + value[blocks : 2 * blocks]) + value[0:blocks]


def pair_kernel(keep, away, both, both_in, both_out, *outs):
    n_chip, per, cols = keep.shape[:3]
    blocks = 2 * n_chip * per
    chip = places()[1] // 2
    parts = pieces_of(three(both, blocks) + three(both_in, blocks))
    for i, value in enumerate(parts):
        both_out[i * blocks : (i + 1) * blocks] = value
    lands = both[3 * blocks :].astype(F32) + both_in[3 * blocks :].astype(F32)
    both_out[3 * blocks :] = lands.astype(BF16)
    for k, out in enumerate(outs):
        to = lax.rem(chip + k, n_chip)
        for j in range(per):
            value = keep[to, j] + away[to, j].astype(F32)
            out[j * cols : (j + 1) * cols] = value.astype(BF16)


def gram_kernel(n_land, cols, per, *refs):
    marks = refs[0]
    gram, scaling_out, own, inverse, stage, land_stage = refs[-6:]
    parts = refs[1:-6]
    n = len(parts)
    me_row, me_col = places()
    blocks = scaling_out.shape[0]
    for k, part in enumerate(parts):
        place = shifted(me_col // 2, k, n)
        stage[place] = three(part, blocks)
        land_stage[place] = part[3 * blocks :]
    inverse[...] = 1.0 / tree_sum([stage[i] for i in range(n)])
    scaling_out[...] = SCALE * inverse[...]
    for j in range(per):
        own[j : j + 1, :] = inverse[pl.ds(me_col * per + j, 1), :]
    total = None
    for i in range(n_land):
        summed = tree_sum(
            [land_stage[k, i * cols : (i + 1) * cols].astype(F32) for k in range(n)]
        )
        block = marks[me_row * n_land + i] - me_row * blocks
        projected = summed * inverse[pl.ds(block, 1), :]
        product = lax.dot_general(
            projected,
            projected,
            (((1,), (1,)), ((), ())),
            precision=lax.Precision.HIGHEST,
            preferred_element_type=F32,
        )
        total = product if total is None else total + product
    gram[...] = total


WIDE = 4


def eliminate(gram):
    cols = gram.shape[0]
    rows = lax.broadcasted_iota(jnp.int32, (cols, 2 * cols), 0)
    lanes = lax.broadcasted_iota(jnp.int32, (cols, 2 * cols), 1)
    unit = (rows[:, :cols] == lanes[:, :cols]).astype(F32)
    work = jnp.concatenate([gram, unit], axis=1)
    for first in range(0, cols, WIDE):
        tops = [work[first + i : first + i + 1, :] for i in range(WIDE)]
        sides = [
            jnp.broadcast_to(work[:, first + i : first + i + 1], work.shape)
            for i in range(WIDE)
        ]
        change = None
        for i in range(WIDE):
            pivot = first + i
            unit_top = tops[i] / sides[i][pivot : pivot + 1, :]
            for m in range(i + 1, WIDE):
                factor = sides[i][first + m : first + m + 1, :]
                tops[m] = tops[m] - factor * unit_top
                inner = factor / sides[i][pivot : pivot + 1, :]
                sides[m] = sides[m] - sides[i] * inner
            term = sides[i] * unit_top
            change = term if change is None else change + term
        reduced = work - change
        kept = work
        for i in range(WIDE):
            kept = jnp.where(rows == first + i, tops[i], kept)
        work = jnp.where(rows >= first + WIDE, reduced, kept)
    pivots = jnp.sum(jnp.where(rows == lanes, work, 0.0), axis=1, keepdims=True)
    return (work * lax.rsqrt(pivots))[:, cols:]


def ritz_kernel(n_row, cells, *refs):
    grams, parts = refs[:n_row], refs[n_row:-3]
    own, out, stage = refs[-3:]
    cols = grams[0].shape[0]
    per = out.shape[1] // BLK
    inverse = eliminate(ordered_sum(stage, grams, places()[0]) * (1.0 / cells))
    for j in range(per):
        summed = tree_sum([m[j * cols : (j + 1) * cols].astype(F32) for m in parts])
        projected = summed * own[j : j + 1, :]
        out[:, j * BLK : (j + 1) * BLK] = jnp.dot(
            inverse, projected, precision=lax.Precision.HIGHEST, preferred_element_type=F32
        )


def swap(x, axis, k):
    return lax.ppermute(x, axis, [(i, i ^ k) for i in range(lax.axis_size(axis))])


def shift(x, axis, k):
    n = lax.axis_size(axis)
    return lax.ppermute(x, axis, [(i, (i + k) % n) for i in range(n)])


def shifts(x, axis):
    return [x] + [shift(x, axis, k) for k in range(1, lax.axis_size(axis))]


def chip_shift(x, k):
    n = lax.axis_size("col") // 2
    return lax.ppermute(
        x,
        "col",
        [(2 * q + p, 2 * ((q + k) % n) + p) for q in range(n) for p in range(2)],
    )


def chip_shifts(x):
    return [x] + [chip_shift(x, k) for k in range(1, lax.axis_size("col") // 2)]


def sibling(x):
    return swap(x, "col", 1)


def vec(*arrays):
    return [("vmem", a) for a in arrays]


def strip_body(profiles, cell_width, basis, block_lists, block_counts, landmarks):
    n_row, n_col = lax.axis_size("row"), lax.axis_size("col")
    n_chip = n_col // 2
    pcs, share = profiles.shape
    cols = basis.shape[0]
    per = share // BLK
    row_blocks, col_blocks = n_col * per, n_row * per
    all_rows = n_row * row_blocks
    slots = block_lists.shape[-1]
    n_land = landmarks.shape[0] // n_row

    def shape(*dims, dtype=F32):
        return jax.ShapeDtypeStruct(dims, dtype)

    (packed,) = call(
        pack_kernel,
        [shape(PACK, share, dtype=BF16)],
        [("hbm", a) for a in (profiles, cell_width, block_lists)] + [("smem", block_counts)],
        [
            pltpu.VMEM((PACK, share), F32),
            pltpu.VMEM(profiles.shape, BF16),
            pltpu.VMEM(cell_width.shape, BF16),
            pltpu.VMEM(block_lists.shape, jnp.int32),
            pltpu.SemaphoreType.DMA((3,)),
        ],
    )
    near = [chip_shift(packed, k) for k in range(1, n_chip)]
    near_in = [sibling(pack) for pack in near]
    rest, table = call(
        functools.partial(stack_kernel, pcs, n_row),
        [shape(n_row - 1, PACK, share, dtype=BF16), shape(n_row, 8, BLK, dtype=jnp.int32)],
        vec(*shifts(packed, "row")) + [("near", pack) for pack in near_in],
    )
    table = ("smem", table.reshape(n_row * 8, BLK))
    marks = ("smem", landmarks)
    far = [chip_shift(rest, k) for k in range(1, n_chip)]
    own, col_prof, col_inv, sums = call(
        functools.partial(own_kernel, pcs),
        [
            pltpu.VMEM((slots, BLK, BLK), BF16),
            pltpu.VMEM((col_blocks, BLK, FEAT), BF16),
            pltpu.VMEM((col_blocks, BLK, BLK), F32),
            shape(col_blocks, BLK),
        ],
        [table] + vec(packed, rest, sibling(packed), sibling(rest)),
        [
            pltpu.VMEM((row_blocks, FEAT, BLK), BF16),
            pltpu.VMEM((row_blocks, 8, BLK), F32),
            pltpu.VMEM((col_blocks + 1, 8, BLK), F32),
        ],
    )
    basis, sums = lax.optimization_barrier((basis, sums))
    bases = shifts(basis, "row")
    far, sums = lax.optimization_barrier((far, sums))
    far[-1], bases = lax.optimization_barrier((far[-1], bases))
    stacks = []
    for pack, other, group in zip(near, near_in, far):
        stacks += [pack, group, other, sibling(group)]
    far_slots = (n_row - 1) * slots
    others, part = call(
        functools.partial(strip_kernel, pcs, n_row),
        [pltpu.VMEM((far_slots, BLK, BLK), BF16), shape(all_rows, BLK)],
        [table, ("keep", own), ("keep", col_prof), ("keep", col_inv)]
        + vec(sums, *stacks),
        [
            pltpu.VMEM((all_rows - row_blocks, FEAT, BLK), BF16),
            pltpu.VMEM((all_rows - row_blocks, 8, BLK), F32),
            pltpu.VMEM((col_blocks, BLK, BLK), F32),
            pltpu.VMEM((all_rows + 1, 8, BLK), F32),
            pltpu.VMEM((col_blocks + 1, 8, BLK), F32),
        ],
    )
    tiles = [("keep", own), ("keep", others)]

    def chip_parts(part):
        return chip_shifts((part + sibling(part)).astype(BF16))

    for _ in range(SWEEPS - 2):
        (part,) = call(
            functools.partial(sweep_kernel, n_row, n_chip),
            [shape(all_rows, BLK)],
            [table] + tiles + vec(*chip_parts(part)),
            [
                pltpu.VMEM((n_chip, all_rows, BLK), F32),
                pltpu.VMEM((2, all_rows, PIECES, 2 * BLK), BF16),
                pltpu.VMEM((col_blocks, BLK, BLK), F32),
                pltpu.VMEM((all_rows + 1, 8, BLK), F32),
                pltpu.VMEM((col_blocks + 1, 8, BLK), F32),
            ],
        )
    both_rows = 3 * row_blocks + n_land * cols
    keep, away, both, col_scaling = call(
        functools.partial(last_kernel, n_row, n_chip, n_land),
        [
            shape(n_chip, per, cols, BLK),
            shape(n_chip, per, cols, BLK, dtype=BF16),
            shape(both_rows, BLK, dtype=BF16),
            shape(col_blocks, BLK),
        ],
        [table, marks] + tiles + vec(*chip_parts(part), *bases),
        [
            pltpu.VMEM((n_chip, all_rows, BLK), F32),
            pltpu.VMEM((2, all_rows, PIECES, 2 * BLK), BF16),
            pltpu.VMEM((col_blocks + 1, 8, BLK), F32),
            pltpu.VMEM((col_blocks, cols + PIECES, BLK), BF16),
            pltpu.VMEM((row_blocks + 1, cols + 8, BLK), F32),
        ],
    )
    pairs = call(
        pair_kernel,
        [shape(both_rows, BLK, dtype=BF16)]
        + [shape(per * cols, BLK, dtype=BF16)] * n_chip,
        vec(keep, sibling(away), both, sibling(both)),
    )
    sums = [pairs[0]] + [chip_shift(pairs[0], k) for k in range(1, n_chip)]
    shares = [pairs[1]] + [chip_shift(pairs[1 + k], k) for k in range(1, n_chip)]
    gram, row_scaling, own = call(
        functools.partial(gram_kernel, n_land, cols, per),
        [shape(cols, cols), shape(row_blocks, BLK), shape(per, BLK)],
        [marks] + vec(*sums),
        [
            pltpu.VMEM((row_blocks, BLK), F32),
            pltpu.VMEM((n_chip, row_blocks, BLK), F32),
            pltpu.VMEM((n_chip, n_land * cols, BLK), BF16),
        ],
    )
    (ritz,) = call(
        functools.partial(ritz_kernel, n_row, landmarks.shape[0] * BLK),
        [shape(cols, share)],
        vec(*shifts(gram, "row"), *shares, own),
        [pltpu.VMEM((n_row, cols, cols), F32)],
    )
    return row_scaling.reshape(-1), col_scaling.reshape(-1), ritz


def tile_pack_kernel(prof_ref, width_ref, out_ref, work):
    pcs = prof_ref.shape[0]
    prof = prof_ref[...].astype(F32)
    norm = jnp.sum(prof * prof, axis=0, keepdims=True)
    high, mid, low = split3(norm)
    work[...] = jnp.zeros_like(work)
    work[0:pcs, :] = prof
    work[pcs : pcs + 1, :] = high
    work[pcs + 1 : pcs + 2, :] = mid
    work[pcs + 2 : pcs + 3, :] = low
    work[pcs + 3 : pcs + 6, :] = jnp.ones((3, prof.shape[1]), F32)
    work[pcs + 6 : pcs + 7, :] = width_ref[...].astype(F32)
    out_ref[...] = work[...].astype(BF16)


def tile_square(tile, slots):
    a, b, c, d = [tile[s] for s in slots]
    return jnp.concatenate(
        [jnp.concatenate([a, b], axis=1), jnp.concatenate([c, d], axis=1)], axis=0
    )


def tile_add_rows(acc, lists, target, slots, sums, total, spare, firsts):
    for i, (s, (row, lane)) in enumerate(zip(slots, firsts)):
        place = jnp.where(s < total, lists[0, 0, target, s], spare)
        acc[place] += sums[row : row + 8, lane : lane + BLK]


def tile_row_sums(lists, tile, left, acc, total, spare):
    def step(*slots):
        low = [left[0, lists[0, 0, 1, s]] for s in slots[:2]]
        high = [left[1, lists[0, 0, 1, s]] for s in slots[2:]]
        sums = jnp.dot(
            jnp.concatenate(low + high, axis=0),
            tile_square(tile, slots),
            preferred_element_type=F32,
        )
        firsts = [(0, 0), (PIECES, BLK), (2 * PIECES, 0), (3 * PIECES, BLK)]
        tile_add_rows(acc, lists, 0, slots, sums, total, spare, firsts)

    slot_loop(step, total, 4, 4 * TILE_GROUP)


def tile_col_sums(lists, tile, left, acc, total, spare):
    def step(*slots):
        pieces = [left[i % 2, lists[0, 0, 0, s]] for i, s in enumerate(slots)]
        sums = lax.dot_general(
            jnp.concatenate(pieces, axis=0),
            tile_square(tile, slots),
            (((1,), (1,)), ((), ())),
            preferred_element_type=F32,
        )
        firsts = [(0, 0), (PIECES, 0), (2 * PIECES, BLK), (3 * PIECES, BLK)]
        tile_add_rows(acc, lists, 1, slots, sums, total, spare, firsts)

    slot_loop(step, total, 4, 4 * TILE_GROUP)


def tile_build_kernel(pcs, n_row, n_col, *refs):
    lists, counts = refs[:2]
    col_in = refs[2 : 2 + n_row]
    row_in = refs[2 + n_row : 2 + n_row + n_col]
    tile, part, row_prof, row_inv, col_prof, col_inv, acc, left = refs[2 + n_row + n_col :]
    per = row_in[0].shape[1] // BLK
    col_blocks, row_blocks = n_row * per, n_col * per
    total = counts[0, 0]
    me_row, me_col = places()
    for k, ref in enumerate(row_in):
        core = lax.rem(me_col + k, 2)
        piece = shifted(me_col // 2, k // 2, n_col // 2) * 2 + core
        for j in range(per):
            block = ref[:, j * BLK : (j + 1) * BLK]
            row_prof[piece * per + j] = block
            width = block.astype(F32)[pcs + 6 : pcs + 7, :]
            row_inv[piece * per + j] = jnp.broadcast_to(1.0 / width, (8, BLK))
    rows = lax.broadcasted_iota(jnp.int32, (FEAT, BLK), 0)
    for k, ref in enumerate(col_in):
        piece = shifted(me_row, k, n_row)
        for j in range(per):
            block = ref[0:FEAT, j * BLK : (j + 1) * BLK].astype(F32)
            turned = jnp.where(rows < pcs, -2.0 * block, 0.0)
            turned = jnp.where((rows >= pcs) & (rows < pcs + 3), 1.0, turned)
            turned = jnp.where(
                (rows >= pcs + 3) & (rows < pcs + 6), pltpu.roll(block, 3, 0), turned
            )
            turned = jnp.where(rows == pcs + 7, pltpu.roll(block, 1, 0), turned)
            turned = turned.T
            col_prof[piece * per + j] = turned.astype(BF16)
            col_inv[piece * per + j] = jnp.broadcast_to(
                -LOG2E / turned[:, pcs + 7 : pcs + 8], (BLK, BLK)
            )

    def step(s):
        rb, cb = lists[0, 0, 0, s], lists[0, 0, 1, s]
        distance = jnp.dot(col_prof[cb], row_prof[rb], preferred_element_type=F32)
        block = jnp.exp2(distance * col_inv[cb] * row_inv[rb][0:1, :])
        tile[s] = block.astype(BF16)

    slot_loop(step, total, 1, TILE_GROUP)
    ones = (lax.broadcasted_iota(jnp.int32, (PIECES, BLK), 0) == 0).astype(F32).astype(BF16)
    empty = jnp.zeros_like(ones)
    for b in range(row_blocks):
        left[0, b] = jnp.concatenate([ones, empty], axis=1)
        left[1, b] = jnp.concatenate([empty, ones], axis=1)
    acc[...] = jnp.zeros_like(acc)
    tile_col_sums(lists, tile, left, acc, total, col_blocks)
    part[...] = jnp.sum(acc[0:col_blocks], axis=1)


def tile_pass_kernel(over_rows, n_parts, *refs):
    lists, counts, tile = refs[:3]
    parts = refs[3 : 3 + n_parts]
    out, stage, left, acc = refs[-4:]
    total = counts[0, 0]
    blocks = out.shape[0]
    me_row, me_col = places()
    scaling = SCALE / ordered_sum(stage, parts, me_row if over_rows else me_col // 2)
    fill_pieces(left, scaling)
    acc[...] = jnp.zeros_like(acc)
    (tile_row_sums if over_rows else tile_col_sums)(lists, tile, left, acc, total, blocks)
    out[...] = jnp.sum(acc[0:blocks], axis=1)


def tile_last_kernel(n_row, n_col, n_land, *refs):
    lists, counts, marks, tile = refs[:4]
    parts, bases = refs[4 : 4 + n_row], refs[4 + n_row : 4 + 2 * n_row]
    keep, away, both, scaling_out, stage, scaled, acc = refs[4 + 2 * n_row :]
    cols = bases[0].shape[0]
    per = bases[0].shape[1] // BLK
    blocks = n_col * per
    total = counts[0, 0]
    me_row, me_col = places()
    scaling = SCALE / ordered_sum(stage, parts, me_row)
    scaling_out[...] = scaling
    for k in range(n_row):
        piece = shifted(me_row, k, n_row)
        for j in range(per):
            block = bases[k][:, j * BLK : (j + 1) * BLK].astype(F32)
            b = piece * per + j
            scaled[b, 0:cols] = (block * scaling_out[pl.ds(b, 1), :]).astype(BF16)
    high, mid, low = split3(scaling)
    shape = (PIECES, BLK)
    rows = lax.broadcasted_iota(jnp.int32, shape, 0)
    for b in range(scaling.shape[0]):
        value = jnp.where(
            rows == 0,
            jnp.broadcast_to(high[b : b + 1], shape),
            jnp.where(
                rows == 1,
                jnp.broadcast_to(mid[b : b + 1], shape),
                jnp.where(rows == 2, jnp.broadcast_to(low[b : b + 1], shape), 0.0),
            ),
        )
        scaled[b, cols : cols + PIECES] = value.astype(BF16)
    acc[...] = jnp.zeros_like(acc)

    def step(s):
        target = jnp.where(s < total, lists[0, 0, 0, s], blocks)
        sums = jnp.dot(scaled[lists[0, 0, 1, s]], tile[s], preferred_element_type=F32)
        acc[target] += sums[0 : cols + 8]

    slot_loop(step, total, 1, TILE_GROUP)
    core = lax.rem(me_col, 2)
    for q in range(n_col // 2):
        own = (2 * q + core) * per
        other = (2 * q + 1 - core) * per
        for j in range(per):
            keep[q, j] = acc[own + j, 0:cols]
            away[q, j] = acc[other + j, 0:cols].astype(BF16)
    row_part = jnp.sum(acc[0:blocks, cols : cols + 8], axis=1)
    for i, value in enumerate(pieces_of(row_part)):
        both[i * blocks : (i + 1) * blocks] = value
    for i in range(n_land):
        first = 3 * blocks + i * cols
        both[first : first + cols] = acc[marks[me_row * n_land + i] - me_row * blocks, 0:cols].astype(BF16)


def tile_body(profiles, cell_width, basis, block_lists, block_counts, landmarks):
    n_row, n_col = lax.axis_size("row"), lax.axis_size("col")
    n_chip = n_col // 2
    pcs, share = profiles.shape
    cols = basis.shape[0]
    per = share // BLK
    row_blocks, col_blocks = n_col * per, n_row * per
    slots = block_lists.shape[-1]
    n_land = landmarks.shape[0] // n_row

    def shape(*dims, dtype=F32):
        return jax.ShapeDtypeStruct(dims, dtype)

    (packed,) = call(
        tile_pack_kernel,
        [shape(FEAT, share, dtype=BF16)],
        vec(profiles, cell_width.reshape(1, share)),
        [pltpu.VMEM((FEAT, share), F32)],
    )
    spread = lax.ppermute(
        packed,
        ("row", "col"),
        [((q % n_row) * n_col + q // n_row, q) for q in range(n_row * n_col)],
    )
    row_packs = []
    for pack in chip_shifts(spread):
        row_packs += [pack, sibling(pack)]
    col_packs = shifts(packed, "row")
    bases = shifts(basis, "row")
    lists = [("smem", block_lists), ("smem", block_counts)]
    marks = [("smem", landmarks)]
    tile, part = call(
        functools.partial(tile_build_kernel, pcs, n_row, n_col),
        [pltpu.VMEM((slots, BLK, BLK), BF16), shape(col_blocks, BLK)],
        lists + vec(*col_packs, *row_packs),
        [
            pltpu.VMEM((row_blocks, FEAT, BLK), BF16),
            pltpu.VMEM((row_blocks, 8, BLK), F32),
            pltpu.VMEM((col_blocks, BLK, FEAT), BF16),
            pltpu.VMEM((col_blocks, BLK, BLK), F32),
            pltpu.VMEM((col_blocks + 1, 8, BLK), F32),
            pltpu.VMEM((2, row_blocks, PIECES, 2 * BLK), BF16),
        ],
    )
    for number in range(SWEEPS - 1):
        early = [("near", b) for b in bases[1:]] if number == 0 else []
        (part,) = call(
            functools.partial(tile_pass_kernel, True, n_row),
            [shape(row_blocks, BLK)],
            lists + [("keep", tile)] + vec(*shifts(part, "row")) + early,
            [
                pltpu.VMEM((n_row, col_blocks, BLK), F32),
                pltpu.VMEM((2, col_blocks, PIECES, 2 * BLK), BF16),
                pltpu.VMEM((row_blocks + 1, 8, BLK), F32),
            ],
        )
        (part,) = call(
            functools.partial(tile_pass_kernel, False, n_chip),
            [shape(col_blocks, BLK)],
            lists + [("keep", tile)] + vec(*chip_shifts(part + sibling(part))),
            [
                pltpu.VMEM((n_chip, row_blocks, BLK), F32),
                pltpu.VMEM((2, row_blocks, PIECES, 2 * BLK), BF16),
                pltpu.VMEM((col_blocks + 1, 8, BLK), F32),
            ],
        )
    both_rows = 3 * row_blocks + n_land * cols
    keep, away, both, col_scaling = call(
        functools.partial(tile_last_kernel, n_row, n_col, n_land),
        [
            shape(n_chip, per, cols, BLK),
            shape(n_chip, per, cols, BLK, dtype=BF16),
            shape(both_rows, BLK, dtype=BF16),
            shape(col_blocks, BLK),
        ],
        lists + marks + [("keep", tile)] + vec(*shifts(part, "row"), *bases),
        [
            pltpu.VMEM((n_row, col_blocks, BLK), F32),
            pltpu.VMEM((col_blocks, cols + PIECES, BLK), BF16),
            pltpu.VMEM((row_blocks + 1, cols + 8, BLK), F32),
        ],
    )
    pairs = call(
        pair_kernel,
        [shape(both_rows, BLK, dtype=BF16)]
        + [shape(per * cols, BLK, dtype=BF16)] * n_chip,
        vec(keep, sibling(away), both, sibling(both)),
    )
    sums = [pairs[0]] + [chip_shift(pairs[0], k) for k in range(1, n_chip)]
    shares = [pairs[1]] + [chip_shift(pairs[1 + k], k) for k in range(1, n_chip)]
    gram, row_scaling, own = call(
        functools.partial(gram_kernel, n_land, cols, per),
        [shape(cols, cols), shape(row_blocks, BLK), shape(per, BLK)],
        marks + vec(*sums),
        [
            pltpu.VMEM((row_blocks, BLK), F32),
            pltpu.VMEM((n_chip, row_blocks, BLK), F32),
            pltpu.VMEM((n_chip, n_land * cols, BLK), BF16),
        ],
    )
    (ritz,) = call(
        functools.partial(ritz_kernel, n_row, landmarks.shape[0] * BLK),
        [shape(cols, share)],
        vec(*shifts(gram, "row"), *shares, own),
        [pltpu.VMEM((n_row, cols, cols), F32)],
    )
    return row_scaling.reshape(-1), col_scaling.reshape(-1), ritz


def solution(mesh):
    placed = (
        P(None, ("col", "row")),
        P(("col", "row")),
        P(None, ("col", "row")),
        P("row", "col", None, None),
        P("row", "col"),
        P(),
    )
    return jax.shard_map(
        strip_body if mesh.shape["row"] <= STRIP_TILES else tile_body,
        mesh=mesh,
        in_specs=placed,
        out_specs=(P("row"), P("col"), P(None, ("row", "col"))),
        check_vma=False,
    )
```

```python
import functools

import jax
import jax.numpy as jnp
from jax import lax
from jax.experimental import pallas as pl
from jax.experimental.pallas import tpu as pltpu
from jax.sharding import PartitionSpec as P

BLK = 128
SWEEPS = 3
GROUP = 32
BUILD_GROUP = 32
TILE_GROUP = 16
ROWS, COLUMNS, COUNT = 0, 1, 2
FEAT = 64
PACK = 56
PIECES = 16
SCALE = 512.0
LOG2E = 1.4426950408889634
F32 = jnp.float32
BF16 = jnp.bfloat16
MIB = 1 << 20
STRIP_TILES = 8

VMEM_SPEC = pl.BlockSpec(memory_space=pltpu.VMEM)
SMEM_SPEC = pl.BlockSpec(memory_space=pltpu.SMEM)


def split3(x):
    high = x.astype(BF16).astype(F32)
    mid = (x - high).astype(BF16).astype(F32)
    low = (x - high - mid).astype(BF16).astype(F32)
    return high, mid, low


def tree_sum(values):
    values = list(values)
    while len(values) > 1:
        values = [a + b for a, b in zip(values[::2], values[1::2])]
    return values[0]


def call(kernel, outs, ins, scratch=(), limit=24, flops=1 << 24):
    args, specs = [], []
    for kind, array in ins:
        if kind == "smem":
            specs.append(SMEM_SPEC)
        elif kind == "near":
            specs.append(pl.BlockSpec(memory_space=pl.ANY))
        elif kind == "hbm":
            specs.append(pl.BlockSpec(memory_space=pltpu.HBM))
            array = pltpu.with_memory_space_constraint(array, pltpu.HBM)
        else:
            specs.append(VMEM_SPEC)
            if kind == "keep":
                array = pltpu.with_memory_space_constraint(array, pltpu.VMEM)
        args.append(array)
    return pl.pallas_call(
        kernel,
        out_shape=tuple(outs),
        in_specs=specs,
        out_specs=tuple(VMEM_SPEC for _ in outs),
        scratch_shapes=list(scratch),
        compiler_params=pltpu.CompilerParams(vmem_limit_bytes=limit * MIB),
        cost_estimate=pl.CostEstimate(flops=flops, bytes_accessed=1 << 20, transcendentals=0),
    )(*args)


def pack_kernel(prof_hbm, width_hbm, lists_hbm, counts, out_ref, *scratch):
    work, prof_ref, width_ref, lists_ref, sems = scratch
    pairs = [
        (prof_hbm, prof_ref),
        (width_hbm, width_ref),
        (lists_hbm, lists_ref),
    ]
    copies = [pltpu.make_async_copy(a, b, sems.at[i]) for i, (a, b) in enumerate(pairs)]
    for copy in copies:
        copy.start()
    for copy in copies:
        copy.wait()
    pcs = prof_ref.shape[0]
    prof = prof_ref[...].astype(F32)
    norm = jnp.sum(prof * prof, axis=0, keepdims=True)
    high, mid, low = split3(norm)
    work[...] = jnp.zeros_like(work)
    work[0:pcs, :] = prof
    work[pcs : pcs + 1, :] = high
    work[pcs + 1 : pcs + 2, :] = mid
    work[pcs + 2 : pcs + 3, :] = low
    work[pcs + 3 : pcs + 4, :] = width_ref[...].astype(F32).reshape(1, -1)
    lists = lists_ref[0, 0].astype(F32)
    slots = slice(pcs + 4, pcs + 5)
    work[slots, 0:BLK] = lists[0:1]
    work[slots, BLK : 2 * BLK] = lists[1:2]
    count = jnp.full((1, BLK), counts[0, 0], jnp.int32)
    work[slots, 2 * BLK : 3 * BLK] = count.astype(F32)
    out_ref[...] = work[...].astype(BF16)


def places():
    return lax.axis_index("row"), lax.axis_index("col")


def stack_kernel(pcs, n, *refs):
    packs, (rest, table) = refs[:n], refs[-2:]
    me_row, _ = places()
    for k, pack in enumerate(packs):
        if k:
            rest[k - 1] = pack[...]
        slots = pack[:, 0 : 3 * BLK].astype(F32)[pcs + 4 : pcs + 5]
        for row in (ROWS, COLUMNS, COUNT):
            values = slots[:, row * BLK : (row + 1) * BLK].astype(jnp.int32)
            table[shifted(me_row, k, n), row : row + 1] = values


def slot_loop(step, count, size, group):
    def advance(number, carry):
        for i in range(0, group, size):
            step(*[number * group + i + j for j in range(size)])
        return carry

    lax.fori_loop(0, (count + group - 1) // group, advance, 0)


class Tile:
    def __init__(self, table, n_row, k, own, others):
        _, me_col = places()
        self.group = shifted(me_col // 2, k, n_row)
        self.table, self.k = table, k
        slots = own.shape[0]
        self.blocks, self.base = (own, 0) if k == 0 else (others, (k - 1) * slots)
        self.total = table[self.group * 8 + COUNT, 0]

    def row(self, s):
        return self.table[self.group * 8 + ROWS, s]

    def column(self, s):
        return self.table[self.group * 8 + COLUMNS, s]

    def block(self, s):
        return self.blocks[self.base + s]


def shifted(me, k, n):
    return lax.rem(me + (n - k), n)


def ordered_sum(stage, refs, me):
    n = len(refs)
    for k, ref in enumerate(refs):
        stage[shifted(me, k, n)] = ref[...]
    return tree_sum([stage[i] for i in range(n)])


def square(tile, slots):
    a, b, c, d = [tile.block(s) for s in slots]
    return jnp.concatenate(
        [jnp.concatenate([a, b], axis=1), jnp.concatenate([c, d], axis=1)], axis=0
    )


def add_rows(acc, sums, firsts, targets):
    for (row, lane), target in zip(firsts, targets):
        acc[target] += sums[row : row + 8, lane : lane + BLK]


def row_sums(tile, wide, acc, row_blocks, spare):
    first = tile.group * row_blocks

    def step(s):
        product = tile.block(s).astype(F32) * wide[tile.column(s)]
        sums = jnp.sum(product.reshape(BLK // 8, 8, BLK), axis=0)
        acc[jnp.where(s < tile.total, first + tile.row(s), spare)] += sums

    slot_loop(step, tile.total, 1, GROUP)


def spread_lanes(wide, scaling):
    turned = scaling.T
    for b in range(scaling.shape[0]):
        wide[b] = jnp.broadcast_to(turned[:, b : b + 1], (BLK, BLK))


def col_sums(tile, left, acc, row_blocks, spare):
    first = tile.group * row_blocks

    def step(*slots):
        if left is None:
            rows = lax.broadcasted_iota(jnp.int32, (4 * PIECES, 2 * BLK), 0)
            lanes = lax.broadcasted_iota(jnp.int32, (4 * PIECES, 2 * BLK), 1)
            block = rows // PIECES
            pieces = (rows % PIECES == 0) & (block % 2 == lanes // BLK)
            pieces = pieces.astype(F32).astype(BF16)
        else:
            pieces = [left[i % 2, first + tile.row(s)] for i, s in enumerate(slots)]
            pieces = jnp.concatenate(pieces, axis=0)
        sums = lax.dot_general(
            pieces,
            square(tile, slots),
            (((1,), (1,)), ((), ())),
            preferred_element_type=F32,
        )
        firsts = [(0, 0), (PIECES, 0), (2 * PIECES, BLK), (3 * PIECES, BLK)]
        targets = [jnp.where(s < tile.total, tile.column(s), spare) for s in slots]
        add_rows(acc, sums, firsts, targets)

    slot_loop(step, tile.total, 4, 2 * GROUP if tile.k == 0 else GROUP)


def fill_pieces(left, scaling):
    high, mid, low = split3(scaling)
    shape = (PIECES, BLK)
    rows = lax.broadcasted_iota(jnp.int32, shape, 0)
    empty = jnp.zeros(shape, F32).astype(BF16)
    for b in range(scaling.shape[0]):
        value = jnp.where(
            rows == 0,
            jnp.broadcast_to(high[b : b + 1], shape),
            jnp.where(
                rows == 1,
                jnp.broadcast_to(mid[b : b + 1], shape),
                jnp.where(rows == 2, jnp.broadcast_to(low[b : b + 1], shape), 0.0),
            ),
        ).astype(BF16)
        left[0, b] = jnp.concatenate([value, empty], axis=1)
        left[1, b] = jnp.concatenate([empty, value], axis=1)


def build(tile, offset, row_prof, row_inv, col_prof, col_inv):
    def step(s):
        row, column = offset + tile.row(s), tile.column(s)
        distance = jnp.dot(col_prof[column], row_prof[row], preferred_element_type=F32)
        block = jnp.exp2(distance * col_inv[column] * row_inv[row][0:1, :])
        tile.blocks[tile.base + s] = block.astype(BF16)

    slot_loop(step, tile.total, 1, BUILD_GROUP)


def piece_block(pieces, k, j):
    lanes = slice(j * BLK, (j + 1) * BLK)
    return pieces[0][:, lanes] if k == 0 else pieces[1][k - 1, :, lanes]


def fill_rows(pcs, sources, row_prof, row_inv, offset):
    me_row, me_col = places()
    n_row = sources[0][1].shape[0] + 1
    per = sources[0][0].shape[1] // BLK
    ones = lax.broadcasted_iota(jnp.int32, (FEAT - PACK, BLK), 0) < 3
    ones = ones.astype(F32)
    for i, pieces in enumerate(sources):
        core = lax.rem(me_col + i, 2)
        for k in range(n_row):
            piece = core * n_row + shifted(me_row, k, n_row)
            for j in range(per):
                block = piece_block(pieces, k, j).astype(F32)
                whole = jnp.concatenate([block, ones], axis=0)
                row_prof[offset + piece * per + j] = whole.astype(BF16)
                width = block[pcs + 3 : pcs + 4, :]
                row_inv[offset + piece * per + j] = jnp.broadcast_to(1.0 / width, (8, BLK))


def own_kernel(pcs, table, pack, rest, pack_in, rest_in, *refs):
    tile, col_prof, col_inv, sums, row_prof, row_inv, acc = refs[-7:]
    n_row = rest.shape[0] + 1
    per = pack.shape[1] // BLK
    me_row, _ = places()
    fill_rows(pcs, [(pack, rest), (pack_in, rest_in)], row_prof, row_inv, 0)
    rows = lax.broadcasted_iota(jnp.int32, (FEAT, BLK), 0)
    for k in range(n_row):
        piece = shifted(me_row, k, n_row)
        for j in range(per):
            block = piece_block((pack, rest), k, j).astype(F32)
            block = jnp.concatenate([block, jnp.zeros((FEAT - PACK, BLK), F32)], axis=0)
            turned = jnp.where(rows < pcs, -2.0 * block, 0.0)
            turned = jnp.where((rows >= pcs) & (rows < pcs + 3), 1.0, turned)
            turned = jnp.where(rows == PACK - 1, pltpu.roll(block, PACK - 4 - pcs, 0), turned)
            turned = jnp.where(
                (rows >= PACK) & (rows < PACK + 3), pltpu.roll(block, PACK - pcs, 0), turned
            )
            turned = turned.T
            col_prof[piece * per + j] = turned.astype(BF16)
            col_inv[piece * per + j] = jnp.broadcast_to(
                -LOG2E / turned[:, PACK - 1 : PACK], (BLK, BLK)
            )
    own = Tile(table, n_row, 0, tile, None)
    build(own, 0, row_prof, row_inv, col_prof, col_inv)
    sums[...] = column_totals([own], None, acc, row_prof.shape[0])


def column_totals(tiles, left, acc, row_blocks):
    col_blocks = acc.shape[0] - 1
    acc[...] = jnp.zeros_like(acc)
    for tile in tiles:
        col_sums(tile, left, acc, row_blocks, col_blocks)
    return jnp.sum(acc[0:col_blocks], axis=1)


def row_part(tiles, wide, acc, row_blocks, out):
    blocks = acc.shape[0] - 1
    acc[...] = jnp.zeros_like(acc)
    for tile in tiles:
        row_sums(tile, wide, acc, row_blocks, blocks)
    out[...] = jnp.sum(acc[0:blocks], axis=1)


def strip_kernel(pcs, n_row, *refs):
    table, own, col_prof, col_inv, own_sums = refs[:5]
    sources = [refs[i : i + 2] for i in range(5, 5 + 4 * (n_row - 1), 2)]
    others, out, row_prof, row_inv, wide, row_acc, col_acc = refs[-7:]
    row_blocks = row_prof.shape[0] // (n_row - 1)
    tiles = [Tile(table, n_row, k, own, others) for k in range(n_row)]
    for k in range(1, n_row):
        first = (k - 1) * row_blocks
        fill_rows(pcs, sources[2 * k - 2 : 2 * k], row_prof, row_inv, first)
    for k in range(1, n_row):
        first = (k - 1) * row_blocks
        build(tiles[k], first, row_prof, row_inv, col_prof, col_inv)
    totals = column_totals(tiles[1:], None, col_acc, row_blocks) + own_sums[...]
    spread_lanes(wide, SCALE / totals)
    row_part(tiles, wide, row_acc, row_blocks, out)


def row_scalings(stage, parts):
    for k, part in enumerate(parts):
        stage[shifted(places()[1] // 2, k, len(parts))] = part[...].astype(F32)
    return SCALE / tree_sum([stage[i] for i in range(len(parts))])


def sweep_kernel(n_row, n_chip, *refs):
    table, own, others = refs[:3]
    parts = refs[3 : 3 + n_chip]
    out, stage, row_left, wide, row_acc, col_acc = refs[-6:]
    row_blocks = out.shape[0] // n_row
    tiles = [Tile(table, n_row, k, own, others) for k in range(n_row)]
    fill_pieces(row_left, row_scalings(stage, parts))
    totals = column_totals(tiles, row_left, col_acc, row_blocks)
    spread_lanes(wide, SCALE / totals)
    row_part(tiles, wide, row_acc, row_blocks, out)


def pieces_of(value):
    return [v.astype(BF16) for v in split3(value)]


def last_kernel(n_row, n_chip, n_land, *refs):
    table, marks, own, others = refs[:4]
    parts, bases = refs[4 : 4 + n_chip], refs[4 + n_chip : 4 + n_chip + n_row]
    keep, away, both, scaling_out, stage, row_left, col_acc, scaled, acc = refs[-9:]
    cols = bases[0].shape[0]
    per = bases[0].shape[1] // BLK
    blocks = 2 * n_chip * per
    me_row, me_col = places()
    tiles = [Tile(table, n_row, k, own, others) for k in range(n_row)]
    fill_pieces(row_left, row_scalings(stage, parts))
    scaling = SCALE / column_totals(tiles, row_left, col_acc, blocks)
    scaling_out[...] = scaling
    for k in range(n_row):
        piece = lax.bitwise_xor(me_row, k)
        for j in range(per):
            block = bases[k][:, j * BLK : (j + 1) * BLK].astype(F32)
            b = piece * per + j
            scaled[b, 0:cols] = (block * scaling_out[pl.ds(b, 1), :]).astype(BF16)
    high, mid, low = split3(scaling)
    shape = (PIECES, BLK)
    rows = lax.broadcasted_iota(jnp.int32, shape, 0)
    for b in range(scaling.shape[0]):
        value = jnp.where(
            rows == 0,
            jnp.broadcast_to(high[b : b + 1], shape),
            jnp.where(
                rows == 1,
                jnp.broadcast_to(mid[b : b + 1], shape),
                jnp.where(rows == 2, jnp.broadcast_to(low[b : b + 1], shape), 0.0),
            ),
        )
        scaled[b, cols : cols + PIECES] = value.astype(BF16)
    acc[...] = jnp.zeros_like(acc)
    for k in range(n_row):
        tile = tiles[k]

        def step(s, tile=tile):
            target = jnp.where(s < tile.total, tile.row(s), blocks)
            sums = jnp.dot(scaled[tile.column(s)], tile.block(s), preferred_element_type=F32)
            acc[target] += sums[0 : cols + 8]

        slot_loop(step, jnp.where(tile.group == me_row, tile.total, 0), 1, BUILD_GROUP)
    core = lax.rem(me_col, 2)
    for q in range(n_chip):
        mine = (2 * q + core) * per
        other = (2 * q + 1 - core) * per
        for j in range(per):
            keep[q, j] = acc[mine + j, 0:cols]
            away[q, j] = acc[other + j, 0:cols].astype(BF16)
    part = jnp.sum(acc[0:blocks, cols : cols + 8], axis=1)
    for i, value in enumerate(pieces_of(part)):
        both[i * blocks : (i + 1) * blocks] = value
    for i in range(n_land):
        first = 3 * blocks + i * cols
        both[first : first + cols] = acc[marks[me_row * n_land + i] - me_row * blocks, 0:cols].astype(BF16)


def three(ref, blocks):
    value = ref[0 : 3 * blocks].astype(F32)
    return (value[2 * blocks :] + value[blocks : 2 * blocks]) + value[0:blocks]


def pair_kernel(keep, away, both, both_in, both_out, *outs):
    n_chip, per, cols = keep.shape[:3]
    blocks = 2 * n_chip * per
    chip = places()[1] // 2
    parts = pieces_of(three(both, blocks) + three(both_in, blocks))
    for i, value in enumerate(parts):
        both_out[i * blocks : (i + 1) * blocks] = value
    lands = both[3 * blocks :].astype(F32) + both_in[3 * blocks :].astype(F32)
    both_out[3 * blocks :] = lands.astype(BF16)
    for k, out in enumerate(outs):
        to = lax.rem(chip + k, n_chip)
        for j in range(per):
            value = keep[to, j] + away[to, j].astype(F32)
            out[j * cols : (j + 1) * cols] = value.astype(BF16)


def gram_kernel(n_land, cols, per, *refs):
    marks = refs[0]
    gram, scaling_out, own, inverse, stage, land_stage = refs[-6:]
    parts = refs[1:-6]
    n = len(parts)
    me_row, me_col = places()
    blocks = scaling_out.shape[0]
    for k, part in enumerate(parts):
        place = shifted(me_col // 2, k, n)
        stage[place] = three(part, blocks)
        land_stage[place] = part[3 * blocks :]
    inverse[...] = 1.0 / tree_sum([stage[i] for i in range(n)])
    scaling_out[...] = SCALE * inverse[...]
    for j in range(per):
        own[j : j + 1, :] = inverse[pl.ds(me_col * per + j, 1), :]
    total = None
    for i in range(n_land):
        summed = tree_sum(
            [land_stage[k, i * cols : (i + 1) * cols].astype(F32) for k in range(n)]
        )
        block = marks[me_row * n_land + i] - me_row * blocks
        projected = summed * inverse[pl.ds(block, 1), :]
        product = lax.dot_general(
            projected,
            projected,
            (((1,), (1,)), ((), ())),
            precision=lax.Precision.HIGHEST,
            preferred_element_type=F32,
        )
        total = product if total is None else total + product
    gram[...] = total


WIDE = 4


def eliminate(gram):
    cols = gram.shape[0]
    rows = lax.broadcasted_iota(jnp.int32, (cols, 2 * cols), 0)
    lanes = lax.broadcasted_iota(jnp.int32, (cols, 2 * cols), 1)
    unit = (rows[:, :cols] == lanes[:, :cols]).astype(F32)
    work = jnp.concatenate([gram, unit], axis=1)
    for first in range(0, cols, WIDE):
        tops = [work[first + i : first + i + 1, :] for i in range(WIDE)]
        sides = [
            jnp.broadcast_to(work[:, first + i : first + i + 1], work.shape)
            for i in range(WIDE)
        ]
        change = None
        for i in range(WIDE):
            pivot = first + i
            unit_top = tops[i] / sides[i][pivot : pivot + 1, :]
            for m in range(i + 1, WIDE):
                factor = sides[i][first + m : first + m + 1, :]
                tops[m] = tops[m] - factor * unit_top
                inner = factor / sides[i][pivot : pivot + 1, :]
                sides[m] = sides[m] - sides[i] * inner
            term = sides[i] * unit_top
            change = term if change is None else change + term
        reduced = work - change
        kept = work
        for i in range(WIDE):
            kept = jnp.where(rows == first + i, tops[i], kept)
        work = jnp.where(rows >= first + WIDE, reduced, kept)
    pivots = jnp.sum(jnp.where(rows == lanes, work, 0.0), axis=1, keepdims=True)
    return (work * lax.rsqrt(pivots))[:, cols:]


def ritz_kernel(n_row, cells, *refs):
    grams, parts = refs[:n_row], refs[n_row:-3]
    own, out, stage = refs[-3:]
    cols = grams[0].shape[0]
    per = out.shape[1] // BLK
    inverse = eliminate(ordered_sum(stage, grams, places()[0]) * (1.0 / cells))
    for j in range(per):
        summed = tree_sum([m[j * cols : (j + 1) * cols].astype(F32) for m in parts])
        projected = summed * own[j : j + 1, :]
        out[:, j * BLK : (j + 1) * BLK] = jnp.dot(
            inverse, projected, precision=lax.Precision.HIGHEST, preferred_element_type=F32
        )


def swap(x, axis, k):
    return lax.ppermute(x, axis, [(i, i ^ k) for i in range(lax.axis_size(axis))])


def shift(x, axis, k):
    n = lax.axis_size(axis)
    return lax.ppermute(x, axis, [(i, (i + k) % n) for i in range(n)])


def shifts(x, axis):
    return [x] + [shift(x, axis, k) for k in range(1, lax.axis_size(axis))]


def chip_shift(x, k):
    n = lax.axis_size("col") // 2
    return lax.ppermute(
        x,
        "col",
        [(2 * q + p, 2 * ((q + k) % n) + p) for q in range(n) for p in range(2)],
    )


def chip_shifts(x):
    return [x] + [chip_shift(x, k) for k in range(1, lax.axis_size("col") // 2)]


def sibling(x):
    return swap(x, "col", 1)


def vec(*arrays):
    return [("vmem", a) for a in arrays]


def strip_body(profiles, cell_width, basis, block_lists, block_counts, landmarks):
    n_row, n_col = lax.axis_size("row"), lax.axis_size("col")
    n_chip = n_col // 2
    pcs, share = profiles.shape
    cols = basis.shape[0]
    per = share // BLK
    row_blocks, col_blocks = n_col * per, n_row * per
    all_rows = n_row * row_blocks
    slots = block_lists.shape[-1]
    n_land = landmarks.shape[0] // n_row

    def shape(*dims, dtype=F32):
        return jax.ShapeDtypeStruct(dims, dtype)

    (packed,) = call(
        pack_kernel,
        [shape(PACK, share, dtype=BF16)],
        [("hbm", a) for a in (profiles, cell_width, block_lists)] + [("smem", block_counts)],
        [
            pltpu.VMEM((PACK, share), F32),
            pltpu.VMEM(profiles.shape, BF16),
            pltpu.VMEM(cell_width.shape, BF16),
            pltpu.VMEM(block_lists.shape, jnp.int32),
            pltpu.SemaphoreType.DMA((3,)),
        ],
    )
    near = [chip_shift(packed, k) for k in range(1, n_chip)]
    near_in = [sibling(pack) for pack in near]
    rest, table = call(
        functools.partial(stack_kernel, pcs, n_row),
        [shape(n_row - 1, PACK, share, dtype=BF16), shape(n_row, 8, BLK, dtype=jnp.int32)],
        vec(*shifts(packed, "row")) + [("near", pack) for pack in near_in],
    )
    table = ("smem", table.reshape(n_row * 8, BLK))
    marks = ("smem", landmarks)
    far = [chip_shift(rest, k) for k in range(1, n_chip)]
    own, col_prof, col_inv, sums = call(
        functools.partial(own_kernel, pcs),
        [
            pltpu.VMEM((slots, BLK, BLK), BF16),
            pltpu.VMEM((col_blocks, BLK, FEAT), BF16),
            pltpu.VMEM((col_blocks, BLK, BLK), F32),
            shape(col_blocks, BLK),
        ],
        [table] + vec(packed, rest, sibling(packed), sibling(rest)),
        [
            pltpu.VMEM((row_blocks, FEAT, BLK), BF16),
            pltpu.VMEM((row_blocks, 8, BLK), F32),
            pltpu.VMEM((col_blocks + 1, 8, BLK), F32),
        ],
    )
    far, sums = lax.optimization_barrier((far, sums))
    stacks = []
    for pack, other, group in zip(near, near_in, far):
        stacks += [pack, group, other, sibling(group)]
    far_slots = (n_row - 1) * slots
    others, part = call(
        functools.partial(strip_kernel, pcs, n_row),
        [pltpu.VMEM((far_slots, BLK, BLK), BF16), shape(all_rows, BLK)],
        [table, ("keep", own), ("keep", col_prof), ("keep", col_inv)]
        + vec(sums, *stacks),
        [
            pltpu.VMEM((all_rows - row_blocks, FEAT, BLK), BF16),
            pltpu.VMEM((all_rows - row_blocks, 8, BLK), F32),
            pltpu.VMEM((col_blocks, BLK, BLK), F32),
            pltpu.VMEM((all_rows + 1, 8, BLK), F32),
            pltpu.VMEM((col_blocks + 1, 8, BLK), F32),
        ],
    )
    tiles = [("keep", own), ("keep", others)]

    def chip_parts(part):
        return chip_shifts((part + sibling(part)).astype(BF16))

    bases = [basis]
    for _ in range(SWEEPS - 2):
        part, bases[0] = lax.optimization_barrier((part, bases[0]))
        bases = bases[:1] + [swap(bases[0], "row", 1)]
        (part,) = call(
            functools.partial(sweep_kernel, n_row, n_chip),
            [shape(all_rows, BLK)],
            [table] + tiles + vec(*chip_parts(part)) + [("near", bases[1])],
            [
                pltpu.VMEM((n_chip, all_rows, BLK), F32),
                pltpu.VMEM((2, all_rows, PIECES, 2 * BLK), BF16),
                pltpu.VMEM((col_blocks, BLK, BLK), F32),
                pltpu.VMEM((all_rows + 1, 8, BLK), F32),
                pltpu.VMEM((col_blocks + 1, 8, BLK), F32),
            ],
        )
    both_rows = 3 * row_blocks + n_land * cols
    part, bases = lax.optimization_barrier((part, bases))
    while len(bases) < n_row:
        bases = bases + [swap(base, "row", len(bases)) for base in bases]
    keep, away, both, col_scaling = call(
        functools.partial(last_kernel, n_row, n_chip, n_land),
        [
            shape(n_chip, per, cols, BLK),
            shape(n_chip, per, cols, BLK, dtype=BF16),
            shape(both_rows, BLK, dtype=BF16),
            shape(col_blocks, BLK),
        ],
        [table, marks] + tiles + vec(*chip_parts(part), *bases),
        [
            pltpu.VMEM((n_chip, all_rows, BLK), F32),
            pltpu.VMEM((2, all_rows, PIECES, 2 * BLK), BF16),
            pltpu.VMEM((col_blocks + 1, 8, BLK), F32),
            pltpu.VMEM((col_blocks, cols + PIECES, BLK), BF16),
            pltpu.VMEM((row_blocks + 1, cols + 8, BLK), F32),
        ],
    )
    pairs = call(
        pair_kernel,
        [shape(both_rows, BLK, dtype=BF16)]
        + [shape(per * cols, BLK, dtype=BF16)] * n_chip,
        vec(keep, sibling(away), both, sibling(both)),
    )
    sums = [pairs[0]] + [chip_shift(pairs[0], k) for k in range(1, n_chip)]
    shares = [pairs[1]] + [chip_shift(pairs[1 + k], k) for k in range(1, n_chip)]
    gram, row_scaling, own = call(
        functools.partial(gram_kernel, n_land, cols, per),
        [shape(cols, cols), shape(row_blocks, BLK), shape(per, BLK)],
        [marks] + vec(*sums),
        [
            pltpu.VMEM((row_blocks, BLK), F32),
            pltpu.VMEM((n_chip, row_blocks, BLK), F32),
            pltpu.VMEM((n_chip, n_land * cols, BLK), BF16),
        ],
    )
    (ritz,) = call(
        functools.partial(ritz_kernel, n_row, landmarks.shape[0] * BLK),
        [shape(cols, share)],
        vec(*shifts(gram, "row"), *shares, own),
        [pltpu.VMEM((n_row, cols, cols), F32)],
    )
    return row_scaling.reshape(-1), col_scaling.reshape(-1), ritz


def tile_pack_kernel(prof_ref, width_ref, out_ref, work):
    pcs = prof_ref.shape[0]
    prof = prof_ref[...].astype(F32)
    norm = jnp.sum(prof * prof, axis=0, keepdims=True)
    high, mid, low = split3(norm)
    work[...] = jnp.zeros_like(work)
    work[0:pcs, :] = prof
    work[pcs : pcs + 1, :] = high
    work[pcs + 1 : pcs + 2, :] = mid
    work[pcs + 2 : pcs + 3, :] = low
    work[pcs + 3 : pcs + 6, :] = jnp.ones((3, prof.shape[1]), F32)
    work[pcs + 6 : pcs + 7, :] = width_ref[...].astype(F32)
    out_ref[...] = work[...].astype(BF16)


def tile_square(tile, slots):
    a, b, c, d = [tile[s] for s in slots]
    return jnp.concatenate(
        [jnp.concatenate([a, b], axis=1), jnp.concatenate([c, d], axis=1)], axis=0
    )


def tile_add_rows(acc, lists, target, slots, sums, total, spare, firsts):
    for i, (s, (row, lane)) in enumerate(zip(slots, firsts)):
        place = jnp.where(s < total, lists[0, 0, target, s], spare)
        acc[place] += sums[row : row + 8, lane : lane + BLK]


def tile_row_sums(lists, tile, left, acc, total, spare):
    def step(*slots):
        low = [left[0, lists[0, 0, 1, s]] for s in slots[:2]]
        high = [left[1, lists[0, 0, 1, s]] for s in slots[2:]]
        sums = jnp.dot(
            jnp.concatenate(low + high, axis=0),
            tile_square(tile, slots),
            preferred_element_type=F32,
        )
        firsts = [(0, 0), (PIECES, BLK), (2 * PIECES, 0), (3 * PIECES, BLK)]
        tile_add_rows(acc, lists, 0, slots, sums, total, spare, firsts)

    slot_loop(step, total, 4, 4 * TILE_GROUP)


def tile_col_sums(lists, tile, left, acc, total, spare):
    def step(*slots):
        pieces = [left[i % 2, lists[0, 0, 0, s]] for i, s in enumerate(slots)]
        sums = lax.dot_general(
            jnp.concatenate(pieces, axis=0),
            tile_square(tile, slots),
            (((1,), (1,)), ((), ())),
            preferred_element_type=F32,
        )
        firsts = [(0, 0), (PIECES, 0), (2 * PIECES, BLK), (3 * PIECES, BLK)]
        tile_add_rows(acc, lists, 1, slots, sums, total, spare, firsts)

    slot_loop(step, total, 4, 4 * TILE_GROUP)


def tile_build_kernel(pcs, n_row, n_col, *refs):
    lists, counts = refs[:2]
    col_in = refs[2 : 2 + n_row]
    row_in = refs[2 + n_row : 2 + n_row + n_col]
    tile, part, row_prof, row_inv, col_prof, col_inv, acc, left = refs[2 + n_row + n_col :]
    per = row_in[0].shape[1] // BLK
    col_blocks, row_blocks = n_row * per, n_col * per
    total = counts[0, 0]
    me_row, me_col = places()
    for k, ref in enumerate(row_in):
        core = lax.rem(me_col + k, 2)
        piece = shifted(me_col // 2, k // 2, n_col // 2) * 2 + core
        for j in range(per):
            block = ref[:, j * BLK : (j + 1) * BLK]
            row_prof[piece * per + j] = block
            width = block.astype(F32)[pcs + 6 : pcs + 7, :]
            row_inv[piece * per + j] = jnp.broadcast_to(1.0 / width, (8, BLK))
    rows = lax.broadcasted_iota(jnp.int32, (FEAT, BLK), 0)
    for k, ref in enumerate(col_in):
        piece = shifted(me_row, k, n_row)
        for j in range(per):
            block = ref[0:FEAT, j * BLK : (j + 1) * BLK].astype(F32)
            turned = jnp.where(rows < pcs, -2.0 * block, 0.0)
            turned = jnp.where((rows >= pcs) & (rows < pcs + 3), 1.0, turned)
            turned = jnp.where(
                (rows >= pcs + 3) & (rows < pcs + 6), pltpu.roll(block, 3, 0), turned
            )
            turned = jnp.where(rows == pcs + 7, pltpu.roll(block, 1, 0), turned)
            turned = turned.T
            col_prof[piece * per + j] = turned.astype(BF16)
            col_inv[piece * per + j] = jnp.broadcast_to(
                -LOG2E / turned[:, pcs + 7 : pcs + 8], (BLK, BLK)
            )

    def step(s):
        rb, cb = lists[0, 0, 0, s], lists[0, 0, 1, s]
        distance = jnp.dot(col_prof[cb], row_prof[rb], preferred_element_type=F32)
        block = jnp.exp2(distance * col_inv[cb] * row_inv[rb][0:1, :])
        tile[s] = block.astype(BF16)

    slot_loop(step, total, 1, TILE_GROUP)
    ones = (lax.broadcasted_iota(jnp.int32, (PIECES, BLK), 0) == 0).astype(F32).astype(BF16)
    empty = jnp.zeros_like(ones)
    for b in range(row_blocks):
        left[0, b] = jnp.concatenate([ones, empty], axis=1)
        left[1, b] = jnp.concatenate([empty, ones], axis=1)
    acc[...] = jnp.zeros_like(acc)
    tile_col_sums(lists, tile, left, acc, total, col_blocks)
    part[...] = jnp.sum(acc[0:col_blocks], axis=1)


def tile_pass_kernel(over_rows, n_parts, *refs):
    lists, counts, tile = refs[:3]
    parts = refs[3 : 3 + n_parts]
    out, stage, left, acc = refs[-4:]
    total = counts[0, 0]
    blocks = out.shape[0]
    me_row, me_col = places()
    scaling = SCALE / ordered_sum(stage, parts, me_row if over_rows else me_col // 2)
    fill_pieces(left, scaling)
    acc[...] = jnp.zeros_like(acc)
    (tile_row_sums if over_rows else tile_col_sums)(lists, tile, left, acc, total, blocks)
    out[...] = jnp.sum(acc[0:blocks], axis=1)


def tile_last_kernel(n_row, n_col, n_land, *refs):
    lists, counts, marks, tile = refs[:4]
    parts, bases = refs[4 : 4 + n_row], refs[4 + n_row : 4 + 2 * n_row]
    keep, away, both, scaling_out, stage, scaled, acc = refs[4 + 2 * n_row :]
    cols = bases[0].shape[0]
    per = bases[0].shape[1] // BLK
    blocks = n_col * per
    total = counts[0, 0]
    me_row, me_col = places()
    scaling = SCALE / ordered_sum(stage, parts, me_row)
    scaling_out[...] = scaling
    for k in range(n_row):
        piece = shifted(me_row, k, n_row)
        for j in range(per):
            block = bases[k][:, j * BLK : (j + 1) * BLK].astype(F32)
            b = piece * per + j
            scaled[b, 0:cols] = (block * scaling_out[pl.ds(b, 1), :]).astype(BF16)
    high, mid, low = split3(scaling)
    shape = (PIECES, BLK)
    rows = lax.broadcasted_iota(jnp.int32, shape, 0)
    for b in range(scaling.shape[0]):
        value = jnp.where(
            rows == 0,
            jnp.broadcast_to(high[b : b + 1], shape),
            jnp.where(
                rows == 1,
                jnp.broadcast_to(mid[b : b + 1], shape),
                jnp.where(rows == 2, jnp.broadcast_to(low[b : b + 1], shape), 0.0),
            ),
        )
        scaled[b, cols : cols + PIECES] = value.astype(BF16)
    acc[...] = jnp.zeros_like(acc)

    def step(s):
        target = jnp.where(s < total, lists[0, 0, 0, s], blocks)
        sums = jnp.dot(scaled[lists[0, 0, 1, s]], tile[s], preferred_element_type=F32)
        acc[target] += sums[0 : cols + 8]

    slot_loop(step, total, 1, TILE_GROUP)
    core = lax.rem(me_col, 2)
    for q in range(n_col // 2):
        own = (2 * q + core) * per
        other = (2 * q + 1 - core) * per
        for j in range(per):
            keep[q, j] = acc[own + j, 0:cols]
            away[q, j] = acc[other + j, 0:cols].astype(BF16)
    row_part = jnp.sum(acc[0:blocks, cols : cols + 8], axis=1)
    for i, value in enumerate(pieces_of(row_part)):
        both[i * blocks : (i + 1) * blocks] = value
    for i in range(n_land):
        first = 3 * blocks + i * cols
        both[first : first + cols] = acc[marks[me_row * n_land + i] - me_row * blocks, 0:cols].astype(BF16)


def tile_body(profiles, cell_width, basis, block_lists, block_counts, landmarks):
    n_row, n_col = lax.axis_size("row"), lax.axis_size("col")
    n_chip = n_col // 2
    pcs, share = profiles.shape
    cols = basis.shape[0]
    per = share // BLK
    row_blocks, col_blocks = n_col * per, n_row * per
    slots = block_lists.shape[-1]
    n_land = landmarks.shape[0] // n_row

    def shape(*dims, dtype=F32):
        return jax.ShapeDtypeStruct(dims, dtype)

    (packed,) = call(
        tile_pack_kernel,
        [shape(FEAT, share, dtype=BF16)],
        vec(profiles, cell_width.reshape(1, share)),
        [pltpu.VMEM((FEAT, share), F32)],
    )
    spread = lax.ppermute(
        packed,
        ("row", "col"),
        [((q % n_row) * n_col + q // n_row, q) for q in range(n_row * n_col)],
    )
    row_packs = []
    for pack in chip_shifts(spread):
        row_packs += [pack, sibling(pack)]
    col_packs = shifts(packed, "row")
    bases = shifts(basis, "row")
    lists = [("smem", block_lists), ("smem", block_counts)]
    marks = [("smem", landmarks)]
    tile, part = call(
        functools.partial(tile_build_kernel, pcs, n_row, n_col),
        [pltpu.VMEM((slots, BLK, BLK), BF16), shape(col_blocks, BLK)],
        lists + vec(*col_packs, *row_packs),
        [
            pltpu.VMEM((row_blocks, FEAT, BLK), BF16),
            pltpu.VMEM((row_blocks, 8, BLK), F32),
            pltpu.VMEM((col_blocks, BLK, FEAT), BF16),
            pltpu.VMEM((col_blocks, BLK, BLK), F32),
            pltpu.VMEM((col_blocks + 1, 8, BLK), F32),
            pltpu.VMEM((2, row_blocks, PIECES, 2 * BLK), BF16),
        ],
    )
    for number in range(SWEEPS - 1):
        early = [("near", b) for b in bases[1:]] if number == 0 else []
        (part,) = call(
            functools.partial(tile_pass_kernel, True, n_row),
            [shape(row_blocks, BLK)],
            lists + [("keep", tile)] + vec(*shifts(part, "row")) + early,
            [
                pltpu.VMEM((n_row, col_blocks, BLK), F32),
                pltpu.VMEM((2, col_blocks, PIECES, 2 * BLK), BF16),
                pltpu.VMEM((row_blocks + 1, 8, BLK), F32),
            ],
        )
        (part,) = call(
            functools.partial(tile_pass_kernel, False, n_chip),
            [shape(col_blocks, BLK)],
            lists + [("keep", tile)] + vec(*chip_shifts(part + sibling(part))),
            [
                pltpu.VMEM((n_chip, row_blocks, BLK), F32),
                pltpu.VMEM((2, row_blocks, PIECES, 2 * BLK), BF16),
                pltpu.VMEM((col_blocks + 1, 8, BLK), F32),
            ],
        )
    both_rows = 3 * row_blocks + n_land * cols
    keep, away, both, col_scaling = call(
        functools.partial(tile_last_kernel, n_row, n_col, n_land),
        [
            shape(n_chip, per, cols, BLK),
            shape(n_chip, per, cols, BLK, dtype=BF16),
            shape(both_rows, BLK, dtype=BF16),
            shape(col_blocks, BLK),
        ],
        lists + marks + [("keep", tile)] + vec(*shifts(part, "row"), *bases),
        [
            pltpu.VMEM((n_row, col_blocks, BLK), F32),
            pltpu.VMEM((col_blocks, cols + PIECES, BLK), BF16),
            pltpu.VMEM((row_blocks + 1, cols + 8, BLK), F32),
        ],
    )
    pairs = call(
        pair_kernel,
        [shape(both_rows, BLK, dtype=BF16)]
        + [shape(per * cols, BLK, dtype=BF16)] * n_chip,
        vec(keep, sibling(away), both, sibling(both)),
    )
    sums = [pairs[0]] + [chip_shift(pairs[0], k) for k in range(1, n_chip)]
    shares = [pairs[1]] + [chip_shift(pairs[1 + k], k) for k in range(1, n_chip)]
    gram, row_scaling, own = call(
        functools.partial(gram_kernel, n_land, cols, per),
        [shape(cols, cols), shape(row_blocks, BLK), shape(per, BLK)],
        marks + vec(*sums),
        [
            pltpu.VMEM((row_blocks, BLK), F32),
            pltpu.VMEM((n_chip, row_blocks, BLK), F32),
            pltpu.VMEM((n_chip, n_land * cols, BLK), BF16),
        ],
    )
    (ritz,) = call(
        functools.partial(ritz_kernel, n_row, landmarks.shape[0] * BLK),
        [shape(cols, share)],
        vec(*shifts(gram, "row"), *shares, own),
        [pltpu.VMEM((n_row, cols, cols), F32)],
    )
    return row_scaling.reshape(-1), col_scaling.reshape(-1), ritz


def solution(mesh):
    placed = (
        P(None, ("col", "row")),
        P(("col", "row")),
        P(None, ("col", "row")),
        P("row", "col", None, None),
        P("row", "col"),
        P(),
    )
    return jax.shard_map(
        strip_body if mesh.shape["row"] <= STRIP_TILES else tile_body,
        mesh=mesh,
        in_specs=placed,
        out_specs=(P("row"), P("col"), P(None, ("row", "col"))),
        check_vma=False,
    )
```

```python
import functools

import jax
import jax.numpy as jnp
from jax import lax
from jax.experimental import pallas as pl
from jax.experimental.pallas import tpu as pltpu
from jax.sharding import PartitionSpec as P

BLK = 128
SWEEPS = 3
GROUP = 32
TILE_GROUP = 16
ROWS, COLUMNS, COUNT = 0, 1, 2
FEAT = 64
PACK = 56
PIECES = 16
SCALE = 512.0
LOG2E = 1.4426950408889634
F32 = jnp.float32
BF16 = jnp.bfloat16
MIB = 1 << 20
STRIP_TILES = 8

VMEM_SPEC = pl.BlockSpec(memory_space=pltpu.VMEM)
SMEM_SPEC = pl.BlockSpec(memory_space=pltpu.SMEM)


def split3(x):
    high = x.astype(BF16).astype(F32)
    mid = (x - high).astype(BF16).astype(F32)
    low = (x - high - mid).astype(BF16).astype(F32)
    return high, mid, low


def tree_sum(values):
    values = list(values)
    while len(values) > 1:
        values = [a + b for a, b in zip(values[::2], values[1::2])]
    return values[0]


def call(kernel, outs, ins, scratch=(), limit=24, flops=1 << 24):
    args, specs = [], []
    for kind, array in ins:
        if kind == "smem":
            specs.append(SMEM_SPEC)
        elif kind == "near":
            specs.append(pl.BlockSpec(memory_space=pl.ANY))
        elif kind == "hbm":
            specs.append(pl.BlockSpec(memory_space=pltpu.HBM))
            array = pltpu.with_memory_space_constraint(array, pltpu.HBM)
        else:
            specs.append(VMEM_SPEC)
            if kind == "keep":
                array = pltpu.with_memory_space_constraint(array, pltpu.VMEM)
        args.append(array)
    return pl.pallas_call(
        kernel,
        out_shape=tuple(outs),
        in_specs=specs,
        out_specs=tuple(VMEM_SPEC for _ in outs),
        scratch_shapes=list(scratch),
        compiler_params=pltpu.CompilerParams(vmem_limit_bytes=limit * MIB),
        cost_estimate=pl.CostEstimate(flops=flops, bytes_accessed=1 << 20, transcendentals=0),
    )(*args)


def pack_kernel(prof_hbm, width_hbm, lists_hbm, counts, out_ref, *scratch):
    work, prof_ref, width_ref, lists_ref, sems = scratch
    pairs = [
        (prof_hbm, prof_ref),
        (width_hbm, width_ref),
        (lists_hbm, lists_ref),
    ]
    copies = [pltpu.make_async_copy(a, b, sems.at[i]) for i, (a, b) in enumerate(pairs)]
    for copy in copies:
        copy.start()
    for copy in copies:
        copy.wait()
    pcs = prof_ref.shape[0]
    prof = prof_ref[...].astype(F32)
    norm = jnp.sum(prof * prof, axis=0, keepdims=True)
    high, mid, low = split3(norm)
    work[...] = jnp.zeros_like(work)
    work[0:pcs, :] = prof
    work[pcs : pcs + 1, :] = high
    work[pcs + 1 : pcs + 2, :] = mid
    work[pcs + 2 : pcs + 3, :] = low
    work[pcs + 3 : pcs + 4, :] = width_ref[...].astype(F32).reshape(1, -1)
    lists = lists_ref[0, 0].astype(F32)
    slots = slice(pcs + 4, pcs + 5)
    work[slots, 0:BLK] = lists[0:1]
    work[slots, BLK : 2 * BLK] = lists[1:2]
    count = jnp.full((1, BLK), counts[0, 0], jnp.int32)
    work[slots, 2 * BLK : 3 * BLK] = count.astype(F32)
    out_ref[...] = work[...].astype(BF16)


def places():
    return lax.axis_index("row"), lax.axis_index("col")


def stack_kernel(pcs, n, *refs):
    packs, (rest, table) = refs[:n], refs[-2:]
    me_row, _ = places()
    for k, pack in enumerate(packs):
        if k:
            rest[k - 1] = pack[...]
        slots = pack[:, 0 : 3 * BLK].astype(F32)[pcs + 4 : pcs + 5]
        for row in (ROWS, COLUMNS, COUNT):
            values = slots[:, row * BLK : (row + 1) * BLK].astype(jnp.int32)
            table[shifted(me_row, k, n), row : row + 1] = values


def slot_loop(step, count, size, group):
    def advance(number, carry):
        for i in range(0, group, size):
            step(*[number * group + i + j for j in range(size)])
        return carry

    lax.fori_loop(0, (count + group - 1) // group, advance, 0)


class Tile:
    def __init__(self, table, n_row, k, own, others):
        _, me_col = places()
        self.group = shifted(me_col // 2, k, n_row)
        self.table, self.k = table, k
        slots = own.shape[0]
        self.blocks, self.base = (own, 0) if k == 0 else (others, (k - 1) * slots)
        self.total = table[self.group * 8 + COUNT, 0]

    def group_size(self, times):
        return times * GROUP if self.k == 0 else GROUP

    def row(self, s):
        return self.table[self.group * 8 + ROWS, s]

    def column(self, s):
        return self.table[self.group * 8 + COLUMNS, s]

    def block(self, s):
        return self.blocks[self.base + s]


def shifted(me, k, n):
    return lax.rem(me + (n - k), n)


def ordered_sum(stage, refs, me):
    n = len(refs)
    for k, ref in enumerate(refs):
        stage[shifted(me, k, n)] = ref[...]
    return tree_sum([stage[i] for i in range(n)])


def square(tile, slots):
    a, b, c, d = [tile.block(s) for s in slots]
    return jnp.concatenate(
        [jnp.concatenate([a, b], axis=1), jnp.concatenate([c, d], axis=1)], axis=0
    )


def add_rows(acc, sums, firsts, targets):
    for (row, lane), target in zip(firsts, targets):
        acc[target] += sums[row : row + 8, lane : lane + BLK]


def row_sums(tile, wide, acc, row_blocks, spare):
    first = tile.group * row_blocks

    def step(s):
        product = tile.block(s).astype(F32) * wide[tile.column(s)]
        sums = jnp.sum(product.reshape(BLK // 8, 8, BLK), axis=0)
        acc[jnp.where(s < tile.total, first + tile.row(s), spare)] += sums

    slot_loop(step, tile.total, 1, tile.group_size(2))


def spread_lanes(wide, scaling):
    turned = scaling.T
    for b in range(scaling.shape[0]):
        wide[b] = jnp.broadcast_to(turned[:, b : b + 1], (BLK, BLK))


def col_sums(tile, left, acc, row_blocks, spare):
    first = tile.group * row_blocks

    def step(*slots):
        if left is None:
            rows = lax.broadcasted_iota(jnp.int32, (4 * PIECES, 2 * BLK), 0)
            lanes = lax.broadcasted_iota(jnp.int32, (4 * PIECES, 2 * BLK), 1)
            block = rows // PIECES
            pieces = (rows % PIECES == 0) & (block % 2 == lanes // BLK)
            pieces = pieces.astype(F32).astype(BF16)
        else:
            pieces = [left[i % 2, first + tile.row(s)] for i, s in enumerate(slots)]
            pieces = jnp.concatenate(pieces, axis=0)
        sums = lax.dot_general(
            pieces,
            square(tile, slots),
            (((1,), (1,)), ((), ())),
            preferred_element_type=F32,
        )
        firsts = [(0, 0), (PIECES, 0), (2 * PIECES, BLK), (3 * PIECES, BLK)]
        targets = [jnp.where(s < tile.total, tile.column(s), spare) for s in slots]
        add_rows(acc, sums, firsts, targets)

    slot_loop(step, tile.total, 4, tile.group_size(4))


def fill_pieces(left, scaling):
    high, mid, low = split3(scaling)
    shape = (PIECES, BLK)
    rows = lax.broadcasted_iota(jnp.int32, shape, 0)
    empty = jnp.zeros(shape, F32).astype(BF16)
    for b in range(scaling.shape[0]):
        value = jnp.where(
            rows == 0,
            jnp.broadcast_to(high[b : b + 1], shape),
            jnp.where(
                rows == 1,
                jnp.broadcast_to(mid[b : b + 1], shape),
                jnp.where(rows == 2, jnp.broadcast_to(low[b : b + 1], shape), 0.0),
            ),
        ).astype(BF16)
        left[0, b] = jnp.concatenate([value, empty], axis=1)
        left[1, b] = jnp.concatenate([empty, value], axis=1)


def build(tile, offset, row_prof, row_inv, col_prof, col_inv):
    def step(s):
        row, column = offset + tile.row(s), tile.column(s)
        distance = jnp.dot(col_prof[column], row_prof[row], preferred_element_type=F32)
        block = jnp.exp2(distance * col_inv[column] * row_inv[row][0:1, :])
        tile.blocks[tile.base + s] = block.astype(BF16)

    slot_loop(step, tile.total, 1, tile.group_size(2))


def piece_block(pieces, k, j):
    lanes = slice(j * BLK, (j + 1) * BLK)
    return pieces[0][:, lanes] if k == 0 else pieces[1][k - 1, :, lanes]


def fill_rows(pcs, sources, row_prof, row_inv, offset):
    me_row, me_col = places()
    n_row = sources[0][1].shape[0] + 1
    per = sources[0][0].shape[1] // BLK
    ones = lax.broadcasted_iota(jnp.int32, (FEAT - PACK, BLK), 0) < 3
    ones = ones.astype(F32)
    for i, pieces in enumerate(sources):
        core = lax.rem(me_col + i, 2)
        for k in range(n_row):
            piece = core * n_row + shifted(me_row, k, n_row)
            for j in range(per):
                block = piece_block(pieces, k, j).astype(F32)
                whole = jnp.concatenate([block, ones], axis=0)
                row_prof[offset + piece * per + j] = whole.astype(BF16)
                width = block[pcs + 3 : pcs + 4, :]
                row_inv[offset + piece * per + j] = jnp.broadcast_to(1.0 / width, (8, BLK))


def own_kernel(pcs, table, pack, rest, pack_in, rest_in, *refs):
    tile, col_prof, col_inv, sums, row_prof, row_inv, acc = refs[-7:]
    n_row = rest.shape[0] + 1
    per = pack.shape[1] // BLK
    me_row, _ = places()
    fill_rows(pcs, [(pack, rest), (pack_in, rest_in)], row_prof, row_inv, 0)
    rows = lax.broadcasted_iota(jnp.int32, (FEAT, BLK), 0)
    for k in range(n_row):
        piece = shifted(me_row, k, n_row)
        for j in range(per):
            block = piece_block((pack, rest), k, j).astype(F32)
            block = jnp.concatenate([block, jnp.zeros((FEAT - PACK, BLK), F32)], axis=0)
            turned = jnp.where(rows < pcs, -2.0 * block, 0.0)
            turned = jnp.where((rows >= pcs) & (rows < pcs + 3), 1.0, turned)
            turned = jnp.where(rows == PACK - 1, pltpu.roll(block, PACK - 4 - pcs, 0), turned)
            turned = jnp.where(
                (rows >= PACK) & (rows < PACK + 3), pltpu.roll(block, PACK - pcs, 0), turned
            )
            turned = turned.T
            col_prof[piece * per + j] = turned.astype(BF16)
            col_inv[piece * per + j] = jnp.broadcast_to(
                -LOG2E / turned[:, PACK - 1 : PACK], (BLK, BLK)
            )
    own = Tile(table, n_row, 0, tile, None)
    build(own, 0, row_prof, row_inv, col_prof, col_inv)
    sums[...] = column_totals([own], None, acc, row_prof.shape[0])


def column_totals(tiles, left, acc, row_blocks):
    col_blocks = acc.shape[0] - 1
    acc[...] = jnp.zeros_like(acc)
    for tile in tiles:
        col_sums(tile, left, acc, row_blocks, col_blocks)
    return jnp.sum(acc[0:col_blocks], axis=1)


def row_part(tiles, wide, acc, row_blocks, out):
    blocks = acc.shape[0] - 1
    acc[...] = jnp.zeros_like(acc)
    for tile in tiles:
        row_sums(tile, wide, acc, row_blocks, blocks)
    out[...] = jnp.sum(acc[0:blocks], axis=1)


def strip_kernel(pcs, n_row, *refs):
    table, own, col_prof, col_inv, own_sums = refs[:5]
    sources = [refs[i : i + 2] for i in range(5, 5 + 4 * (n_row - 1), 2)]
    others, out, row_prof, row_inv, wide, row_acc, col_acc = refs[-7:]
    row_blocks = row_prof.shape[0] // (n_row - 1)
    tiles = [Tile(table, n_row, k, own, others) for k in range(n_row)]
    for k in range(1, n_row):
        first = (k - 1) * row_blocks
        fill_rows(pcs, sources[2 * k - 2 : 2 * k], row_prof, row_inv, first)
    for k in range(1, n_row):
        first = (k - 1) * row_blocks
        build(tiles[k], first, row_prof, row_inv, col_prof, col_inv)
    totals = column_totals(tiles[1:], None, col_acc, row_blocks) + own_sums[...]
    spread_lanes(wide, SCALE / totals)
    row_part(tiles, wide, row_acc, row_blocks, out)


def row_scalings(stage, parts):
    for k, part in enumerate(parts):
        stage[shifted(places()[1] // 2, k, len(parts))] = part[...].astype(F32)
    return SCALE / tree_sum([stage[i] for i in range(len(parts))])


def sweep_kernel(n_row, n_chip, *refs):
    table, own, others = refs[:3]
    parts = refs[3 : 3 + n_chip]
    out, stage, row_left, wide, row_acc, col_acc = refs[-6:]
    row_blocks = out.shape[0] // n_row
    tiles = [Tile(table, n_row, k, own, others) for k in range(n_row)]
    fill_pieces(row_left, row_scalings(stage, parts))
    totals = column_totals(tiles, row_left, col_acc, row_blocks)
    spread_lanes(wide, SCALE / totals)
    row_part(tiles, wide, row_acc, row_blocks, out)


def pieces_of(value):
    return [v.astype(BF16) for v in split3(value)]


def last_kernel(n_row, n_chip, n_land, *refs):
    table, marks, own, others = refs[:4]
    parts, bases = refs[4 : 4 + n_chip], refs[4 + n_chip : 4 + n_chip + n_row]
    keep, away, both, scaling_out, stage, row_left, col_acc, scaled, acc = refs[-9:]
    cols = bases[0].shape[0]
    per = bases[0].shape[1] // BLK
    blocks = 2 * n_chip * per
    me_row, me_col = places()
    tiles = [Tile(table, n_row, k, own, others) for k in range(n_row)]
    fill_pieces(row_left, row_scalings(stage, parts))
    scaling = SCALE / column_totals(tiles, row_left, col_acc, blocks)
    scaling_out[...] = scaling
    for k in range(n_row):
        piece = lax.bitwise_xor(me_row, k)
        for j in range(per):
            block = bases[k][:, j * BLK : (j + 1) * BLK].astype(F32)
            b = piece * per + j
            scaled[b, 0:cols] = (block * scaling_out[pl.ds(b, 1), :]).astype(BF16)
    high, mid, low = split3(scaling)
    shape = (PIECES, BLK)
    rows = lax.broadcasted_iota(jnp.int32, shape, 0)
    for b in range(scaling.shape[0]):
        value = jnp.where(
            rows == 0,
            jnp.broadcast_to(high[b : b + 1], shape),
            jnp.where(
                rows == 1,
                jnp.broadcast_to(mid[b : b + 1], shape),
                jnp.where(rows == 2, jnp.broadcast_to(low[b : b + 1], shape), 0.0),
            ),
        )
        scaled[b, cols : cols + PIECES] = value.astype(BF16)
    acc[...] = jnp.zeros_like(acc)
    for k in range(n_row):
        tile = tiles[k]

        def step(s, tile=tile):
            target = jnp.where(s < tile.total, tile.row(s), blocks)
            sums = jnp.dot(scaled[tile.column(s)], tile.block(s), preferred_element_type=F32)
            acc[target] += sums[0 : cols + 8]

        slot_loop(step, jnp.where(tile.group == me_row, tile.total, 0), 1, tile.group_size(2))
    core = lax.rem(me_col, 2)
    for q in range(n_chip):
        mine = (2 * q + core) * per
        other = (2 * q + 1 - core) * per
        for j in range(per):
            keep[q, j] = acc[mine + j, 0:cols]
            away[q, j] = acc[other + j, 0:cols].astype(BF16)
    part = jnp.sum(acc[0:blocks, cols : cols + 8], axis=1)
    for i, value in enumerate(pieces_of(part)):
        both[i * blocks : (i + 1) * blocks] = value
    for i in range(n_land):
        first = 3 * blocks + i * cols
        both[first : first + cols] = acc[marks[me_row * n_land + i] - me_row * blocks, 0:cols].astype(BF16)


def three(ref, blocks):
    value = ref[0 : 3 * blocks].astype(F32)
    return (value[2 * blocks :] + value[blocks : 2 * blocks]) + value[0:blocks]


def pair_kernel(keep, away, both, both_in, both_out, *outs):
    n_chip, per, cols = keep.shape[:3]
    blocks = 2 * n_chip * per
    chip = places()[1] // 2
    parts = pieces_of(three(both, blocks) + three(both_in, blocks))
    for i, value in enumerate(parts):
        both_out[i * blocks : (i + 1) * blocks] = value
    lands = both[3 * blocks :].astype(F32) + both_in[3 * blocks :].astype(F32)
    both_out[3 * blocks :] = lands.astype(BF16)
    for k, out in enumerate(outs):
        to = lax.rem(chip + k, n_chip)
        for j in range(per):
            value = keep[to, j] + away[to, j].astype(F32)
            out[j * cols : (j + 1) * cols] = value.astype(BF16)


def gram_kernel(n_land, cols, per, *refs):
    marks = refs[0]
    gram, scaling_out, own, inverse, stage, land_stage = refs[-6:]
    parts = refs[1:-6]
    n = len(parts)
    me_row, me_col = places()
    blocks = scaling_out.shape[0]
    for k, part in enumerate(parts):
        place = shifted(me_col // 2, k, n)
        stage[place] = three(part, blocks)
        land_stage[place] = part[3 * blocks :]
    inverse[...] = 1.0 / tree_sum([stage[i] for i in range(n)])
    scaling_out[...] = SCALE * inverse[...]
    for j in range(per):
        own[j : j + 1, :] = inverse[pl.ds(me_col * per + j, 1), :]
    total = None
    for i in range(n_land):
        summed = tree_sum(
            [land_stage[k, i * cols : (i + 1) * cols].astype(F32) for k in range(n)]
        )
        block = marks[me_row * n_land + i] - me_row * blocks
        projected = summed * inverse[pl.ds(block, 1), :]
        product = lax.dot_general(
            projected,
            projected,
            (((1,), (1,)), ((), ())),
            precision=lax.Precision.HIGHEST,
            preferred_element_type=F32,
        )
        total = product if total is None else total + product
    gram[...] = total


WIDE = 4


def eliminate(gram):
    cols = gram.shape[0]
    rows = lax.broadcasted_iota(jnp.int32, (cols, 2 * cols), 0)
    lanes = lax.broadcasted_iota(jnp.int32, (cols, 2 * cols), 1)
    unit = (rows[:, :cols] == lanes[:, :cols]).astype(F32)
    work = jnp.concatenate([gram, unit], axis=1)
    for first in range(0, cols, WIDE):
        tops = [work[first + i : first + i + 1, :] for i in range(WIDE)]
        sides = [
            jnp.broadcast_to(work[:, first + i : first + i + 1], work.shape)
            for i in range(WIDE)
        ]
        change = None
        for i in range(WIDE):
            pivot = first + i
            inverse = 1.0 / sides[i][pivot : pivot + 1, :]
            unit_top = tops[i] * inverse
            for m in range(i + 1, WIDE):
                factor = sides[i][first + m : first + m + 1, :]
                tops[m] = tops[m] - factor * unit_top
                inner = factor * inverse
                sides[m] = sides[m] - sides[i] * inner
            term = sides[i] * unit_top
            change = term if change is None else change + term
        reduced = work - change
        kept = work
        for i in range(WIDE):
            kept = jnp.where(rows == first + i, tops[i], kept)
        work = jnp.where(rows >= first + WIDE, reduced, kept)
    pivots = jnp.sum(jnp.where(rows == lanes, work, 0.0), axis=1, keepdims=True)
    return (work * lax.rsqrt(pivots))[:, cols:]


def ritz_kernel(n_row, cells, *refs):
    grams, parts = refs[:n_row], refs[n_row:-3]
    own, out, stage = refs[-3:]
    cols = grams[0].shape[0]
    per = out.shape[1] // BLK
    inverse = eliminate(ordered_sum(stage, grams, places()[0]) * (1.0 / cells))
    for j in range(per):
        summed = tree_sum([m[j * cols : (j + 1) * cols].astype(F32) for m in parts])
        projected = summed * own[j : j + 1, :]
        out[:, j * BLK : (j + 1) * BLK] = jnp.dot(
            inverse, projected, precision=lax.Precision.HIGHEST, preferred_element_type=F32
        )


def swap(x, axis, k):
    return lax.ppermute(x, axis, [(i, i ^ k) for i in range(lax.axis_size(axis))])


def shift(x, axis, k):
    n = lax.axis_size(axis)
    return lax.ppermute(x, axis, [(i, (i + k) % n) for i in range(n)])


def shifts(x, axis):
    return [x] + [shift(x, axis, k) for k in range(1, lax.axis_size(axis))]


def chip_shift(x, k):
    n = lax.axis_size("col") // 2
    return lax.ppermute(
        x,
        "col",
        [(2 * q + p, 2 * ((q + k) % n) + p) for q in range(n) for p in range(2)],
    )


def chip_shifts(x):
    return [x] + [chip_shift(x, k) for k in range(1, lax.axis_size("col") // 2)]


def sibling(x):
    return swap(x, "col", 1)


def vec(*arrays):
    return [("vmem", a) for a in arrays]


def strip_body(profiles, cell_width, basis, block_lists, block_counts, landmarks):
    n_row, n_col = lax.axis_size("row"), lax.axis_size("col")
    n_chip = n_col // 2
    pcs, share = profiles.shape
    cols = basis.shape[0]
    per = share // BLK
    row_blocks, col_blocks = n_col * per, n_row * per
    all_rows = n_row * row_blocks
    slots = block_lists.shape[-1]
    n_land = landmarks.shape[0] // n_row

    def shape(*dims, dtype=F32):
        return jax.ShapeDtypeStruct(dims, dtype)

    (packed,) = call(
        pack_kernel,
        [shape(PACK, share, dtype=BF16)],
        [("hbm", a) for a in (profiles, cell_width, block_lists)] + [("smem", block_counts)],
        [
            pltpu.VMEM((PACK, share), F32),
            pltpu.VMEM(profiles.shape, BF16),
            pltpu.VMEM(cell_width.shape, BF16),
            pltpu.VMEM(block_lists.shape, jnp.int32),
            pltpu.SemaphoreType.DMA((3,)),
        ],
    )
    near = [chip_shift(packed, k) for k in range(1, n_chip)]
    near_in = [sibling(pack) for pack in near]
    pack_in = sibling(packed)
    rest, table = call(
        functools.partial(stack_kernel, pcs, n_row),
        [shape(n_row - 1, PACK, share, dtype=BF16), shape(n_row, 8, BLK, dtype=jnp.int32)],
        vec(*shifts(packed, "row")) + [("near", pack) for pack in near_in + [pack_in]],
    )
    table = ("smem", table.reshape(n_row * 8, BLK))
    marks = ("smem", landmarks)
    far = [chip_shift(rest, k) for k in range(1, n_chip)]
    own, col_prof, col_inv, sums = call(
        functools.partial(own_kernel, pcs),
        [
            pltpu.VMEM((slots, BLK, BLK), BF16),
            pltpu.VMEM((col_blocks, BLK, FEAT), BF16),
            pltpu.VMEM((col_blocks, BLK, BLK), F32),
            shape(col_blocks, BLK),
        ],
        [table] + vec(packed, rest, pack_in, sibling(rest)),
        [
            pltpu.VMEM((row_blocks, FEAT, BLK), BF16),
            pltpu.VMEM((row_blocks, 8, BLK), F32),
            pltpu.VMEM((col_blocks + 1, 8, BLK), F32),
        ],
    )
    far, sums = lax.optimization_barrier((far, sums))
    stacks = []
    for pack, other, group in zip(near, near_in, far):
        stacks += [pack, group, other, sibling(group)]
    far_slots = (n_row - 1) * slots
    others, part = call(
        functools.partial(strip_kernel, pcs, n_row),
        [pltpu.VMEM((far_slots, BLK, BLK), BF16), shape(all_rows, BLK)],
        [table, ("keep", own), ("keep", col_prof), ("keep", col_inv)]
        + vec(sums, *stacks),
        [
            pltpu.VMEM((all_rows - row_blocks, FEAT, BLK), BF16),
            pltpu.VMEM((all_rows - row_blocks, 8, BLK), F32),
            pltpu.VMEM((col_blocks, BLK, BLK), F32),
            pltpu.VMEM((all_rows + 1, 8, BLK), F32),
            pltpu.VMEM((col_blocks + 1, 8, BLK), F32),
        ],
    )
    tiles = [("keep", own), ("keep", others)]

    def chip_parts(part):
        return chip_shifts((part + sibling(part)).astype(BF16))

    bases = [basis]
    for _ in range(SWEEPS - 2):
        part, bases[0] = lax.optimization_barrier((part, bases[0]))
        bases = bases[:1] + [swap(bases[0], "row", 1)]
        (part,) = call(
            functools.partial(sweep_kernel, n_row, n_chip),
            [shape(all_rows, BLK)],
            [table] + tiles + vec(*chip_parts(part)) + [("near", bases[1])],
            [
                pltpu.VMEM((n_chip, all_rows, BLK), F32),
                pltpu.VMEM((2, all_rows, PIECES, 2 * BLK), BF16),
                pltpu.VMEM((col_blocks, BLK, BLK), F32),
                pltpu.VMEM((all_rows + 1, 8, BLK), F32),
                pltpu.VMEM((col_blocks + 1, 8, BLK), F32),
            ],
        )
    both_rows = 3 * row_blocks + n_land * cols
    part, bases = lax.optimization_barrier((part, bases))
    while len(bases) < n_row:
        bases = bases + [swap(base, "row", len(bases)) for base in bases]
    keep, away, both, col_scaling = call(
        functools.partial(last_kernel, n_row, n_chip, n_land),
        [
            shape(n_chip, per, cols, BLK),
            shape(n_chip, per, cols, BLK, dtype=BF16),
            shape(both_rows, BLK, dtype=BF16),
            shape(col_blocks, BLK),
        ],
        [table, marks] + tiles + vec(*chip_parts(part), *bases),
        [
            pltpu.VMEM((n_chip, all_rows, BLK), F32),
            pltpu.VMEM((2, all_rows, PIECES, 2 * BLK), BF16),
            pltpu.VMEM((col_blocks + 1, 8, BLK), F32),
            pltpu.VMEM((col_blocks, cols + PIECES, BLK), BF16),
            pltpu.VMEM((row_blocks + 1, cols + 8, BLK), F32),
        ],
    )
    pairs = call(
        pair_kernel,
        [shape(both_rows, BLK, dtype=BF16)]
        + [shape(per * cols, BLK, dtype=BF16)] * n_chip,
        vec(keep, sibling(away), both, sibling(both)),
    )
    sums = [pairs[0]] + [chip_shift(pairs[0], k) for k in range(1, n_chip)]
    shares = [pairs[1]] + [chip_shift(pairs[1 + k], k) for k in range(1, n_chip)]
    gram, row_scaling, own = call(
        functools.partial(gram_kernel, n_land, cols, per),
        [shape(cols, cols), shape(row_blocks, BLK), shape(per, BLK)],
        [marks] + vec(*sums),
        [
            pltpu.VMEM((row_blocks, BLK), F32),
            pltpu.VMEM((n_chip, row_blocks, BLK), F32),
            pltpu.VMEM((n_chip, n_land * cols, BLK), BF16),
        ],
    )
    (ritz,) = call(
        functools.partial(ritz_kernel, n_row, landmarks.shape[0] * BLK),
        [shape(cols, share)],
        vec(*shifts(gram, "row"), *shares, own),
        [pltpu.VMEM((n_row, cols, cols), F32)],
    )
    return row_scaling.reshape(-1), col_scaling.reshape(-1), ritz


def tile_pack_kernel(prof_ref, width_ref, out_ref, work):
    pcs = prof_ref.shape[0]
    prof = prof_ref[...].astype(F32)
    norm = jnp.sum(prof * prof, axis=0, keepdims=True)
    high, mid, low = split3(norm)
    work[...] = jnp.zeros_like(work)
    work[0:pcs, :] = prof
    work[pcs : pcs + 1, :] = high
    work[pcs + 1 : pcs + 2, :] = mid
    work[pcs + 2 : pcs + 3, :] = low
    work[pcs + 3 : pcs + 6, :] = jnp.ones((3, prof.shape[1]), F32)
    work[pcs + 6 : pcs + 7, :] = width_ref[...].astype(F32)
    out_ref[...] = work[...].astype(BF16)


def tile_square(tile, slots):
    a, b, c, d = [tile[s] for s in slots]
    return jnp.concatenate(
        [jnp.concatenate([a, b], axis=1), jnp.concatenate([c, d], axis=1)], axis=0
    )


def tile_add_rows(acc, lists, target, slots, sums, total, spare, firsts):
    for i, (s, (row, lane)) in enumerate(zip(slots, firsts)):
        place = jnp.where(s < total, lists[0, 0, target, s], spare)
        acc[place] += sums[row : row + 8, lane : lane + BLK]


def tile_row_sums(lists, tile, left, acc, total, spare):
    def step(*slots):
        low = [left[0, lists[0, 0, 1, s]] for s in slots[:2]]
        high = [left[1, lists[0, 0, 1, s]] for s in slots[2:]]
        sums = jnp.dot(
            jnp.concatenate(low + high, axis=0),
            tile_square(tile, slots),
            preferred_element_type=F32,
        )
        firsts = [(0, 0), (PIECES, BLK), (2 * PIECES, 0), (3 * PIECES, BLK)]
        tile_add_rows(acc, lists, 0, slots, sums, total, spare, firsts)

    slot_loop(step, total, 4, 4 * TILE_GROUP)


def tile_col_sums(lists, tile, left, acc, total, spare):
    def step(*slots):
        pieces = [left[i % 2, lists[0, 0, 0, s]] for i, s in enumerate(slots)]
        sums = lax.dot_general(
            jnp.concatenate(pieces, axis=0),
            tile_square(tile, slots),
            (((1,), (1,)), ((), ())),
            preferred_element_type=F32,
        )
        firsts = [(0, 0), (PIECES, 0), (2 * PIECES, BLK), (3 * PIECES, BLK)]
        tile_add_rows(acc, lists, 1, slots, sums, total, spare, firsts)

    slot_loop(step, total, 4, 4 * TILE_GROUP)


def tile_build_kernel(pcs, n_row, n_col, *refs):
    lists, counts = refs[:2]
    col_in = refs[2 : 2 + n_row]
    row_in = refs[2 + n_row : 2 + n_row + n_col]
    tile, part, row_prof, row_inv, col_prof, col_inv, acc, left = refs[2 + n_row + n_col :]
    per = row_in[0].shape[1] // BLK
    col_blocks, row_blocks = n_row * per, n_col * per
    total = counts[0, 0]
    me_row, me_col = places()
    for k, ref in enumerate(row_in):
        core = lax.rem(me_col + k, 2)
        piece = shifted(me_col // 2, k // 2, n_col // 2) * 2 + core
        for j in range(per):
            block = ref[:, j * BLK : (j + 1) * BLK]
            row_prof[piece * per + j] = block
            width = block.astype(F32)[pcs + 6 : pcs + 7, :]
            row_inv[piece * per + j] = jnp.broadcast_to(1.0 / width, (8, BLK))
    rows = lax.broadcasted_iota(jnp.int32, (FEAT, BLK), 0)
    for k, ref in enumerate(col_in):
        piece = shifted(me_row, k, n_row)
        for j in range(per):
            block = ref[0:FEAT, j * BLK : (j + 1) * BLK].astype(F32)
            turned = jnp.where(rows < pcs, -2.0 * block, 0.0)
            turned = jnp.where((rows >= pcs) & (rows < pcs + 3), 1.0, turned)
            turned = jnp.where(
                (rows >= pcs + 3) & (rows < pcs + 6), pltpu.roll(block, 3, 0), turned
            )
            turned = jnp.where(rows == pcs + 7, pltpu.roll(block, 1, 0), turned)
            turned = turned.T
            col_prof[piece * per + j] = turned.astype(BF16)
            col_inv[piece * per + j] = jnp.broadcast_to(
                -LOG2E / turned[:, pcs + 7 : pcs + 8], (BLK, BLK)
            )

    def step(s):
        rb, cb = lists[0, 0, 0, s], lists[0, 0, 1, s]
        distance = jnp.dot(col_prof[cb], row_prof[rb], preferred_element_type=F32)
        block = jnp.exp2(distance * col_inv[cb] * row_inv[rb][0:1, :])
        tile[s] = block.astype(BF16)

    slot_loop(step, total, 1, TILE_GROUP)
    ones = (lax.broadcasted_iota(jnp.int32, (PIECES, BLK), 0) == 0).astype(F32).astype(BF16)
    empty = jnp.zeros_like(ones)
    for b in range(row_blocks):
        left[0, b] = jnp.concatenate([ones, empty], axis=1)
        left[1, b] = jnp.concatenate([empty, ones], axis=1)
    acc[...] = jnp.zeros_like(acc)
    tile_col_sums(lists, tile, left, acc, total, col_blocks)
    part[...] = jnp.sum(acc[0:col_blocks], axis=1)


def tile_pass_kernel(over_rows, n_parts, *refs):
    lists, counts, tile = refs[:3]
    parts = refs[3 : 3 + n_parts]
    out, stage, left, acc = refs[-4:]
    total = counts[0, 0]
    blocks = out.shape[0]
    me_row, me_col = places()
    scaling = SCALE / ordered_sum(stage, parts, me_row if over_rows else me_col // 2)
    fill_pieces(left, scaling)
    acc[...] = jnp.zeros_like(acc)
    (tile_row_sums if over_rows else tile_col_sums)(lists, tile, left, acc, total, blocks)
    out[...] = jnp.sum(acc[0:blocks], axis=1)


def tile_last_kernel(n_row, n_col, n_land, *refs):
    lists, counts, marks, tile = refs[:4]
    parts, bases = refs[4 : 4 + n_row], refs[4 + n_row : 4 + 2 * n_row]
    keep, away, both, scaling_out, stage, scaled, acc = refs[4 + 2 * n_row :]
    cols = bases[0].shape[0]
    per = bases[0].shape[1] // BLK
    blocks = n_col * per
    total = counts[0, 0]
    me_row, me_col = places()
    scaling = SCALE / ordered_sum(stage, parts, me_row)
    scaling_out[...] = scaling
    for k in range(n_row):
        piece = shifted(me_row, k, n_row)
        for j in range(per):
            block = bases[k][:, j * BLK : (j + 1) * BLK].astype(F32)
            b = piece * per + j
            scaled[b, 0:cols] = (block * scaling_out[pl.ds(b, 1), :]).astype(BF16)
    high, mid, low = split3(scaling)
    shape = (PIECES, BLK)
    rows = lax.broadcasted_iota(jnp.int32, shape, 0)
    for b in range(scaling.shape[0]):
        value = jnp.where(
            rows == 0,
            jnp.broadcast_to(high[b : b + 1], shape),
            jnp.where(
                rows == 1,
                jnp.broadcast_to(mid[b : b + 1], shape),
                jnp.where(rows == 2, jnp.broadcast_to(low[b : b + 1], shape), 0.0),
            ),
        )
        scaled[b, cols : cols + PIECES] = value.astype(BF16)
    acc[...] = jnp.zeros_like(acc)

    def step(s):
        target = jnp.where(s < total, lists[0, 0, 0, s], blocks)
        sums = jnp.dot(scaled[lists[0, 0, 1, s]], tile[s], preferred_element_type=F32)
        acc[target] += sums[0 : cols + 8]

    slot_loop(step, total, 1, TILE_GROUP)
    core = lax.rem(me_col, 2)
    for q in range(n_col // 2):
        own = (2 * q + core) * per
        other = (2 * q + 1 - core) * per
        for j in range(per):
            keep[q, j] = acc[own + j, 0:cols]
            away[q, j] = acc[other + j, 0:cols].astype(BF16)
    row_part = jnp.sum(acc[0:blocks, cols : cols + 8], axis=1)
    for i, value in enumerate(pieces_of(row_part)):
        both[i * blocks : (i + 1) * blocks] = value
    for i in range(n_land):
        first = 3 * blocks + i * cols
        both[first : first + cols] = acc[marks[me_row * n_land + i] - me_row * blocks, 0:cols].astype(BF16)


def tile_body(profiles, cell_width, basis, block_lists, block_counts, landmarks):
    n_row, n_col = lax.axis_size("row"), lax.axis_size("col")
    n_chip = n_col // 2
    pcs, share = profiles.shape
    cols = basis.shape[0]
    per = share // BLK
    row_blocks, col_blocks = n_col * per, n_row * per
    slots = block_lists.shape[-1]
    n_land = landmarks.shape[0] // n_row

    def shape(*dims, dtype=F32):
        return jax.ShapeDtypeStruct(dims, dtype)

    (packed,) = call(
        tile_pack_kernel,
        [shape(FEAT, share, dtype=BF16)],
        vec(profiles, cell_width.reshape(1, share)),
        [pltpu.VMEM((FEAT, share), F32)],
    )
    spread = lax.ppermute(
        packed,
        ("row", "col"),
        [((q % n_row) * n_col + q // n_row, q) for q in range(n_row * n_col)],
    )
    row_packs = []
    for pack in chip_shifts(spread):
        row_packs += [pack, sibling(pack)]
    col_packs = shifts(packed, "row")
    bases = shifts(basis, "row")
    lists = [("smem", block_lists), ("smem", block_counts)]
    marks = [("smem", landmarks)]
    tile, part = call(
        functools.partial(tile_build_kernel, pcs, n_row, n_col),
        [pltpu.VMEM((slots, BLK, BLK), BF16), shape(col_blocks, BLK)],
        lists + vec(*col_packs, *row_packs),
        [
            pltpu.VMEM((row_blocks, FEAT, BLK), BF16),
            pltpu.VMEM((row_blocks, 8, BLK), F32),
            pltpu.VMEM((col_blocks, BLK, FEAT), BF16),
            pltpu.VMEM((col_blocks, BLK, BLK), F32),
            pltpu.VMEM((col_blocks + 1, 8, BLK), F32),
            pltpu.VMEM((2, row_blocks, PIECES, 2 * BLK), BF16),
        ],
    )
    for number in range(SWEEPS - 1):
        early = [("near", b) for b in bases[1:]] if number == 0 else []
        (part,) = call(
            functools.partial(tile_pass_kernel, True, n_row),
            [shape(row_blocks, BLK)],
            lists + [("keep", tile)] + vec(*shifts(part, "row")) + early,
            [
                pltpu.VMEM((n_row, col_blocks, BLK), F32),
                pltpu.VMEM((2, col_blocks, PIECES, 2 * BLK), BF16),
                pltpu.VMEM((row_blocks + 1, 8, BLK), F32),
            ],
        )
        (part,) = call(
            functools.partial(tile_pass_kernel, False, n_chip),
            [shape(col_blocks, BLK)],
            lists + [("keep", tile)] + vec(*chip_shifts(part + sibling(part))),
            [
                pltpu.VMEM((n_chip, row_blocks, BLK), F32),
                pltpu.VMEM((2, row_blocks, PIECES, 2 * BLK), BF16),
                pltpu.VMEM((col_blocks + 1, 8, BLK), F32),
            ],
        )
    both_rows = 3 * row_blocks + n_land * cols
    keep, away, both, col_scaling = call(
        functools.partial(tile_last_kernel, n_row, n_col, n_land),
        [
            shape(n_chip, per, cols, BLK),
            shape(n_chip, per, cols, BLK, dtype=BF16),
            shape(both_rows, BLK, dtype=BF16),
            shape(col_blocks, BLK),
        ],
        lists + marks + [("keep", tile)] + vec(*shifts(part, "row"), *bases),
        [
            pltpu.VMEM((n_row, col_blocks, BLK), F32),
            pltpu.VMEM((col_blocks, cols + PIECES, BLK), BF16),
            pltpu.VMEM((row_blocks + 1, cols + 8, BLK), F32),
        ],
    )
    pairs = call(
        pair_kernel,
        [shape(both_rows, BLK, dtype=BF16)]
        + [shape(per * cols, BLK, dtype=BF16)] * n_chip,
        vec(keep, sibling(away), both, sibling(both)),
    )
    sums = [pairs[0]] + [chip_shift(pairs[0], k) for k in range(1, n_chip)]
    shares = [pairs[1]] + [chip_shift(pairs[1 + k], k) for k in range(1, n_chip)]
    gram, row_scaling, own = call(
        functools.partial(gram_kernel, n_land, cols, per),
        [shape(cols, cols), shape(row_blocks, BLK), shape(per, BLK)],
        marks + vec(*sums),
        [
            pltpu.VMEM((row_blocks, BLK), F32),
            pltpu.VMEM((n_chip, row_blocks, BLK), F32),
            pltpu.VMEM((n_chip, n_land * cols, BLK), BF16),
        ],
    )
    (ritz,) = call(
        functools.partial(ritz_kernel, n_row, landmarks.shape[0] * BLK),
        [shape(cols, share)],
        vec(*shifts(gram, "row"), *shares, own),
        [pltpu.VMEM((n_row, cols, cols), F32)],
    )
    return row_scaling.reshape(-1), col_scaling.reshape(-1), ritz


def solution(mesh):
    placed = (
        P(None, ("col", "row")),
        P(("col", "row")),
        P(None, ("col", "row")),
        P("row", "col", None, None),
        P("row", "col"),
        P(),
    )
    return jax.shard_map(
        strip_body if mesh.shape["row"] <= STRIP_TILES else tile_body,
        mesh=mesh,
        in_specs=placed,
        out_specs=(P("row"), P("col"), P(None, ("row", "col"))),
        check_vma=False,
    )
```

```python
import functools

import jax
import jax.numpy as jnp
from jax import lax
from jax.experimental import pallas as pl
from jax.experimental.pallas import tpu as pltpu
from jax.sharding import PartitionSpec as P

BLK = 128
SWEEPS = 3
GROUP = 32
TILE_GROUP = 16
ROWS, COLUMNS, COUNT = 0, 1, 2
FEAT = 64
PACK = 56
PIECES = 16
SCALE = 512.0
LOG2E = 1.4426950408889634
F32 = jnp.float32
BF16 = jnp.bfloat16
MIB = 1 << 20
STRIP_TILES = 8

VMEM_SPEC = pl.BlockSpec(memory_space=pltpu.VMEM)
SMEM_SPEC = pl.BlockSpec(memory_space=pltpu.SMEM)


def split3(x):
    high = x.astype(BF16).astype(F32)
    mid = (x - high).astype(BF16).astype(F32)
    low = (x - high - mid).astype(BF16).astype(F32)
    return high, mid, low


def tree_sum(values):
    values = list(values)
    while len(values) > 1:
        values = [a + b for a, b in zip(values[::2], values[1::2])]
    return values[0]


def call(kernel, outs, ins, scratch=(), limit=24, flops=1 << 24):
    args, specs = [], []
    for kind, array in ins:
        if kind == "smem":
            specs.append(SMEM_SPEC)
        elif kind == "near":
            specs.append(pl.BlockSpec(memory_space=pl.ANY))
        elif kind == "hbm":
            specs.append(pl.BlockSpec(memory_space=pltpu.HBM))
            array = pltpu.with_memory_space_constraint(array, pltpu.HBM)
        else:
            specs.append(VMEM_SPEC)
            if kind == "keep":
                array = pltpu.with_memory_space_constraint(array, pltpu.VMEM)
        args.append(array)
    return pl.pallas_call(
        kernel,
        out_shape=tuple(outs),
        in_specs=specs,
        out_specs=tuple(VMEM_SPEC for _ in outs),
        scratch_shapes=list(scratch),
        compiler_params=pltpu.CompilerParams(vmem_limit_bytes=limit * MIB),
        cost_estimate=pl.CostEstimate(flops=flops, bytes_accessed=1 << 20, transcendentals=0),
    )(*args)


def pack_kernel(prof_hbm, width_hbm, lists_hbm, counts, out_ref, *scratch):
    work, prof_ref, width_ref, lists_ref, sems = scratch
    pairs = [
        (prof_hbm, prof_ref),
        (width_hbm, width_ref),
        (lists_hbm, lists_ref),
    ]
    copies = [pltpu.make_async_copy(a, b, sems.at[i]) for i, (a, b) in enumerate(pairs)]
    for copy in copies:
        copy.start()
    for copy in copies:
        copy.wait()
    pcs = prof_ref.shape[0]
    prof = prof_ref[...].astype(F32)
    norm = jnp.sum(prof * prof, axis=0, keepdims=True)
    high, mid, low = split3(norm)
    work[...] = jnp.zeros_like(work)
    work[0:pcs, :] = prof
    work[pcs : pcs + 1, :] = high
    work[pcs + 1 : pcs + 2, :] = mid
    work[pcs + 2 : pcs + 3, :] = low
    work[pcs + 3 : pcs + 4, :] = width_ref[...].astype(F32).reshape(1, -1)
    lists = lists_ref[0, 0].astype(F32)
    slots = slice(pcs + 4, pcs + 5)
    work[slots, 0:BLK] = lists[0:1]
    work[slots, BLK : 2 * BLK] = lists[1:2]
    count = jnp.full((1, BLK), counts[0, 0], jnp.int32)
    work[slots, 2 * BLK : 3 * BLK] = count.astype(F32)
    out_ref[...] = work[...].astype(BF16)


def places():
    return lax.axis_index("row"), lax.axis_index("col")


def stack_kernel(pcs, n, *refs):
    packs, (rest, table) = refs[:n], refs[-2:]
    me_row, _ = places()
    for k, pack in enumerate(packs):
        if k:
            rest[k - 1] = pack[...]
        slots = pack[:, 0 : 3 * BLK].astype(F32)[pcs + 4 : pcs + 5]
        for row in (ROWS, COLUMNS, COUNT):
            values = slots[:, row * BLK : (row + 1) * BLK].astype(jnp.int32)
            table[shifted(me_row, k, n), row : row + 1] = values


def slot_loop(step, count, size, group):
    def advance(number, carry):
        for i in range(0, group, size):
            step(*[number * group + i + j for j in range(size)])
        return carry

    lax.fori_loop(0, (count + group - 1) // group, advance, 0)


class Tile:
    def __init__(self, table, n_row, k, own, others):
        _, me_col = places()
        self.group = shifted(me_col // 2, k, n_row)
        self.table, self.k = table, k
        slots = own.shape[0]
        self.blocks, self.base = (own, 0) if k == 0 else (others, (k - 1) * slots)
        self.total = table[self.group * 8 + COUNT, 0]

    def group_size(self, times):
        return times * GROUP if self.k == 0 else GROUP

    def row(self, s):
        return self.table[self.group * 8 + ROWS, s]

    def column(self, s):
        return self.table[self.group * 8 + COLUMNS, s]

    def block(self, s):
        return self.blocks[self.base + s]


def shifted(me, k, n):
    return lax.rem(me + (n - k), n)


def ordered_sum(stage, refs, me):
    n = len(refs)
    for k, ref in enumerate(refs):
        stage[shifted(me, k, n)] = ref[...]
    return tree_sum([stage[i] for i in range(n)])


def square(tile, slots):
    a, b, c, d = [tile.block(s) for s in slots]
    return jnp.concatenate(
        [jnp.concatenate([a, b], axis=1), jnp.concatenate([c, d], axis=1)], axis=0
    )


def add_rows(acc, sums, firsts, targets):
    for (row, lane), target in zip(firsts, targets):
        acc[target] += sums[row : row + 8, lane : lane + BLK]


def row_sums(tile, wide, acc, row_blocks, spare):
    first = tile.group * row_blocks

    def step(s):
        product = tile.block(s).astype(F32) * wide[tile.column(s)]
        sums = jnp.sum(product.reshape(BLK // 8, 8, BLK), axis=0)
        acc[jnp.where(s < tile.total, first + tile.row(s), spare)] += sums

    slot_loop(step, tile.total, 1, tile.group_size(2))


def spread_lanes(wide, scaling):
    turned = scaling.T
    for b in range(scaling.shape[0]):
        wide[b] = jnp.broadcast_to(turned[:, b : b + 1], (BLK, BLK))


def col_sums(tile, left, acc, row_blocks, spare):
    first = tile.group * row_blocks

    def step(*slots):
        if left is None:
            rows = lax.broadcasted_iota(jnp.int32, (4 * PIECES, 2 * BLK), 0)
            lanes = lax.broadcasted_iota(jnp.int32, (4 * PIECES, 2 * BLK), 1)
            block = rows // PIECES
            pieces = (rows % PIECES == 0) & (block % 2 == lanes // BLK)
            pieces = pieces.astype(F32).astype(BF16)
        else:
            pieces = [left[i % 2, first + tile.row(s)] for i, s in enumerate(slots)]
            pieces = jnp.concatenate(pieces, axis=0)
        sums = lax.dot_general(
            pieces,
            square(tile, slots),
            (((1,), (1,)), ((), ())),
            preferred_element_type=F32,
        )
        firsts = [(0, 0), (PIECES, 0), (2 * PIECES, BLK), (3 * PIECES, BLK)]
        targets = [jnp.where(s < tile.total, tile.column(s), spare) for s in slots]
        add_rows(acc, sums, firsts, targets)

    slot_loop(step, tile.total, 4, tile.group_size(4))


def fill_pieces(left, scaling):
    high, mid, low = split3(scaling)
    shape = (PIECES, BLK)
    rows = lax.broadcasted_iota(jnp.int32, shape, 0)
    empty = jnp.zeros(shape, F32).astype(BF16)
    for b in range(scaling.shape[0]):
        value = jnp.where(
            rows == 0,
            jnp.broadcast_to(high[b : b + 1], shape),
            jnp.where(
                rows == 1,
                jnp.broadcast_to(mid[b : b + 1], shape),
                jnp.where(rows == 2, jnp.broadcast_to(low[b : b + 1], shape), 0.0),
            ),
        ).astype(BF16)
        left[0, b] = jnp.concatenate([value, empty], axis=1)
        left[1, b] = jnp.concatenate([empty, value], axis=1)


def build(tile, offset, row_prof, row_inv, col_prof, col_inv):
    def step(s):
        row, column = offset + tile.row(s), tile.column(s)
        distance = jnp.dot(col_prof[column], row_prof[row], preferred_element_type=F32)
        block = jnp.exp2(distance * col_inv[column] * row_inv[row][0:1, :])
        tile.blocks[tile.base + s] = block.astype(BF16)

    slot_loop(step, tile.total, 1, tile.group_size(2))


def piece_block(pieces, k, j):
    lanes = slice(j * BLK, (j + 1) * BLK)
    return pieces[0][:, lanes] if k == 0 else pieces[1][k - 1, :, lanes]


def fill_rows(pcs, sources, row_prof, row_inv, offset):
    me_row, me_col = places()
    n_row = sources[0][1].shape[0] + 1
    per = sources[0][0].shape[1] // BLK
    ones = lax.broadcasted_iota(jnp.int32, (FEAT - PACK, BLK), 0) < 3
    ones = ones.astype(F32)
    for i, pieces in enumerate(sources):
        core = lax.rem(me_col + i, 2)
        for k in range(n_row):
            piece = core * n_row + shifted(me_row, k, n_row)
            for j in range(per):
                block = piece_block(pieces, k, j).astype(F32)
                whole = jnp.concatenate([block, ones], axis=0)
                row_prof[offset + piece * per + j] = whole.astype(BF16)
                width = block[pcs + 3 : pcs + 4, :]
                row_inv[offset + piece * per + j] = jnp.broadcast_to(1.0 / width, (8, BLK))


def own_kernel(pcs, table, pack, rest, pack_in, rest_in, *refs):
    tile, col_prof, col_inv, sums, row_prof, row_inv, acc = refs[-7:]
    n_row = rest.shape[0] + 1
    per = pack.shape[1] // BLK
    me_row, _ = places()
    fill_rows(pcs, [(pack, rest), (pack_in, rest_in)], row_prof, row_inv, 0)
    rows = lax.broadcasted_iota(jnp.int32, (FEAT, BLK), 0)
    for k in range(n_row):
        piece = shifted(me_row, k, n_row)
        for j in range(per):
            block = piece_block((pack, rest), k, j).astype(F32)
            block = jnp.concatenate([block, jnp.zeros((FEAT - PACK, BLK), F32)], axis=0)
            turned = jnp.where(rows < pcs, -2.0 * block, 0.0)
            turned = jnp.where((rows >= pcs) & (rows < pcs + 3), 1.0, turned)
            turned = jnp.where(rows == PACK - 1, pltpu.roll(block, PACK - 4 - pcs, 0), turned)
            turned = jnp.where(
                (rows >= PACK) & (rows < PACK + 3), pltpu.roll(block, PACK - pcs, 0), turned
            )
            turned = turned.T
            col_prof[piece * per + j] = turned.astype(BF16)
            col_inv[piece * per + j] = jnp.broadcast_to(
                -LOG2E / turned[:, PACK - 1 : PACK], (BLK, BLK)
            )
    own = Tile(table, n_row, 0, tile, None)
    build(own, 0, row_prof, row_inv, col_prof, col_inv)
    sums[...] = column_totals([own], None, acc, row_prof.shape[0])


def column_totals(tiles, left, acc, row_blocks):
    col_blocks = acc.shape[0] - 1
    acc[...] = jnp.zeros_like(acc)
    for tile in tiles:
        col_sums(tile, left, acc, row_blocks, col_blocks)
    return jnp.sum(acc[0:col_blocks], axis=1)


def row_part(tiles, wide, acc, row_blocks, out):
    blocks = acc.shape[0] - 1
    acc[...] = jnp.zeros_like(acc)
    for tile in tiles:
        row_sums(tile, wide, acc, row_blocks, blocks)
    out[...] = jnp.sum(acc[0:blocks], axis=1)


def strip_kernel(pcs, n_row, *refs):
    table, own, col_prof, col_inv, own_sums = refs[:5]
    sources = [refs[i : i + 2] for i in range(5, 5 + 4 * (n_row - 1), 2)]
    others, out, row_prof, row_inv, wide, row_acc, col_acc = refs[-7:]
    row_blocks = row_prof.shape[0] // (n_row - 1)
    tiles = [Tile(table, n_row, k, own, others) for k in range(n_row)]
    for k in range(1, n_row):
        first = (k - 1) * row_blocks
        fill_rows(pcs, sources[2 * k - 2 : 2 * k], row_prof, row_inv, first)
    for k in range(1, n_row):
        first = (k - 1) * row_blocks
        build(tiles[k], first, row_prof, row_inv, col_prof, col_inv)
    totals = column_totals(tiles[1:], None, col_acc, row_blocks) + own_sums[...]
    spread_lanes(wide, SCALE / totals)
    row_part(tiles, wide, row_acc, row_blocks, out)


def row_scalings(stage, parts):
    for k, part in enumerate(parts):
        stage[shifted(places()[1] // 2, k, len(parts))] = part[...].astype(F32)
    return SCALE / tree_sum([stage[i] for i in range(len(parts))])


def sweep_kernel(n_row, n_chip, *refs):
    table, own, others = refs[:3]
    parts = refs[3 : 3 + n_chip]
    out, stage, row_left, wide, row_acc, col_acc = refs[-6:]
    row_blocks = out.shape[0] // n_row
    tiles = [Tile(table, n_row, k, own, others) for k in range(n_row)]
    fill_pieces(row_left, row_scalings(stage, parts))
    totals = column_totals(tiles, row_left, col_acc, row_blocks)
    spread_lanes(wide, SCALE / totals)
    row_part(tiles, wide, row_acc, row_blocks, out)


def pieces_of(value):
    return [v.astype(BF16) for v in split3(value)]


def last_kernel(n_row, n_chip, n_land, *refs):
    table, marks, own, others = refs[:4]
    parts, bases = refs[4 : 4 + n_chip], refs[4 + n_chip : 4 + n_chip + n_row]
    keep, away, both, scaling_out, stage, row_left, col_acc, scaled, acc = refs[-9:]
    cols = bases[0].shape[0]
    per = bases[0].shape[1] // BLK
    blocks = 2 * n_chip * per
    me_row, me_col = places()
    tiles = [Tile(table, n_row, k, own, others) for k in range(n_row)]
    fill_pieces(row_left, row_scalings(stage, parts))
    scaling = SCALE / column_totals(tiles, row_left, col_acc, blocks)
    scaling_out[...] = scaling
    for k in range(n_row):
        piece = lax.bitwise_xor(me_row, k)
        for j in range(per):
            block = bases[k][:, j * BLK : (j + 1) * BLK].astype(F32)
            b = piece * per + j
            scaled[b, 0:cols] = (block * scaling_out[pl.ds(b, 1), :]).astype(BF16)
    high, mid, low = split3(scaling)
    shape = (PIECES, BLK)
    rows = lax.broadcasted_iota(jnp.int32, shape, 0)
    for b in range(scaling.shape[0]):
        value = jnp.where(
            rows == 0,
            jnp.broadcast_to(high[b : b + 1], shape),
            jnp.where(
                rows == 1,
                jnp.broadcast_to(mid[b : b + 1], shape),
                jnp.where(rows == 2, jnp.broadcast_to(low[b : b + 1], shape), 0.0),
            ),
        )
        scaled[b, cols : cols + PIECES] = value.astype(BF16)
    acc[...] = jnp.zeros_like(acc)
    for k in range(n_row):
        tile = tiles[k]

        def step(s, tile=tile):
            target = jnp.where(s < tile.total, tile.row(s), blocks)
            sums = jnp.dot(scaled[tile.column(s)], tile.block(s), preferred_element_type=F32)
            acc[target] += sums[0 : cols + 8]

        slot_loop(step, jnp.where(tile.group == me_row, tile.total, 0), 1, tile.group_size(2))
    core = lax.rem(me_col, 2)
    for q in range(n_chip):
        mine = (2 * q + core) * per
        other = (2 * q + 1 - core) * per
        for j in range(per):
            keep[q, j] = acc[mine + j, 0:cols]
            away[q, j] = acc[other + j, 0:cols].astype(BF16)
    part = jnp.sum(acc[0:blocks, cols : cols + 8], axis=1)
    for i, value in enumerate(pieces_of(part)):
        both[i * blocks : (i + 1) * blocks] = value
    for i in range(n_land):
        first = 3 * blocks + i * cols
        both[first : first + cols] = acc[marks[me_row * n_land + i] - me_row * blocks, 0:cols].astype(BF16)


def three(ref, blocks):
    value = ref[0 : 3 * blocks].astype(F32)
    return (value[2 * blocks :] + value[blocks : 2 * blocks]) + value[0:blocks]


def pair_kernel(keep, away, both, both_in, both_out, *outs):
    n_chip, per, cols = keep.shape[:3]
    blocks = 2 * n_chip * per
    chip = places()[1] // 2
    parts = pieces_of(three(both, blocks) + three(both_in, blocks))
    for i, value in enumerate(parts):
        both_out[i * blocks : (i + 1) * blocks] = value
    lands = both[3 * blocks :].astype(F32) + both_in[3 * blocks :].astype(F32)
    both_out[3 * blocks :] = lands.astype(BF16)
    for k, out in enumerate(outs):
        to = lax.rem(chip + k, n_chip)
        for j in range(per):
            value = keep[to, j] + away[to, j].astype(F32)
            out[j * cols : (j + 1) * cols] = value.astype(BF16)


def gram_kernel(n_land, cols, per, *refs):
    marks = refs[0]
    gram, scaling_out, own, inverse, stage, land_stage = refs[-6:]
    parts = refs[1:-6]
    n = len(parts)
    me_row, me_col = places()
    blocks = scaling_out.shape[0]
    for k, part in enumerate(parts):
        place = shifted(me_col // 2, k, n)
        stage[place] = three(part, blocks)
        land_stage[place] = part[3 * blocks :]
    inverse[...] = 1.0 / tree_sum([stage[i] for i in range(n)])
    scaling_out[...] = SCALE * inverse[...]
    for j in range(per):
        own[j : j + 1, :] = inverse[pl.ds(me_col * per + j, 1), :]
    total = None
    for i in range(n_land):
        summed = tree_sum(
            [land_stage[k, i * cols : (i + 1) * cols].astype(F32) for k in range(n)]
        )
        block = marks[me_row * n_land + i] - me_row * blocks
        projected = summed * inverse[pl.ds(block, 1), :]
        product = lax.dot_general(
            projected,
            projected,
            (((1,), (1,)), ((), ())),
            precision=lax.Precision.HIGHEST,
            preferred_element_type=F32,
        )
        total = product if total is None else total + product
    gram[...] = total


WIDE = 4


def eliminate(gram):
    cols = gram.shape[0]
    rows = lax.broadcasted_iota(jnp.int32, (cols, 2 * cols), 0)
    lanes = lax.broadcasted_iota(jnp.int32, (cols, 2 * cols), 1)
    unit = (rows[:, :cols] == lanes[:, :cols]).astype(F32)
    work = jnp.concatenate([gram, unit], axis=1)
    for first in range(0, cols, WIDE):
        tops = [work[first + i : first + i + 1, :] for i in range(WIDE)]
        sides = [
            jnp.broadcast_to(work[:, first + i : first + i + 1], work.shape)
            for i in range(WIDE)
        ]
        change = None
        for i in range(WIDE):
            pivot = first + i
            inverse = 1.0 / sides[i][pivot : pivot + 1, :]
            unit_top = tops[i] * inverse
            for m in range(i + 1, WIDE):
                factor = sides[i][first + m : first + m + 1, :]
                tops[m] = tops[m] - factor * unit_top
                inner = factor * inverse
                sides[m] = sides[m] - sides[i] * inner
            term = sides[i] * unit_top
            change = term if change is None else change + term
        reduced = work - change
        kept = work
        for i in range(WIDE):
            kept = jnp.where(rows == first + i, tops[i], kept)
        work = jnp.where(rows >= first + WIDE, reduced, kept)
    pivots = jnp.sum(jnp.where(rows == lanes, work, 0.0), axis=1, keepdims=True)
    return (work * lax.rsqrt(pivots))[:, cols:]


def ritz_kernel(n_row, cells, *refs):
    grams, parts = refs[:n_row], refs[n_row:-3]
    own, out, stage = refs[-3:]
    cols = grams[0].shape[0]
    per = out.shape[1] // BLK
    inverse = eliminate(ordered_sum(stage, grams, places()[0]) * (1.0 / cells))
    for j in range(per):
        summed = tree_sum([m[j * cols : (j + 1) * cols].astype(F32) for m in parts])
        projected = summed * own[j : j + 1, :]
        out[:, j * BLK : (j + 1) * BLK] = jnp.dot(
            inverse, projected, precision=lax.Precision.HIGHEST, preferred_element_type=F32
        )


def swap(x, axis, k):
    return lax.ppermute(x, axis, [(i, i ^ k) for i in range(lax.axis_size(axis))])


def shift(x, axis, k):
    n = lax.axis_size(axis)
    return lax.ppermute(x, axis, [(i, (i + k) % n) for i in range(n)])


def shifts(x, axis):
    return [x] + [shift(x, axis, k) for k in range(1, lax.axis_size(axis))]


def chip_shift(x, k):
    n = lax.axis_size("col") // 2
    return lax.ppermute(
        x,
        "col",
        [(2 * q + p, 2 * ((q + k) % n) + p) for q in range(n) for p in range(2)],
    )


def chip_shifts(x):
    return [x] + [chip_shift(x, k) for k in range(1, lax.axis_size("col") // 2)]


def sibling(x):
    return swap(x, "col", 1)


def vec(*arrays):
    return [("vmem", a) for a in arrays]


def strip_body(profiles, cell_width, basis, block_lists, block_counts, landmarks):
    n_row, n_col = lax.axis_size("row"), lax.axis_size("col")
    n_chip = n_col // 2
    pcs, share = profiles.shape
    cols = basis.shape[0]
    per = share // BLK
    row_blocks, col_blocks = n_col * per, n_row * per
    all_rows = n_row * row_blocks
    slots = block_lists.shape[-1]
    n_land = landmarks.shape[0] // n_row

    def shape(*dims, dtype=F32):
        return jax.ShapeDtypeStruct(dims, dtype)

    (packed,) = call(
        pack_kernel,
        [shape(PACK, share, dtype=BF16)],
        [("hbm", a) for a in (profiles, cell_width, block_lists)] + [("smem", block_counts)],
        [
            pltpu.VMEM((PACK, share), F32),
            pltpu.VMEM(profiles.shape, BF16),
            pltpu.VMEM(cell_width.shape, BF16),
            pltpu.VMEM(block_lists.shape, jnp.int32),
            pltpu.SemaphoreType.DMA((3,)),
        ],
    )
    near = [chip_shift(packed, k) for k in range(1, n_chip)]
    near_in = [sibling(pack) for pack in near]
    pack_in = sibling(packed)
    rest, table = call(
        functools.partial(stack_kernel, pcs, n_row),
        [shape(n_row - 1, PACK, share, dtype=BF16), shape(n_row, 8, BLK, dtype=jnp.int32)],
        vec(*shifts(packed, "row")) + [("near", pack) for pack in near_in + [pack_in]],
    )
    table = ("smem", table.reshape(n_row * 8, BLK))
    marks = ("smem", landmarks)
    far = [chip_shift(rest, k) for k in range(1, n_chip)]
    own, col_prof, col_inv, sums = call(
        functools.partial(own_kernel, pcs),
        [
            pltpu.VMEM((slots, BLK, BLK), BF16),
            pltpu.VMEM((col_blocks, BLK, FEAT), BF16),
            pltpu.VMEM((col_blocks, BLK, BLK), F32),
            shape(col_blocks, BLK),
        ],
        [table] + vec(packed, rest, pack_in, sibling(rest)),
        [
            pltpu.VMEM((row_blocks, FEAT, BLK), BF16),
            pltpu.VMEM((row_blocks, 8, BLK), F32),
            pltpu.VMEM((col_blocks + 1, 8, BLK), F32),
        ],
    )
    basis, sums = lax.optimization_barrier((basis, sums))
    bases = [basis, swap(basis, "row", 1)]
    far, sums, bases = lax.optimization_barrier((far, sums, bases))
    stacks = []
    for pack, other, group in zip(near, near_in, far):
        stacks += [pack, group, other, sibling(group)]
    far_slots = (n_row - 1) * slots
    others, part = call(
        functools.partial(strip_kernel, pcs, n_row),
        [pltpu.VMEM((far_slots, BLK, BLK), BF16), shape(all_rows, BLK)],
        [table, ("keep", own), ("keep", col_prof), ("keep", col_inv)]
        + vec(sums, *stacks),
        [
            pltpu.VMEM((all_rows - row_blocks, FEAT, BLK), BF16),
            pltpu.VMEM((all_rows - row_blocks, 8, BLK), F32),
            pltpu.VMEM((col_blocks, BLK, BLK), F32),
            pltpu.VMEM((all_rows + 1, 8, BLK), F32),
            pltpu.VMEM((col_blocks + 1, 8, BLK), F32),
        ],
    )
    tiles = [("keep", own), ("keep", others)]

    def chip_parts(part):
        return chip_shifts((part + sibling(part)).astype(BF16))

    part, bases = lax.optimization_barrier((part, bases))
    while len(bases) < n_row:
        bases = bases + [swap(base, "row", len(bases)) for base in bases]
    for _ in range(SWEEPS - 2):
        (part,) = call(
            functools.partial(sweep_kernel, n_row, n_chip),
            [shape(all_rows, BLK)],
            [table] + tiles + vec(*chip_parts(part)) + [("near", base) for base in bases[2:]],
            [
                pltpu.VMEM((n_chip, all_rows, BLK), F32),
                pltpu.VMEM((2, all_rows, PIECES, 2 * BLK), BF16),
                pltpu.VMEM((col_blocks, BLK, BLK), F32),
                pltpu.VMEM((all_rows + 1, 8, BLK), F32),
                pltpu.VMEM((col_blocks + 1, 8, BLK), F32),
            ],
        )
    both_rows = 3 * row_blocks + n_land * cols
    keep, away, both, col_scaling = call(
        functools.partial(last_kernel, n_row, n_chip, n_land),
        [
            shape(n_chip, per, cols, BLK),
            shape(n_chip, per, cols, BLK, dtype=BF16),
            shape(both_rows, BLK, dtype=BF16),
            shape(col_blocks, BLK),
        ],
        [table, marks] + tiles + vec(*chip_parts(part), *bases),
        [
            pltpu.VMEM((n_chip, all_rows, BLK), F32),
            pltpu.VMEM((2, all_rows, PIECES, 2 * BLK), BF16),
            pltpu.VMEM((col_blocks + 1, 8, BLK), F32),
            pltpu.VMEM((col_blocks, cols + PIECES, BLK), BF16),
            pltpu.VMEM((row_blocks + 1, cols + 8, BLK), F32),
        ],
    )
    pairs = call(
        pair_kernel,
        [shape(both_rows, BLK, dtype=BF16)]
        + [shape(per * cols, BLK, dtype=BF16)] * n_chip,
        vec(keep, sibling(away), both, sibling(both)),
    )
    sums = [pairs[0]] + [chip_shift(pairs[0], k) for k in range(1, n_chip)]
    shares = [pairs[1]] + [chip_shift(pairs[1 + k], k) for k in range(1, n_chip)]
    gram, row_scaling, own = call(
        functools.partial(gram_kernel, n_land, cols, per),
        [shape(cols, cols), shape(row_blocks, BLK), shape(per, BLK)],
        [marks] + vec(*sums),
        [
            pltpu.VMEM((row_blocks, BLK), F32),
            pltpu.VMEM((n_chip, row_blocks, BLK), F32),
            pltpu.VMEM((n_chip, n_land * cols, BLK), BF16),
        ],
    )
    (ritz,) = call(
        functools.partial(ritz_kernel, n_row, landmarks.shape[0] * BLK),
        [shape(cols, share)],
        vec(*shifts(gram, "row"), *shares, own),
        [pltpu.VMEM((n_row, cols, cols), F32)],
    )
    return row_scaling.reshape(-1), col_scaling.reshape(-1), ritz


def tile_pack_kernel(prof_ref, width_ref, out_ref, work):
    pcs = prof_ref.shape[0]
    prof = prof_ref[...].astype(F32)
    norm = jnp.sum(prof * prof, axis=0, keepdims=True)
    high, mid, low = split3(norm)
    work[...] = jnp.zeros_like(work)
    work[0:pcs, :] = prof
    work[pcs : pcs + 1, :] = high
    work[pcs + 1 : pcs + 2, :] = mid
    work[pcs + 2 : pcs + 3, :] = low
    work[pcs + 3 : pcs + 6, :] = jnp.ones((3, prof.shape[1]), F32)
    work[pcs + 6 : pcs + 7, :] = width_ref[...].astype(F32)
    out_ref[...] = work[...].astype(BF16)


def tile_square(tile, slots):
    a, b, c, d = [tile[s] for s in slots]
    return jnp.concatenate(
        [jnp.concatenate([a, b], axis=1), jnp.concatenate([c, d], axis=1)], axis=0
    )


def tile_add_rows(acc, lists, target, slots, sums, total, spare, firsts):
    for i, (s, (row, lane)) in enumerate(zip(slots, firsts)):
        place = jnp.where(s < total, lists[0, 0, target, s], spare)
        acc[place] += sums[row : row + 8, lane : lane + BLK]


def tile_row_sums(lists, tile, left, acc, total, spare):
    def step(*slots):
        low = [left[0, lists[0, 0, 1, s]] for s in slots[:2]]
        high = [left[1, lists[0, 0, 1, s]] for s in slots[2:]]
        sums = jnp.dot(
            jnp.concatenate(low + high, axis=0),
            tile_square(tile, slots),
            preferred_element_type=F32,
        )
        firsts = [(0, 0), (PIECES, BLK), (2 * PIECES, 0), (3 * PIECES, BLK)]
        tile_add_rows(acc, lists, 0, slots, sums, total, spare, firsts)

    slot_loop(step, total, 4, 4 * TILE_GROUP)


def tile_col_sums(lists, tile, left, acc, total, spare):
    def step(*slots):
        pieces = [left[i % 2, lists[0, 0, 0, s]] for i, s in enumerate(slots)]
        sums = lax.dot_general(
            jnp.concatenate(pieces, axis=0),
            tile_square(tile, slots),
            (((1,), (1,)), ((), ())),
            preferred_element_type=F32,
        )
        firsts = [(0, 0), (PIECES, 0), (2 * PIECES, BLK), (3 * PIECES, BLK)]
        tile_add_rows(acc, lists, 1, slots, sums, total, spare, firsts)

    slot_loop(step, total, 4, 4 * TILE_GROUP)


def tile_build_kernel(pcs, n_row, n_col, *refs):
    lists, counts = refs[:2]
    col_in = refs[2 : 2 + n_row]
    row_in = refs[2 + n_row : 2 + n_row + n_col]
    tile, part, row_prof, row_inv, col_prof, col_inv, acc, left = refs[2 + n_row + n_col :]
    per = row_in[0].shape[1] // BLK
    col_blocks, row_blocks = n_row * per, n_col * per
    total = counts[0, 0]
    me_row, me_col = places()
    for k, ref in enumerate(row_in):
        core = lax.rem(me_col + k, 2)
        piece = shifted(me_col // 2, k // 2, n_col // 2) * 2 + core
        for j in range(per):
            block = ref[:, j * BLK : (j + 1) * BLK]
            row_prof[piece * per + j] = block
            width = block.astype(F32)[pcs + 6 : pcs + 7, :]
            row_inv[piece * per + j] = jnp.broadcast_to(1.0 / width, (8, BLK))
    rows = lax.broadcasted_iota(jnp.int32, (FEAT, BLK), 0)
    for k, ref in enumerate(col_in):
        piece = shifted(me_row, k, n_row)
        for j in range(per):
            block = ref[0:FEAT, j * BLK : (j + 1) * BLK].astype(F32)
            turned = jnp.where(rows < pcs, -2.0 * block, 0.0)
            turned = jnp.where((rows >= pcs) & (rows < pcs + 3), 1.0, turned)
            turned = jnp.where(
                (rows >= pcs + 3) & (rows < pcs + 6), pltpu.roll(block, 3, 0), turned
            )
            turned = jnp.where(rows == pcs + 7, pltpu.roll(block, 1, 0), turned)
            turned = turned.T
            col_prof[piece * per + j] = turned.astype(BF16)
            col_inv[piece * per + j] = jnp.broadcast_to(
                -LOG2E / turned[:, pcs + 7 : pcs + 8], (BLK, BLK)
            )

    def step(s):
        rb, cb = lists[0, 0, 0, s], lists[0, 0, 1, s]
        distance = jnp.dot(col_prof[cb], row_prof[rb], preferred_element_type=F32)
        block = jnp.exp2(distance * col_inv[cb] * row_inv[rb][0:1, :])
        tile[s] = block.astype(BF16)

    slot_loop(step, total, 1, TILE_GROUP)
    ones = (lax.broadcasted_iota(jnp.int32, (PIECES, BLK), 0) == 0).astype(F32).astype(BF16)
    empty = jnp.zeros_like(ones)
    for b in range(row_blocks):
        left[0, b] = jnp.concatenate([ones, empty], axis=1)
        left[1, b] = jnp.concatenate([empty, ones], axis=1)
    acc[...] = jnp.zeros_like(acc)
    tile_col_sums(lists, tile, left, acc, total, col_blocks)
    part[...] = jnp.sum(acc[0:col_blocks], axis=1)


def tile_pass_kernel(over_rows, n_parts, *refs):
    lists, counts, tile = refs[:3]
    parts = refs[3 : 3 + n_parts]
    out, stage, left, acc = refs[-4:]
    total = counts[0, 0]
    blocks = out.shape[0]
    me_row, me_col = places()
    scaling = SCALE / ordered_sum(stage, parts, me_row if over_rows else me_col // 2)
    fill_pieces(left, scaling)
    acc[...] = jnp.zeros_like(acc)
    (tile_row_sums if over_rows else tile_col_sums)(lists, tile, left, acc, total, blocks)
    out[...] = jnp.sum(acc[0:blocks], axis=1)


def tile_last_kernel(n_row, n_col, n_land, *refs):
    lists, counts, marks, tile = refs[:4]
    parts, bases = refs[4 : 4 + n_row], refs[4 + n_row : 4 + 2 * n_row]
    keep, away, both, scaling_out, stage, scaled, acc = refs[4 + 2 * n_row :]
    cols = bases[0].shape[0]
    per = bases[0].shape[1] // BLK
    blocks = n_col * per
    total = counts[0, 0]
    me_row, me_col = places()
    scaling = SCALE / ordered_sum(stage, parts, me_row)
    scaling_out[...] = scaling
    for k in range(n_row):
        piece = shifted(me_row, k, n_row)
        for j in range(per):
            block = bases[k][:, j * BLK : (j + 1) * BLK].astype(F32)
            b = piece * per + j
            scaled[b, 0:cols] = (block * scaling_out[pl.ds(b, 1), :]).astype(BF16)
    high, mid, low = split3(scaling)
    shape = (PIECES, BLK)
    rows = lax.broadcasted_iota(jnp.int32, shape, 0)
    for b in range(scaling.shape[0]):
        value = jnp.where(
            rows == 0,
            jnp.broadcast_to(high[b : b + 1], shape),
            jnp.where(
                rows == 1,
                jnp.broadcast_to(mid[b : b + 1], shape),
                jnp.where(rows == 2, jnp.broadcast_to(low[b : b + 1], shape), 0.0),
            ),
        )
        scaled[b, cols : cols + PIECES] = value.astype(BF16)
    acc[...] = jnp.zeros_like(acc)

    def step(s):
        target = jnp.where(s < total, lists[0, 0, 0, s], blocks)
        sums = jnp.dot(scaled[lists[0, 0, 1, s]], tile[s], preferred_element_type=F32)
        acc[target] += sums[0 : cols + 8]

    slot_loop(step, total, 1, TILE_GROUP)
    core = lax.rem(me_col, 2)
    for q in range(n_col // 2):
        own = (2 * q + core) * per
        other = (2 * q + 1 - core) * per
        for j in range(per):
            keep[q, j] = acc[own + j, 0:cols]
            away[q, j] = acc[other + j, 0:cols].astype(BF16)
    row_part = jnp.sum(acc[0:blocks, cols : cols + 8], axis=1)
    for i, value in enumerate(pieces_of(row_part)):
        both[i * blocks : (i + 1) * blocks] = value
    for i in range(n_land):
        first = 3 * blocks + i * cols
        both[first : first + cols] = acc[marks[me_row * n_land + i] - me_row * blocks, 0:cols].astype(BF16)


def tile_body(profiles, cell_width, basis, block_lists, block_counts, landmarks):
    n_row, n_col = lax.axis_size("row"), lax.axis_size("col")
    n_chip = n_col // 2
    pcs, share = profiles.shape
    cols = basis.shape[0]
    per = share // BLK
    row_blocks, col_blocks = n_col * per, n_row * per
    slots = block_lists.shape[-1]
    n_land = landmarks.shape[0] // n_row

    def shape(*dims, dtype=F32):
        return jax.ShapeDtypeStruct(dims, dtype)

    (packed,) = call(
        tile_pack_kernel,
        [shape(FEAT, share, dtype=BF16)],
        vec(profiles, cell_width.reshape(1, share)),
        [pltpu.VMEM((FEAT, share), F32)],
    )
    spread = lax.ppermute(
        packed,
        ("row", "col"),
        [((q % n_row) * n_col + q // n_row, q) for q in range(n_row * n_col)],
    )
    row_packs = []
    for pack in chip_shifts(spread):
        row_packs += [pack, sibling(pack)]
    col_packs = shifts(packed, "row")
    bases = shifts(basis, "row")
    lists = [("smem", block_lists), ("smem", block_counts)]
    marks = [("smem", landmarks)]
    tile, part = call(
        functools.partial(tile_build_kernel, pcs, n_row, n_col),
        [pltpu.VMEM((slots, BLK, BLK), BF16), shape(col_blocks, BLK)],
        lists + vec(*col_packs, *row_packs),
        [
            pltpu.VMEM((row_blocks, FEAT, BLK), BF16),
            pltpu.VMEM((row_blocks, 8, BLK), F32),
            pltpu.VMEM((col_blocks, BLK, FEAT), BF16),
            pltpu.VMEM((col_blocks, BLK, BLK), F32),
            pltpu.VMEM((col_blocks + 1, 8, BLK), F32),
            pltpu.VMEM((2, row_blocks, PIECES, 2 * BLK), BF16),
        ],
    )
    for number in range(SWEEPS - 1):
        early = [("near", b) for b in bases[1:]] if number == 0 else []
        (part,) = call(
            functools.partial(tile_pass_kernel, True, n_row),
            [shape(row_blocks, BLK)],
            lists + [("keep", tile)] + vec(*shifts(part, "row")) + early,
            [
                pltpu.VMEM((n_row, col_blocks, BLK), F32),
                pltpu.VMEM((2, col_blocks, PIECES, 2 * BLK), BF16),
                pltpu.VMEM((row_blocks + 1, 8, BLK), F32),
            ],
        )
        (part,) = call(
            functools.partial(tile_pass_kernel, False, n_chip),
            [shape(col_blocks, BLK)],
            lists + [("keep", tile)] + vec(*chip_shifts(part + sibling(part))),
            [
                pltpu.VMEM((n_chip, row_blocks, BLK), F32),
                pltpu.VMEM((2, row_blocks, PIECES, 2 * BLK), BF16),
                pltpu.VMEM((col_blocks + 1, 8, BLK), F32),
            ],
        )
    both_rows = 3 * row_blocks + n_land * cols
    keep, away, both, col_scaling = call(
        functools.partial(tile_last_kernel, n_row, n_col, n_land),
        [
            shape(n_chip, per, cols, BLK),
            shape(n_chip, per, cols, BLK, dtype=BF16),
            shape(both_rows, BLK, dtype=BF16),
            shape(col_blocks, BLK),
        ],
        lists + marks + [("keep", tile)] + vec(*shifts(part, "row"), *bases),
        [
            pltpu.VMEM((n_row, col_blocks, BLK), F32),
            pltpu.VMEM((col_blocks, cols + PIECES, BLK), BF16),
            pltpu.VMEM((row_blocks + 1, cols + 8, BLK), F32),
        ],
    )
    pairs = call(
        pair_kernel,
        [shape(both_rows, BLK, dtype=BF16)]
        + [shape(per * cols, BLK, dtype=BF16)] * n_chip,
        vec(keep, sibling(away), both, sibling(both)),
    )
    sums = [pairs[0]] + [chip_shift(pairs[0], k) for k in range(1, n_chip)]
    shares = [pairs[1]] + [chip_shift(pairs[1 + k], k) for k in range(1, n_chip)]
    gram, row_scaling, own = call(
        functools.partial(gram_kernel, n_land, cols, per),
        [shape(cols, cols), shape(row_blocks, BLK), shape(per, BLK)],
        marks + vec(*sums),
        [
            pltpu.VMEM((row_blocks, BLK), F32),
            pltpu.VMEM((n_chip, row_blocks, BLK), F32),
            pltpu.VMEM((n_chip, n_land * cols, BLK), BF16),
        ],
    )
    (ritz,) = call(
        functools.partial(ritz_kernel, n_row, landmarks.shape[0] * BLK),
        [shape(cols, share)],
        vec(*shifts(gram, "row"), *shares, own),
        [pltpu.VMEM((n_row, cols, cols), F32)],
    )
    return row_scaling.reshape(-1), col_scaling.reshape(-1), ritz


def solution(mesh):
    placed = (
        P(None, ("col", "row")),
        P(("col", "row")),
        P(None, ("col", "row")),
        P("row", "col", None, None),
        P("row", "col"),
        P(),
    )
    return jax.shard_map(
        strip_body if mesh.shape["row"] <= STRIP_TILES else tile_body,
        mesh=mesh,
        in_specs=placed,
        out_specs=(P("row"), P("col"), P(None, ("row", "col"))),
        check_vma=False,
    )
```
